32 devices in a mesh: ta: 4 (over y, x), gz: 4 (over z), gy: 2 (over core).
Axes of the slice: x: 2, y: 2, z: 4, core: 2. Of those that a mesh axis runs over, the one named last changes fastest.
Arguments:
- source: float32 [4, 3, 2, 24, 8, 256], P(None, None, None, 'ta', 'gz', 'gy'), may hold values from -810 to 810
- gauge_links: float32 [4, 3, 3, 2, 24, 8, 256], P(None, None, None, None, 'ta', 'gz', 'gy'), may hold values from -1 to 1, as said below
Outputs:
- residual: float32 [4, 3, 2, 24, 8, 256], P(None, None, None, 'ta', 'gz', 'gy')
- coefficients: float32 [3], replicated
The draws below stay inside these ranges and needn't reach their ends.
Inputs may be any that keep to these rules, and one draw needn't show every extreme that they name: `gauge_links`: each 3 x 3 link matrix, taken with its real and imaginary parts, is special unitary.
All inputs are finite; a program needn't handle non-finite values.
Results may differ from the reference program's by a relative error of at most 0.0022.
Values sent between devices are 32-bit elements; how exact they have to be, the bound alone decides.
No kernel may reach another device: no remote copies, remote signals or barrier semaphores. Data moves between devices by JAX's collectives and lax.ppermute only.
A program may use at most 64 MiB of HBM per device.

```python
import math
import jax
import jax.numpy as jnp
from jax import lax

X = 32
NT = 24
NZ = 8
NY = 8


def draw_source(key, part):
    key = jax.random.fold_in(key, 11)
    key_rough, key_scale = jax.random.split(key)
    block_shape = (4, 3, 2, NT, NZ, NY * X // 4)
    time_fraction = jnp.arange(NT, dtype=jnp.float32) / NT
    depth_fraction = jnp.arange(NZ, dtype=jnp.float32) / NZ
    column_fraction = (jnp.arange(NY * X) // X).astype(jnp.float32) / NY
    ramp_scale = jnp.exp(math.log(3.0) * (time_fraction[:, None, None] + depth_fraction[None, :, None] + column_fraction[None, None, :]))
    site_scale = jnp.exp(jax.random.uniform(key_scale, (NT, NZ, NY * X), jnp.float32, 0.0, math.log(10.0)))
    rough_block = jnp.clip(jax.random.normal(key_rough, block_shape, jnp.float32), -3.0, 3.0)
    rough_part = jnp.repeat(rough_block, 4, axis=5)
    return (rough_part * (site_scale * ramp_scale)).astype(jnp.float32)


def unit_pair(key, amount):
    key_mixing, key_first, key_second = jax.random.split(key, 3)
    mixing = jax.random.uniform(key_mixing, (amount,), jnp.float32, -0.3, 0.3)
    phase_first = jax.random.uniform(key_first, (amount,), jnp.float32, -0.3, 0.3)
    phase_second = jax.random.uniform(key_second, (amount,), jnp.float32, -0.3, 0.3)
    diagonal = jnp.cos(mixing) * jnp.exp(1j * phase_first)
    offdiag = jnp.sin(mixing) * jnp.exp(1j * phase_second)
    return (diagonal, offdiag)


def embed(diagonal, offdiag, lower_block):
    zeros_part = jnp.zeros_like(diagonal)
    ones_part = jnp.ones_like(diagonal)
    if lower_block:
        matrix_rows = [[ones_part, zeros_part, zeros_part], [zeros_part, diagonal, offdiag], [zeros_part, -jnp.conj(offdiag), jnp.conj(diagonal)]]
    else:
        matrix_rows = [[diagonal, offdiag, zeros_part], [-jnp.conj(offdiag), jnp.conj(diagonal), zeros_part], [zeros_part, zeros_part, ones_part]]
    return jnp.stack([jnp.stack(matrix_row, axis=-1) for matrix_row in matrix_rows], axis=-2)


def draw_gauge_links(key, part):
    key = jax.random.fold_in(key, 23)
    site_count = NT * NZ * NY * X
    amount = 4 * site_count
    block_keys = jax.random.split(key, 3)
    product = None
    for block_index, lower_block in ((0, False), (1, True), (2, False)):
        diagonal, offdiag = unit_pair(block_keys[block_index], amount)
        matrix = embed(diagonal, offdiag, lower_block)
        if product is None:
            product = matrix
        else:
            product = jnp.einsum('nij,njk->nik', product, matrix, precision=lax.Precision.HIGHEST)
    product = product.reshape(4, site_count, 3, 3).transpose(0, 2, 3, 1)
    stacked = jnp.stack([jnp.real(product), jnp.imag(product)], axis=3)
    return stacked.reshape(4, 3, 3, 2, NT, NZ, NY * X).astype(jnp.float32)


def setup_inputs(seed: int = 0) -> dict:
    key_of = jax.random.split(jax.random.key(seed), 3)
    return {
        "source": draw_source(jax.random.fold_in(key_of[2], 71), 0),
        "gauge_links": draw_gauge_links(jax.random.fold_in(key_of[2], 71), 0),
    }


hop_kappa = 0.19
epsilon = 1e-06
spin_table = (((1, 0), ((0.0, -1.0), (0.0, -1.0))), ((1, 0), ((-1.0, 0.0), (1.0, 0.0))), ((0, 1), ((0.0, -1.0), (0.0, 1.0))), ((0, 1), ((1.0, 0.0), (1.0, 0.0))))

def times_unit(component, factor):
    real_part = component[:, 0]
    imag_part = component[:, 1]
    return jnp.stack([factor[0] * real_part - factor[1] * imag_part, factor[0] * imag_part + factor[1] * real_part], axis=1)

def apply_lower(lower_spins, direction):
    spin_order, phases = spin_table[direction]
    return jnp.stack([times_unit(lower_spins[spin_order[spin_row]], phases[spin_row]) for spin_row in range(2)], axis=0)

def apply_dagger(half_spinor, direction):
    spin_order, phases = spin_table[direction]
    rows_out = []
    for spin_row in range(2):
        source_row = spin_order[spin_row]
        factor = (phases[source_row][0], -phases[source_row][1])
        rows_out.append(times_unit(half_spinor[source_row], factor))
    return jnp.stack(rows_out, axis=0)

def project(spinor, direction, parity):
    return spinor[0:2] + parity * apply_lower(spinor[2:4], direction)

def rebuild(half_spinor, direction, parity):
    return jnp.concatenate([half_spinor, parity * apply_dagger(half_spinor, direction)], axis=0)

def mul_link(gauge_link, half_spinor):
    link_real = gauge_link[:, :, 0][None]
    link_imag = gauge_link[:, :, 1][None]
    spin_real = half_spinor[:, :, 0][:, None]
    spin_imag = half_spinor[:, :, 1][:, None]
    out_real = lax.optimization_barrier(jnp.sum(link_real * spin_real - link_imag * spin_imag, axis=2))
    out_imag = lax.optimization_barrier(jnp.sum(link_real * spin_imag + link_imag * spin_real, axis=2))
    return jnp.stack([out_real, out_imag], axis=2)

def mul_link_dag(gauge_link, half_spinor):
    flipped = jnp.swapaxes(gauge_link, 0, 1)
    link_real = flipped[:, :, 0][None]
    link_imag = flipped[:, :, 1][None]
    spin_real = half_spinor[:, :, 0][:, None]
    spin_imag = half_spinor[:, :, 1][:, None]
    out_real = lax.optimization_barrier(jnp.sum(link_real * spin_real + link_imag * spin_imag, axis=2))
    out_imag = lax.optimization_barrier(jnp.sum(link_real * spin_imag - link_imag * spin_real, axis=2))
    return jnp.stack([out_real, out_imag], axis=2)

def gamma_five(spinor):
    return jnp.concatenate([spinor[0:2], -spinor[2:4]], axis=0)

def lattice_total(values):
    partial_sums = lax.optimization_barrier(jnp.sum(values, axis=(0, 1, 2)))
    while partial_sums.ndim > 0:
        partial_sums = lax.optimization_barrier(jnp.sum(partial_sums, axis=-1))
    return partial_sums

def wilson_full(spinor, links_in):
    time_index = jnp.arange(NT)[:, None, None, None]
    parity_ahead = jnp.where(time_index == NT - 1, -1.0, 1.0).astype(jnp.float32)
    parity_behind = jnp.where(time_index == 0, -1.0, 1.0).astype(jnp.float32)
    hopping = None
    for direction in range(4):
        lattice_dim = 6 - direction
        gauge_link = links_in[direction]
        ahead = jnp.roll(project(spinor, direction, -1.0), -1, lattice_dim)
        behind = jnp.roll(mul_link_dag(gauge_link, project(spinor, direction, 1.0)), 1, lattice_dim)
        if direction == 3:
            ahead = ahead * parity_ahead
            behind = behind * parity_behind
        term = rebuild(mul_link(gauge_link, ahead), direction, -1.0) + rebuild(behind, direction, 1.0)
        hopping = term if direction == 0 else hopping + term
    return spinor - hop_kappa * hopping

def reference(source, gauge_links):
    lattice_shape = (NT, NZ, NY, X)
    links_in = gauge_links.reshape(gauge_links.shape[:4] + lattice_shape)
    entries = source.size

    def square_apply(vector_in):
        return gamma_five(wilson_full(gamma_five(wilson_full(vector_in, links_in)), links_in))
    field = source.reshape(source.shape[:3] + lattice_shape)
    norm_start = jnp.sqrt(lattice_total(field * field) / entries + epsilon)
    first_vector = field / norm_start
    image_one = square_apply(first_vector)
    alpha_one = lattice_total(first_vector * image_one) / entries
    remain = image_one - alpha_one * first_vector
    beta_one = jnp.sqrt(lattice_total(remain * remain) / entries + epsilon)
    second = remain / beta_one
    image_two = square_apply(second) - beta_one * first_vector
    alpha_two = lattice_total(second * image_two) / entries
    residual = image_two - alpha_two * second
    return (residual.reshape(source.shape), jnp.stack([alpha_one, beta_one, alpha_two]))
```

```python
import functools

import jax
import jax.numpy as jnp
from jax import lax
from jax.experimental import pallas as pl
from jax.experimental.pallas import tpu as pltpu
from jax.sharding import PartitionSpec as P

X = 32

hop_kappa = 0.19
epsilon = 1e-06
spin_table = (
    ((1, 0), (-1j, -1j)),
    ((1, 0), (-1, 1)),
    ((0, 1), (-1j, 1j)),
    ((0, 1), (1, 1)),
)
SPIN_COLOUR = [(spin, colour) for spin in range(2) for colour in range(3)]


def add_phased(left, phase, right):
    phase = complex(phase)
    if phase == 1:
        return (left[0] + right[0], left[1] + right[1])
    if phase == -1:
        return (left[0] - right[0], left[1] - right[1])
    if phase == 1j:
        return (left[0] - right[1], left[1] + right[0])
    return (left[0] + right[1], left[1] - right[0])


def project(psi, direction, parity):
    order, phases = spin_table[direction]
    return {
        (s, c): add_phased(psi[s, c], parity * phases[s], psi[2 + order[s], c])
        for s, c in SPIN_COLOUR
    }


def add_rebuilt(total, half, direction, parity):
    order, phases = spin_table[direction]
    for s, c in SPIN_COLOUR:
        total[s, c] = add_phased(total[s, c], 1, half[s, c])
        row = order[s]
        phase = parity * complex(phases[row]).conjugate()
        total[2 + s, c] = add_phased(total[2 + s, c], phase, half[row, c])


def mul_link(links, direction, z, half):
    out = {}
    for row in range(3):
        for s in range(2):
            real, imag = None, None
            for col in range(3):
                u_real, u_imag = links[direction, row, col, z]
                h_real, h_imag = half[s, col]
                term_real = u_real * h_real - u_imag * h_imag
                term_imag = u_real * h_imag + u_imag * h_real
                real = term_real if real is None else real + term_real
                imag = term_imag if imag is None else imag + term_imag
            out[s, row] = (real, imag)
    return out


def mul_link_dag(links, direction, z, half):
    out = {}
    for row in range(3):
        for s in range(2):
            real, imag = None, None
            for col in range(3):
                u_real, u_imag = links[direction, col, row, z]
                h_real, h_imag = half[s, col]
                term_real = u_real * h_real + u_imag * h_imag
                term_imag = u_real * h_imag - u_imag * h_real
                real = term_real if real is None else real + term_real
                imag = term_imag if imag is None else imag + term_imag
            out[s, row] = (real, imag)
    return out


def mapped(function, *halves):
    return {
        key: tuple(function(*(half[key][part] for half in halves)) for part in range(2))
        for key in SPIN_COLOUR
    }


class Links:
    def __init__(self, ref):
        self.ref = ref

    def __getitem__(self, index):
        direction, row, col, z = index
        first = ((direction * 3 + row) * 3 + col) * 2
        return (self.ref[first, z], self.ref[first + 1, z])


def load_psi(ref, z):
    return {
        (s, c): (ref[(s * 3 + c) * 2, z], ref[(s * 3 + c) * 2 + 1, z])
        for s in range(4)
        for c in range(3)
    }


def load_half(ref, z):
    return {
        (s, c): (ref[(s * 3 + c) * 2, z], ref[(s * 3 + c) * 2 + 1, z]) for s, c in SPIN_COLOUR
    }


def store_half(ref, z, half):
    for (s, c), pair in half.items():
        for part in range(2):
            ref[(s * 3 + c) * 2 + part, z] = pair[part]


class Shape:
    def __init__(self, t_extent, z_extent, lanes):
        self.t = t_extent
        self.z = z_extent
        self.rows = -(-t_extent // 8) * 8
        self.lanes = lanes

    def row(self):
        return lax.broadcasted_iota(jnp.int32, (self.rows, self.lanes), 0)

    def lane(self):
        return lax.broadcasted_iota(jnp.int32, (self.rows, self.lanes), 1)


def emit_messages(shape, psi_ref, links, refs):
    y_msg, z_up, z_down, t_up, t_down, carried_y, carried_t = refs
    lane = shape.lane()
    last_z, last_t = shape.z - 1, shape.t - 1
    for z in range(shape.z):
        psi = load_psi(psi_ref, z)
        minus = project(psi, 3, -1)
        carried = mul_link_dag(links, 3, z, project(psi, 3, 1))
        store_half(carried_t, z, carried)
        for s, c in SPIN_COLOUR:
            for part in range(2):
                at = ((s * 3 + c) * 2 + part) * shape.z + z
                t_down[at : at + 1] = minus[s, c][part][0:1]
                t_up[at : at + 1] = carried[s, c][part][last_t : last_t + 1]
        if z == 0:
            minus = project(psi, 2, -1)
            for s, c in SPIN_COLOUR:
                for part in range(2):
                    at = ((s * 3 + c) * 2 + part) * shape.t
                    z_down[at : at + shape.t] = minus[s, c][part][0 : shape.t]
        if z == last_z:
            carried = mul_link_dag(links, 2, z, project(psi, 2, 1))
            for s, c in SPIN_COLOUR:
                for part in range(2):
                    at = ((s * 3 + c) * 2 + part) * shape.t
                    z_up[at : at + shape.t] = carried[s, c][part][0 : shape.t]
        minus = project(psi, 1, -1)
        carried = mul_link_dag(links, 1, z, project(psi, 1, 1))
        store_half(carried_y, z, carried)
        store_half(
            y_msg,
            z,
            mapped(lambda low, high: jnp.where(lane < X, low, high), minus, carried),
        )


def prep_kernel(shape, sign_ref, source_ref, links_in, psi_ref, links_ref, dot_ref, *messages):
    t, z_extent = shape.t, shape.z
    if shape.rows != t:
        links_ref[...] = jnp.zeros_like(links_ref)
        psi_ref[...] = jnp.zeros_like(psi_ref)
    last = lax.broadcasted_iota(jnp.int32, (t, shape.lanes), 0) == t - 1
    flip = jnp.where(last, sign_ref[0], 1.0)
    for k in range(72):
        for z in range(z_extent):
            value = links_in[pl.ds(k * t * z_extent + z, t, stride=z_extent), :]
            links_ref[k, z, 0:t] = value * flip if k >= 54 else value
    for k in range(24):
        for z in range(z_extent):
            psi_ref[k, z, 0:t] = source_ref[pl.ds(k * t * z_extent + z, t, stride=z_extent), :]
    dot_ref[...] = dot_block(shape, [(psi_ref, psi_ref)])
    emit_messages(shape, psi_ref, Links(links_ref), messages)


def dot_block(shape, pairs):
    rows = []
    for left, right in pairs:
        total = None
        for k in range(24):
            for z in range(shape.z):
                term = left[k, z] * right[k, z]
                total = term if total is None else total + term
        rows.append(jnp.sum(total, axis=0, keepdims=True))
    rows += [jnp.zeros((1, shape.lanes), jnp.float32)] * (8 - len(rows))
    return jnp.concatenate(rows, axis=0)


def inner_kernel(shape, psi_ref, links_ref, total_ref):
    links = Links(links_ref)
    x = shape.lane() % X
    lanes = shape.lanes
    at_end, at_start = x == X - 1, x == 0

    def ahead(value):
        return jnp.where(
            at_end, pltpu.roll(value, X - 1, 1), pltpu.roll(value, lanes - 1, 1)
        )

    def behind(value):
        return jnp.where(at_start, pltpu.roll(value, lanes - X + 1, 1), pltpu.roll(value, 1, 1))

    for z in range(shape.z):
        psi = load_psi(psi_ref, z)
        zero = jnp.zeros((shape.rows, lanes), jnp.float32)
        total = {key: (zero, zero) for key in psi}
        half = mapped(ahead, project(psi, 0, -1))
        add_rebuilt(total, mul_link(links, 0, z, half), 0, -1)
        half = mapped(behind, mul_link_dag(links, 0, z, project(psi, 0, 1)))
        add_rebuilt(total, half, 0, 1)
        if z + 1 < shape.z:
            half = project(load_psi(psi_ref, z + 1), 2, -1)
            add_rebuilt(total, mul_link(links, 2, z, half), 2, -1)
        if z > 0:
            half = project(load_psi(psi_ref, z - 1), 2, 1)
            add_rebuilt(total, mul_link_dag(links, 2, z - 1, half), 2, 1)
        for (s, c), pair in total.items():
            for part in range(2):
                total_ref[(s * 3 + c) * 2 + part, z] = pair[part]


def finish_hops(shape, psi_ref, links, total_ref, halo, carried_y, carried_t, store):
    y_msg, z_up, z_down, t_up, t_down = halo
    lane, row = shape.lane(), shape.row()
    lanes, rows, t = shape.lanes, shape.rows, shape.t
    last_z = shape.z - 1

    for z in range(shape.z):
        psi = load_psi(psi_ref, z)
        total = load_psi(total_ref, z)

        def rim_rows(ref):
            half = {}
            for s, c in SPIN_COLOUR:
                ats = [((s * 3 + c) * 2 + part) * shape.z + z for part in range(2)]
                half[s, c] = tuple(
                    jnp.broadcast_to(ref[at : at + 1], (rows, lanes)) for at in ats
                )
            return half

        def rim_plane(ref):
            half = {}
            for s, c in SPIN_COLOUR:
                pair = []
                for part in range(2):
                    at = ((s * 3 + c) * 2 + part) * t
                    plane = ref[at : at + t]
                    if rows != t:
                        pad = jnp.zeros((rows - t, lanes), jnp.float32)
                        plane = jnp.concatenate([plane, pad], axis=0)
                    pair.append(plane)
                half[s, c] = tuple(pair)
            return half

        received = load_half(y_msg, z)
        half = mapped(
            lambda own, other: pltpu.roll(jnp.where(lane < X, other, own), lanes - X, 1),
            project(psi, 1, -1),
            received,
        )
        add_rebuilt(total, mul_link(links, 1, z, half), 1, -1)
        half = mapped(
            lambda own, other: pltpu.roll(jnp.where(lane >= lanes - X, other, own), X, 1),
            load_half(carried_y, z),
            received,
        )
        add_rebuilt(total, half, 1, 1)
        if z == last_z:
            add_rebuilt(total, mul_link(links, 2, z, rim_plane(z_down)), 2, -1)
        if z == 0:
            add_rebuilt(total, rim_plane(z_up), 2, 1)
        half = mapped(
            lambda own, other: jnp.where(row == t - 1, other, pltpu.roll(own, rows - 1, 0)),
            project(psi, 3, -1),
            rim_rows(t_down),
        )
        add_rebuilt(total, mul_link(links, 3, z, half), 3, -1)
        half = mapped(
            lambda own, other: jnp.where(row == 0, other, pltpu.roll(own, 1, 0)),
            load_half(carried_t, z),
            rim_rows(t_up),
        )
        add_rebuilt(total, half, 3, 1)
        for (s, c), pair in total.items():
            for part in range(2):
                value = psi[s, c][part] - hop_kappa * pair[part]
                value = value if s < 2 else -value
                if rows != t:
                    value = jnp.where(row < t, value, 0.0)
                store((s * 3 + c) * 2 + part, z, value)


def mid_kernel(shape, what, entries, *refs):
    psi_ref, links_ref, total_ref, carried_y, carried_t = refs[:5]
    halo = refs[5:10]
    extra = refs[10 : 10 + {"first": 1, "plain": 0, "dots": 4}[what]]
    rest = refs[10 + len(extra) :]
    out_ref, rest = rest[0], rest[1:]
    links = Links(links_ref)

    def store(k, z, value):
        out_ref[k, z] = value

    finish_hops(shape, psi_ref, links, total_ref, halo, carried_y, carried_t, store)
    if what == "first":
        dot_ref, rest = rest[0], rest[1:]
        block = dot_block(shape, [(out_ref, out_ref)])
        dot_ref[...] = jnp.concatenate([extra[0][0:1], block[0:1], block[2:8]], axis=0)
    if what == "dots":
        dot_ref, rest = rest[0], rest[1:]
        source_ref, one_ref, gathered = extra[0], extra[1], extra[2]
        _, alpha_one = first_scalars(gathered, entries)
        sums = [None] * 3
        for k in range(24):
            for z in range(shape.z):
                start = source_ref[k, z]
                remain = psi_ref[k, z] - alpha_one * start
                image = out_ref[k, z] - alpha_one * one_ref[k, z]
                terms = (remain * remain, remain * start, image * image)
                sums = [b if a is None else a + b for a, b in zip(sums, terms)]
        rows = [jnp.sum(value, axis=0, keepdims=True) for value in sums]
        rows.append(jnp.zeros((5, shape.lanes), jnp.float32))
        dot_ref[...] = jnp.concatenate(rows, axis=0)
    emit_messages(shape, out_ref, links, rest)


def gathered_sums(gathered, count):
    blocks = gathered.shape[0] // 8
    block = gathered[0:8]
    if blocks <= 64:
        for k in range(1, blocks):
            block = block + gathered[8 * k : 8 * k + 8]
    else:
        block = lax.fori_loop(
            1, blocks, lambda k, acc: acc + gathered[pl.ds(pl.multiple_of(8 * k, 8), 8)], block
        )
    column = jnp.sum(block, axis=1, keepdims=True)
    return [column[k : k + 1] for k in range(count)]


def first_scalars(gathered, entries):
    square, image = gathered_sums(gathered, 2)
    norm_square = square / entries + epsilon
    return norm_square, (image / entries) / norm_square


def last_kernel(
    shape, entries, psi_ref, links_ref, total_ref, carried_y, carried_t,
    y_msg, z_up, z_down, t_up, t_down,
    source_ref, two_ref, gathered_one, gathered_two, out_ref, coefficients,
):
    norm_square, alpha_one = first_scalars(gathered_one, entries)
    remain_square, overlap, image_square = gathered_sums(gathered_two, 3)
    norm = jnp.sqrt(norm_square)
    beta_one = jnp.sqrt(remain_square / entries / norm_square + epsilon)
    scale = 1.0 / (norm * beta_one)
    overlap = overlap / entries / (norm_square * beta_one)
    alpha_two = image_square / entries / (norm_square * beta_one * beta_one) - beta_one * overlap
    first_factor = beta_one / norm
    t, z_extent = shape.t, shape.z

    def store(k, z, value):
        two, start = two_ref[k, z], source_ref[k, z]
        remain = two - alpha_one * start
        result = (value - alpha_one * two - alpha_two * remain) * scale - first_factor * start
        out_ref[pl.ds(k * t * z_extent + z, t, stride=z_extent), :] = result[0:t]

    finish_hops(
        shape, psi_ref, Links(links_ref), total_ref,
        (y_msg, z_up, z_down, t_up, t_down), carried_y, carried_t, store,
    )
    coefficients[0] = alpha_one[0, 0]
    coefficients[1] = beta_one[0, 0]
    coefficients[2] = alpha_two[0, 0]


def send(value, axis, step):
    count = lax.axis_size(axis)
    return lax.ppermute(value, axis, [(i, (i + step) % count) for i in range(count)])


def exchange(messages, lanes):
    y_msg, z_up, z_down, t_up, t_down = messages
    z_halo = send(z_up, "gz", 1), send(z_down, "gz", -1)
    t_halo = send(t_up, "ta", 1), send(t_down, "ta", -1)
    if lax.axis_size("gy") == 2:
        y_halo = send(y_msg, "gy", 1)
    else:
        lane = lax.broadcasted_iota(jnp.int32, y_msg.shape, y_msg.ndim - 1)
        y_halo = jnp.where(lane < lanes // 2, send(y_msg, "gy", -1), send(y_msg, "gy", 1))
    return (y_halo, *z_halo, *t_halo)


def shards(source, gauge_links):
    devices_all = lax.axis_size("ta") * lax.axis_size("gz") * lax.axis_size("gy")
    entries = float(source.size * devices_all)
    shape = Shape(source.shape[3], source.shape[4], source.shape[5])
    t, z, rows, lanes = shape.t, shape.z, shape.rows, shape.lanes
    everywhere = ("ta", "gz", "gy")
    vmem = pl.BlockSpec(memory_space=pltpu.VMEM)
    smem = pl.BlockSpec(memory_space=pltpu.SMEM)

    def held(*dims):
        return pltpu.VMEM(dims, jnp.float32)

    field = held(24, z, rows, lanes)
    half = held(12, z, rows, lanes)
    dots = held(8, lanes)
    messages = (
        half, held(12 * t, lanes), held(12 * t, lanes), held(12 * z, lanes), held(12 * z, lanes),
        half, half,
    )

    def call(kernel, name, flops, out_shape, out_specs=None, in_specs=None):
        def run(*operands):
            return pl.pallas_call(
                kernel,
                name=name,
                out_shape=out_shape,
                in_specs=in_specs or [vmem] * len(operands),
                out_specs=out_specs or jax.tree.map(lambda _: vmem, out_shape),
                cost_estimate=pl.CostEstimate(
                    flops=flops, bytes_accessed=1 << 20, transcendentals=0
                ),
            )(*operands)

        return run

    sites = t * z * lanes
    is_last = lax.axis_index("ta") == lax.axis_size("ta") - 1
    sign = jnp.where(is_last, -1.0, 1.0).astype(jnp.float32).reshape(1)
    psi, links, dot_zero, *sent = call(
        functools.partial(prep_kernel, shape), "prep", 400 * sites,
        (field, held(72, z, rows, lanes), dots, *messages), in_specs=[smem, vmem, vmem],
    )(sign, source.reshape(24 * t * z, lanes), gauge_links.reshape(72 * t * z, lanes))
    start = psi
    powers = [psi]
    gathered = []
    for step in range(4):
        halo = exchange(sent[:5], lanes)
        carried = sent[5:]
        total = call(functools.partial(inner_kernel, shape), "inner", 700 * sites, field)(
            psi, links
        )
        operands = (psi, links, total, *carried, *halo)
        if step == 0:
            kernel = functools.partial(mid_kernel, shape, "first", entries)
            psi, dot, *sent = call(kernel, "mid_first", 1000 * sites, (field, dots, *messages))(
                *operands, dot_zero
            )
            gathered.append(lax.all_gather(dot, everywhere, tiled=True))
        elif step == 1:
            kernel = functools.partial(mid_kernel, shape, "plain", entries)
            psi, *sent = call(kernel, "mid_plain", 1000 * sites, (field, *messages))(*operands)
        elif step == 2:
            kernel = functools.partial(mid_kernel, shape, "dots", entries)
            psi, dot, *sent = call(kernel, "mid_dots", 1000 * sites, (field, dots, *messages))(
                *operands, start, powers[1], gathered[0], dot_zero
            )
            gathered.append(lax.all_gather(dot, everywhere, tiled=True))
        else:
            residual, coefficients = call(
                functools.partial(last_kernel, shape, entries), "last", 1000 * sites,
                (
                    jax.ShapeDtypeStruct((24 * t * z, lanes), jnp.float32),
                    jax.ShapeDtypeStruct((3,), jnp.float32),
                ),
                out_specs=(vmem, smem),
            )(*operands, start, powers[2], *gathered)
        powers.append(psi)
    return (residual.reshape(source.shape), coefficients)


def solution(mesh):
    placed = (P(None, None, None, "ta", "gz", "gy"), P(None, None, None, None, "ta", "gz", "gy"))
    return jax.shard_map(
        shards,
        mesh=mesh,
        in_specs=placed,
        out_specs=(P(None, None, None, "ta", "gz", "gy"), P()),
        check_vma=False,
    )
```

```python
import functools

import jax
import jax.numpy as jnp
from jax import lax
from jax.experimental import pallas as pl
from jax.experimental.pallas import tpu as pltpu
from jax.sharding import PartitionSpec as P

X = 32

hop_kappa = 0.19
epsilon = 1e-06
spin_table = (
    ((1, 0), (-1j, -1j)),
    ((1, 0), (-1, 1)),
    ((0, 1), (-1j, 1j)),
    ((0, 1), (1, 1)),
)
SPIN_COLOUR = [(spin, colour) for spin in range(2) for colour in range(3)]


def add_phased(left, phase, right):
    phase = complex(phase)
    if phase == 1:
        return (left[0] + right[0], left[1] + right[1])
    if phase == -1:
        return (left[0] - right[0], left[1] - right[1])
    if phase == 1j:
        return (left[0] - right[1], left[1] + right[0])
    return (left[0] + right[1], left[1] - right[0])


def project(psi, direction, parity):
    order, phases = spin_table[direction]
    return {
        (s, c): add_phased(psi[s, c], parity * phases[s], psi[2 + order[s], c])
        for s, c in SPIN_COLOUR
    }


def add_rebuilt(total, half, direction, parity):
    order, phases = spin_table[direction]
    for s, c in SPIN_COLOUR:
        total[s, c] = add_phased(total[s, c], 1, half[s, c])
        row = order[s]
        phase = parity * complex(phases[row]).conjugate()
        total[2 + s, c] = add_phased(total[2 + s, c], phase, half[row, c])


def mul_link(links, direction, z, half):
    out = {}
    for row in range(3):
        for s in range(2):
            real, imag = None, None
            for col in range(3):
                u_real, u_imag = links[direction, row, col, z]
                h_real, h_imag = half[s, col]
                term_real = u_real * h_real - u_imag * h_imag
                term_imag = u_real * h_imag + u_imag * h_real
                real = term_real if real is None else real + term_real
                imag = term_imag if imag is None else imag + term_imag
            out[s, row] = (real, imag)
    return out


def mul_link_dag(links, direction, z, half):
    out = {}
    for row in range(3):
        for s in range(2):
            real, imag = None, None
            for col in range(3):
                u_real, u_imag = links[direction, col, row, z]
                h_real, h_imag = half[s, col]
                term_real = u_real * h_real + u_imag * h_imag
                term_imag = u_real * h_imag - u_imag * h_real
                real = term_real if real is None else real + term_real
                imag = term_imag if imag is None else imag + term_imag
            out[s, row] = (real, imag)
    return out


def mapped(function, *halves):
    return {
        key: tuple(function(*(half[key][part] for half in halves)) for part in range(2))
        for key in SPIN_COLOUR
    }


class Links:
    def __init__(self, ref):
        self.ref = ref

    def __getitem__(self, index):
        direction, row, col, z = index
        first = ((direction * 3 + row) * 3 + col) * 2
        return (self.ref[first, z], self.ref[first + 1, z])


def load_psi(ref, z):
    return {
        (s, c): (ref[(s * 3 + c) * 2, z], ref[(s * 3 + c) * 2 + 1, z])
        for s in range(4)
        for c in range(3)
    }


def load_half(ref, z):
    return {
        (s, c): (ref[(s * 3 + c) * 2, z], ref[(s * 3 + c) * 2 + 1, z]) for s, c in SPIN_COLOUR
    }


def store_half(ref, z, half):
    for (s, c), pair in half.items():
        for part in range(2):
            ref[(s * 3 + c) * 2 + part, z] = pair[part]


class Shape:
    def __init__(self, t_extent, z_extent, lanes):
        self.t = t_extent
        self.z = z_extent
        self.rows = -(-t_extent // 8) * 8
        self.lanes = lanes

    def row(self):
        return lax.broadcasted_iota(jnp.int32, (self.rows, self.lanes), 0)

    def lane(self):
        return lax.broadcasted_iota(jnp.int32, (self.rows, self.lanes), 1)


def emit_messages(shape, psi_ref, links, refs):
    y_msg, z_up, z_down, t_up, t_down, carried_y, carried_t = refs
    lane = shape.lane()
    last_z, last_t = shape.z - 1, shape.t - 1
    for z in range(shape.z):
        psi = load_psi(psi_ref, z)
        minus = project(psi, 3, -1)
        carried = mul_link_dag(links, 3, z, project(psi, 3, 1))
        store_half(carried_t, z, carried)
        for s, c in SPIN_COLOUR:
            for part in range(2):
                at = ((s * 3 + c) * 2 + part) * shape.z + z
                t_down[at : at + 1] = minus[s, c][part][0:1]
                t_up[at : at + 1] = carried[s, c][part][last_t : last_t + 1]
        if z == 0:
            minus = project(psi, 2, -1)
            for s, c in SPIN_COLOUR:
                for part in range(2):
                    at = ((s * 3 + c) * 2 + part) * shape.t
                    z_down[at : at + shape.t] = minus[s, c][part][0 : shape.t]
        if z == last_z:
            carried = mul_link_dag(links, 2, z, project(psi, 2, 1))
            for s, c in SPIN_COLOUR:
                for part in range(2):
                    at = ((s * 3 + c) * 2 + part) * shape.t
                    z_up[at : at + shape.t] = carried[s, c][part][0 : shape.t]
        minus = project(psi, 1, -1)
        carried = mul_link_dag(links, 1, z, project(psi, 1, 1))
        store_half(carried_y, z, carried)
        store_half(
            y_msg,
            z,
            mapped(lambda low, high: jnp.where(lane < X, low, high), minus, carried),
        )


def prep_kernel(shape, sign_ref, source_ref, links_in, psi_ref, links_ref, dot_ref, *messages):
    t, z_extent = shape.t, shape.z
    if shape.rows != t:
        links_ref[...] = jnp.zeros_like(links_ref)
        psi_ref[...] = jnp.zeros_like(psi_ref)
    last = lax.broadcasted_iota(jnp.int32, (t, shape.lanes), 0) == t - 1
    flip = jnp.where(last, sign_ref[0], 1.0)
    for k in range(72):
        for z in range(z_extent):
            value = links_in[pl.ds(k * t * z_extent + z, t, stride=z_extent), :]
            links_ref[k, z, 0:t] = value * flip if k >= 54 else value
    for k in range(24):
        for z in range(z_extent):
            psi_ref[k, z, 0:t] = source_ref[pl.ds(k * t * z_extent + z, t, stride=z_extent), :]
    dot_ref[...] = dot_block(shape, [(psi_ref, psi_ref)])
    emit_messages(shape, psi_ref, Links(links_ref), messages)


def dot_block(shape, pairs):
    rows = []
    for left, right in pairs:
        total = None
        for k in range(24):
            for z in range(shape.z):
                term = left[k, z] * right[k, z]
                total = term if total is None else total + term
        rows.append(jnp.sum(total, axis=0, keepdims=True))
    rows += [jnp.zeros((1, shape.lanes), jnp.float32)] * (8 - len(rows))
    return jnp.concatenate(rows, axis=0)


def inner_kernel(shape, psi_ref, links_ref, total_ref):
    links = Links(links_ref)
    x = shape.lane() % X
    lanes = shape.lanes
    at_end, at_start = x == X - 1, x == 0

    def ahead(value):
        return jnp.where(
            at_end, pltpu.roll(value, X - 1, 1), pltpu.roll(value, lanes - 1, 1)
        )

    def behind(value):
        return jnp.where(at_start, pltpu.roll(value, lanes - X + 1, 1), pltpu.roll(value, 1, 1))

    for z in range(shape.z):
        psi = load_psi(psi_ref, z)
        zero = jnp.zeros((shape.rows, lanes), jnp.float32)
        total = {key: (zero, zero) for key in psi}
        half = mapped(ahead, project(psi, 0, -1))
        add_rebuilt(total, mul_link(links, 0, z, half), 0, -1)
        half = mapped(behind, mul_link_dag(links, 0, z, project(psi, 0, 1)))
        add_rebuilt(total, half, 0, 1)
        if z + 1 < shape.z:
            half = project(load_psi(psi_ref, z + 1), 2, -1)
            add_rebuilt(total, mul_link(links, 2, z, half), 2, -1)
        if z > 0:
            half = project(load_psi(psi_ref, z - 1), 2, 1)
            add_rebuilt(total, mul_link_dag(links, 2, z - 1, half), 2, 1)
        for (s, c), pair in total.items():
            for part in range(2):
                total_ref[(s * 3 + c) * 2 + part, z] = pair[part]


def finish_hops(shape, psi_ref, links, total_ref, halo, carried_y, carried_t, store):
    y_msg, z_up, z_down, t_up, t_down = halo
    lane, row = shape.lane(), shape.row()
    lanes, rows, t = shape.lanes, shape.rows, shape.t
    last_z = shape.z - 1

    for z in range(shape.z):
        psi = load_psi(psi_ref, z)
        total = load_psi(total_ref, z)

        def rim_rows(ref):
            half = {}
            for s, c in SPIN_COLOUR:
                ats = [((s * 3 + c) * 2 + part) * shape.z + z for part in range(2)]
                half[s, c] = tuple(
                    jnp.broadcast_to(ref[at : at + 1], (rows, lanes)) for at in ats
                )
            return half

        def rim_plane(ref):
            half = {}
            for s, c in SPIN_COLOUR:
                pair = []
                for part in range(2):
                    at = ((s * 3 + c) * 2 + part) * t
                    plane = ref[at : at + t]
                    if rows != t:
                        pad = jnp.zeros((rows - t, lanes), jnp.float32)
                        plane = jnp.concatenate([plane, pad], axis=0)
                    pair.append(plane)
                half[s, c] = tuple(pair)
            return half

        received = load_half(y_msg, z)
        half = mapped(
            lambda own, other: pltpu.roll(jnp.where(lane < X, other, own), lanes - X, 1),
            project(psi, 1, -1),
            received,
        )
        add_rebuilt(total, mul_link(links, 1, z, half), 1, -1)
        half = mapped(
            lambda own, other: pltpu.roll(jnp.where(lane >= lanes - X, other, own), X, 1),
            load_half(carried_y, z),
            received,
        )
        add_rebuilt(total, half, 1, 1)
        if z == last_z:
            add_rebuilt(total, mul_link(links, 2, z, rim_plane(z_down)), 2, -1)
        if z == 0:
            add_rebuilt(total, rim_plane(z_up), 2, 1)
        half = mapped(
            lambda own, other: jnp.where(row == t - 1, other, pltpu.roll(own, rows - 1, 0)),
            project(psi, 3, -1),
            rim_rows(t_down),
        )
        add_rebuilt(total, mul_link(links, 3, z, half), 3, -1)
        half = mapped(
            lambda own, other: jnp.where(row == 0, other, pltpu.roll(own, 1, 0)),
            load_half(carried_t, z),
            rim_rows(t_up),
        )
        add_rebuilt(total, half, 3, 1)
        for (s, c), pair in total.items():
            for part in range(2):
                value = psi[s, c][part] - hop_kappa * pair[part]
                value = value if s < 2 else -value
                if rows != t:
                    value = jnp.where(row < t, value, 0.0)
                store((s * 3 + c) * 2 + part, z, value)


def mid_kernel(shape, what, entries, *refs):
    psi_ref, links_ref, total_ref, carried_y, carried_t = refs[:5]
    halo = refs[5:10]
    extra = refs[10 : 10 + {"first": 1, "plain": 0, "dots": 4}[what]]
    rest = refs[10 + len(extra) :]
    out_ref, rest = rest[0], rest[1:]
    links = Links(links_ref)

    def store(k, z, value):
        out_ref[k, z] = value

    finish_hops(shape, psi_ref, links, total_ref, halo, carried_y, carried_t, store)
    if what == "first":
        dot_ref, rest = rest[0], rest[1:]
        block = dot_block(shape, [(out_ref, out_ref)])
        dot_ref[...] = jnp.concatenate([extra[0][0:1], block[0:1], block[2:8]], axis=0)
    if what == "dots":
        dot_ref, rest = rest[0], rest[1:]
        source_ref, one_ref, gathered = extra[0], extra[1], extra[2]
        _, alpha_one = first_scalars(gathered, entries)
        sums = [None] * 3
        for k in range(24):
            for z in range(shape.z):
                start = source_ref[k, z]
                remain = psi_ref[k, z] - alpha_one * start
                image = out_ref[k, z] - alpha_one * one_ref[k, z]
                terms = (remain * remain, remain * start, image * image)
                sums = [b if a is None else a + b for a, b in zip(sums, terms)]
        rows = [jnp.sum(value, axis=0, keepdims=True) for value in sums]
        rows.append(jnp.zeros((5, shape.lanes), jnp.float32))
        dot_ref[...] = jnp.concatenate(rows, axis=0)
    emit_messages(shape, out_ref, links, rest)


def gathered_sums(gathered, count):
    blocks = gathered.shape[0] // 8
    block = gathered[0:8]
    if blocks <= 64:
        for k in range(1, blocks):
            block = block + gathered[8 * k : 8 * k + 8]
    else:
        block = lax.fori_loop(
            1, blocks, lambda k, acc: acc + gathered[pl.ds(pl.multiple_of(8 * k, 8), 8)], block
        )
    column = jnp.sum(block, axis=1, keepdims=True)
    return [column[k : k + 1] for k in range(count)]


def first_scalars(gathered, entries):
    square, image = gathered_sums(gathered, 2)
    norm_square = square / entries + epsilon
    return norm_square, (image / entries) / norm_square


def last_kernel(
    shape, entries, psi_ref, links_ref, total_ref, carried_y, carried_t,
    y_msg, z_up, z_down, t_up, t_down,
    source_ref, two_ref, gathered_one, gathered_two, out_ref, coefficients,
):
    norm_square, alpha_one = first_scalars(gathered_one, entries)
    remain_square, overlap, image_square = gathered_sums(gathered_two, 3)
    norm = jnp.sqrt(norm_square)
    beta_one = jnp.sqrt(remain_square / entries / norm_square + epsilon)
    scale = 1.0 / (norm * beta_one)
    overlap = overlap / entries / (norm_square * beta_one)
    alpha_two = image_square / entries / (norm_square * beta_one * beta_one) - beta_one * overlap
    first_factor = beta_one / norm
    t, z_extent = shape.t, shape.z

    def store(k, z, value):
        two, start = two_ref[k, z], source_ref[k, z]
        remain = two - alpha_one * start
        result = (value - alpha_one * two - alpha_two * remain) * scale - first_factor * start
        out_ref[pl.ds(k * t * z_extent + z, t, stride=z_extent), :] = result[0:t]

    finish_hops(
        shape, psi_ref, Links(links_ref), total_ref,
        (y_msg, z_up, z_down, t_up, t_down), carried_y, carried_t, store,
    )
    coefficients[0] = alpha_one[0, 0]
    coefficients[1] = beta_one[0, 0]
    coefficients[2] = alpha_two[0, 0]


def send(value, axis, step):
    count = lax.axis_size(axis)
    return lax.ppermute(value, axis, [(i, (i + step) % count) for i in range(count)])


def exchange(messages, lanes):
    y_msg, z_up, z_down, t_up, t_down = messages
    z_halo = send(z_up, "gz", 1), send(z_down, "gz", -1)
    t_halo = send(t_up, "ta", 1), send(t_down, "ta", -1)
    if lax.axis_size("gy") == 2:
        y_halo = send(y_msg, "gy", 1)
    else:
        lane = lax.broadcasted_iota(jnp.int32, y_msg.shape, y_msg.ndim - 1)
        y_halo = jnp.where(lane < lanes // 2, send(y_msg, "gy", -1), send(y_msg, "gy", 1))
    return (y_halo, *z_halo, *t_halo)


def from_everyone(dot):
    everywhere = ("ta", "gz", "gy")
    count = lax.axis_size("ta") * lax.axis_size("gz") * lax.axis_size("gy")
    copies = jnp.broadcast_to(dot[None], (count, *dot.shape))
    received = lax.all_to_all(copies, everywhere, split_axis=0, concat_axis=0, tiled=True)
    return received.reshape(count * dot.shape[0], dot.shape[1])


def shards(source, gauge_links):
    devices_all = lax.axis_size("ta") * lax.axis_size("gz") * lax.axis_size("gy")
    entries = float(source.size * devices_all)
    shape = Shape(source.shape[3], source.shape[4], source.shape[5])
    t, z, rows, lanes = shape.t, shape.z, shape.rows, shape.lanes
    vmem = pl.BlockSpec(memory_space=pltpu.VMEM)
    smem = pl.BlockSpec(memory_space=pltpu.SMEM)

    def held(*dims):
        return pltpu.VMEM(dims, jnp.float32)

    field = held(24, z, rows, lanes)
    half = held(12, z, rows, lanes)
    dots = held(8, lanes)
    messages = (
        half, held(12 * t, lanes), held(12 * t, lanes), held(12 * z, lanes), held(12 * z, lanes),
        half, half,
    )

    def call(kernel, name, flops, out_shape, out_specs=None, in_specs=None):
        def run(*operands):
            return pl.pallas_call(
                kernel,
                name=name,
                out_shape=out_shape,
                in_specs=in_specs or [vmem] * len(operands),
                out_specs=out_specs or jax.tree.map(lambda _: vmem, out_shape),
                compiler_params=pltpu.CompilerParams(vmem_limit_bytes=8 << 20),
                cost_estimate=pl.CostEstimate(
                    flops=flops, bytes_accessed=1 << 20, transcendentals=0
                ),
            )(*operands)

        return run

    sites = t * z * lanes
    is_last = lax.axis_index("ta") == lax.axis_size("ta") - 1
    sign = jnp.where(is_last, -1.0, 1.0).astype(jnp.float32).reshape(1)
    psi, links, dot_zero, *sent = call(
        functools.partial(prep_kernel, shape), "prep", 400 * sites,
        (field, held(72, z, rows, lanes), dots, *messages), in_specs=[smem, vmem, vmem],
    )(sign, source.reshape(24 * t * z, lanes), gauge_links.reshape(72 * t * z, lanes))
    start = psi
    powers = [psi]
    gathered = []
    for step in range(4):
        halo = exchange(sent[:5], lanes)
        carried = sent[5:]
        total = call(functools.partial(inner_kernel, shape), "inner", 700 * sites, field)(
            psi, links
        )
        operands = (psi, links, total, *carried, *halo)
        if step == 0:
            kernel = functools.partial(mid_kernel, shape, "first", entries)
            psi, dot, *sent = call(kernel, "mid_first", 1000 * sites, (field, dots, *messages))(
                *operands, dot_zero
            )
            gathered.append(from_everyone(dot))
        elif step == 1:
            kernel = functools.partial(mid_kernel, shape, "plain", entries)
            psi, *sent = call(kernel, "mid_plain", 1000 * sites, (field, *messages))(*operands)
        elif step == 2:
            kernel = functools.partial(mid_kernel, shape, "dots", entries)
            psi, dot, *sent = call(kernel, "mid_dots", 1000 * sites, (field, dots, *messages))(
                *operands, start, powers[1], gathered[0], dot_zero
            )
            gathered.append(from_everyone(dot))
        else:
            residual, coefficients = call(
                functools.partial(last_kernel, shape, entries), "last", 1000 * sites,
                (
                    jax.ShapeDtypeStruct((24 * t * z, lanes), jnp.float32),
                    jax.ShapeDtypeStruct((3,), jnp.float32),
                ),
                out_specs=(vmem, smem),
            )(*operands, start, powers[2], *gathered)
        powers.append(psi)
    return (residual.reshape(source.shape), coefficients)


def solution(mesh):
    placed = (P(None, None, None, "ta", "gz", "gy"), P(None, None, None, None, "ta", "gz", "gy"))
    return jax.shard_map(
        shards,
        mesh=mesh,
        in_specs=placed,
        out_specs=(P(None, None, None, "ta", "gz", "gy"), P()),
        check_vma=False,
    )
```

```python
import functools

import jax
import jax.numpy as jnp
from jax import lax
from jax.experimental import pallas as pl
from jax.experimental.pallas import tpu as pltpu
from jax.sharding import PartitionSpec as P

X = 32

hop_kappa = 0.19
epsilon = 1e-06
spin_table = (
    ((1, 0), (-1j, -1j)),
    ((1, 0), (-1, 1)),
    ((0, 1), (-1j, 1j)),
    ((0, 1), (1, 1)),
)
SPIN_COLOUR = [(spin, colour) for spin in range(2) for colour in range(3)]


def add_phased(left, phase, right):
    phase = complex(phase)
    if phase == 1:
        return (left[0] + right[0], left[1] + right[1])
    if phase == -1:
        return (left[0] - right[0], left[1] - right[1])
    if phase == 1j:
        return (left[0] - right[1], left[1] + right[0])
    return (left[0] + right[1], left[1] - right[0])


def project(psi, direction, parity):
    order, phases = spin_table[direction]
    return {
        (s, c): add_phased(psi[s, c], parity * phases[s], psi[2 + order[s], c])
        for s, c in SPIN_COLOUR
    }


def add_rebuilt(total, half, direction, parity):
    order, phases = spin_table[direction]
    for s, c in SPIN_COLOUR:
        total[s, c] = add_phased(total[s, c], 1, half[s, c])
        row = order[s]
        phase = parity * complex(phases[row]).conjugate()
        total[2 + s, c] = add_phased(total[2 + s, c], phase, half[row, c])


def mul_link(links, direction, z, half):
    out = {}
    for row in range(3):
        for s in range(2):
            real, imag = None, None
            for col in range(3):
                u_real, u_imag = links[direction, row, col, z]
                h_real, h_imag = half[s, col]
                term_real = u_real * h_real - u_imag * h_imag
                term_imag = u_real * h_imag + u_imag * h_real
                real = term_real if real is None else real + term_real
                imag = term_imag if imag is None else imag + term_imag
            out[s, row] = (real, imag)
    return out


def mul_link_dag(links, direction, z, half):
    out = {}
    for row in range(3):
        for s in range(2):
            real, imag = None, None
            for col in range(3):
                u_real, u_imag = links[direction, col, row, z]
                h_real, h_imag = half[s, col]
                term_real = u_real * h_real + u_imag * h_imag
                term_imag = u_real * h_imag - u_imag * h_real
                real = term_real if real is None else real + term_real
                imag = term_imag if imag is None else imag + term_imag
            out[s, row] = (real, imag)
    return out


def mapped(function, *halves):
    return {
        key: tuple(function(*(half[key][part] for half in halves)) for part in range(2))
        for key in SPIN_COLOUR
    }


class Links:
    def __init__(self, ref):
        self.ref = ref

    def __getitem__(self, index):
        direction, row, col, z = index
        first = ((direction * 3 + row) * 3 + col) * 2
        return (self.ref[first, z], self.ref[first + 1, z])


def load_psi(ref, z):
    return {
        (s, c): (ref[(s * 3 + c) * 2, z], ref[(s * 3 + c) * 2 + 1, z])
        for s in range(4)
        for c in range(3)
    }


def load_half(ref, z):
    return {
        (s, c): (ref[(s * 3 + c) * 2, z], ref[(s * 3 + c) * 2 + 1, z]) for s, c in SPIN_COLOUR
    }


def store_half(ref, z, half):
    for (s, c), pair in half.items():
        for part in range(2):
            ref[(s * 3 + c) * 2 + part, z] = pair[part]


class Shape:
    def __init__(self, t_extent, z_extent, lanes):
        self.t = t_extent
        self.z = z_extent
        self.rows = -(-t_extent // 8) * 8
        self.lanes = lanes

    def row(self):
        return lax.broadcasted_iota(jnp.int32, (self.rows, self.lanes), 0)

    def lane(self):
        return lax.broadcasted_iota(jnp.int32, (self.rows, self.lanes), 1)


def is_even(axis):
    return jnp.bitwise_and(lax.axis_index(axis), 1) == 0


def either(choice, first, second):
    return jnp.where(choice, first, second)


def emit_messages(shape, psi_ref, links, refs):
    z_second, t_second, z_first, t_first, y_msg, carried_y, carried_t = refs
    t_even, z_even = is_even("ta"), is_even("gz")
    lane = shape.lane()
    last_z, last_t = shape.z - 1, shape.t - 1
    for z in range(shape.z):
        psi = load_psi(psi_ref, z)
        minus = project(psi, 3, -1)
        carried = mul_link_dag(links, 3, z, project(psi, 3, 1))
        store_half(carried_t, z, carried)
        for s, c in SPIN_COLOUR:
            for part in range(2):
                at = ((s * 3 + c) * 2 + part) * shape.z + z
                down = minus[s, c][part][0:1]
                up = carried[s, c][part][last_t : last_t + 1]
                t_first[at : at + 1] = either(t_even, up, down)
                t_second[at : at + 1] = either(t_even, down, up)
        minus = project(psi, 1, -1)
        carried = mul_link_dag(links, 1, z, project(psi, 1, 1))
        store_half(carried_y, z, carried)
        store_half(
            y_msg,
            z,
            mapped(lambda low, high: jnp.where(lane < X, low, high), minus, carried),
        )
    minus = project(load_psi(psi_ref, 0), 2, -1)
    carried = mul_link_dag(links, 2, last_z, project(load_psi(psi_ref, last_z), 2, 1))
    for s, c in SPIN_COLOUR:
        for part in range(2):
            at = ((s * 3 + c) * 2 + part) * shape.t
            down, up = minus[s, c][part][0 : shape.t], carried[s, c][part][0 : shape.t]
            z_first[at : at + shape.t] = either(z_even, up, down)
            z_second[at : at + shape.t] = either(z_even, down, up)


def prep_kernel(shape, source_ref, links_in, psi_ref, links_ref, *messages):
    t, z_extent = shape.t, shape.z
    if shape.rows != t:
        links_ref[...] = jnp.zeros_like(links_ref)
        psi_ref[...] = jnp.zeros_like(psi_ref)
    last = lax.broadcasted_iota(jnp.int32, (t, shape.lanes), 0) == t - 1
    sign = jnp.where(lax.axis_index("ta") == lax.axis_size("ta") - 1, -1.0, 1.0)
    flip = jnp.where(last, sign, 1.0)
    for k in range(72):
        for z in range(z_extent):
            value = links_in[pl.ds(k * t * z_extent + z, t, stride=z_extent), :]
            links_ref[k, z, 0:t] = value * flip if k >= 54 else value
    for k in range(24):
        for z in range(z_extent):
            psi_ref[k, z, 0:t] = source_ref[pl.ds(k * t * z_extent + z, t, stride=z_extent), :]
    emit_messages(shape, psi_ref, Links(links_ref), messages)


def summed(shape, term):
    total = None
    for k in range(24):
        for z in range(shape.z):
            value = term(k, z)
            total = value if total is None else total + value
    return total


def over_lanes(total):
    return jnp.sum(jnp.sum(total, axis=0, keepdims=True), axis=1, keepdims=True)


def local_sums(shape, image, origin):
    square = summed(shape, lambda k, z: origin[k, z] * origin[k, z])
    mixed = over_lanes(summed(shape, lambda k, z: image[k, z] * origin[k, z]))
    whole = over_lanes(square)
    factor = jnp.where(whole > 0.0, mixed / jnp.where(whole > 0.0, whole, 1.0), 0.0)
    spread = jnp.broadcast_to(factor, (shape.rows, shape.lanes))
    rest_square, rest_mixed = None, None
    for k in range(24):
        for z in range(shape.z):
            start = origin[k, z]
            rest = image[k, z] - spread * start
            terms = rest * rest, rest * start
            if rest_square is None:
                rest_square, rest_mixed = terms
            else:
                rest_square, rest_mixed = rest_square + terms[0], rest_mixed + terms[1]
    rows = [jnp.sum(value, axis=0, keepdims=True) for value in (square, rest_square, rest_mixed)]
    return [spread[0:1], *rows]


def inner_kernel(shape, psi_ref, links_ref, total_ref):
    links = Links(links_ref)
    x = shape.lane() % X
    lanes = shape.lanes
    at_end, at_start = x == X - 1, x == 0

    def ahead(value):
        return jnp.where(
            at_end, pltpu.roll(value, X - 1, 1), pltpu.roll(value, lanes - 1, 1)
        )

    def behind(value):
        return jnp.where(at_start, pltpu.roll(value, lanes - X + 1, 1), pltpu.roll(value, 1, 1))

    for z in range(shape.z):
        psi = load_psi(psi_ref, z)
        zero = jnp.zeros((shape.rows, lanes), jnp.float32)
        total = {key: (zero, zero) for key in psi}
        half = mapped(ahead, project(psi, 0, -1))
        add_rebuilt(total, mul_link(links, 0, z, half), 0, -1)
        half = mapped(behind, mul_link_dag(links, 0, z, project(psi, 0, 1)))
        add_rebuilt(total, half, 0, 1)
        if z + 1 < shape.z:
            half = project(load_psi(psi_ref, z + 1), 2, -1)
            add_rebuilt(total, mul_link(links, 2, z, half), 2, -1)
        if z > 0:
            half = project(load_psi(psi_ref, z - 1), 2, 1)
            add_rebuilt(total, mul_link_dag(links, 2, z - 1, half), 2, 1)
        for (s, c), pair in total.items():
            for part in range(2):
                total_ref[(s * 3 + c) * 2 + part, z] = pair[part]


def finish_hops(
    shape, psi_ref, links, total_ref, carried_y, carried_t, halo, store
):
    z_second, t_second, z_first, t_first, y_msg = halo
    t_even, z_even = is_even("ta"), is_even("gz")
    lane, row = shape.lane(), shape.row()
    lanes, rows, t = shape.lanes, shape.rows, shape.t
    last_z = shape.z - 1

    for z in range(shape.z):
        psi = load_psi(psi_ref, z)
        total = load_psi(total_ref, z)

        def rim_rows(from_even, from_odd):
            half = {}
            for s, c in SPIN_COLOUR:
                ats = [((s * 3 + c) * 2 + part) * shape.z + z for part in range(2)]
                half[s, c] = tuple(
                    jnp.broadcast_to(
                        either(t_even, from_even[at : at + 1], from_odd[at : at + 1]),
                        (rows, lanes),
                    )
                    for at in ats
                )
            return half

        def rim_plane(from_even, from_odd):
            half = {}
            for s, c in SPIN_COLOUR:
                pair = []
                for part in range(2):
                    at = ((s * 3 + c) * 2 + part) * t
                    plane = either(z_even, from_even[at : at + t], from_odd[at : at + t])
                    if rows != t:
                        pad = jnp.zeros((rows - t, lanes), jnp.float32)
                        plane = jnp.concatenate([plane, pad], axis=0)
                    pair.append(plane)
                half[s, c] = tuple(pair)
            return half

        received = load_half(y_msg, z)
        half = mapped(
            lambda own, other: pltpu.roll(jnp.where(lane < X, other, own), lanes - X, 1),
            project(psi, 1, -1),
            received,
        )
        add_rebuilt(total, mul_link(links, 1, z, half), 1, -1)
        half = mapped(
            lambda own, other: pltpu.roll(jnp.where(lane >= lanes - X, other, own), X, 1),
            load_half(carried_y, z),
            received,
        )
        add_rebuilt(total, half, 1, 1)
        if z == last_z:
            add_rebuilt(total, mul_link(links, 2, z, rim_plane(z_first, z_second)), 2, -1)
        if z == 0:
            add_rebuilt(total, rim_plane(z_second, z_first), 2, 1)
        half = mapped(
            lambda own, other: jnp.where(row == t - 1, other, pltpu.roll(own, rows - 1, 0)),
            project(psi, 3, -1),
            rim_rows(t_first, t_second),
        )
        add_rebuilt(total, mul_link(links, 3, z, half), 3, -1)
        half = mapped(
            lambda own, other: jnp.where(row == 0, other, pltpu.roll(own, 1, 0)),
            load_half(carried_t, z),
            rim_rows(t_second, t_first),
        )
        add_rebuilt(total, half, 3, 1)
        for (s, c), pair in total.items():
            for part in range(2):
                value = psi[s, c][part] - hop_kappa * pair[part]
                value = value if s < 2 else -value
                if rows != t:
                    value = jnp.where(row < t, value, 0.0)
                store((s * 3 + c) * 2 + part, z, value)


def mid_kernel(shape, psi_ref, links_ref, total_ref, carried_y, carried_t, *refs):
    halo, out_ref, messages = refs[:5], refs[5], refs[6:]
    links = Links(links_ref)

    def store(k, z, value):
        out_ref[k, z] = value

    finish_hops(
        shape, psi_ref, links, total_ref, carried_y, carried_t, halo, store
    )
    emit_messages(shape, out_ref, links, messages)


def sums_kernel(shape, start_ref, one_ref, two_ref, three_ref, copies_ref):
    rows = local_sums(shape, two_ref, start_ref) + local_sums(shape, three_ref, one_ref)
    block = jnp.concatenate(rows, axis=0)
    copies_ref[...] = jnp.broadcast_to(block[None], copies_ref.shape)


def scalars_kernel(entries, gathered, factors_ref, coefficients):
    count = gathered.shape[0] // 8
    rows = [gathered[pl.ds(k, count, stride=8), :] for k in range(8)]
    factor_two, start_square, two_square, two_mixed = rows[:4]
    factor_three, one_square, three_square, three_mixed = rows[4:]
    norm_square = over_lanes(start_square) / entries + epsilon
    alpha_one = over_lanes(one_square) / entries / norm_square
    gap = alpha_one - factor_two
    remain_square = over_lanes(two_square - gap * (2.0 * two_mixed - gap * start_square)) / entries
    overlap = over_lanes(two_mixed - gap * start_square) / entries
    gap = alpha_one - factor_three
    image_square = over_lanes(three_square - gap * (2.0 * three_mixed - gap * one_square)) / entries
    norm = jnp.sqrt(norm_square)
    beta_one = jnp.sqrt(remain_square / norm_square + epsilon)
    overlap = overlap / (norm_square * beta_one)
    alpha_two = image_square / (norm_square * beta_one * beta_one) - beta_one * overlap
    values = [alpha_one, alpha_two, 1.0 / (norm * beta_one), beta_one / norm]
    lanes = gathered.shape[1]
    values = [jnp.broadcast_to(value, (1, lanes)) for value in values]
    values.append(jnp.zeros((4, lanes), jnp.float32))
    factors_ref[...] = jnp.concatenate(values, axis=0)
    coefficients[0] = alpha_one[0, 0]
    coefficients[1] = beta_one[0, 0]
    coefficients[2] = alpha_two[0, 0]


def last_kernel(
    shape, psi_ref, links_ref, total_ref, carried_y, carried_t, *refs
):
    halo, (source_ref, two_ref, factors_ref, out_ref) = refs[:5], refs[5:]
    alpha_one, alpha_two, scale, first_factor = (
        jnp.broadcast_to(factors_ref[k : k + 1], (shape.rows, shape.lanes)) for k in range(4)
    )
    t, z_extent = shape.t, shape.z

    def store(k, z, value):
        two, start = two_ref[k, z], source_ref[k, z]
        remain = two - alpha_one * start
        result = (value - alpha_one * two - alpha_two * remain) * scale - first_factor * start
        out_ref[pl.ds(k * t * z_extent + z, t, stride=z_extent), :] = result[0:t]

    finish_hops(
        shape, psi_ref, Links(links_ref), total_ref, carried_y, carried_t, halo, store
    )


def swap(value, axis, second):
    count = lax.axis_size(axis)
    pairs = []
    for low in range(1 if second else 0, count, 2):
        high = (low + 1) % count
        pairs += [(low, high), (high, low)]
    return lax.ppermute(value, axis, pairs)


def exchange(messages, lanes):
    z_second, t_second, z_first, t_first, y_msg = messages
    halo = (
        swap(z_second, "gz", True),
        swap(t_second, "ta", True),
        swap(z_first, "gz", False),
        swap(t_first, "ta", False),
    )
    y_halo = swap(y_msg, "gy", False)
    if lax.axis_size("gy") > 2:
        even = lax.axis_index("gy") % 2 == 0
        lane = lax.broadcasted_iota(jnp.int32, y_msg.shape, y_msg.ndim - 1)
        y_halo = jnp.where((lane < lanes // 2) == even, y_halo, swap(y_msg, "gy", True))
    return (*halo, y_halo)


def from_everyone(copies):
    received = lax.all_to_all(copies, ("ta", "gz", "gy"), split_axis=0, concat_axis=0, tiled=True)
    return received.reshape(-1, copies.shape[-1])


def shards(source, gauge_links):
    devices_all = lax.axis_size("ta") * lax.axis_size("gz") * lax.axis_size("gy")
    entries = float(source.size * devices_all)
    shape = Shape(source.shape[3], source.shape[4], source.shape[5])
    t, z, rows, lanes = shape.t, shape.z, shape.rows, shape.lanes
    vmem = pl.BlockSpec(memory_space=pltpu.VMEM)
    smem = pl.BlockSpec(memory_space=pltpu.SMEM)

    def held(*dims):
        return pltpu.VMEM(dims, jnp.float32)

    field = held(24, z, rows, lanes)
    half = held(12, z, rows, lanes)
    z_face, t_face = held(12 * t, lanes), held(12 * z, lanes)
    messages = (z_face, t_face, z_face, t_face, half, half, half)

    def call(kernel, name, flops, out_shape, operands, out_specs=None):
        return pl.pallas_call(
            kernel,
            name=name,
            out_shape=out_shape,
            in_specs=[vmem] * len(operands),
            out_specs=out_specs or jax.tree.map(lambda _: vmem, out_shape),
            compiler_params=pltpu.CompilerParams(vmem_limit_bytes=8 << 20),
            cost_estimate=pl.CostEstimate(flops=flops, bytes_accessed=1 << 20, transcendentals=0),
        )(*operands)

    sites = t * z * lanes
    psi, links, *sent = call(
        functools.partial(prep_kernel, shape), "prep", 400 * sites,
        (field, held(72, z, rows, lanes), *messages),
        (source.reshape(24 * t * z, lanes), gauge_links.reshape(72 * t * z, lanes)),
    )
    powers = [psi]
    for step in range(4):
        if step == 3:
            copies = call(
                functools.partial(sums_kernel, shape), "sums", 400 * sites,
                held(devices_all, 8, lanes), powers,
            )
            gathered = from_everyone(copies)
        halo = exchange(sent[:5], lanes)
        inner = functools.partial(inner_kernel, shape)
        total = call(inner, "inner", 700 * sites, field, (psi, links))
        operands = (psi, links, total, *sent[5:], *halo)
        if step < 3:
            psi, *sent = call(
                functools.partial(mid_kernel, shape), "mid", 1000 * sites,
                (field, *messages), operands,
            )
            powers.append(psi)
    factors, coefficients = call(
        functools.partial(scalars_kernel, entries), "scalars", 10 * sites,
        (held(8, lanes), jax.ShapeDtypeStruct((3,), jnp.float32)), (gathered,), (vmem, smem),
    )
    residual = call(
        functools.partial(last_kernel, shape), "last", 1000 * sites,
        jax.ShapeDtypeStruct((24 * t * z, lanes), jnp.float32),
        (*operands, powers[0], powers[2], factors),
    )
    return (residual.reshape(source.shape), coefficients)


def solution(mesh):
    placed = (P(None, None, None, "ta", "gz", "gy"), P(None, None, None, None, "ta", "gz", "gy"))
    return jax.shard_map(
        shards,
        mesh=mesh,
        in_specs=placed,
        out_specs=(P(None, None, None, "ta", "gz", "gy"), P()),
        check_vma=False,
    )
```

```python
import functools

import jax
import jax.numpy as jnp
from jax import lax
from jax.experimental import pallas as pl
from jax.experimental.pallas import tpu as pltpu
from jax.sharding import PartitionSpec as P

X = 32

hop_kappa = 0.19
epsilon = 1e-06
spin_table = (
    ((1, 0), (-1j, -1j)),
    ((1, 0), (-1, 1)),
    ((0, 1), (-1j, 1j)),
    ((0, 1), (1, 1)),
)
SPIN_COLOUR = [(spin, colour) for spin in range(2) for colour in range(3)]


def add_phased(left, phase, right):
    phase = complex(phase)
    if phase == 1:
        return (left[0] + right[0], left[1] + right[1])
    if phase == -1:
        return (left[0] - right[0], left[1] - right[1])
    if phase == 1j:
        return (left[0] - right[1], left[1] + right[0])
    return (left[0] + right[1], left[1] - right[0])


def project(psi, direction, parity):
    order, phases = spin_table[direction]
    return {
        (s, c): add_phased(psi[s, c], parity * phases[s], psi[2 + order[s], c])
        for s, c in SPIN_COLOUR
    }


def add_rebuilt(total, half, direction, parity):
    order, phases = spin_table[direction]
    for s, c in SPIN_COLOUR:
        total[s, c] = add_phased(total[s, c], 1, half[s, c])
        row = order[s]
        phase = parity * complex(phases[row]).conjugate()
        total[2 + s, c] = add_phased(total[2 + s, c], phase, half[row, c])


def mul_link(links, direction, z, half):
    out = {}
    for row in range(3):
        for s in range(2):
            real, imag = None, None
            for col in range(3):
                u_real, u_imag = links[direction, row, col, z]
                h_real, h_imag = half[s, col]
                term_real = u_real * h_real - u_imag * h_imag
                term_imag = u_real * h_imag + u_imag * h_real
                real = term_real if real is None else real + term_real
                imag = term_imag if imag is None else imag + term_imag
            out[s, row] = (real, imag)
    return out


def mul_link_dag(links, direction, z, half):
    out = {}
    for row in range(3):
        for s in range(2):
            real, imag = None, None
            for col in range(3):
                u_real, u_imag = links[direction, col, row, z]
                h_real, h_imag = half[s, col]
                term_real = u_real * h_real + u_imag * h_imag
                term_imag = u_real * h_imag - u_imag * h_real
                real = term_real if real is None else real + term_real
                imag = term_imag if imag is None else imag + term_imag
            out[s, row] = (real, imag)
    return out


def mapped(function, *halves):
    return {
        key: tuple(function(*(half[key][part] for half in halves)) for part in range(2))
        for key in SPIN_COLOUR
    }


class Links:
    def __init__(self, ref):
        self.ref = ref

    def __getitem__(self, index):
        direction, row, col, z = index
        first = ((direction * 3 + row) * 3 + col) * 2
        return (self.ref[first, z], self.ref[first + 1, z])


def load_psi(ref, z):
    return {
        (s, c): (ref[(s * 3 + c) * 2, z], ref[(s * 3 + c) * 2 + 1, z])
        for s in range(4)
        for c in range(3)
    }


def load_half(ref, z):
    return {
        (s, c): (ref[(s * 3 + c) * 2, z], ref[(s * 3 + c) * 2 + 1, z]) for s, c in SPIN_COLOUR
    }


def store_half(ref, z, half):
    for (s, c), pair in half.items():
        for part in range(2):
            ref[(s * 3 + c) * 2 + part, z] = pair[part]


class Shape:
    def __init__(self, t_extent, z_extent, lanes):
        self.t = t_extent
        self.z = z_extent
        self.rows = -(-t_extent // 8) * 8
        self.lanes = lanes

    def row(self):
        return lax.broadcasted_iota(jnp.int32, (self.rows, self.lanes), 0)

    def lane(self):
        return lax.broadcasted_iota(jnp.int32, (self.rows, self.lanes), 1)


def ring_neighbours(axis):
    index, count = lax.axis_index(axis), lax.axis_size(axis)
    ahead = jnp.where(index == count - 1, 0, index + 1)
    behind = jnp.where(index == 0, count - 1, index - 1)
    return ahead, behind


def emit_messages(shape, psi_ref, links, refs):
    z_msg, t_msg, y_msg, carried_y, carried_t = refs
    t_ahead, t_behind = ring_neighbours("ta")
    z_ahead, z_behind = ring_neighbours("gz")
    lane = shape.lane()
    last_z, last_t = shape.z - 1, shape.t - 1
    for z in range(shape.z):
        psi = load_psi(psi_ref, z)
        minus = project(psi, 3, -1)
        carried = mul_link_dag(links, 3, z, project(psi, 3, 1))
        store_half(carried_t, z, carried)
        for s, c in SPIN_COLOUR:
            for part in range(2):
                at = ((s * 3 + c) * 2 + part) * shape.z + z
                down = minus[s, c][part][0:1]
                up = carried[s, c][part][last_t : last_t + 1]
                t_msg[t_behind, at : at + 1] = down
                t_msg[t_ahead, at : at + 1] = up
        minus = project(psi, 1, -1)
        carried = mul_link_dag(links, 1, z, project(psi, 1, 1))
        store_half(carried_y, z, carried)
        store_half(
            y_msg,
            z,
            mapped(lambda low, high: jnp.where(lane < X, low, high), minus, carried),
        )
    minus = project(load_psi(psi_ref, 0), 2, -1)
    carried = mul_link_dag(links, 2, last_z, project(load_psi(psi_ref, last_z), 2, 1))
    for s, c in SPIN_COLOUR:
        for part in range(2):
            at = ((s * 3 + c) * 2 + part) * shape.t
            z_msg[z_behind, at : at + shape.t] = minus[s, c][part][0 : shape.t]
            z_msg[z_ahead, at : at + shape.t] = carried[s, c][part][0 : shape.t]


def prep_kernel(shape, source_hbm, links_hbm, psi_ref, links_ref, *refs):
    messages, (source_ref, links_in, arrived) = refs[:-3], refs[-3:]
    t, z_extent = shape.t, shape.z
    part = 18 * t * z_extent
    copies = [pltpu.make_async_copy(source_hbm, source_ref, arrived.at[4])]
    for direction in (3, 2, 1, 0):
        rows = pl.ds(direction * part, part)
        copies.append(
            pltpu.make_async_copy(links_hbm.at[rows], links_in.at[rows], arrived.at[direction])
        )
    for copy in copies:
        copy.start()
    if shape.rows != t:
        links_ref[...] = jnp.zeros_like(links_ref)
        psi_ref[...] = jnp.zeros_like(psi_ref)
    last = lax.broadcasted_iota(jnp.int32, (t, shape.lanes), 0) == t - 1
    sign = jnp.where(lax.axis_index("ta") == lax.axis_size("ta") - 1, -1.0, 1.0)
    flip = jnp.where(last, sign, 1.0)
    copies[0].wait()
    for k in range(24):
        for z in range(z_extent):
            psi_ref[k, z, 0:t] = source_ref[pl.ds(k * t * z_extent + z, t, stride=z_extent), :]
    for direction in (3, 2, 1, 0):
        copies[4 - direction].wait()
        for k in range(18 * direction, 18 * direction + 18):
            for z in range(z_extent):
                value = links_in[pl.ds(k * t * z_extent + z, t, stride=z_extent), :]
                links_ref[k, z, 0:t] = value * flip if direction == 3 else value
    emit_messages(shape, psi_ref, Links(links_ref), messages)


def summed(shape, term):
    total = None
    for k in range(24):
        for z in range(shape.z):
            value = term(k, z)
            total = value if total is None else total + value
    return total


def over_lanes(total):
    return jnp.sum(jnp.sum(total, axis=0, keepdims=True), axis=1, keepdims=True)


def local_sums(shape, image, origin):
    square = summed(shape, lambda k, z: origin[k, z] * origin[k, z])
    mixed = over_lanes(summed(shape, lambda k, z: image[k, z] * origin[k, z]))
    whole = over_lanes(square)
    factor = jnp.where(whole > 0.0, mixed / jnp.where(whole > 0.0, whole, 1.0), 0.0)
    spread = jnp.broadcast_to(factor, (shape.rows, shape.lanes))
    rest_square, rest_mixed = None, None
    for k in range(24):
        for z in range(shape.z):
            start = origin[k, z]
            rest = image[k, z] - spread * start
            terms = rest * rest, rest * start
            if rest_square is None:
                rest_square, rest_mixed = terms
            else:
                rest_square, rest_mixed = rest_square + terms[0], rest_mixed + terms[1]
    rows = [jnp.sum(value, axis=0, keepdims=True) for value in (square, rest_square, rest_mixed)]
    return [spread[0:1], *rows]


def inner_kernel(shape, psi_ref, links_ref, total_ref):
    links = Links(links_ref)
    x = shape.lane() % X
    lanes = shape.lanes
    at_end, at_start = x == X - 1, x == 0

    def ahead(value):
        return jnp.where(
            at_end, pltpu.roll(value, X - 1, 1), pltpu.roll(value, lanes - 1, 1)
        )

    def behind(value):
        return jnp.where(at_start, pltpu.roll(value, lanes - X + 1, 1), pltpu.roll(value, 1, 1))

    for z in range(shape.z):
        psi = load_psi(psi_ref, z)
        zero = jnp.zeros((shape.rows, lanes), jnp.float32)
        total = {key: (zero, zero) for key in psi}
        half = mapped(ahead, project(psi, 0, -1))
        add_rebuilt(total, mul_link(links, 0, z, half), 0, -1)
        half = mapped(behind, mul_link_dag(links, 0, z, project(psi, 0, 1)))
        add_rebuilt(total, half, 0, 1)
        if z + 1 < shape.z:
            half = project(load_psi(psi_ref, z + 1), 2, -1)
            add_rebuilt(total, mul_link(links, 2, z, half), 2, -1)
        if z > 0:
            half = project(load_psi(psi_ref, z - 1), 2, 1)
            add_rebuilt(total, mul_link_dag(links, 2, z - 1, half), 2, 1)
        for (s, c), pair in total.items():
            for part in range(2):
                total_ref[(s * 3 + c) * 2 + part, z] = pair[part]


def finish_hops(
    shape, psi_ref, links, total_ref, carried_y, carried_t, halo, store
):
    z_halo, t_halo, y_msg = halo
    t_ahead, t_behind = ring_neighbours("ta")
    z_ahead, z_behind = ring_neighbours("gz")
    lane, row = shape.lane(), shape.row()
    lanes, rows, t = shape.lanes, shape.rows, shape.t
    last_z = shape.z - 1

    for z in range(shape.z):
        psi = load_psi(psi_ref, z)
        total = load_psi(total_ref, z)

        def rim_rows(sender):
            half = {}
            for s, c in SPIN_COLOUR:
                ats = [((s * 3 + c) * 2 + part) * shape.z + z for part in range(2)]
                half[s, c] = tuple(
                    jnp.broadcast_to(t_halo[sender, at : at + 1], (rows, lanes)) for at in ats
                )
            return half

        def rim_plane(sender):
            half = {}
            for s, c in SPIN_COLOUR:
                pair = []
                for part in range(2):
                    at = ((s * 3 + c) * 2 + part) * t
                    plane = z_halo[sender, at : at + t]
                    if rows != t:
                        pad = jnp.zeros((rows - t, lanes), jnp.float32)
                        plane = jnp.concatenate([plane, pad], axis=0)
                    pair.append(plane)
                half[s, c] = tuple(pair)
            return half

        received = load_half(y_msg, z)
        half = mapped(
            lambda own, other: pltpu.roll(jnp.where(lane < X, other, own), lanes - X, 1),
            project(psi, 1, -1),
            received,
        )
        add_rebuilt(total, mul_link(links, 1, z, half), 1, -1)
        half = mapped(
            lambda own, other: pltpu.roll(jnp.where(lane >= lanes - X, other, own), X, 1),
            load_half(carried_y, z),
            received,
        )
        add_rebuilt(total, half, 1, 1)
        if z == last_z:
            add_rebuilt(total, mul_link(links, 2, z, rim_plane(z_ahead)), 2, -1)
        if z == 0:
            add_rebuilt(total, rim_plane(z_behind), 2, 1)
        half = mapped(
            lambda own, other: jnp.where(row == t - 1, other, pltpu.roll(own, rows - 1, 0)),
            project(psi, 3, -1),
            rim_rows(t_ahead),
        )
        add_rebuilt(total, mul_link(links, 3, z, half), 3, -1)
        half = mapped(
            lambda own, other: jnp.where(row == 0, other, pltpu.roll(own, 1, 0)),
            load_half(carried_t, z),
            rim_rows(t_behind),
        )
        add_rebuilt(total, half, 3, 1)
        for (s, c), pair in total.items():
            for part in range(2):
                value = psi[s, c][part] - hop_kappa * pair[part]
                value = value if s < 2 else -value
                if rows != t:
                    value = jnp.where(row < t, value, 0.0)
                store((s * 3 + c) * 2 + part, z, value)


def mid_kernel(shape, psi_ref, links_ref, total_ref, carried_y, carried_t, *refs):
    halo, out_ref, messages = refs[:3], refs[3], refs[4:]
    links = Links(links_ref)

    def store(k, z, value):
        out_ref[k, z] = value

    finish_hops(
        shape, psi_ref, links, total_ref, carried_y, carried_t, halo, store
    )
    emit_messages(shape, out_ref, links, messages)


def sums_kernel(shape, start_ref, one_ref, two_ref, three_ref, copies_ref):
    rows = local_sums(shape, two_ref, start_ref) + local_sums(shape, three_ref, one_ref)
    block = jnp.concatenate(rows, axis=0)
    copies_ref[...] = jnp.broadcast_to(block[None], copies_ref.shape)


def scalars_kernel(entries, gathered, factors_ref, coefficients):
    count = gathered.shape[0] // 8
    rows = [gathered[pl.ds(k, count, stride=8), :] for k in range(8)]
    factor_two, start_square, two_square, two_mixed = rows[:4]
    factor_three, one_square, three_square, three_mixed = rows[4:]
    norm_square = over_lanes(start_square) / entries + epsilon
    alpha_one = over_lanes(one_square) / entries / norm_square
    gap = alpha_one - factor_two
    remain_square = over_lanes(two_square - gap * (2.0 * two_mixed - gap * start_square)) / entries
    overlap = over_lanes(two_mixed - gap * start_square) / entries
    gap = alpha_one - factor_three
    image_square = over_lanes(three_square - gap * (2.0 * three_mixed - gap * one_square)) / entries
    norm = jnp.sqrt(norm_square)
    beta_one = jnp.sqrt(remain_square / norm_square + epsilon)
    overlap = overlap / (norm_square * beta_one)
    alpha_two = image_square / (norm_square * beta_one * beta_one) - beta_one * overlap
    values = [alpha_one, alpha_two, 1.0 / (norm * beta_one), beta_one / norm]
    lanes = gathered.shape[1]
    values = [jnp.broadcast_to(value, (1, lanes)) for value in values]
    values.append(jnp.zeros((4, lanes), jnp.float32))
    factors_ref[...] = jnp.concatenate(values, axis=0)
    coefficients[0] = alpha_one[0, 0]
    coefficients[1] = beta_one[0, 0]
    coefficients[2] = alpha_two[0, 0]


def last_kernel(
    shape, psi_ref, links_ref, total_ref, carried_y, carried_t, *refs
):
    halo, (source_ref, two_ref, factors_ref, out_ref) = refs[:3], refs[3:]
    alpha_one, alpha_two, scale, first_factor = (
        jnp.broadcast_to(factors_ref[k : k + 1], (shape.rows, shape.lanes)) for k in range(4)
    )
    t, z_extent = shape.t, shape.z

    def store(k, z, value):
        two, start = two_ref[k, z], source_ref[k, z]
        remain = two - alpha_one * start
        result = (value - alpha_one * two - alpha_two * remain) * scale - first_factor * start
        out_ref[pl.ds(k * t * z_extent + z, t, stride=z_extent), :] = result[0:t]

    finish_hops(
        shape, psi_ref, Links(links_ref), total_ref, carried_y, carried_t, halo, store
    )


def swap(value, axis, second):
    count = lax.axis_size(axis)
    pairs = []
    for low in range(1 if second else 0, count, 2):
        high = (low + 1) % count
        pairs += [(low, high), (high, low)]
    return lax.ppermute(value, axis, pairs)


def exchange(messages, lanes):
    z_msg, t_msg, y_msg = messages
    halo = spread(z_msg, "gz"), spread(t_msg, "ta")
    y_halo = swap(y_msg, "gy", False)
    if lax.axis_size("gy") > 2:
        even = lax.axis_index("gy") % 2 == 0
        lane = lax.broadcasted_iota(jnp.int32, y_msg.shape, y_msg.ndim - 1)
        y_halo = jnp.where((lane < lanes // 2) == even, y_halo, swap(y_msg, "gy", True))
    return (*halo, y_halo)


def spread(blocks, axes):
    return lax.all_to_all(blocks, axes, split_axis=0, concat_axis=0, tiled=True)


def from_everyone(copies):
    received = spread(copies, ("ta", "gz", "gy"))
    return received.reshape(-1, copies.shape[-1])


def shards(source, gauge_links):
    devices_all = lax.axis_size("ta") * lax.axis_size("gz") * lax.axis_size("gy")
    entries = float(source.size * devices_all)
    shape = Shape(source.shape[3], source.shape[4], source.shape[5])
    t, z, rows, lanes = shape.t, shape.z, shape.rows, shape.lanes
    vmem = pl.BlockSpec(memory_space=pltpu.VMEM)
    smem = pl.BlockSpec(memory_space=pltpu.SMEM)

    def held(*dims):
        return pltpu.VMEM(dims, jnp.float32)

    field = held(24, z, rows, lanes)
    half = held(12, z, rows, lanes)
    z_faces = held(lax.axis_size("gz"), 12 * t, lanes)
    t_faces = held(lax.axis_size("ta"), 12 * z, lanes)
    messages = (z_faces, t_faces, half, half, half)

    def call(kernel, name, flops, out_shape, operands, out_specs=None, in_spec=vmem, scratch=()):
        return pl.pallas_call(
            kernel,
            name=name,
            out_shape=out_shape,
            in_specs=[in_spec] * len(operands),
            out_specs=out_specs or jax.tree.map(lambda _: vmem, out_shape),
            scratch_shapes=scratch,
            compiler_params=pltpu.CompilerParams(vmem_limit_bytes=8 << 20),
            cost_estimate=pl.CostEstimate(flops=flops, bytes_accessed=1 << 20, transcendentals=0),
        )(*operands)

    sites = t * z * lanes
    psi, links, *sent = call(
        functools.partial(prep_kernel, shape), "prep", 400 * sites,
        (field, held(72, z, rows, lanes), *messages),
        (
            pltpu.with_memory_space_constraint(source.reshape(24 * t * z, lanes), pltpu.HBM),
            pltpu.with_memory_space_constraint(gauge_links.reshape(72 * t * z, lanes), pltpu.HBM),
        ),
        in_spec=pl.BlockSpec(memory_space=pltpu.HBM),
        scratch=(
            held(24 * t * z, lanes), held(72 * t * z, lanes), pltpu.SemaphoreType.DMA((5,)),
        ),
    )
    powers = [psi]
    for step in range(4):
        if step == 3:
            copies = call(
                functools.partial(sums_kernel, shape), "sums", 400 * sites,
                held(devices_all, 8, lanes), powers,
            )
            gathered = from_everyone(copies)
        halo = exchange(sent[:3], lanes)
        inner = functools.partial(inner_kernel, shape)
        total = call(inner, "inner", 700 * sites, field, (psi, links))
        operands = (psi, links, total, *sent[3:], *halo)
        if step < 3:
            psi, *sent = call(
                functools.partial(mid_kernel, shape), "mid", 1000 * sites,
                (field, *messages), operands,
            )
            powers.append(psi)
    factors, coefficients = call(
        functools.partial(scalars_kernel, entries), "scalars", 10 * sites,
        (held(8, lanes), jax.ShapeDtypeStruct((3,), jnp.float32)), (gathered,), (vmem, smem),
    )
    residual = call(
        functools.partial(last_kernel, shape), "last", 1000 * sites,
        jax.ShapeDtypeStruct((24 * t * z, lanes), jnp.float32),
        (*operands, powers[0], powers[2], factors),
    )
    return (residual.reshape(source.shape), coefficients)


def solution(mesh):
    placed = (P(None, None, None, "ta", "gz", "gy"), P(None, None, None, None, "ta", "gz", "gy"))
    return jax.shard_map(
        shards,
        mesh=mesh,
        in_specs=placed,
        out_specs=(P(None, None, None, "ta", "gz", "gy"), P()),
        check_vma=False,
    )
```

```python
import functools

import jax
import jax.numpy as jnp
from jax import lax
from jax.experimental import pallas as pl
from jax.experimental.pallas import tpu as pltpu
from jax.sharding import PartitionSpec as P

X = 32

hop_kappa = 0.19
epsilon = 1e-06
spin_table = (
    ((1, 0), (-1j, -1j)),
    ((1, 0), (-1, 1)),
    ((0, 1), (-1j, 1j)),
    ((0, 1), (1, 1)),
)
SPIN_COLOUR = [(spin, colour) for spin in range(2) for colour in range(3)]


def add_phased(left, phase, right):
    phase = complex(phase)
    if phase == 1:
        return (left[0] + right[0], left[1] + right[1])
    if phase == -1:
        return (left[0] - right[0], left[1] - right[1])
    if phase == 1j:
        return (left[0] - right[1], left[1] + right[0])
    return (left[0] + right[1], left[1] - right[0])


def project(psi, direction, parity):
    order, phases = spin_table[direction]
    return {
        (s, c): add_phased(psi[s, c], parity * phases[s], psi[2 + order[s], c])
        for s, c in SPIN_COLOUR
    }


def add_rebuilt(total, half, direction, parity):
    order, phases = spin_table[direction]
    for s, c in SPIN_COLOUR:
        total[s, c] = add_phased(total[s, c], 1, half[s, c])
        row = order[s]
        phase = parity * complex(phases[row]).conjugate()
        total[2 + s, c] = add_phased(total[2 + s, c], phase, half[row, c])


def mul_link(links, direction, z, half):
    out = {}
    for row in range(3):
        for s in range(2):
            real, imag = None, None
            for col in range(3):
                u_real, u_imag = links[direction, row, col, z]
                h_real, h_imag = half[s, col]
                term_real = u_real * h_real - u_imag * h_imag
                term_imag = u_real * h_imag + u_imag * h_real
                real = term_real if real is None else real + term_real
                imag = term_imag if imag is None else imag + term_imag
            out[s, row] = (real, imag)
    return out


def mul_link_dag(links, direction, z, half):
    out = {}
    for row in range(3):
        for s in range(2):
            real, imag = None, None
            for col in range(3):
                u_real, u_imag = links[direction, col, row, z]
                h_real, h_imag = half[s, col]
                term_real = u_real * h_real + u_imag * h_imag
                term_imag = u_real * h_imag - u_imag * h_real
                real = term_real if real is None else real + term_real
                imag = term_imag if imag is None else imag + term_imag
            out[s, row] = (real, imag)
    return out


def mapped(function, *halves):
    return {
        key: tuple(function(*(half[key][part] for half in halves)) for part in range(2))
        for key in SPIN_COLOUR
    }


class Links:
    def __init__(self, ref):
        self.ref = ref

    def __getitem__(self, index):
        direction, row, col, z = index
        first = ((direction * 3 + row) * 3 + col) * 2
        return (self.ref[first, z], self.ref[first + 1, z])


def load_psi(ref, z):
    return {
        (s, c): (ref[(s * 3 + c) * 2, z], ref[(s * 3 + c) * 2 + 1, z])
        for s in range(4)
        for c in range(3)
    }


def load_half(ref, z):
    return {
        (s, c): (ref[(s * 3 + c) * 2, z], ref[(s * 3 + c) * 2 + 1, z]) for s, c in SPIN_COLOUR
    }


def store_half(ref, z, half):
    for (s, c), pair in half.items():
        for part in range(2):
            ref[(s * 3 + c) * 2 + part, z] = pair[part]


class Shape:
    def __init__(self, t_extent, z_extent, lanes):
        self.t = t_extent
        self.z = z_extent
        self.rows = -(-t_extent // 8) * 8
        self.lanes = lanes

    def row(self):
        return lax.broadcasted_iota(jnp.int32, (self.rows, self.lanes), 0)

    def lane(self):
        return lax.broadcasted_iota(jnp.int32, (self.rows, self.lanes), 1)


def is_even(axis):
    return jnp.bitwise_and(lax.axis_index(axis), 1) == 0


def either(choice, first, second):
    return jnp.where(choice, first, second)


def emit_messages(shape, psi_ref, links, refs):
    z_second, t_second, z_first, t_first, y_msg, carried_y, carried_t = refs
    t_even, z_even = is_even("ta"), is_even("gz")
    lane = shape.lane()
    last_z, last_t = shape.z - 1, shape.t - 1
    for z in range(shape.z):
        psi = load_psi(psi_ref, z)
        minus = project(psi, 3, -1)
        carried = mul_link_dag(links, 3, z, project(psi, 3, 1))
        store_half(carried_t, z, carried)
        for s, c in SPIN_COLOUR:
            for part in range(2):
                at = ((s * 3 + c) * 2 + part) * shape.z + z
                down = minus[s, c][part][0:1]
                up = carried[s, c][part][last_t : last_t + 1]
                t_first[at : at + 1] = either(t_even, up, down)
                t_second[at : at + 1] = either(t_even, down, up)
        minus = project(psi, 1, -1)
        carried = mul_link_dag(links, 1, z, project(psi, 1, 1))
        store_half(carried_y, z, carried)
        store_half(
            y_msg,
            z,
            mapped(lambda low, high: jnp.where(lane < X, low, high), minus, carried),
        )
    minus = project(load_psi(psi_ref, 0), 2, -1)
    carried = mul_link_dag(links, 2, last_z, project(load_psi(psi_ref, last_z), 2, 1))
    for s, c in SPIN_COLOUR:
        for part in range(2):
            at = ((s * 3 + c) * 2 + part) * shape.t
            down, up = minus[s, c][part][0 : shape.t], carried[s, c][part][0 : shape.t]
            z_first[at : at + shape.t] = either(z_even, up, down)
            z_second[at : at + shape.t] = either(z_even, down, up)


def prep_kernel(shape, source_hbm, links_hbm, psi_ref, links_ref, *refs):
    messages, (source_ref, links_in, arrived) = refs[3:-3], refs[-3:]
    t, z_extent = shape.t, shape.z
    part = 18 * t * z_extent
    copies = [pltpu.make_async_copy(source_hbm, source_ref, arrived.at[4])]
    for direction in (3, 2, 1, 0):
        rows = pl.ds(direction * part, part)
        copies.append(
            pltpu.make_async_copy(links_hbm.at[rows], links_in.at[rows], arrived.at[direction])
        )
    for copy in copies:
        copy.start()
    if shape.rows != t:
        links_ref[...] = jnp.zeros_like(links_ref)
        psi_ref[...] = jnp.zeros_like(psi_ref)
    last = lax.broadcasted_iota(jnp.int32, (t, shape.lanes), 0) == t - 1
    sign = jnp.where(lax.axis_index("ta") == lax.axis_size("ta") - 1, -1.0, 1.0)
    flip = jnp.where(last, sign, 1.0)
    copies[0].wait()
    for k in range(24):
        for z in range(z_extent):
            psi_ref[k, z, 0:t] = source_ref[pl.ds(k * t * z_extent + z, t, stride=z_extent), :]
    for direction in (3, 2, 1, 0):
        copies[4 - direction].wait()
        for k in range(18 * direction, 18 * direction + 18):
            for z in range(z_extent):
                value = links_in[pl.ds(k * t * z_extent + z, t, stride=z_extent), :]
                links_ref[k, z, 0:t] = value * flip if direction == 3 else value
    emit_messages(shape, psi_ref, Links(links_ref), messages)


def summed(shape, term):
    total = None
    for k in range(24):
        for z in range(shape.z):
            value = term(k, z)
            total = value if total is None else total + value
    return total


def over_lanes(total):
    return jnp.sum(jnp.sum(total, axis=0, keepdims=True), axis=1, keepdims=True)


def local_sums(shape, image, origin):
    square = summed(shape, lambda k, z: origin[k, z] * origin[k, z])
    mixed = over_lanes(summed(shape, lambda k, z: image[k, z] * origin[k, z]))
    whole = over_lanes(square)
    factor = jnp.where(whole > 0.0, mixed / jnp.where(whole > 0.0, whole, 1.0), 0.0)
    spread = jnp.broadcast_to(factor, (shape.rows, shape.lanes))
    rest_square, rest_mixed = None, None
    for k in range(24):
        for z in range(shape.z):
            start = origin[k, z]
            rest = image[k, z] - spread * start
            terms = rest * rest, rest * start
            if rest_square is None:
                rest_square, rest_mixed = terms
            else:
                rest_square, rest_mixed = rest_square + terms[0], rest_mixed + terms[1]
    rows = [jnp.sum(value, axis=0, keepdims=True) for value in (square, rest_square, rest_mixed)]
    return [spread[0:1], *rows]


def inner_kernel(shape, psi_ref, links_ref, total_ref):
    links = Links(links_ref)
    x = shape.lane() % X
    lanes = shape.lanes
    at_end, at_start = x == X - 1, x == 0

    def ahead(value):
        return jnp.where(
            at_end, pltpu.roll(value, X - 1, 1), pltpu.roll(value, lanes - 1, 1)
        )

    def behind(value):
        return jnp.where(at_start, pltpu.roll(value, lanes - X + 1, 1), pltpu.roll(value, 1, 1))

    for z in range(shape.z):
        psi = load_psi(psi_ref, z)
        zero = jnp.zeros((shape.rows, lanes), jnp.float32)
        total = {key: (zero, zero) for key in psi}
        half = mapped(ahead, project(psi, 0, -1))
        add_rebuilt(total, mul_link(links, 0, z, half), 0, -1)
        half = mapped(behind, mul_link_dag(links, 0, z, project(psi, 0, 1)))
        add_rebuilt(total, half, 0, 1)
        if z + 1 < shape.z:
            half = project(load_psi(psi_ref, z + 1), 2, -1)
            add_rebuilt(total, mul_link(links, 2, z, half), 2, -1)
        if z > 0:
            half = project(load_psi(psi_ref, z - 1), 2, 1)
            add_rebuilt(total, mul_link_dag(links, 2, z - 1, half), 2, 1)
        for (s, c), pair in total.items():
            for part in range(2):
                total_ref[(s * 3 + c) * 2 + part, z] = pair[part]


def finish_hops(
    shape, psi_ref, links, total_ref, carried_y, carried_t, halo, store
):
    z_second, t_second, z_first, t_first, y_msg = halo
    t_even, z_even = is_even("ta"), is_even("gz")
    lane, row = shape.lane(), shape.row()
    lanes, rows, t = shape.lanes, shape.rows, shape.t
    last_z = shape.z - 1

    for z in range(shape.z):
        psi = load_psi(psi_ref, z)
        total = load_psi(total_ref, z)

        def rim_rows(from_even, from_odd):
            half = {}
            for s, c in SPIN_COLOUR:
                ats = [((s * 3 + c) * 2 + part) * shape.z + z for part in range(2)]
                half[s, c] = tuple(
                    jnp.broadcast_to(
                        either(t_even, from_even[at : at + 1], from_odd[at : at + 1]),
                        (rows, lanes),
                    )
                    for at in ats
                )
            return half

        def rim_plane(from_even, from_odd):
            half = {}
            for s, c in SPIN_COLOUR:
                pair = []
                for part in range(2):
                    at = ((s * 3 + c) * 2 + part) * t
                    plane = either(z_even, from_even[at : at + t], from_odd[at : at + t])
                    if rows != t:
                        pad = jnp.zeros((rows - t, lanes), jnp.float32)
                        plane = jnp.concatenate([plane, pad], axis=0)
                    pair.append(plane)
                half[s, c] = tuple(pair)
            return half

        received = load_half(y_msg, z)
        half = mapped(
            lambda own, other: pltpu.roll(jnp.where(lane < X, other, own), lanes - X, 1),
            project(psi, 1, -1),
            received,
        )
        add_rebuilt(total, mul_link(links, 1, z, half), 1, -1)
        half = mapped(
            lambda own, other: pltpu.roll(jnp.where(lane >= lanes - X, other, own), X, 1),
            load_half(carried_y, z),
            received,
        )
        add_rebuilt(total, half, 1, 1)
        if z == last_z:
            add_rebuilt(total, mul_link(links, 2, z, rim_plane(z_first, z_second)), 2, -1)
        if z == 0:
            add_rebuilt(total, rim_plane(z_second, z_first), 2, 1)
        half = mapped(
            lambda own, other: jnp.where(row == t - 1, other, pltpu.roll(own, rows - 1, 0)),
            project(psi, 3, -1),
            rim_rows(t_first, t_second),
        )
        add_rebuilt(total, mul_link(links, 3, z, half), 3, -1)
        half = mapped(
            lambda own, other: jnp.where(row == 0, other, pltpu.roll(own, 1, 0)),
            load_half(carried_t, z),
            rim_rows(t_second, t_first),
        )
        add_rebuilt(total, half, 3, 1)
        for (s, c), pair in total.items():
            for part in range(2):
                value = psi[s, c][part] - hop_kappa * pair[part]
                value = value if s < 2 else -value
                if rows != t:
                    value = jnp.where(row < t, value, 0.0)
                store((s * 3 + c) * 2 + part, z, value)


def mid_kernel(shape, links_ref, total_ref, *refs):
    halo, held_in, refs = refs[:5], refs[5:11], refs[11:]
    history, carried, messages, new_ref = refs[:4], refs[4:6], refs[6:11], refs[11]
    psi_ref = history[3]
    links = Links(links_ref)

    def store(k, z, value):
        new_ref[k, z] = value

    finish_hops(shape, psi_ref, links, total_ref, *carried, halo, store)
    for older, newer in zip(history, (*history[1:], new_ref)):
        older[...] = newer[...]
    emit_messages(shape, psi_ref, links, (*messages, *carried))


def sums_kernel(shape, start_ref, one_ref, two_ref, three_ref, copies_ref):
    rows = local_sums(shape, two_ref, start_ref) + local_sums(shape, three_ref, one_ref)
    block = jnp.concatenate(rows, axis=0)
    copies_ref[...] = jnp.broadcast_to(block[None], copies_ref.shape)


def last_kernel(
    shape, entries, start_ref, two_ref, four_ref, gathered, out_ref, coefficients
):
    count = gathered.shape[0] // 8
    rows = [gathered[pl.ds(k, count, stride=8), :] for k in range(8)]
    factor_two, start_square, two_square, two_mixed = rows[:4]
    factor_three, one_square, three_square, three_mixed = rows[4:]
    norm_square = over_lanes(start_square) / entries + epsilon
    alpha_one = over_lanes(one_square) / entries / norm_square
    gap = alpha_one - factor_two
    remain_square = over_lanes(two_square - gap * (2.0 * two_mixed - gap * start_square)) / entries
    overlap = over_lanes(two_mixed - gap * start_square) / entries
    gap = alpha_one - factor_three
    image_square = over_lanes(three_square - gap * (2.0 * three_mixed - gap * one_square)) / entries
    norm = jnp.sqrt(norm_square)
    beta_one = jnp.sqrt(remain_square / norm_square + epsilon)
    overlap = overlap / (norm_square * beta_one)
    alpha_two = image_square / (norm_square * beta_one * beta_one) - beta_one * overlap
    scale = 1.0 / (norm * beta_one)
    first_factor = beta_one / norm
    t, z_extent = shape.t, shape.z
    for k in range(24):
        for z in range(z_extent):
            two, start = two_ref[k, z], start_ref[k, z]
            remain = two - alpha_one * start
            result = (four_ref[k, z] - alpha_one * two - alpha_two * remain) * scale
            result = result - first_factor * start
            out_ref[pl.ds(k * t * z_extent + z, t, stride=z_extent), :] = result[0:t]
    coefficients[0] = alpha_one[0, 0]
    coefficients[1] = beta_one[0, 0]
    coefficients[2] = alpha_two[0, 0]


def swap(value, axis, second):
    count = lax.axis_size(axis)
    pairs = []
    for low in range(1 if second else 0, count, 2):
        high = (low + 1) % count
        pairs += [(low, high), (high, low)]
    return lax.ppermute(value, axis, pairs)


def exchange(messages, lanes):
    z_second, t_second, z_first, t_first, y_msg = messages
    halo = (
        swap(z_second, "gz", True),
        swap(t_second, "ta", True),
        swap(z_first, "gz", False),
        swap(t_first, "ta", False),
    )
    y_halo = swap(y_msg, "gy", False)
    if lax.axis_size("gy") > 2:
        even = lax.axis_index("gy") % 2 == 0
        lane = lax.broadcasted_iota(jnp.int32, y_msg.shape, y_msg.ndim - 1)
        y_halo = jnp.where((lane < lanes // 2) == even, y_halo, swap(y_msg, "gy", True))
    return (*halo, y_halo)


def from_everyone(copies):
    received = lax.all_to_all(copies, ("ta", "gz", "gy"), split_axis=0, concat_axis=0, tiled=True)
    return received.reshape(-1, copies.shape[-1])


def shards(source, gauge_links):
    devices_all = lax.axis_size("ta") * lax.axis_size("gz") * lax.axis_size("gy")
    entries = float(source.size * devices_all)
    shape = Shape(source.shape[3], source.shape[4], source.shape[5])
    t, z, rows, lanes = shape.t, shape.z, shape.rows, shape.lanes
    vmem = pl.BlockSpec(memory_space=pltpu.VMEM)
    smem = pl.BlockSpec(memory_space=pltpu.SMEM)

    def held(*dims):
        return pltpu.VMEM(dims, jnp.float32)

    field = held(24, z, rows, lanes)
    half = held(12, z, rows, lanes)
    z_face, t_face = held(12 * t, lanes), held(12 * z, lanes)
    messages = (z_face, t_face, z_face, t_face, half, half, half)

    def call(kernel, name, flops, out_shape, operands, out_specs=None, **options):
        return pl.pallas_call(
            kernel,
            name=name,
            out_shape=out_shape,
            in_specs=options.pop("in_specs", [vmem] * len(operands)),
            out_specs=out_specs or jax.tree.map(lambda _: vmem, out_shape),
            compiler_params=pltpu.CompilerParams(vmem_limit_bytes=8 << 20),
            cost_estimate=pl.CostEstimate(flops=flops, bytes_accessed=1 << 20, transcendentals=0),
            **options,
        )(*operands)

    sites = t * z * lanes
    start, links, *rest = call(
        functools.partial(prep_kernel, shape), "prep", 400 * sites,
        (field, held(72, z, rows, lanes), field, field, field, *messages),
        (
            pltpu.with_memory_space_constraint(source.reshape(24 * t * z, lanes), pltpu.HBM),
            pltpu.with_memory_space_constraint(gauge_links.reshape(72 * t * z, lanes), pltpu.HBM),
        ),
        in_specs=[pl.BlockSpec(memory_space=pltpu.HBM)] * 2,
        scratch_shapes=(
            held(24 * t * z, lanes), held(72 * t * z, lanes), pltpu.SemaphoreType.DMA((5,)),
        ),
    )

    def apply_once(_, carry):
        history, carried, sent = carry[:4], carry[4:6], carry[6:]
        halo = exchange(sent, lanes)
        inner = functools.partial(inner_kernel, shape)
        total = call(inner, "inner", 700 * sites, field, (history[3], links))
        return tuple(
            call(
                functools.partial(mid_kernel, shape), "mid", 1000 * sites,
                (field, field, field, field, half, half, *messages[:5]),
                (links, total, *halo, *history, *carried),
                input_output_aliases={7 + k: k for k in range(6)},
                scratch_shapes=(field,),
            )
        )

    carry = (*rest[:3], start, *rest[8:], *rest[3:8])
    one, two, three, four, *_ = lax.fori_loop(0, 4, apply_once, carry)
    copies = call(
        functools.partial(sums_kernel, shape), "sums", 400 * sites,
        held(devices_all, 8, lanes), (start, one, two, three),
    )
    residual, coefficients = call(
        functools.partial(last_kernel, shape, entries), "last", 100 * sites,
        (
            jax.ShapeDtypeStruct((24 * t * z, lanes), jnp.float32),
            jax.ShapeDtypeStruct((3,), jnp.float32),
        ),
        (start, two, four, from_everyone(copies)), (vmem, smem),
    )
    return (residual.reshape(source.shape), coefficients)


def solution(mesh):
    placed = (P(None, None, None, "ta", "gz", "gy"), P(None, None, None, None, "ta", "gz", "gy"))
    return jax.shard_map(
        shards,
        mesh=mesh,
        in_specs=placed,
        out_specs=(P(None, None, None, "ta", "gz", "gy"), P()),
        check_vma=False,
    )
```

```python
import functools

import jax
import jax.numpy as jnp
from jax import lax
from jax.experimental import pallas as pl
from jax.experimental.pallas import tpu as pltpu
from jax.sharding import PartitionSpec as P

X = 32

hop_kappa = 0.19
epsilon = 1e-06
spin_table = (
    ((1, 0), (-1j, -1j)),
    ((1, 0), (-1, 1)),
    ((0, 1), (-1j, 1j)),
    ((0, 1), (1, 1)),
)
SPIN_COLOUR = [(spin, colour) for spin in range(2) for colour in range(3)]


def add_phased(left, phase, right):
    phase = complex(phase)
    if phase == 1:
        return (left[0] + right[0], left[1] + right[1])
    if phase == -1:
        return (left[0] - right[0], left[1] - right[1])
    if phase == 1j:
        return (left[0] - right[1], left[1] + right[0])
    return (left[0] + right[1], left[1] - right[0])


def project(psi, direction, parity):
    order, phases = spin_table[direction]
    return {
        (s, c): add_phased(psi[s, c], parity * phases[s], psi[2 + order[s], c])
        for s, c in SPIN_COLOUR
    }


def add_rebuilt(total, half, direction, parity):
    order, phases = spin_table[direction]
    for s, c in SPIN_COLOUR:
        total[s, c] = add_phased(total[s, c], 1, half[s, c])
        row = order[s]
        phase = parity * complex(phases[row]).conjugate()
        total[2 + s, c] = add_phased(total[2 + s, c], phase, half[row, c])


def mul_link(links, direction, z, half):
    out = {}
    for row in range(3):
        for s in range(2):
            real, imag = None, None
            for col in range(3):
                u_real, u_imag = links[direction, row, col, z]
                h_real, h_imag = half[s, col]
                term_real = u_real * h_real - u_imag * h_imag
                term_imag = u_real * h_imag + u_imag * h_real
                real = term_real if real is None else real + term_real
                imag = term_imag if imag is None else imag + term_imag
            out[s, row] = (real, imag)
    return out


def mul_link_dag(links, direction, z, half):
    out = {}
    for row in range(3):
        for s in range(2):
            real, imag = None, None
            for col in range(3):
                u_real, u_imag = links[direction, col, row, z]
                h_real, h_imag = half[s, col]
                term_real = u_real * h_real + u_imag * h_imag
                term_imag = u_real * h_imag - u_imag * h_real
                real = term_real if real is None else real + term_real
                imag = term_imag if imag is None else imag + term_imag
            out[s, row] = (real, imag)
    return out


def mapped(function, *halves):
    return {
        key: tuple(function(*(half[key][part] for half in halves)) for part in range(2))
        for key in SPIN_COLOUR
    }


class Links:
    def __init__(self, ref):
        self.ref = ref

    def __getitem__(self, index):
        direction, row, col, z = index
        first = ((direction * 3 + row) * 3 + col) * 2
        return (self.ref[first, z], self.ref[first + 1, z])


def load_psi(ref, z):
    return {
        (s, c): (ref[(s * 3 + c) * 2, z], ref[(s * 3 + c) * 2 + 1, z])
        for s in range(4)
        for c in range(3)
    }


def load_half(ref, z):
    return {
        (s, c): (ref[(s * 3 + c) * 2, z], ref[(s * 3 + c) * 2 + 1, z]) for s, c in SPIN_COLOUR
    }


def store_half(ref, z, half):
    for (s, c), pair in half.items():
        for part in range(2):
            ref[(s * 3 + c) * 2 + part, z] = pair[part]


class Shape:
    def __init__(self, t_extent, z_extent, lanes):
        self.t = t_extent
        self.z = z_extent
        self.rows = -(-t_extent // 8) * 8
        self.lanes = lanes

    def row(self):
        return lax.broadcasted_iota(jnp.int32, (self.rows, self.lanes), 0)

    def lane(self):
        return lax.broadcasted_iota(jnp.int32, (self.rows, self.lanes), 1)


def is_even(axis):
    return jnp.bitwise_and(lax.axis_index(axis), 1) == 0


def either(choice, first, second):
    return jnp.where(choice, first, second)


def emit_messages(shape, psi_ref, links, refs):
    z_second, t_second, z_first, t_first, y_msg, carried_y, carried_t = refs
    t_even, z_even = is_even("ta"), is_even("gz")
    lane = shape.lane()
    last_z, last_t = shape.z - 1, shape.t - 1
    for z in range(shape.z):
        psi = load_psi(psi_ref, z)
        minus = project(psi, 3, -1)
        carried = mul_link_dag(links, 3, z, project(psi, 3, 1))
        store_half(carried_t, z, carried)
        for s, c in SPIN_COLOUR:
            for part in range(2):
                at = ((s * 3 + c) * 2 + part) * shape.z + z
                down = minus[s, c][part][0:1]
                up = carried[s, c][part][last_t : last_t + 1]
                t_first[at : at + 1] = either(t_even, up, down)
                t_second[at : at + 1] = either(t_even, down, up)
        minus = project(psi, 1, -1)
        carried = mul_link_dag(links, 1, z, project(psi, 1, 1))
        store_half(carried_y, z, carried)
        store_half(
            y_msg,
            z,
            mapped(lambda low, high: jnp.where(lane < X, low, high), minus, carried),
        )
    minus = project(load_psi(psi_ref, 0), 2, -1)
    carried = mul_link_dag(links, 2, last_z, project(load_psi(psi_ref, last_z), 2, 1))
    for s, c in SPIN_COLOUR:
        for part in range(2):
            at = ((s * 3 + c) * 2 + part) * shape.t
            down, up = minus[s, c][part][0 : shape.t], carried[s, c][part][0 : shape.t]
            z_first[at : at + shape.t] = either(z_even, up, down)
            z_second[at : at + shape.t] = either(z_even, down, up)


def prep_kernel(shape, source_ref, links_in, psi_ref, links_ref, *messages):
    t, z_extent = shape.t, shape.z
    if shape.rows != t:
        links_ref[...] = jnp.zeros_like(links_ref)
        psi_ref[...] = jnp.zeros_like(psi_ref)
    last = lax.broadcasted_iota(jnp.int32, (t, shape.lanes), 0) == t - 1
    sign = jnp.where(lax.axis_index("ta") == lax.axis_size("ta") - 1, -1.0, 1.0)
    flip = jnp.where(last, sign, 1.0)
    for k in range(72):
        for z in range(z_extent):
            value = links_in[pl.ds(k * t * z_extent + z, t, stride=z_extent), :]
            links_ref[k, z, 0:t] = value * flip if k >= 54 else value
    for k in range(24):
        for z in range(z_extent):
            psi_ref[k, z, 0:t] = source_ref[pl.ds(k * t * z_extent + z, t, stride=z_extent), :]
    emit_messages(shape, psi_ref, Links(links_ref), messages)


def summed(shape, term):
    total = None
    for k in range(24):
        for z in range(shape.z):
            value = term(k, z)
            total = value if total is None else total + value
    return total


def over_lanes(total):
    return jnp.sum(jnp.sum(total, axis=0, keepdims=True), axis=1, keepdims=True)


def local_sums(shape, image, origin):
    square = summed(shape, lambda k, z: origin[k, z] * origin[k, z])
    mixed = over_lanes(summed(shape, lambda k, z: image[k, z] * origin[k, z]))
    whole = over_lanes(square)
    factor = jnp.where(whole > 0.0, mixed / jnp.where(whole > 0.0, whole, 1.0), 0.0)
    spread = jnp.broadcast_to(factor, (shape.rows, shape.lanes))
    rest_square, rest_mixed = None, None
    for k in range(24):
        for z in range(shape.z):
            start = origin[k, z]
            rest = image[k, z] - spread * start
            terms = rest * rest, rest * start
            if rest_square is None:
                rest_square, rest_mixed = terms
            else:
                rest_square, rest_mixed = rest_square + terms[0], rest_mixed + terms[1]
    rows = [jnp.sum(value, axis=0, keepdims=True) for value in (square, rest_square, rest_mixed)]
    return [spread[0:1], *rows]


def inner_kernel(shape, psi_ref, links_ref, total_ref):
    links = Links(links_ref)
    x = shape.lane() % X
    lanes = shape.lanes
    at_end, at_start = x == X - 1, x == 0

    def ahead(value):
        return jnp.where(
            at_end, pltpu.roll(value, X - 1, 1), pltpu.roll(value, lanes - 1, 1)
        )

    def behind(value):
        return jnp.where(at_start, pltpu.roll(value, lanes - X + 1, 1), pltpu.roll(value, 1, 1))

    for z in range(shape.z):
        psi = load_psi(psi_ref, z)
        zero = jnp.zeros((shape.rows, lanes), jnp.float32)
        total = {key: (zero, zero) for key in psi}
        half = mapped(ahead, project(psi, 0, -1))
        add_rebuilt(total, mul_link(links, 0, z, half), 0, -1)
        half = mapped(behind, mul_link_dag(links, 0, z, project(psi, 0, 1)))
        add_rebuilt(total, half, 0, 1)
        if z + 1 < shape.z:
            half = project(load_psi(psi_ref, z + 1), 2, -1)
            add_rebuilt(total, mul_link(links, 2, z, half), 2, -1)
        if z > 0:
            half = project(load_psi(psi_ref, z - 1), 2, 1)
            add_rebuilt(total, mul_link_dag(links, 2, z - 1, half), 2, 1)
        for (s, c), pair in total.items():
            for part in range(2):
                total_ref[(s * 3 + c) * 2 + part, z] = pair[part]


def finish_hops(
    shape, psi_ref, links, total_ref, carried_y, carried_t, halo, store
):
    z_second, t_second, z_first, t_first, y_msg = halo
    t_even, z_even = is_even("ta"), is_even("gz")
    lane, row = shape.lane(), shape.row()
    lanes, rows, t = shape.lanes, shape.rows, shape.t
    last_z = shape.z - 1

    for z in range(shape.z):
        psi = load_psi(psi_ref, z)
        total = load_psi(total_ref, z)

        def rim_rows(from_even, from_odd):
            half = {}
            for s, c in SPIN_COLOUR:
                ats = [((s * 3 + c) * 2 + part) * shape.z + z for part in range(2)]
                half[s, c] = tuple(
                    jnp.broadcast_to(
                        either(t_even, from_even[at : at + 1], from_odd[at : at + 1]),
                        (rows, lanes),
                    )
                    for at in ats
                )
            return half

        def rim_plane(from_even, from_odd):
            half = {}
            for s, c in SPIN_COLOUR:
                pair = []
                for part in range(2):
                    at = ((s * 3 + c) * 2 + part) * t
                    plane = either(z_even, from_even[at : at + t], from_odd[at : at + t])
                    if rows != t:
                        pad = jnp.zeros((rows - t, lanes), jnp.float32)
                        plane = jnp.concatenate([plane, pad], axis=0)
                    pair.append(plane)
                half[s, c] = tuple(pair)
            return half

        received = load_half(y_msg, z)
        half = mapped(
            lambda own, other: pltpu.roll(jnp.where(lane < X, other, own), lanes - X, 1),
            project(psi, 1, -1),
            received,
        )
        add_rebuilt(total, mul_link(links, 1, z, half), 1, -1)
        half = mapped(
            lambda own, other: pltpu.roll(jnp.where(lane >= lanes - X, other, own), X, 1),
            load_half(carried_y, z),
            received,
        )
        add_rebuilt(total, half, 1, 1)
        if z == last_z:
            add_rebuilt(total, mul_link(links, 2, z, rim_plane(z_first, z_second)), 2, -1)
        if z == 0:
            add_rebuilt(total, rim_plane(z_second, z_first), 2, 1)
        half = mapped(
            lambda own, other: jnp.where(row == t - 1, other, pltpu.roll(own, rows - 1, 0)),
            project(psi, 3, -1),
            rim_rows(t_first, t_second),
        )
        add_rebuilt(total, mul_link(links, 3, z, half), 3, -1)
        half = mapped(
            lambda own, other: jnp.where(row == 0, other, pltpu.roll(own, 1, 0)),
            load_half(carried_t, z),
            rim_rows(t_second, t_first),
        )
        add_rebuilt(total, half, 3, 1)
        for (s, c), pair in total.items():
            for part in range(2):
                value = psi[s, c][part] - hop_kappa * pair[part]
                value = value if s < 2 else -value
                if rows != t:
                    value = jnp.where(row < t, value, 0.0)
                store((s * 3 + c) * 2 + part, z, value)


def mid_kernel(shape, psi_ref, links_ref, total_ref, carried_y, carried_t, *refs):
    halo, out_ref, messages = refs[:5], refs[5], refs[6:]
    links = Links(links_ref)

    def store(k, z, value):
        out_ref[k, z] = value

    finish_hops(
        shape, psi_ref, links, total_ref, carried_y, carried_t, halo, store
    )
    emit_messages(shape, out_ref, links, messages)


def sums_kernel(shape, start_ref, one_ref, two_ref, three_ref, copies_ref):
    rows = local_sums(shape, two_ref, start_ref) + local_sums(shape, three_ref, one_ref)
    block = jnp.concatenate(rows, axis=0)
    copies_ref[...] = jnp.broadcast_to(block[None], copies_ref.shape)


def scalars_kernel(entries, gathered, factors_ref, coefficients):
    count = gathered.shape[0] // 8
    rows = [gathered[pl.ds(k, count, stride=8), :] for k in range(8)]
    factor_two, start_square, two_square, two_mixed = rows[:4]
    factor_three, one_square, three_square, three_mixed = rows[4:]
    norm_square = over_lanes(start_square) / entries + epsilon
    alpha_one = over_lanes(one_square) / entries / norm_square
    gap = alpha_one - factor_two
    remain_square = over_lanes(two_square - gap * (2.0 * two_mixed - gap * start_square)) / entries
    overlap = over_lanes(two_mixed - gap * start_square) / entries
    gap = alpha_one - factor_three
    image_square = over_lanes(three_square - gap * (2.0 * three_mixed - gap * one_square)) / entries
    norm = jnp.sqrt(norm_square)
    beta_one = jnp.sqrt(remain_square / norm_square + epsilon)
    overlap = overlap / (norm_square * beta_one)
    alpha_two = image_square / (norm_square * beta_one * beta_one) - beta_one * overlap
    values = [alpha_one, alpha_two, 1.0 / (norm * beta_one), beta_one / norm]
    lanes = gathered.shape[1]
    values = [jnp.broadcast_to(value, (1, lanes)) for value in values]
    values.append(jnp.zeros((4, lanes), jnp.float32))
    factors_ref[...] = jnp.concatenate(values, axis=0)
    coefficients[0] = alpha_one[0, 0]
    coefficients[1] = beta_one[0, 0]
    coefficients[2] = alpha_two[0, 0]


def last_kernel(
    shape, psi_ref, links_ref, total_ref, carried_y, carried_t, *refs
):
    halo, (source_ref, two_ref, factors_ref, out_ref) = refs[:5], refs[5:]
    alpha_one, alpha_two, scale, first_factor = (
        jnp.broadcast_to(factors_ref[k : k + 1], (shape.rows, shape.lanes)) for k in range(4)
    )
    t, z_extent = shape.t, shape.z

    def store(k, z, value):
        two, start = two_ref[k, z], source_ref[k, z]
        remain = two - alpha_one * start
        result = (value - alpha_one * two - alpha_two * remain) * scale - first_factor * start
        out_ref[pl.ds(k * t * z_extent + z, t, stride=z_extent), :] = result[0:t]

    finish_hops(
        shape, psi_ref, Links(links_ref), total_ref, carried_y, carried_t, halo, store
    )


def swap(value, axis, second):
    count = lax.axis_size(axis)
    pairs = []
    for low in range(1 if second else 0, count, 2):
        high = (low + 1) % count
        pairs += [(low, high), (high, low)]
    return lax.ppermute(value, axis, pairs)


def exchange(messages, lanes):
    z_second, t_second, z_first, t_first, y_msg = messages
    halo = (
        swap(z_second, "gz", True),
        swap(t_second, "ta", True),
        swap(z_first, "gz", False),
        swap(t_first, "ta", False),
    )
    y_halo = swap(y_msg, "gy", False)
    if lax.axis_size("gy") > 2:
        even = lax.axis_index("gy") % 2 == 0
        lane = lax.broadcasted_iota(jnp.int32, y_msg.shape, y_msg.ndim - 1)
        y_halo = jnp.where((lane < lanes // 2) == even, y_halo, swap(y_msg, "gy", True))
    return (*halo, y_halo)


def from_everyone(copies):
    received = lax.all_to_all(copies, ("ta", "gz", "gy"), split_axis=0, concat_axis=0, tiled=True)
    return received.reshape(-1, copies.shape[-1])


def shards(source, gauge_links):
    devices_all = lax.axis_size("ta") * lax.axis_size("gz") * lax.axis_size("gy")
    entries = float(source.size * devices_all)
    shape = Shape(source.shape[3], source.shape[4], source.shape[5])
    t, z, rows, lanes = shape.t, shape.z, shape.rows, shape.lanes
    vmem = pl.BlockSpec(memory_space=pltpu.VMEM)
    smem = pl.BlockSpec(memory_space=pltpu.SMEM)

    def held(*dims):
        return pltpu.VMEM(dims, jnp.float32)

    field = held(24, z, rows, lanes)
    half = held(12, z, rows, lanes)
    z_face, t_face = held(12 * t, lanes), held(12 * z, lanes)
    messages = (z_face, t_face, z_face, t_face, half, half, half)

    def call(kernel, name, flops, out_shape, operands, out_specs=None):
        return pl.pallas_call(
            kernel,
            name=name,
            out_shape=out_shape,
            in_specs=[vmem] * len(operands),
            out_specs=out_specs or jax.tree.map(lambda _: vmem, out_shape),
            compiler_params=pltpu.CompilerParams(vmem_limit_bytes=8 << 20),
            cost_estimate=pl.CostEstimate(flops=flops, bytes_accessed=1 << 20, transcendentals=0),
        )(*operands)

    sites = t * z * lanes
    psi, links, *sent = call(
        functools.partial(prep_kernel, shape), "prep", 400 * sites,
        (field, held(72, z, rows, lanes), *messages),
        (source.reshape(24 * t * z, lanes), gauge_links.reshape(72 * t * z, lanes)),
    )
    powers = [psi]
    for step in range(4):
        if step == 3:
            copies = call(
                functools.partial(sums_kernel, shape), "sums", 400 * sites,
                held(devices_all, 8, lanes), powers,
            )
            gathered = from_everyone(copies)
        halo = exchange(sent[:5], lanes)
        inner = functools.partial(inner_kernel, shape)
        total = call(inner, "inner", 700 * sites, field, (psi, links))
        operands = (psi, links, total, *sent[5:], *halo)
        if step < 3:
            psi, *sent = call(
                functools.partial(mid_kernel, shape), "mid", 1000 * sites,
                (field, *messages), operands,
            )
            powers.append(psi)
    factors, coefficients = call(
        functools.partial(scalars_kernel, entries), "scalars", 10 * sites,
        (held(8, lanes), jax.ShapeDtypeStruct((3,), jnp.float32)), (gathered,), (vmem, smem),
    )
    residual = call(
        functools.partial(last_kernel, shape), "last", 1000 * sites,
        jax.ShapeDtypeStruct((24 * t * z, lanes), jnp.float32),
        (*operands, powers[0], powers[2], factors),
    )
    return (residual.reshape(source.shape), coefficients)


class ChipShape(Shape):
    def __init__(self, t_extent, z_extent, lanes):
        super().__init__(t_extent, z_extent, lanes)
        self.parts = 2 * z_extent
        self.z_rows = 24 * t_extent
        self.t_rows = 12 * self.parts

    def block(self, k, part):
        first = (k * self.parts + part) * self.rows
        return pl.ds(first, self.rows)

    def edge(self, k, row):
        return pl.ds(k * self.parts * self.rows + row, self.parts, stride=self.rows)


class ChipLinks:
    def __init__(self, shape, ref, row=None):
        self.shape, self.ref, self.row = shape, ref, row

    def __getitem__(self, index):
        direction, row, col, part = index
        first = ((direction * 3 + row) * 3 + col) * 2
        if self.row is None:
            return tuple(self.ref[self.shape.block(first + n, part), :] for n in range(2))
        return tuple(self.ref[self.shape.edge(first + n, self.row), :] for n in range(2))


def components(spins):
    return [(s, c, part, (s * 3 + c) * 2 + part) for s in range(spins) for c in range(3) for part in range(2)]


def gathered_pairs(spins, value):
    out = {}
    for s in range(spins):
        for c in range(3):
            out[s, c] = tuple(value((s * 3 + c) * 2 + part) for part in range(2))
    return out


def chip_psi(shape, ref, part):
    return gathered_pairs(4, lambda k: ref[shape.block(k, part), :])


def chip_edge(shape, ref, row):
    return gathered_pairs(4, lambda k: ref[shape.edge(k, row), :])


def on_first_core():
    return lax.axis_index("gy") == 0


def chip_messages(shape, psi_ref, links_ref, first_msg, second_msg):
    t, last = shape.t, shape.t - 1
    first_core = on_first_core()

    def put(rows, even, up, down):
        first_msg[rows, :] = either(even, up, down)
        second_msg[rows, :] = either(even, down, up)

    @pl.when(first_core)
    def _():
        even = is_even("ta")
        minus = project(chip_edge(shape, psi_ref, 0), 3, -1)
        half = project(chip_edge(shape, psi_ref, last), 3, 1)
        carried = mul_link_dag(ChipLinks(shape, links_ref, last), 3, 0, half)
        for s, c, part, k in components(2):
            rows = pl.ds(k * shape.parts, shape.parts)
            put(rows, even, carried[s, c][part], minus[s, c][part])

    @pl.when(jnp.logical_not(first_core))
    def _():
        even = is_even("gz")
        links = ChipLinks(shape, links_ref)
        for y_half in range(2):
            minus = project(chip_psi(shape, psi_ref, y_half), 2, -1)
            part_last = shape.parts - 2 + y_half
            half = project(chip_psi(shape, psi_ref, part_last), 2, 1)
            carried = mul_link_dag(links, 2, part_last, half)
            for s, c, part, k in components(2):
                rows = pl.ds((k * 2 + y_half) * t, t)
                put(rows, even, carried[s, c][part][0:t], minus[s, c][part][0:t])


def chip_prep_kernel(
    shape, source_ref, links_in, other_source, other_links, psi_ref, links_ref, *messages
):
    t, z_extent = shape.t, shape.z
    first_core = on_first_core()
    if shape.rows != t:
        links_ref[...] = jnp.zeros_like(links_ref)
        psi_ref[...] = jnp.zeros_like(psi_ref)
    last = lax.broadcasted_iota(jnp.int32, (t, shape.lanes), 0) == t - 1
    sign = jnp.where(lax.axis_index("ta") == lax.axis_size("ta") - 1, -1.0, 1.0)
    flip = jnp.where(last, sign, 1.0)

    def bring(own_ref, other_ref, out_ref, k, z, factor=None):
        rows = pl.ds(k * t * z_extent + z, t, stride=z_extent)
        own, other = own_ref[rows, :], other_ref[rows, :]
        if factor is not None:
            own, other = own * factor, other * factor
        at = (k * shape.parts + 2 * z) * shape.rows
        out_ref[pl.ds(at, t), :] = either(first_core, own, other)
        out_ref[pl.ds(at + shape.rows, t), :] = either(first_core, other, own)

    for z in range(z_extent):
        for k in range(24):
            bring(source_ref, other_source, psi_ref, k, z)
        for k in range(72):
            bring(links_in, other_links, links_ref, k, z, flip if k >= 54 else None)
    chip_messages(shape, psi_ref, links_ref, *messages)


def chip_inner_kernel(shape, psi_ref, links_ref, total_ref):
    links = ChipLinks(shape, links_ref)
    lane, row = shape.lane(), shape.row()
    x = lane % X
    lanes, rows, t = shape.lanes, shape.rows, shape.t
    at_end, at_start = x == X - 1, x == 0
    inside_ahead = row < t - 1
    inside_behind = jnp.logical_and(row > 0, row < t)

    def x_ahead(value):
        return jnp.where(
            at_end, pltpu.roll(value, X - 1, 1), pltpu.roll(value, lanes - 1, 1)
        )

    def x_behind(value):
        return jnp.where(at_start, pltpu.roll(value, lanes - X + 1, 1), pltpu.roll(value, 1, 1))

    def t_ahead(value):
        return jnp.where(inside_ahead, pltpu.roll(value, rows - 1, 0), 0.0)

    def t_behind(value):
        return jnp.where(inside_behind, pltpu.roll(value, 1, 0), 0.0)

    for z in range(shape.z):
        for part in (2 * z, 2 * z + 1):
            psi = chip_psi(shape, psi_ref, part)
            zero = jnp.zeros((rows, lanes), jnp.float32)
            total = {key: (zero, zero) for key in psi}
            half = mapped(x_ahead, project(psi, 0, -1))
            add_rebuilt(total, mul_link(links, 0, part, half), 0, -1)
            half = mapped(x_behind, mul_link_dag(links, 0, part, project(psi, 0, 1)))
            add_rebuilt(total, half, 0, 1)
            half = mapped(t_ahead, project(psi, 3, -1))
            add_rebuilt(total, mul_link(links, 3, part, half), 3, -1)
            half = mapped(t_behind, mul_link_dag(links, 3, part, project(psi, 3, 1)))
            add_rebuilt(total, half, 3, 1)
            if z + 1 < shape.z:
                half = project(chip_psi(shape, psi_ref, part + 2), 2, -1)
                add_rebuilt(total, mul_link(links, 2, part, half), 2, -1)
            if z > 0:
                half = project(chip_psi(shape, psi_ref, part - 2), 2, 1)
                add_rebuilt(total, mul_link_dag(links, 2, part - 2, half), 2, 1)
            for s, c, n, k in components(4):
                total_ref[shape.block(k, part), :] = total[s, c][n]
        pair = (2 * z, 2 * z + 1)
        minus, carried = [], []
        for part in pair:
            psi = chip_psi(shape, psi_ref, part)
            minus.append(mapped(lambda v: pltpu.roll(v, lanes - X, 1), project(psi, 1, -1)))
            half = mul_link_dag(links, 1, part, project(psi, 1, 1))
            carried.append(mapped(lambda v: pltpu.roll(v, X, 1), half))
        for own, part in enumerate(pair):
            total = chip_psi(shape, total_ref, part)
            half = mapped(
                lambda a, b: jnp.where(lane >= lanes - X, b, a), minus[own], minus[1 - own]
            )
            add_rebuilt(total, mul_link(links, 1, part, half), 1, -1)
            half = mapped(lambda a, b: jnp.where(lane < X, b, a), carried[own], carried[1 - own])
            add_rebuilt(total, half, 1, 1)
            for s, c, n, k in components(4):
                total_ref[shape.block(k, part), :] = total[s, c][n]


def chip_finish(shape, psi_ref, links_ref, total_ref, received, scratch, out_ref):
    first, second, other_first, other_second = received
    z_down, z_up = scratch
    first_core, t_even, z_even = on_first_core(), is_even("ta"), is_even("gz")
    t, rows, lanes, parts = shape.t, shape.rows, shape.lanes, shape.parts
    own_z = jnp.logical_not(first_core)
    by_first = either(own_z, first[...], other_first[...])
    by_second = either(own_z, second[...], other_second[...])
    z_down[...] = either(z_even, by_first, by_second)
    z_up[...] = either(z_even, by_second, by_first)
    links = ChipLinks(shape, links_ref)

    def plane(ref, y_half):
        def value(k):
            face = ref[pl.ds((k * 2 + y_half) * t, t), :]
            if rows != t:
                pad = jnp.zeros((rows - t, lanes), jnp.float32)
                face = jnp.concatenate([face, pad], axis=0)
            return face

        return gathered_pairs(2, value)

    for part in range(parts):
        total = chip_psi(shape, total_ref, part)
        if part >= parts - 2:
            half = mul_link(links, 2, part, plane(z_down, part - parts + 2))
            add_rebuilt(total, half, 2, -1)
        if part < 2:
            add_rebuilt(total, plane(z_up, part), 2, 1)
        for s, c, n, k in components(4):
            value = psi_ref[shape.block(k, part), :] - hop_kappa * total[s, c][n]
            out_ref[shape.block(k, part), :] = value if s < 2 else -value

    def t_half(from_even, from_odd):
        def value(k):
            at = pl.ds(k * parts, parts)
            picked = [
                either(first_core, own[at, :], other[at, :]) for own, other in (from_even, from_odd)
            ]
            return either(t_even, *picked)

        return gathered_pairs(2, value)

    by_first, by_second = (first, other_first), (second, other_second)
    down = mul_link(ChipLinks(shape, links_ref, t - 1), 3, 0, t_half(by_first, by_second))
    up = t_half(by_second, by_first)
    zero = jnp.zeros((parts, lanes), jnp.float32)
    for half, parity, row in ((down, -1, t - 1), (up, 1, 0)):
        total = {(s, c): (zero, zero) for s in range(4) for c in range(3)}
        add_rebuilt(total, half, 3, parity)
        for s, c, n, k in components(4):
            at = shape.edge(k, row)
            value = hop_kappa * total[s, c][n]
            out_ref[at, :] = out_ref[at, :] - (value if s < 2 else -value)


def chip_mid_kernel(shape, psi_ref, links_ref, total_ref, *refs):
    received, out_ref, messages, scratch = refs[:4], refs[4], refs[5:7], refs[7:]
    chip_finish(shape, psi_ref, links_ref, total_ref, received, scratch, out_ref)
    chip_messages(shape, out_ref, links_ref, *messages)


def chip_sums_kernel(shape, start_ref, one_ref, two_ref, three_ref, copies_ref):
    class View:
        def __init__(self, ref):
            self.ref = ref

        def __getitem__(self, index):
            return self.ref[shape.block(*index), :]

    wide = ChipShape(shape.t, shape.z, shape.lanes)
    wide.z = shape.parts
    rows = local_sums(wide, View(two_ref), View(start_ref))
    rows += local_sums(wide, View(three_ref), View(one_ref))
    block = jnp.concatenate(rows, axis=0)
    copies_ref[...] = jnp.broadcast_to(block[None], copies_ref.shape)


def chip_last_kernel(shape, psi_ref, links_ref, total_ref, *refs):
    received, (start_ref, two_ref, factors_ref, out_ref) = refs[:4], refs[4:8]
    four_ref, scratch = refs[8], refs[9:]
    chip_finish(shape, psi_ref, links_ref, total_ref, received, scratch, four_ref)
    alpha_one, alpha_two, scale, first_factor = (
        jnp.broadcast_to(factors_ref[k : k + 1], (shape.rows, shape.lanes)) for k in range(4)
    )
    t, z_extent = shape.t, shape.z
    first_core = on_first_core()
    for k in range(24):
        for z in range(z_extent):
            start, two, four = (
                either(first_core, *(ref[shape.block(k, 2 * z + n), :] for n in range(2)))
                for ref in (start_ref, two_ref, four_ref)
            )
            remain = two - alpha_one * start
            result = (four - alpha_one * two - alpha_two * remain) * scale - first_factor * start
            out_ref[pl.ds(k * t * z_extent + z, t, stride=z_extent), :] = result[0:t]


def chip_swap(value, second):
    t_count, z_count = lax.axis_size("ta"), lax.axis_size("gz")
    pairs = []
    for t_index in range(t_count):
        for z_index in range(z_count):
            forward = 1 if (t_index % 2 == 0) != second else -1
            partner = (t_index + forward) % t_count
            pairs.append(((t_index * z_count + z_index) * 2, (partner * z_count + z_index) * 2))
            forward = 1 if (z_index % 2 == 0) != second else -1
            partner = (z_index + forward) % z_count
            mine = (t_index * z_count + z_index) * 2 + 1
            pairs.append((mine, (t_index * z_count + partner) * 2 + 1))
    return lax.ppermute(value, ("ta", "gz", "gy"), pairs)


def chip_shards(source, gauge_links):
    devices_all = lax.axis_size("ta") * lax.axis_size("gz") * lax.axis_size("gy")
    entries = float(source.size * devices_all)
    shape = ChipShape(source.shape[3], source.shape[4], source.shape[5])
    t, z, rows, lanes = shape.t, shape.z, shape.rows, shape.lanes
    vmem = pl.BlockSpec(memory_space=pltpu.VMEM)
    smem = pl.BlockSpec(memory_space=pltpu.SMEM)

    def held(*dims):
        return pltpu.VMEM(dims, jnp.float32)

    field = held(24 * shape.parts * rows, lanes)
    faces = held(max(shape.z_rows, shape.t_rows), lanes)
    z_faces = (faces, faces)

    def call(kernel, name, flops, out_shape, operands, out_specs=None, scratch=()):
        return pl.pallas_call(
            kernel,
            name=name,
            out_shape=out_shape,
            in_specs=[vmem] * len(operands),
            out_specs=out_specs or jax.tree.map(lambda _: vmem, out_shape),
            scratch_shapes=scratch,
            compiler_params=pltpu.CompilerParams(vmem_limit_bytes=8 << 20),
            cost_estimate=pl.CostEstimate(flops=flops, bytes_accessed=1 << 20, transcendentals=0),
        )(*operands)

    sites = 2 * t * z * lanes
    own = (source.reshape(24 * t * z, lanes), gauge_links.reshape(72 * t * z, lanes))
    other = tuple(swap(value, "gy", False) for value in own)
    psi, links, *sent = call(
        functools.partial(chip_prep_kernel, shape), "prep", 400 * sites,
        (field, held(72 * shape.parts * rows, lanes), faces, faces), (*own, *other),
    )
    powers = [psi]
    for step in range(4):
        if step == 3:
            copies = call(
                functools.partial(chip_sums_kernel, shape), "sums", 400 * sites,
                held(devices_all, 8, lanes), powers,
            )
            gathered = from_everyone(copies)
        got = [chip_swap(sent[0], False), chip_swap(sent[1], True)]
        got += [swap(value, "gy", False) for value in got]
        inner = functools.partial(chip_inner_kernel, shape)
        total = call(inner, "inner", 1500 * sites, field, (psi, links))
        operands = (psi, links, total, *got)
        if step < 3:
            psi, *sent = call(
                functools.partial(chip_mid_kernel, shape), "mid", 300 * sites,
                (field, faces, faces), operands, scratch=z_faces,
            )
            powers.append(psi)
    factors, coefficients = call(
        functools.partial(scalars_kernel, 2.0 * entries), "scalars", 10 * sites,
        (held(8, lanes), jax.ShapeDtypeStruct((3,), jnp.float32)), (gathered,), (vmem, smem),
    )
    residual = call(
        functools.partial(chip_last_kernel, shape), "last", 300 * sites,
        jax.ShapeDtypeStruct((24 * t * z, lanes), jnp.float32),
        (*operands, powers[0], powers[2], factors), scratch=(field, *z_faces),
    )
    return (residual.reshape(source.shape), coefficients)


def solution(mesh):
    placed = (P(None, None, None, "ta", "gz", "gy"), P(None, None, None, None, "ta", "gz", "gy"))
    return jax.shard_map(
        chip_shards if mesh.shape["gy"] == 2 else shards,
        mesh=mesh,
        in_specs=placed,
        out_specs=(P(None, None, None, "ta", "gz", "gy"), P()),
        check_vma=False,
    )
```

```python
import functools

import jax
import jax.numpy as jnp
from jax import lax
from jax.experimental import pallas as pl
from jax.experimental.pallas import tpu as pltpu
from jax.sharding import PartitionSpec as P

X = 32

hop_kappa = 0.19
epsilon = 1e-06
spin_table = (
    ((1, 0), (-1j, -1j)),
    ((1, 0), (-1, 1)),
    ((0, 1), (-1j, 1j)),
    ((0, 1), (1, 1)),
)
SPIN_COLOUR = [(spin, colour) for spin in range(2) for colour in range(3)]


def add_phased(left, phase, right):
    phase = complex(phase)
    if phase == 1:
        return (left[0] + right[0], left[1] + right[1])
    if phase == -1:
        return (left[0] - right[0], left[1] - right[1])
    if phase == 1j:
        return (left[0] - right[1], left[1] + right[0])
    return (left[0] + right[1], left[1] - right[0])


def project(psi, direction, parity):
    order, phases = spin_table[direction]
    return {
        (s, c): add_phased(psi[s, c], parity * phases[s], psi[2 + order[s], c])
        for s, c in SPIN_COLOUR
    }


def add_rebuilt(total, half, direction, parity):
    order, phases = spin_table[direction]
    for s, c in SPIN_COLOUR:
        total[s, c] = add_phased(total[s, c], 1, half[s, c])
        row = order[s]
        phase = parity * complex(phases[row]).conjugate()
        total[2 + s, c] = add_phased(total[2 + s, c], phase, half[row, c])


def mul_link(links, direction, z, half):
    out = {}
    for row in range(3):
        for s in range(2):
            real, imag = None, None
            for col in range(3):
                u_real, u_imag = links[direction, row, col, z]
                h_real, h_imag = half[s, col]
                term_real = u_real * h_real - u_imag * h_imag
                term_imag = u_real * h_imag + u_imag * h_real
                real = term_real if real is None else real + term_real
                imag = term_imag if imag is None else imag + term_imag
            out[s, row] = (real, imag)
    return out


def mul_link_dag(links, direction, z, half):
    out = {}
    for row in range(3):
        for s in range(2):
            real, imag = None, None
            for col in range(3):
                u_real, u_imag = links[direction, col, row, z]
                h_real, h_imag = half[s, col]
                term_real = u_real * h_real + u_imag * h_imag
                term_imag = u_real * h_imag - u_imag * h_real
                real = term_real if real is None else real + term_real
                imag = term_imag if imag is None else imag + term_imag
            out[s, row] = (real, imag)
    return out


def mapped(function, *halves):
    return {
        key: tuple(function(*(half[key][part] for half in halves)) for part in range(2))
        for key in SPIN_COLOUR
    }


class Links:
    def __init__(self, ref):
        self.ref = ref

    def __getitem__(self, index):
        direction, row, col, z = index
        first = ((direction * 3 + row) * 3 + col) * 2
        return (self.ref[first, z], self.ref[first + 1, z])


def load_psi(ref, z):
    return {
        (s, c): (ref[(s * 3 + c) * 2, z], ref[(s * 3 + c) * 2 + 1, z])
        for s in range(4)
        for c in range(3)
    }


def load_half(ref, z):
    return {
        (s, c): (ref[(s * 3 + c) * 2, z], ref[(s * 3 + c) * 2 + 1, z]) for s, c in SPIN_COLOUR
    }


def store_half(ref, z, half):
    for (s, c), pair in half.items():
        for part in range(2):
            ref[(s * 3 + c) * 2 + part, z] = pair[part]


class Shape:
    def __init__(self, t_extent, z_extent, lanes):
        self.t = t_extent
        self.z = z_extent
        self.rows = -(-t_extent // 8) * 8
        self.lanes = lanes

    def row(self):
        return lax.broadcasted_iota(jnp.int32, (self.rows, self.lanes), 0)

    def lane(self):
        return lax.broadcasted_iota(jnp.int32, (self.rows, self.lanes), 1)


def is_even(axis):
    return jnp.bitwise_and(lax.axis_index(axis), 1) == 0


def either(choice, first, second):
    return jnp.where(choice, first, second)


def emit_messages(shape, psi_ref, links, refs):
    z_second, t_second, z_first, t_first, y_msg, carried_y, carried_t = refs
    t_even, z_even = is_even("ta"), is_even("gz")
    lane = shape.lane()
    last_z, last_t = shape.z - 1, shape.t - 1
    for z in range(shape.z):
        psi = load_psi(psi_ref, z)
        minus = project(psi, 3, -1)
        carried = mul_link_dag(links, 3, z, project(psi, 3, 1))
        store_half(carried_t, z, carried)
        for s, c in SPIN_COLOUR:
            for part in range(2):
                at = ((s * 3 + c) * 2 + part) * shape.z + z
                down = minus[s, c][part][0:1]
                up = carried[s, c][part][last_t : last_t + 1]
                t_first[at : at + 1] = either(t_even, up, down)
                t_second[at : at + 1] = either(t_even, down, up)
        minus = project(psi, 1, -1)
        carried = mul_link_dag(links, 1, z, project(psi, 1, 1))
        store_half(carried_y, z, carried)
        store_half(
            y_msg,
            z,
            mapped(lambda low, high: jnp.where(lane < X, low, high), minus, carried),
        )
    minus = project(load_psi(psi_ref, 0), 2, -1)
    carried = mul_link_dag(links, 2, last_z, project(load_psi(psi_ref, last_z), 2, 1))
    for s, c in SPIN_COLOUR:
        for part in range(2):
            at = ((s * 3 + c) * 2 + part) * shape.t
            down, up = minus[s, c][part][0 : shape.t], carried[s, c][part][0 : shape.t]
            z_first[at : at + shape.t] = either(z_even, up, down)
            z_second[at : at + shape.t] = either(z_even, down, up)


def prep_kernel(shape, source_hbm, links_hbm, psi_ref, links_ref, *refs):
    messages, (source_ref, links_in, arrived) = refs[:-3], refs[-3:]
    t, z_extent = shape.t, shape.z
    part = 18 * t * z_extent
    copies = [pltpu.make_async_copy(source_hbm, source_ref, arrived.at[4])]
    for direction in (3, 2, 1, 0):
        rows = pl.ds(direction * part, part)
        copies.append(
            pltpu.make_async_copy(links_hbm.at[rows], links_in.at[rows], arrived.at[direction])
        )
    for copy in copies:
        copy.start()
    if shape.rows != t:
        links_ref[...] = jnp.zeros_like(links_ref)
        psi_ref[...] = jnp.zeros_like(psi_ref)
    last = lax.broadcasted_iota(jnp.int32, (t, shape.lanes), 0) == t - 1
    sign = jnp.where(lax.axis_index("ta") == lax.axis_size("ta") - 1, -1.0, 1.0)
    flip = jnp.where(last, sign, 1.0)
    copies[0].wait()
    for k in range(24):
        for z in range(z_extent):
            psi_ref[k, z, 0:t] = source_ref[pl.ds(k * t * z_extent + z, t, stride=z_extent), :]
    for direction in (3, 2, 1, 0):
        copies[4 - direction].wait()
        for k in range(18 * direction, 18 * direction + 18):
            for z in range(z_extent):
                value = links_in[pl.ds(k * t * z_extent + z, t, stride=z_extent), :]
                links_ref[k, z, 0:t] = value * flip if direction == 3 else value
    emit_messages(shape, psi_ref, Links(links_ref), messages)


def summed(shape, term):
    total = None
    for k in range(24):
        for z in range(shape.z):
            value = term(k, z)
            total = value if total is None else total + value
    return total


def over_lanes(total):
    return jnp.sum(jnp.sum(total, axis=0, keepdims=True), axis=1, keepdims=True)


def local_sums(shape, image, origin):
    square = summed(shape, lambda k, z: origin[k, z] * origin[k, z])
    mixed = over_lanes(summed(shape, lambda k, z: image[k, z] * origin[k, z]))
    whole = over_lanes(square)
    factor = jnp.where(whole > 0.0, mixed / jnp.where(whole > 0.0, whole, 1.0), 0.0)
    spread = jnp.broadcast_to(factor, (shape.rows, shape.lanes))
    rest_square, rest_mixed = None, None
    for k in range(24):
        for z in range(shape.z):
            start = origin[k, z]
            rest = image[k, z] - spread * start
            terms = rest * rest, rest * start
            if rest_square is None:
                rest_square, rest_mixed = terms
            else:
                rest_square, rest_mixed = rest_square + terms[0], rest_mixed + terms[1]
    rows = [jnp.sum(value, axis=0, keepdims=True) for value in (square, rest_square, rest_mixed)]
    return [spread[0:1], *rows]


def inner_kernel(shape, psi_ref, links_ref, total_ref):
    links = Links(links_ref)
    x = shape.lane() % X
    lanes = shape.lanes
    at_end, at_start = x == X - 1, x == 0

    def ahead(value):
        return jnp.where(
            at_end, pltpu.roll(value, X - 1, 1), pltpu.roll(value, lanes - 1, 1)
        )

    def behind(value):
        return jnp.where(at_start, pltpu.roll(value, lanes - X + 1, 1), pltpu.roll(value, 1, 1))

    for z in range(shape.z):
        psi = load_psi(psi_ref, z)
        zero = jnp.zeros((shape.rows, lanes), jnp.float32)
        total = {key: (zero, zero) for key in psi}
        half = mapped(ahead, project(psi, 0, -1))
        add_rebuilt(total, mul_link(links, 0, z, half), 0, -1)
        half = mapped(behind, mul_link_dag(links, 0, z, project(psi, 0, 1)))
        add_rebuilt(total, half, 0, 1)
        if z + 1 < shape.z:
            half = project(load_psi(psi_ref, z + 1), 2, -1)
            add_rebuilt(total, mul_link(links, 2, z, half), 2, -1)
        if z > 0:
            half = project(load_psi(psi_ref, z - 1), 2, 1)
            add_rebuilt(total, mul_link_dag(links, 2, z - 1, half), 2, 1)
        for (s, c), pair in total.items():
            for part in range(2):
                total_ref[(s * 3 + c) * 2 + part, z] = pair[part]


def finish_hops(
    shape, psi_ref, links, total_ref, carried_y, carried_t, halo, store
):
    z_second, t_second, z_first, t_first, y_msg = halo
    t_even, z_even = is_even("ta"), is_even("gz")
    lane, row = shape.lane(), shape.row()
    lanes, rows, t = shape.lanes, shape.rows, shape.t
    last_z = shape.z - 1

    for z in range(shape.z):
        psi = load_psi(psi_ref, z)
        total = load_psi(total_ref, z)

        def rim_rows(from_even, from_odd):
            half = {}
            for s, c in SPIN_COLOUR:
                ats = [((s * 3 + c) * 2 + part) * shape.z + z for part in range(2)]
                half[s, c] = tuple(
                    jnp.broadcast_to(
                        either(t_even, from_even[at : at + 1], from_odd[at : at + 1]),
                        (rows, lanes),
                    )
                    for at in ats
                )
            return half

        def rim_plane(from_even, from_odd):
            half = {}
            for s, c in SPIN_COLOUR:
                pair = []
                for part in range(2):
                    at = ((s * 3 + c) * 2 + part) * t
                    plane = either(z_even, from_even[at : at + t], from_odd[at : at + t])
                    if rows != t:
                        pad = jnp.zeros((rows - t, lanes), jnp.float32)
                        plane = jnp.concatenate([plane, pad], axis=0)
                    pair.append(plane)
                half[s, c] = tuple(pair)
            return half

        received = load_half(y_msg, z)
        half = mapped(
            lambda own, other: pltpu.roll(jnp.where(lane < X, other, own), lanes - X, 1),
            project(psi, 1, -1),
            received,
        )
        add_rebuilt(total, mul_link(links, 1, z, half), 1, -1)
        half = mapped(
            lambda own, other: pltpu.roll(jnp.where(lane >= lanes - X, other, own), X, 1),
            load_half(carried_y, z),
            received,
        )
        add_rebuilt(total, half, 1, 1)
        if z == last_z:
            add_rebuilt(total, mul_link(links, 2, z, rim_plane(z_first, z_second)), 2, -1)
        if z == 0:
            add_rebuilt(total, rim_plane(z_second, z_first), 2, 1)
        half = mapped(
            lambda own, other: jnp.where(row == t - 1, other, pltpu.roll(own, rows - 1, 0)),
            project(psi, 3, -1),
            rim_rows(t_first, t_second),
        )
        add_rebuilt(total, mul_link(links, 3, z, half), 3, -1)
        half = mapped(
            lambda own, other: jnp.where(row == 0, other, pltpu.roll(own, 1, 0)),
            load_half(carried_t, z),
            rim_rows(t_second, t_first),
        )
        add_rebuilt(total, half, 3, 1)
        for (s, c), pair in total.items():
            for part in range(2):
                value = psi[s, c][part] - hop_kappa * pair[part]
                value = value if s < 2 else -value
                if rows != t:
                    value = jnp.where(row < t, value, 0.0)
                store((s * 3 + c) * 2 + part, z, value)


def mid_kernel(shape, psi_ref, links_ref, total_ref, carried_y, carried_t, *refs):
    halo, out_ref, messages = refs[:5], refs[5], refs[6:]
    links = Links(links_ref)

    def store(k, z, value):
        out_ref[k, z] = value

    finish_hops(
        shape, psi_ref, links, total_ref, carried_y, carried_t, halo, store
    )
    emit_messages(shape, out_ref, links, messages)


def inner_sums_kernel(
    shape, psi_ref, links_ref, start_ref, one_ref, two_ref, total_ref, copies_ref
):
    rows = local_sums(shape, two_ref, start_ref) + local_sums(shape, psi_ref, one_ref)
    block = jnp.concatenate(rows, axis=0)
    copies_ref[...] = jnp.broadcast_to(block[None], copies_ref.shape)
    inner_kernel(shape, psi_ref, links_ref, total_ref)


def finish_kernel(shape, psi_ref, links_ref, total_ref, carried_y, carried_t, *refs):
    halo, out_ref = refs[:5], refs[5]

    def store(k, z, value):
        out_ref[k, z] = value

    finish_hops(
        shape, psi_ref, Links(links_ref), total_ref, carried_y, carried_t, halo, store
    )


def last_kernel(
    shape, entries, start_ref, two_ref, four_ref, gathered, out_ref, coefficients
):
    count = gathered.shape[0] // 8
    rows = [gathered[pl.ds(k, count, stride=8), :] for k in range(8)]
    factor_two, start_square, two_square, two_mixed = rows[:4]
    factor_three, one_square, three_square, three_mixed = rows[4:]
    norm_square = over_lanes(start_square) / entries + epsilon
    alpha_one = over_lanes(one_square) / entries / norm_square
    gap = alpha_one - factor_two
    remain_square = over_lanes(two_square - gap * (2.0 * two_mixed - gap * start_square)) / entries
    overlap = over_lanes(two_mixed - gap * start_square) / entries
    gap = alpha_one - factor_three
    image_square = over_lanes(three_square - gap * (2.0 * three_mixed - gap * one_square)) / entries
    norm = jnp.sqrt(norm_square)
    beta_one = jnp.sqrt(remain_square / norm_square + epsilon)
    overlap = overlap / (norm_square * beta_one)
    alpha_two = image_square / (norm_square * beta_one * beta_one) - beta_one * overlap
    scale = 1.0 / (norm * beta_one)
    first_factor = beta_one / norm
    t, z_extent = shape.t, shape.z
    for k in range(24):
        for z in range(z_extent):
            two, start = two_ref[k, z], start_ref[k, z]
            remain = two - alpha_one * start
            result = (four_ref[k, z] - alpha_one * two - alpha_two * remain) * scale
            result = result - first_factor * start
            out_ref[pl.ds(k * t * z_extent + z, t, stride=z_extent), :] = result[0:t]
    coefficients[0] = alpha_one[0, 0]
    coefficients[1] = beta_one[0, 0]
    coefficients[2] = alpha_two[0, 0]


def swap(value, axis, second):
    count = lax.axis_size(axis)
    pairs = []
    for low in range(1 if second else 0, count, 2):
        high = (low + 1) % count
        pairs += [(low, high), (high, low)]
    return lax.ppermute(value, axis, pairs)


def exchange(messages, lanes):
    z_second, t_second, z_first, t_first, y_msg = messages
    halo = (
        swap(z_second, "gz", True),
        swap(t_second, "ta", True),
        swap(z_first, "gz", False),
        swap(t_first, "ta", False),
    )
    y_halo = swap(y_msg, "gy", False)
    if lax.axis_size("gy") > 2:
        even = lax.axis_index("gy") % 2 == 0
        lane = lax.broadcasted_iota(jnp.int32, y_msg.shape, y_msg.ndim - 1)
        y_halo = jnp.where((lane < lanes // 2) == even, y_halo, swap(y_msg, "gy", True))
    return (*halo, y_halo)


def from_everyone(copies):
    received = lax.all_to_all(copies, ("ta", "gz", "gy"), split_axis=0, concat_axis=0, tiled=True)
    return received.reshape(-1, copies.shape[-1])


def shards(source, gauge_links):
    devices_all = lax.axis_size("ta") * lax.axis_size("gz") * lax.axis_size("gy")
    entries = float(source.size * devices_all)
    shape = Shape(source.shape[3], source.shape[4], source.shape[5])
    t, z, rows, lanes = shape.t, shape.z, shape.rows, shape.lanes
    vmem = pl.BlockSpec(memory_space=pltpu.VMEM)
    smem = pl.BlockSpec(memory_space=pltpu.SMEM)

    def held(*dims):
        return pltpu.VMEM(dims, jnp.float32)

    field = held(24, z, rows, lanes)
    half = held(12, z, rows, lanes)
    z_face, t_face = held(12 * t, lanes), held(12 * z, lanes)
    messages = (z_face, t_face, z_face, t_face, half, half, half)

    def call(kernel, name, flops, out_shape, operands, out_specs=None, in_spec=vmem, scratch=()):
        return pl.pallas_call(
            kernel,
            name=name,
            out_shape=out_shape,
            in_specs=[in_spec] * len(operands),
            out_specs=out_specs or jax.tree.map(lambda _: vmem, out_shape),
            scratch_shapes=scratch,
            compiler_params=pltpu.CompilerParams(vmem_limit_bytes=8 << 20),
            cost_estimate=pl.CostEstimate(flops=flops, bytes_accessed=1 << 20, transcendentals=0),
        )(*operands)

    sites = t * z * lanes
    psi, links, *sent = call(
        functools.partial(prep_kernel, shape), "prep", 400 * sites,
        (field, held(72, z, rows, lanes), *messages),
        (
            pltpu.with_memory_space_constraint(source.reshape(24 * t * z, lanes), pltpu.HBM),
            pltpu.with_memory_space_constraint(gauge_links.reshape(72 * t * z, lanes), pltpu.HBM),
        ),
        in_spec=pl.BlockSpec(memory_space=pltpu.HBM),
        scratch=(
            held(24 * t * z, lanes), held(72 * t * z, lanes), pltpu.SemaphoreType.DMA((5,)),
        ),
    )
    powers = [psi]
    for step in range(3):
        halo = exchange(sent[:5], lanes)
        inner = functools.partial(inner_kernel, shape)
        total = call(inner, "inner", 700 * sites, field, (psi, links))
        psi, *sent = call(
            functools.partial(mid_kernel, shape), "mid", 1000 * sites,
            (field, *messages), (psi, links, total, *sent[5:], *halo),
        )
        powers.append(psi)
    halo = exchange(sent[:5], lanes)
    total, copies = call(
        functools.partial(inner_sums_kernel, shape), "inner_sums", 1100 * sites,
        (field, held(devices_all, 8, lanes)), (psi, links, *powers[:3]),
    )
    gathered = from_everyone(copies)
    four = call(
        functools.partial(finish_kernel, shape), "finish", 700 * sites, field,
        (psi, links, total, *sent[5:], *halo),
    )
    residual, coefficients = call(
        functools.partial(last_kernel, shape, entries), "last", 100 * sites,
        (
            jax.ShapeDtypeStruct((24 * t * z, lanes), jnp.float32),
            jax.ShapeDtypeStruct((3,), jnp.float32),
        ),
        (powers[0], powers[2], four, gathered), (vmem, smem),
    )
    return (residual.reshape(source.shape), coefficients)


def solution(mesh):
    placed = (P(None, None, None, "ta", "gz", "gy"), P(None, None, None, None, "ta", "gz", "gy"))
    return jax.shard_map(
        shards,
        mesh=mesh,
        in_specs=placed,
        out_specs=(P(None, None, None, "ta", "gz", "gy"), P()),
        check_vma=False,
    )
```

```python
import functools

import jax
import jax.numpy as jnp
from jax import lax
from jax.experimental import pallas as pl
from jax.experimental.pallas import tpu as pltpu
from jax.sharding import PartitionSpec as P

X = 32

hop_kappa = 0.19
epsilon = 1e-06
spin_table = (
    ((1, 0), (-1j, -1j)),
    ((1, 0), (-1, 1)),
    ((0, 1), (-1j, 1j)),
    ((0, 1), (1, 1)),
)
SPIN_COLOUR = [(spin, colour) for spin in range(2) for colour in range(3)]


def add_phased(left, phase, right):
    phase = complex(phase)
    if phase == 1:
        return (left[0] + right[0], left[1] + right[1])
    if phase == -1:
        return (left[0] - right[0], left[1] - right[1])
    if phase == 1j:
        return (left[0] - right[1], left[1] + right[0])
    return (left[0] + right[1], left[1] - right[0])


def project(psi, direction, parity):
    order, phases = spin_table[direction]
    return {
        (s, c): add_phased(psi[s, c], parity * phases[s], psi[2 + order[s], c])
        for s, c in SPIN_COLOUR
    }


def add_rebuilt(total, half, direction, parity):
    order, phases = spin_table[direction]
    for s, c in SPIN_COLOUR:
        total[s, c] = add_phased(total[s, c], 1, half[s, c])
        row = order[s]
        phase = parity * complex(phases[row]).conjugate()
        total[2 + s, c] = add_phased(total[2 + s, c], phase, half[row, c])


def mul_link(links, direction, z, half):
    out = {}
    for row in range(3):
        for s in range(2):
            real, imag = None, None
            for col in range(3):
                u_real, u_imag = links[direction, row, col, z]
                h_real, h_imag = half[s, col]
                term_real = u_real * h_real - u_imag * h_imag
                term_imag = u_real * h_imag + u_imag * h_real
                real = term_real if real is None else real + term_real
                imag = term_imag if imag is None else imag + term_imag
            out[s, row] = (real, imag)
    return out


def mul_link_dag(links, direction, z, half):
    out = {}
    for row in range(3):
        for s in range(2):
            real, imag = None, None
            for col in range(3):
                u_real, u_imag = links[direction, col, row, z]
                h_real, h_imag = half[s, col]
                term_real = u_real * h_real + u_imag * h_imag
                term_imag = u_real * h_imag - u_imag * h_real
                real = term_real if real is None else real + term_real
                imag = term_imag if imag is None else imag + term_imag
            out[s, row] = (real, imag)
    return out


def mapped(function, *halves):
    return {
        key: tuple(function(*(half[key][part] for half in halves)) for part in range(2))
        for key in SPIN_COLOUR
    }


class Links:
    def __init__(self, ref):
        self.ref = ref

    def __getitem__(self, index):
        direction, row, col, z = index
        first = ((direction * 3 + row) * 3 + col) * 2
        return (self.ref[first, z], self.ref[first + 1, z])


def load_psi(ref, z):
    return {
        (s, c): (ref[(s * 3 + c) * 2, z], ref[(s * 3 + c) * 2 + 1, z])
        for s in range(4)
        for c in range(3)
    }


def load_half(ref, z):
    return {
        (s, c): (ref[(s * 3 + c) * 2, z], ref[(s * 3 + c) * 2 + 1, z]) for s, c in SPIN_COLOUR
    }


def store_half(ref, z, half):
    for (s, c), pair in half.items():
        for part in range(2):
            ref[(s * 3 + c) * 2 + part, z] = pair[part]


class Shape:
    def __init__(self, t_extent, z_extent, lanes):
        self.t = t_extent
        self.z = z_extent
        self.rows = -(-t_extent // 8) * 8
        self.lanes = lanes

    def row(self):
        return lax.broadcasted_iota(jnp.int32, (self.rows, self.lanes), 0)

    def lane(self):
        return lax.broadcasted_iota(jnp.int32, (self.rows, self.lanes), 1)


def is_even(axis):
    return jnp.bitwise_and(lax.axis_index(axis), 1) == 0


def either(choice, first, second):
    return jnp.where(choice, first, second)


def emit_messages(shape, psi_ref, links, refs):
    z_second, t_second, z_first, t_first, y_msg, carried_y, carried_t = refs
    t_even, z_even = is_even("ta"), is_even("gz")
    lane = shape.lane()
    last_z, last_t = shape.z - 1, shape.t - 1
    for z in range(shape.z):
        psi = load_psi(psi_ref, z)
        minus = project(psi, 3, -1)
        carried = mul_link_dag(links, 3, z, project(psi, 3, 1))
        store_half(carried_t, z, carried)
        for s, c in SPIN_COLOUR:
            for part in range(2):
                at = ((s * 3 + c) * 2 + part) * shape.z + z
                down = minus[s, c][part][0:1]
                up = carried[s, c][part][last_t : last_t + 1]
                t_first[at : at + 1] = either(t_even, up, down)
                t_second[at : at + 1] = either(t_even, down, up)
        minus = project(psi, 1, -1)
        carried = mul_link_dag(links, 1, z, project(psi, 1, 1))
        store_half(carried_y, z, carried)
        store_half(
            y_msg,
            z,
            mapped(lambda low, high: jnp.where(lane < X, low, high), minus, carried),
        )
    minus = project(load_psi(psi_ref, 0), 2, -1)
    carried = mul_link_dag(links, 2, last_z, project(load_psi(psi_ref, last_z), 2, 1))
    for s, c in SPIN_COLOUR:
        for part in range(2):
            at = ((s * 3 + c) * 2 + part) * shape.t
            down, up = minus[s, c][part][0 : shape.t], carried[s, c][part][0 : shape.t]
            z_first[at : at + shape.t] = either(z_even, up, down)
            z_second[at : at + shape.t] = either(z_even, down, up)


def prep_kernel(shape, source_hbm, links_hbm, psi_ref, links_ref, *refs):
    messages, (source_ref, links_in, arrived) = refs[:-3], refs[-3:]
    t, z_extent = shape.t, shape.z
    part = 18 * t * z_extent
    copies = [pltpu.make_async_copy(source_hbm, source_ref, arrived.at[4])]
    for direction in (3, 2, 1, 0):
        rows = pl.ds(direction * part, part)
        copies.append(
            pltpu.make_async_copy(links_hbm.at[rows], links_in.at[rows], arrived.at[direction])
        )
    for copy in copies:
        copy.start()
    if shape.rows != t:
        links_ref[...] = jnp.zeros_like(links_ref)
        psi_ref[...] = jnp.zeros_like(psi_ref)
    last = lax.broadcasted_iota(jnp.int32, (t, shape.lanes), 0) == t - 1
    sign = jnp.where(lax.axis_index("ta") == lax.axis_size("ta") - 1, -1.0, 1.0)
    flip = jnp.where(last, sign, 1.0)
    copies[0].wait()
    for k in range(24):
        for z in range(z_extent):
            psi_ref[k, z, 0:t] = source_ref[pl.ds(k * t * z_extent + z, t, stride=z_extent), :]
    for direction in (3, 2, 1, 0):
        copies[4 - direction].wait()
        for k in range(18 * direction, 18 * direction + 18):
            for z in range(z_extent):
                value = links_in[pl.ds(k * t * z_extent + z, t, stride=z_extent), :]
                links_ref[k, z, 0:t] = value * flip if direction == 3 else value
    emit_messages(shape, psi_ref, Links(links_ref), messages)


def summed(shape, term):
    total = None
    for k in range(24):
        for z in range(shape.z):
            value = term(k, z)
            total = value if total is None else total + value
    return total


def over_lanes(total):
    return jnp.sum(jnp.sum(total, axis=0, keepdims=True), axis=1, keepdims=True)


def local_sums(shape, image, origin):
    square = summed(shape, lambda k, z: origin[k, z] * origin[k, z])
    mixed = over_lanes(summed(shape, lambda k, z: image[k, z] * origin[k, z]))
    whole = over_lanes(square)
    factor = jnp.where(whole > 0.0, mixed / jnp.where(whole > 0.0, whole, 1.0), 0.0)
    spread = jnp.broadcast_to(factor, (shape.rows, shape.lanes))
    rest_square, rest_mixed = None, None
    for k in range(24):
        for z in range(shape.z):
            start = origin[k, z]
            rest = image[k, z] - spread * start
            terms = rest * rest, rest * start
            if rest_square is None:
                rest_square, rest_mixed = terms
            else:
                rest_square, rest_mixed = rest_square + terms[0], rest_mixed + terms[1]
    rows = [jnp.sum(value, axis=0, keepdims=True) for value in (square, rest_square, rest_mixed)]
    return [spread[0:1], *rows]


def inner_kernel(shape, psi_ref, links_ref, total_ref):
    links = Links(links_ref)
    x = shape.lane() % X
    lanes = shape.lanes
    at_end, at_start = x == X - 1, x == 0

    def ahead(value):
        return jnp.where(
            at_end, pltpu.roll(value, X - 1, 1), pltpu.roll(value, lanes - 1, 1)
        )

    def behind(value):
        return jnp.where(at_start, pltpu.roll(value, lanes - X + 1, 1), pltpu.roll(value, 1, 1))

    for z in range(shape.z):
        psi = load_psi(psi_ref, z)
        zero = jnp.zeros((shape.rows, lanes), jnp.float32)
        total = {key: (zero, zero) for key in psi}
        half = mapped(ahead, project(psi, 0, -1))
        add_rebuilt(total, mul_link(links, 0, z, half), 0, -1)
        half = mapped(behind, mul_link_dag(links, 0, z, project(psi, 0, 1)))
        add_rebuilt(total, half, 0, 1)
        if z + 1 < shape.z:
            half = project(load_psi(psi_ref, z + 1), 2, -1)
            add_rebuilt(total, mul_link(links, 2, z, half), 2, -1)
        if z > 0:
            half = project(load_psi(psi_ref, z - 1), 2, 1)
            add_rebuilt(total, mul_link_dag(links, 2, z - 1, half), 2, 1)
        for (s, c), pair in total.items():
            for part in range(2):
                total_ref[(s * 3 + c) * 2 + part, z] = pair[part]


def finish_hops(
    shape, psi_ref, links, total_ref, carried_y, carried_t, halo, store
):
    z_second, t_second, z_first, t_first, y_msg = halo
    t_even, z_even = is_even("ta"), is_even("gz")
    lane, row = shape.lane(), shape.row()
    lanes, rows, t = shape.lanes, shape.rows, shape.t
    last_z = shape.z - 1

    for z in range(shape.z):
        psi = load_psi(psi_ref, z)
        total = load_psi(total_ref, z)

        def rim_rows(from_even, from_odd):
            half = {}
            for s, c in SPIN_COLOUR:
                ats = [((s * 3 + c) * 2 + part) * shape.z + z for part in range(2)]
                half[s, c] = tuple(
                    jnp.broadcast_to(
                        either(t_even, from_even[at : at + 1], from_odd[at : at + 1]),
                        (rows, lanes),
                    )
                    for at in ats
                )
            return half

        def rim_plane(from_even, from_odd):
            half = {}
            for s, c in SPIN_COLOUR:
                pair = []
                for part in range(2):
                    at = ((s * 3 + c) * 2 + part) * t
                    plane = either(z_even, from_even[at : at + t], from_odd[at : at + t])
                    if rows != t:
                        pad = jnp.zeros((rows - t, lanes), jnp.float32)
                        plane = jnp.concatenate([plane, pad], axis=0)
                    pair.append(plane)
                half[s, c] = tuple(pair)
            return half

        received = load_half(y_msg, z)
        half = mapped(
            lambda own, other: pltpu.roll(jnp.where(lane < X, other, own), lanes - X, 1),
            project(psi, 1, -1),
            received,
        )
        add_rebuilt(total, mul_link(links, 1, z, half), 1, -1)
        half = mapped(
            lambda own, other: pltpu.roll(jnp.where(lane >= lanes - X, other, own), X, 1),
            load_half(carried_y, z),
            received,
        )
        add_rebuilt(total, half, 1, 1)
        if z == last_z:
            add_rebuilt(total, mul_link(links, 2, z, rim_plane(z_first, z_second)), 2, -1)
        if z == 0:
            add_rebuilt(total, rim_plane(z_second, z_first), 2, 1)
        half = mapped(
            lambda own, other: jnp.where(row == t - 1, other, pltpu.roll(own, rows - 1, 0)),
            project(psi, 3, -1),
            rim_rows(t_first, t_second),
        )
        add_rebuilt(total, mul_link(links, 3, z, half), 3, -1)
        half = mapped(
            lambda own, other: jnp.where(row == 0, other, pltpu.roll(own, 1, 0)),
            load_half(carried_t, z),
            rim_rows(t_second, t_first),
        )
        add_rebuilt(total, half, 3, 1)
        for (s, c), pair in total.items():
            for part in range(2):
                value = psi[s, c][part] - hop_kappa * pair[part]
                value = value if s < 2 else -value
                if rows != t:
                    value = jnp.where(row < t, value, 0.0)
                store((s * 3 + c) * 2 + part, z, value)


def mid_kernel(shape, psi_ref, links_ref, total_ref, carried_y, carried_t, *refs):
    halo, out_ref, messages = refs[:5], refs[5], refs[6:]
    links = Links(links_ref)

    def store(k, z, value):
        out_ref[k, z] = value

    finish_hops(
        shape, psi_ref, links, total_ref, carried_y, carried_t, halo, store
    )
    emit_messages(shape, out_ref, links, messages)


def inner_sums_kernel(
    shape, psi_ref, links_ref, start_ref, one_ref, two_ref, total_ref, copies_ref
):
    rows = local_sums(shape, two_ref, start_ref) + local_sums(shape, psi_ref, one_ref)
    block = jnp.concatenate(rows, axis=0)
    copies_ref[...] = jnp.broadcast_to(block[None], copies_ref.shape)
    inner_kernel(shape, psi_ref, links_ref, total_ref)


def finish_kernel(shape, psi_ref, links_ref, total_ref, carried_y, carried_t, *refs):
    halo, out_ref = refs[:5], refs[5]

    def store(k, z, value):
        out_ref[k, z] = value

    finish_hops(
        shape, psi_ref, Links(links_ref), total_ref, carried_y, carried_t, halo, store
    )


def scalars(gathered, entries):
    count = gathered.shape[0] // 8
    rows = [gathered[pl.ds(k, count, stride=8), :] for k in range(8)]
    factor_two, start_square, two_square, two_mixed = rows[:4]
    factor_three, one_square, three_square, three_mixed = rows[4:]
    norm_square = over_lanes(start_square) / entries + epsilon
    alpha_one = over_lanes(one_square) / entries / norm_square
    gap = alpha_one - factor_two
    remain_square = over_lanes(two_square - gap * (2.0 * two_mixed - gap * start_square)) / entries
    overlap = over_lanes(two_mixed - gap * start_square) / entries
    gap = alpha_one - factor_three
    image_square = over_lanes(three_square - gap * (2.0 * three_mixed - gap * one_square)) / entries
    norm = jnp.sqrt(norm_square)
    beta_one = jnp.sqrt(remain_square / norm_square + epsilon)
    overlap = overlap / (norm_square * beta_one)
    alpha_two = image_square / (norm_square * beta_one * beta_one) - beta_one * overlap
    scale = 1.0 / (norm * beta_one)
    return alpha_one, beta_one, alpha_two, scale, beta_one / norm


def last_kernel(
    shape, entries, start_ref, two_ref, four_ref, gathered, out_ref, coefficients
):
    alpha_one, beta_one, alpha_two, scale, first_factor = scalars(gathered, entries)
    t, z_extent = shape.t, shape.z
    for k in range(24):
        for z in range(z_extent):
            two, start = two_ref[k, z], start_ref[k, z]
            remain = two - alpha_one * start
            result = (four_ref[k, z] - alpha_one * two - alpha_two * remain) * scale
            result = result - first_factor * start
            out_ref[pl.ds(k * t * z_extent + z, t, stride=z_extent), :] = result[0:t]
    coefficients[0] = alpha_one[0, 0]
    coefficients[1] = beta_one[0, 0]
    coefficients[2] = alpha_two[0, 0]


def swap(value, axis, second):
    count = lax.axis_size(axis)
    pairs = []
    for low in range(1 if second else 0, count, 2):
        high = (low + 1) % count
        pairs += [(low, high), (high, low)]
    return lax.ppermute(value, axis, pairs)


def exchange(messages, lanes):
    z_second, t_second, z_first, t_first, y_msg = messages
    halo = (
        swap(z_second, "gz", True),
        swap(t_second, "ta", True),
        swap(z_first, "gz", False),
        swap(t_first, "ta", False),
    )
    y_halo = swap(y_msg, "gy", False)
    if lax.axis_size("gy") > 2:
        even = lax.axis_index("gy") % 2 == 0
        lane = lax.broadcasted_iota(jnp.int32, y_msg.shape, y_msg.ndim - 1)
        y_halo = jnp.where((lane < lanes // 2) == even, y_halo, swap(y_msg, "gy", True))
    return (*halo, y_halo)


def spread(blocks, axes):
    return lax.all_to_all(blocks, axes, split_axis=0, concat_axis=0, tiled=True)


def from_everyone(copies):
    received = spread(copies, ("ta", "gz", "gy"))
    return received.reshape(-1, copies.shape[-1])


def shards(source, gauge_links):
    devices_all = lax.axis_size("ta") * lax.axis_size("gz") * lax.axis_size("gy")
    entries = float(source.size * devices_all)
    shape = Shape(source.shape[3], source.shape[4], source.shape[5])
    t, z, rows, lanes = shape.t, shape.z, shape.rows, shape.lanes
    vmem = pl.BlockSpec(memory_space=pltpu.VMEM)
    smem = pl.BlockSpec(memory_space=pltpu.SMEM)

    def held(*dims):
        return pltpu.VMEM(dims, jnp.float32)

    field = held(24, z, rows, lanes)
    half = held(12, z, rows, lanes)
    z_face, t_face = held(12 * t, lanes), held(12 * z, lanes)
    messages = (z_face, t_face, z_face, t_face, half, half, half)

    def call(kernel, name, flops, out_shape, operands, out_specs=None, in_spec=vmem, scratch=()):
        return pl.pallas_call(
            kernel,
            name=name,
            out_shape=out_shape,
            in_specs=[in_spec] * len(operands),
            out_specs=out_specs or jax.tree.map(lambda _: vmem, out_shape),
            scratch_shapes=scratch,
            compiler_params=pltpu.CompilerParams(vmem_limit_bytes=8 << 20),
            cost_estimate=pl.CostEstimate(flops=flops, bytes_accessed=1 << 20, transcendentals=0),
        )(*operands)

    sites = t * z * lanes
    psi, links, *sent = call(
        functools.partial(prep_kernel, shape), "prep", 400 * sites,
        (field, held(72, z, rows, lanes), *messages),
        (
            pltpu.with_memory_space_constraint(source.reshape(24 * t * z, lanes), pltpu.HBM),
            pltpu.with_memory_space_constraint(gauge_links.reshape(72 * t * z, lanes), pltpu.HBM),
        ),
        in_spec=pl.BlockSpec(memory_space=pltpu.HBM),
        scratch=(
            held(24 * t * z, lanes), held(72 * t * z, lanes), pltpu.SemaphoreType.DMA((5,)),
        ),
    )
    powers = [psi]
    for step in range(3):
        halo = exchange(sent[:5], lanes)
        inner = functools.partial(inner_kernel, shape)
        total = call(inner, "inner", 700 * sites, field, (psi, links))
        psi, *sent = call(
            functools.partial(mid_kernel, shape), "mid", 1000 * sites,
            (field, *messages), (psi, links, total, *sent[5:], *halo),
        )
        powers.append(psi)
    halo = exchange(sent[:5], lanes)
    total, copies = call(
        functools.partial(inner_sums_kernel, shape), "inner_sums", 1100 * sites,
        (field, held(devices_all, 8, lanes)), (psi, links, *powers[:3]),
    )
    gathered = from_everyone(copies)
    four = call(
        functools.partial(finish_kernel, shape), "finish", 700 * sites, field,
        (psi, links, total, *sent[5:], *halo),
    )
    residual, coefficients = call(
        functools.partial(last_kernel, shape, entries), "last", 100 * sites,
        (
            jax.ShapeDtypeStruct((24 * t * z, lanes), jnp.float32),
            jax.ShapeDtypeStruct((3,), jnp.float32),
        ),
        (powers[0], powers[2], four, gathered), (vmem, smem),
    )
    return (residual.reshape(source.shape), coefficients)


class ChipShape(Shape):
    def __init__(self, t_extent, z_extent, lanes):
        super().__init__(t_extent, z_extent, lanes)
        self.parts = 2 * z_extent
        self.z_rows = 24 * t_extent
        self.t_rows = 12 * self.parts

    def block(self, k, part):
        first = (k * self.parts + part) * self.rows
        return pl.ds(first, self.rows)

    def edge(self, k, row):
        return pl.ds(k * self.parts * self.rows + row, self.parts, stride=self.rows)


class ChipLinks:
    def __init__(self, shape, ref, row=None):
        self.shape, self.ref, self.row = shape, ref, row

    def __getitem__(self, index):
        direction, row, col, part = index
        first = ((direction * 3 + row) * 3 + col) * 2
        if self.row is None:
            return tuple(self.ref[self.shape.block(first + n, part), :] for n in range(2))
        return tuple(self.ref[self.shape.edge(first + n, self.row), :] for n in range(2))


def components(spins):
    return [(s, c, part, (s * 3 + c) * 2 + part) for s in range(spins) for c in range(3) for part in range(2)]


def gathered_pairs(spins, value):
    out = {}
    for s in range(spins):
        for c in range(3):
            out[s, c] = tuple(value((s * 3 + c) * 2 + part) for part in range(2))
    return out


def chip_psi(shape, ref, part):
    return gathered_pairs(4, lambda k: ref[shape.block(k, part), :])


def chip_edge(shape, ref, row):
    return gathered_pairs(4, lambda k: ref[shape.edge(k, row), :])


def on_first_core():
    return lax.axis_index("gy") == 0


def chip_messages(shape, psi_ref, links_ref, z_second, t_second, z_first, t_first):
    t, last = shape.t, shape.t - 1
    even = is_even("ta")
    minus = project(chip_edge(shape, psi_ref, 0), 3, -1)
    half = project(chip_edge(shape, psi_ref, last), 3, 1)
    carried = mul_link_dag(ChipLinks(shape, links_ref, last), 3, 0, half)
    for s, c, part, k in components(2):
        rows = pl.ds(k * shape.parts, shape.parts)
        up, down = carried[s, c][part], minus[s, c][part]
        t_first[rows, :] = either(even, up, down)
        t_second[rows, :] = either(even, down, up)
    even = is_even("gz")
    links = ChipLinks(shape, links_ref)
    for y_half in range(2):
        minus = project(chip_psi(shape, psi_ref, y_half), 2, -1)
        part_last = shape.parts - 2 + y_half
        half = project(chip_psi(shape, psi_ref, part_last), 2, 1)
        carried = mul_link_dag(links, 2, part_last, half)
        for s, c, part, k in components(2):
            rows = pl.ds((k * 2 + y_half) * t, t)
            up, down = carried[s, c][part][0:t], minus[s, c][part][0:t]
            z_first[rows, :] = either(even, up, down)
            z_second[rows, :] = either(even, down, up)


def chip_bring(shape, y_half, source_ref, links_in, psi_ref, links_ref, arrived):
    t, z_extent = shape.t, shape.z
    last = lax.broadcasted_iota(jnp.int32, (t, shape.lanes), 0) == t - 1
    sign = jnp.where(lax.axis_index("ta") == lax.axis_size("ta") - 1, -1.0, 1.0)
    flip = jnp.where(last, sign, 1.0)

    def bring(in_ref, out_ref, k, z, factor=None):
        value = in_ref[pl.ds(k * t * z_extent + z, t, stride=z_extent), :]
        if factor is not None:
            value = value * factor
        at = (k * shape.parts + 2 * z + y_half) * shape.rows
        out_ref[pl.ds(pl.multiple_of(at, 8), t), :] = value

    arrived(4)
    for z in range(z_extent):
        for k in range(24):
            bring(source_ref, psi_ref, k, z)
    for direction in (3, 2, 1, 0):
        arrived(direction)
        for z in range(z_extent):
            for k in range(18 * direction, 18 * direction + 18):
                bring(links_in, links_ref, k, z, flip if direction == 3 else None)


def chip_own_kernel(
    shape, source_hbm, links_hbm, psi_ref, links_ref, source_ref, links_in, semaphores
):
    part = 18 * shape.t * shape.z
    copies = {4: pltpu.make_async_copy(source_hbm, source_ref, semaphores.at[4])}
    for direction in (3, 2, 1, 0):
        rows = pl.ds(direction * part, part)
        copies[direction] = pltpu.make_async_copy(
            links_hbm.at[rows], links_in.at[rows], semaphores.at[direction]
        )
    for copy in copies.values():
        copy.start()
    if shape.rows != shape.t:
        links_ref[...] = jnp.zeros_like(links_ref)
        psi_ref[...] = jnp.zeros_like(psi_ref)
    chip_bring(
        shape, lax.axis_index("gy"), source_ref, links_in, psi_ref, links_ref,
        lambda n: copies[n].wait(),
    )


def chip_prep_kernel(
    shape, source_ref, links_in, psi_in, links_held, psi_ref, links_ref, *messages
):
    chip_bring(
        shape, 1 - lax.axis_index("gy"), source_ref, links_in, psi_ref, links_ref, lambda n: None
    )
    chip_messages(shape, psi_ref, links_ref, *messages)


def chip_inner_kernel(shape, psi_ref, links_ref, total_ref):
    links = ChipLinks(shape, links_ref)
    lane, row = shape.lane(), shape.row()
    x = lane % X
    lanes, rows, t = shape.lanes, shape.rows, shape.t
    at_end, at_start = x == X - 1, x == 0
    inside_ahead = row < t - 1
    inside_behind = jnp.logical_and(row > 0, row < t)

    def x_ahead(value):
        return jnp.where(
            at_end, pltpu.roll(value, X - 1, 1), pltpu.roll(value, lanes - 1, 1)
        )

    def x_behind(value):
        return jnp.where(at_start, pltpu.roll(value, lanes - X + 1, 1), pltpu.roll(value, 1, 1))

    def t_ahead(value):
        return jnp.where(inside_ahead, pltpu.roll(value, rows - 1, 0), 0.0)

    def t_behind(value):
        return jnp.where(inside_behind, pltpu.roll(value, 1, 0), 0.0)

    for z in range(shape.z):
        for part in (2 * z, 2 * z + 1):
            psi = chip_psi(shape, psi_ref, part)
            zero = jnp.zeros((rows, lanes), jnp.float32)
            total = {key: (zero, zero) for key in psi}
            half = mapped(x_ahead, project(psi, 0, -1))
            add_rebuilt(total, mul_link(links, 0, part, half), 0, -1)
            half = mapped(x_behind, mul_link_dag(links, 0, part, project(psi, 0, 1)))
            add_rebuilt(total, half, 0, 1)
            half = mapped(t_ahead, project(psi, 3, -1))
            add_rebuilt(total, mul_link(links, 3, part, half), 3, -1)
            half = mapped(t_behind, mul_link_dag(links, 3, part, project(psi, 3, 1)))
            add_rebuilt(total, half, 3, 1)
            if z + 1 < shape.z:
                half = project(chip_psi(shape, psi_ref, part + 2), 2, -1)
                add_rebuilt(total, mul_link(links, 2, part, half), 2, -1)
            if z > 0:
                half = project(chip_psi(shape, psi_ref, part - 2), 2, 1)
                add_rebuilt(total, mul_link_dag(links, 2, part - 2, half), 2, 1)
            for s, c, n, k in components(4):
                total_ref[shape.block(k, part), :] = total[s, c][n]
        pair = (2 * z, 2 * z + 1)
        minus, carried = [], []
        for part in pair:
            psi = chip_psi(shape, psi_ref, part)
            minus.append(mapped(lambda v: pltpu.roll(v, lanes - X, 1), project(psi, 1, -1)))
            half = mul_link_dag(links, 1, part, project(psi, 1, 1))
            carried.append(mapped(lambda v: pltpu.roll(v, X, 1), half))
        for own, part in enumerate(pair):
            total = chip_psi(shape, total_ref, part)
            half = mapped(
                lambda a, b: jnp.where(lane >= lanes - X, b, a), minus[own], minus[1 - own]
            )
            add_rebuilt(total, mul_link(links, 1, part, half), 1, -1)
            half = mapped(lambda a, b: jnp.where(lane < X, b, a), carried[own], carried[1 - own])
            add_rebuilt(total, half, 1, 1)
            for s, c, n, k in components(4):
                total_ref[shape.block(k, part), :] = total[s, c][n]


def chip_finish(shape, psi_ref, links_ref, total_ref, received, scratch, out_ref):
    z_second, t_second, z_first, t_first = received
    z_down, z_up = scratch
    t_even, z_even = is_even("ta"), is_even("gz")
    t, rows, lanes, parts = shape.t, shape.rows, shape.lanes, shape.parts
    z_down[...] = either(z_even, z_first[...], z_second[...])
    z_up[...] = either(z_even, z_second[...], z_first[...])
    links = ChipLinks(shape, links_ref)

    def plane(ref, y_half):
        def value(k):
            face = ref[pl.ds((k * 2 + y_half) * t, t), :]
            if rows != t:
                pad = jnp.zeros((rows - t, lanes), jnp.float32)
                face = jnp.concatenate([face, pad], axis=0)
            return face

        return gathered_pairs(2, value)

    for part in range(parts):
        total = chip_psi(shape, total_ref, part)
        if part >= parts - 2:
            half = mul_link(links, 2, part, plane(z_down, part - parts + 2))
            add_rebuilt(total, half, 2, -1)
        if part < 2:
            add_rebuilt(total, plane(z_up, part), 2, 1)
        for s, c, n, k in components(4):
            value = psi_ref[shape.block(k, part), :] - hop_kappa * total[s, c][n]
            out_ref[shape.block(k, part), :] = value if s < 2 else -value

    def t_half(from_even, from_odd):
        def value(k):
            at = pl.ds(k * parts, parts)
            return either(t_even, from_even[at, :], from_odd[at, :])

        return gathered_pairs(2, value)

    down = mul_link(ChipLinks(shape, links_ref, t - 1), 3, 0, t_half(t_first, t_second))
    up = t_half(t_second, t_first)
    zero = jnp.zeros((parts, lanes), jnp.float32)
    for half, parity, row in ((down, -1, t - 1), (up, 1, 0)):
        total = {(s, c): (zero, zero) for s in range(4) for c in range(3)}
        add_rebuilt(total, half, 3, parity)
        for s, c, n, k in components(4):
            at = shape.edge(k, row)
            value = hop_kappa * total[s, c][n]
            out_ref[at, :] = out_ref[at, :] - (value if s < 2 else -value)


def chip_mid_kernel(shape, psi_ref, links_ref, total_ref, *refs):
    received, out_ref, messages, scratch = refs[:4], refs[4], refs[5:9], refs[9:]
    chip_finish(shape, psi_ref, links_ref, total_ref, received, scratch, out_ref)
    chip_messages(shape, out_ref, links_ref, *messages)


def chip_inner_sums_kernel(
    shape, psi_ref, links_ref, start_ref, one_ref, two_ref, total_ref, copies_ref
):
    class View:
        def __init__(self, ref):
            self.ref = ref

        def __getitem__(self, index):
            return self.ref[shape.block(*index), :]

    wide = ChipShape(shape.t, shape.z, shape.lanes)
    wide.z = shape.parts
    rows = local_sums(wide, View(two_ref), View(start_ref))
    rows += local_sums(wide, View(psi_ref), View(one_ref))
    block = jnp.concatenate(rows, axis=0)
    copies_ref[...] = jnp.broadcast_to(block[None], copies_ref.shape)
    chip_inner_kernel(shape, psi_ref, links_ref, total_ref)


def chip_finish_kernel(shape, psi_ref, links_ref, total_ref, *refs):
    received, out_ref, scratch = refs[:4], refs[4], refs[5:]
    chip_finish(shape, psi_ref, links_ref, total_ref, received, scratch, out_ref)


def chip_last_kernel(
    shape, entries, start_ref, two_ref, four_ref, gathered, own_ref, other_ref, coefficients
):
    alpha_one, beta_one, alpha_two, scale, first_factor = scalars(gathered, entries)
    t, z_extent = shape.t, shape.z
    for k in range(24):
        for z in range(z_extent):
            for y_half, out_ref in enumerate((other_ref, own_ref)):
                at = shape.block(k, 2 * z + y_half)
                two, start = two_ref[at, :], start_ref[at, :]
                remain = two - alpha_one * start
                result = (four_ref[at, :] - alpha_one * two - alpha_two * remain) * scale
                result = result - first_factor * start
                out_ref[pl.ds(k * t * z_extent + z, t, stride=z_extent), :] = result[0:t]
    values = jnp.concatenate([alpha_one, beta_one, alpha_two], axis=0)
    values = jnp.concatenate([values, jnp.zeros((5, 1), jnp.float32)], axis=0)
    values = jnp.broadcast_to(values, coefficients.shape)
    coefficients[...] = values
    other_ref[pl.ds(24 * t * z_extent, 8), :] = values


def chip_swap(value, axis, second):
    t_count, z_count = lax.axis_size("ta"), lax.axis_size("gz")
    pairs = []
    for t_index in range(t_count):
        for z_index in range(z_count):
            t_other, z_other = t_index, z_index
            if axis == "ta":
                forward = 1 if (t_index % 2 == 0) != second else -1
                t_other = (t_index + forward) % t_count
            else:
                forward = 1 if (z_index % 2 == 0) != second else -1
                z_other = (z_index + forward) % z_count
            pairs.append(
                ((t_index * z_count + z_index) * 2 + 1, (t_other * z_count + z_other) * 2 + 1)
            )
    return lax.ppermute(value, ("ta", "gz", "gy"), pairs)


def chip_shards(source, gauge_links):
    chips = lax.axis_size("ta") * lax.axis_size("gz")
    entries = float(source.size * chips * 2)
    shape = ChipShape(source.shape[3], source.shape[4], source.shape[5])
    t, z, rows, lanes = shape.t, shape.z, shape.rows, shape.lanes
    vmem = pl.BlockSpec(memory_space=pltpu.VMEM)

    def held(*dims):
        return pltpu.VMEM(dims, jnp.float32)

    field = held(24 * shape.parts * rows, lanes)
    z_face, t_face = held(shape.z_rows, lanes), held(shape.t_rows, lanes)
    messages = (z_face, t_face, z_face, t_face)
    z_faces = (z_face, z_face)

    def call(kernel, name, flops, out_shape, operands, scratch=(), in_spec=vmem, aliases=None):
        return pl.pallas_call(
            kernel,
            name=name,
            out_shape=out_shape,
            in_specs=[in_spec] * len(operands),
            input_output_aliases=aliases or {},
            out_specs=jax.tree.map(lambda _: vmem, out_shape),
            scratch_shapes=scratch,
            compiler_params=pltpu.CompilerParams(vmem_limit_bytes=8 << 20),
            cost_estimate=pl.CostEstimate(flops=flops, bytes_accessed=1 << 20, transcendentals=0),
        )(*operands)

    def exchanged(sent):
        z_second, t_second, z_first, t_first = sent
        return (
            chip_swap(z_second, "gz", True), chip_swap(t_second, "ta", True),
            chip_swap(z_first, "gz", False), chip_swap(t_first, "ta", False),
        )

    sites = 2 * t * z * lanes
    own = (source.reshape(24 * t * z, lanes), gauge_links.reshape(72 * t * z, lanes))
    other = tuple(swap(value, "gy", False) for value in own)
    links_field = held(72 * shape.parts * rows, lanes)
    psi, links = call(
        functools.partial(chip_own_kernel, shape), "own", 200 * sites, (field, links_field),
        [pltpu.with_memory_space_constraint(value, pltpu.HBM) for value in own],
        (held(24 * t * z, lanes), held(72 * t * z, lanes), pltpu.SemaphoreType.DMA((5,))),
        pl.BlockSpec(memory_space=pltpu.HBM),
    )
    psi, links, *sent = call(
        functools.partial(chip_prep_kernel, shape), "prep", 400 * sites,
        (field, links_field, *messages), (*other, psi, links), aliases={2: 0, 3: 1},
    )
    powers = [psi]
    for step in range(3):
        halo = exchanged(sent)
        inner = functools.partial(chip_inner_kernel, shape)
        total = call(inner, "inner", 1500 * sites, field, (psi, links))
        psi, *sent = call(
            functools.partial(chip_mid_kernel, shape), "mid", 300 * sites,
            (field, *messages), (psi, links, total, *halo), scratch=z_faces,
        )
        powers.append(psi)
    halo = exchanged(sent)
    total, copies = call(
        functools.partial(chip_inner_sums_kernel, shape), "inner_sums", 1900 * sites,
        (field, held(chips, 8, lanes)), (psi, links, *powers[:3]),
    )
    gathered = spread(copies, ("ta", "gz")).reshape(-1, lanes)
    four = call(
        functools.partial(chip_finish_kernel, shape), "finish", 200 * sites, field,
        (psi, links, total, *halo), scratch=z_faces,
    )
    rows_out = 24 * t * z
    residual, for_other, coefficients = call(
        functools.partial(chip_last_kernel, shape, entries), "last", 100 * sites,
        (held(rows_out, lanes), held(rows_out + 8, lanes), held(8, lanes)),
        (powers[0], powers[2], four, gathered),
    )
    from_other = swap(for_other, "gy", False)
    first_core = on_first_core()
    residual = jnp.where(first_core, from_other[:rows_out], residual)
    coefficients = jnp.where(first_core, from_other[rows_out:], coefficients)
    return (residual.reshape(source.shape), coefficients[:3, 0])


def solution(mesh):
    placed = (P(None, None, None, "ta", "gz", "gy"), P(None, None, None, None, "ta", "gz", "gy"))
    return jax.shard_map(
        chip_shards if mesh.shape["gy"] == 2 else shards,
        mesh=mesh,
        in_specs=placed,
        out_specs=(P(None, None, None, "ta", "gz", "gy"), P()),
        check_vma=False,
    )
```

```python
import functools

import jax
import jax.numpy as jnp
from jax import lax
from jax.experimental import pallas as pl
from jax.experimental.pallas import tpu as pltpu
from jax.sharding import PartitionSpec as P

X = 32

hop_kappa = 0.19
epsilon = 1e-06
spin_table = (
    ((1, 0), (-1j, -1j)),
    ((1, 0), (-1, 1)),
    ((0, 1), (-1j, 1j)),
    ((0, 1), (1, 1)),
)
SPIN_COLOUR = [(spin, colour) for spin in range(2) for colour in range(3)]


def add_phased(left, phase, right):
    phase = complex(phase)
    if phase == 1:
        return (left[0] + right[0], left[1] + right[1])
    if phase == -1:
        return (left[0] - right[0], left[1] - right[1])
    if phase == 1j:
        return (left[0] - right[1], left[1] + right[0])
    return (left[0] + right[1], left[1] - right[0])


def project(psi, direction, parity):
    order, phases = spin_table[direction]
    return {
        (s, c): add_phased(psi[s, c], parity * phases[s], psi[2 + order[s], c])
        for s, c in SPIN_COLOUR
    }


def add_rebuilt(total, half, direction, parity):
    order, phases = spin_table[direction]
    for s, c in SPIN_COLOUR:
        total[s, c] = add_phased(total[s, c], 1, half[s, c])
        row = order[s]
        phase = parity * complex(phases[row]).conjugate()
        total[2 + s, c] = add_phased(total[2 + s, c], phase, half[row, c])


def mul_link(links, direction, z, half):
    out = {}
    for row in range(3):
        for s in range(2):
            real, imag = None, None
            for col in range(3):
                u_real, u_imag = links[direction, row, col, z]
                h_real, h_imag = half[s, col]
                term_real = u_real * h_real - u_imag * h_imag
                term_imag = u_real * h_imag + u_imag * h_real
                real = term_real if real is None else real + term_real
                imag = term_imag if imag is None else imag + term_imag
            out[s, row] = (real, imag)
    return out


def mul_link_dag(links, direction, z, half):
    out = {}
    for row in range(3):
        for s in range(2):
            real, imag = None, None
            for col in range(3):
                u_real, u_imag = links[direction, col, row, z]
                h_real, h_imag = half[s, col]
                term_real = u_real * h_real + u_imag * h_imag
                term_imag = u_real * h_imag - u_imag * h_real
                real = term_real if real is None else real + term_real
                imag = term_imag if imag is None else imag + term_imag
            out[s, row] = (real, imag)
    return out


def mapped(function, *halves):
    return {
        key: tuple(function(*(half[key][part] for half in halves)) for part in range(2))
        for key in SPIN_COLOUR
    }


class Links:
    def __init__(self, ref):
        self.ref = ref

    def __getitem__(self, index):
        direction, row, col, z = index
        first = ((direction * 3 + row) * 3 + col) * 2
        return (self.ref[first, z], self.ref[first + 1, z])


def load_psi(ref, z):
    return {
        (s, c): (ref[(s * 3 + c) * 2, z], ref[(s * 3 + c) * 2 + 1, z])
        for s in range(4)
        for c in range(3)
    }


def load_half(ref, z):
    return {
        (s, c): (ref[(s * 3 + c) * 2, z], ref[(s * 3 + c) * 2 + 1, z]) for s, c in SPIN_COLOUR
    }


def store_half(ref, z, half):
    for (s, c), pair in half.items():
        for part in range(2):
            ref[(s * 3 + c) * 2 + part, z] = pair[part]


class Shape:
    def __init__(self, t_extent, z_extent, lanes):
        self.t = t_extent
        self.z = z_extent
        self.rows = -(-t_extent // 8) * 8
        self.lanes = lanes

    def row(self):
        return lax.broadcasted_iota(jnp.int32, (self.rows, self.lanes), 0)

    def lane(self):
        return lax.broadcasted_iota(jnp.int32, (self.rows, self.lanes), 1)


def is_even(axis):
    return jnp.bitwise_and(lax.axis_index(axis), 1) == 0


def either(choice, first, second):
    return jnp.where(choice, first, second)


def emit_messages(shape, psi_ref, links, refs):
    z_second, t_second, z_first, t_first, y_msg, carried_y, carried_t = refs
    t_even, z_even = is_even("ta"), is_even("gz")
    lane = shape.lane()
    last_z, last_t = shape.z - 1, shape.t - 1
    for z in range(shape.z):
        psi = load_psi(psi_ref, z)
        minus = project(psi, 3, -1)
        carried = mul_link_dag(links, 3, z, project(psi, 3, 1))
        store_half(carried_t, z, carried)
        for s, c in SPIN_COLOUR:
            for part in range(2):
                at = ((s * 3 + c) * 2 + part) * shape.z + z
                down = minus[s, c][part][0:1]
                up = carried[s, c][part][last_t : last_t + 1]
                t_first[at : at + 1] = either(t_even, up, down)
                t_second[at : at + 1] = either(t_even, down, up)
        minus = project(psi, 1, -1)
        carried = mul_link_dag(links, 1, z, project(psi, 1, 1))
        store_half(carried_y, z, carried)
        store_half(
            y_msg,
            z,
            mapped(lambda low, high: jnp.where(lane < X, low, high), minus, carried),
        )
    minus = project(load_psi(psi_ref, 0), 2, -1)
    carried = mul_link_dag(links, 2, last_z, project(load_psi(psi_ref, last_z), 2, 1))
    for s, c in SPIN_COLOUR:
        for part in range(2):
            at = ((s * 3 + c) * 2 + part) * shape.t
            down, up = minus[s, c][part][0 : shape.t], carried[s, c][part][0 : shape.t]
            z_first[at : at + shape.t] = either(z_even, up, down)
            z_second[at : at + shape.t] = either(z_even, down, up)


def prep_kernel(shape, source_hbm, links_hbm, psi_ref, links_ref, *refs):
    messages, (source_ref, links_in, arrived) = refs[:-3], refs[-3:]
    t, z_extent = shape.t, shape.z
    part = 18 * t * z_extent
    copies = [pltpu.make_async_copy(source_hbm, source_ref, arrived.at[4])]
    for direction in (3, 2, 1, 0):
        rows = pl.ds(direction * part, part)
        copies.append(
            pltpu.make_async_copy(links_hbm.at[rows], links_in.at[rows], arrived.at[direction])
        )
    for copy in copies:
        copy.start()
    if shape.rows != t:
        links_ref[...] = jnp.zeros_like(links_ref)
        psi_ref[...] = jnp.zeros_like(psi_ref)
    last = lax.broadcasted_iota(jnp.int32, (t, shape.lanes), 0) == t - 1
    sign = jnp.where(lax.axis_index("ta") == lax.axis_size("ta") - 1, -1.0, 1.0)
    flip = jnp.where(last, sign, 1.0)
    copies[0].wait()
    for k in range(24):
        for z in range(z_extent):
            psi_ref[k, z, 0:t] = source_ref[pl.ds(k * t * z_extent + z, t, stride=z_extent), :]
    for direction in (3, 2, 1, 0):
        copies[4 - direction].wait()
        for k in range(18 * direction, 18 * direction + 18):
            for z in range(z_extent):
                value = links_in[pl.ds(k * t * z_extent + z, t, stride=z_extent), :]
                links_ref[k, z, 0:t] = value * flip if direction == 3 else value
    emit_messages(shape, psi_ref, Links(links_ref), messages)


def summed(shape, term):
    total = None
    for k in range(24):
        for z in range(shape.z):
            value = term(k, z)
            total = value if total is None else total + value
    return total


def over_lanes(total):
    return jnp.sum(jnp.sum(total, axis=0, keepdims=True), axis=1, keepdims=True)


def local_sums(shape, image, origin):
    square = summed(shape, lambda k, z: origin[k, z] * origin[k, z])
    mixed = over_lanes(summed(shape, lambda k, z: image[k, z] * origin[k, z]))
    whole = over_lanes(square)
    factor = jnp.where(whole > 0.0, mixed / jnp.where(whole > 0.0, whole, 1.0), 0.0)
    spread = jnp.broadcast_to(factor, (shape.rows, shape.lanes))
    rest_square, rest_mixed = None, None
    for k in range(24):
        for z in range(shape.z):
            start = origin[k, z]
            rest = image[k, z] - spread * start
            terms = rest * rest, rest * start
            if rest_square is None:
                rest_square, rest_mixed = terms
            else:
                rest_square, rest_mixed = rest_square + terms[0], rest_mixed + terms[1]
    return [factor, *(over_lanes(value) for value in (square, rest_square, rest_mixed))]


def inner_kernel(shape, psi_ref, links_ref, total_ref):
    links = Links(links_ref)
    x = shape.lane() % X
    lanes = shape.lanes
    at_end, at_start = x == X - 1, x == 0

    def ahead(value):
        return jnp.where(
            at_end, pltpu.roll(value, X - 1, 1), pltpu.roll(value, lanes - 1, 1)
        )

    def behind(value):
        return jnp.where(at_start, pltpu.roll(value, lanes - X + 1, 1), pltpu.roll(value, 1, 1))

    for z in range(shape.z):
        psi = load_psi(psi_ref, z)
        zero = jnp.zeros((shape.rows, lanes), jnp.float32)
        total = {key: (zero, zero) for key in psi}
        half = mapped(ahead, project(psi, 0, -1))
        add_rebuilt(total, mul_link(links, 0, z, half), 0, -1)
        half = mapped(behind, mul_link_dag(links, 0, z, project(psi, 0, 1)))
        add_rebuilt(total, half, 0, 1)
        if z + 1 < shape.z:
            half = project(load_psi(psi_ref, z + 1), 2, -1)
            add_rebuilt(total, mul_link(links, 2, z, half), 2, -1)
        if z > 0:
            half = project(load_psi(psi_ref, z - 1), 2, 1)
            add_rebuilt(total, mul_link_dag(links, 2, z - 1, half), 2, 1)
        for (s, c), pair in total.items():
            for part in range(2):
                total_ref[(s * 3 + c) * 2 + part, z] = pair[part]


def add_y_hops(shape, z, psi, total, links, carried_y, y_halo):
    lane, lanes = shape.lane(), shape.lanes
    received = load_half(y_halo, z)
    half = mapped(
        lambda own, other: pltpu.roll(jnp.where(lane < X, other, own), lanes - X, 1),
        project(psi, 1, -1),
        received,
    )
    add_rebuilt(total, mul_link(links, 1, z, half), 1, -1)
    half = mapped(
        lambda own, other: pltpu.roll(jnp.where(lane >= lanes - X, other, own), X, 1),
        load_half(carried_y, z),
        received,
    )
    add_rebuilt(total, half, 1, 1)


def finish_hops(
    shape, psi_ref, links, total_ref, carried_y, carried_t, halo, store
):
    z_second, t_second, z_first, t_first, y_msg = halo
    t_even, z_even = is_even("ta"), is_even("gz")
    row = shape.row()
    lanes, rows, t = shape.lanes, shape.rows, shape.t
    last_z = shape.z - 1

    for z in range(shape.z):
        psi = load_psi(psi_ref, z)
        total = load_psi(total_ref, z)

        def rim_rows(from_even, from_odd):
            half = {}
            for s, c in SPIN_COLOUR:
                ats = [((s * 3 + c) * 2 + part) * shape.z + z for part in range(2)]
                half[s, c] = tuple(
                    jnp.broadcast_to(
                        either(t_even, from_even[at : at + 1], from_odd[at : at + 1]),
                        (rows, lanes),
                    )
                    for at in ats
                )
            return half

        def rim_plane(from_even, from_odd):
            half = {}
            for s, c in SPIN_COLOUR:
                pair = []
                for part in range(2):
                    at = ((s * 3 + c) * 2 + part) * t
                    plane = either(z_even, from_even[at : at + t], from_odd[at : at + t])
                    if rows != t:
                        pad = jnp.zeros((rows - t, lanes), jnp.float32)
                        plane = jnp.concatenate([plane, pad], axis=0)
                    pair.append(plane)
                half[s, c] = tuple(pair)
            return half

        if y_msg is not None:
            add_y_hops(shape, z, psi, total, links, carried_y, y_msg)
        if z == last_z:
            add_rebuilt(total, mul_link(links, 2, z, rim_plane(z_first, z_second)), 2, -1)
        if z == 0:
            add_rebuilt(total, rim_plane(z_second, z_first), 2, 1)
        half = mapped(
            lambda own, other: jnp.where(row == t - 1, other, pltpu.roll(own, rows - 1, 0)),
            project(psi, 3, -1),
            rim_rows(t_first, t_second),
        )
        add_rebuilt(total, mul_link(links, 3, z, half), 3, -1)
        half = mapped(
            lambda own, other: jnp.where(row == 0, other, pltpu.roll(own, 1, 0)),
            load_half(carried_t, z),
            rim_rows(t_second, t_first),
        )
        add_rebuilt(total, half, 3, 1)
        for (s, c), pair in total.items():
            for part in range(2):
                value = psi[s, c][part] - hop_kappa * pair[part]
                value = value if s < 2 else -value
                if rows != t:
                    value = jnp.where(row < t, value, 0.0)
                store((s * 3 + c) * 2 + part, z, value)


def mid_kernel(shape, psi_ref, links_ref, total_ref, carried_y, carried_t, *refs):
    halo, out_ref, messages = refs[:5], refs[5], refs[6:]
    links = Links(links_ref)

    def store(k, z, value):
        out_ref[k, z] = value

    finish_hops(
        shape, psi_ref, links, total_ref, carried_y, carried_t, halo, store
    )
    emit_messages(shape, out_ref, links, messages)


def inner_sums_kernel(
    shape, psi_ref, links_ref, carried_y, y_halo, start_ref, one_ref, two_ref,
    total_ref, copies_ref,
):
    sums = local_sums(shape, two_ref, start_ref) + local_sums(shape, psi_ref, one_ref)
    lane = lax.broadcasted_iota(jnp.int32, (1, shape.lanes), 1)
    row = jnp.zeros((1, shape.lanes), jnp.float32)
    for k, value in enumerate(sums):
        row = jnp.where(lane == k, value, row)
    copies_ref[...] = jnp.broadcast_to(row[None], copies_ref.shape)
    inner_kernel(shape, psi_ref, links_ref, total_ref)
    for z in range(shape.z):
        total = load_psi(total_ref, z)
        add_y_hops(shape, z, load_psi(psi_ref, z), total, Links(links_ref), carried_y, y_halo)
        for (s, c), pair in total.items():
            for part in range(2):
                total_ref[(s * 3 + c) * 2 + part, z] = pair[part]


def finish_kernel(shape, psi_ref, links_ref, total_ref, carried_t, *refs):
    halo, out_ref = (*refs[:4], None), refs[4]

    def store(k, z, value):
        out_ref[k, z] = value

    finish_hops(
        shape, psi_ref, Links(links_ref), total_ref, None, carried_t, halo, store
    )


def last_kernel(
    shape, entries, start_ref, two_ref, four_ref, gathered, out_ref, coefficients
):
    table = gathered[:, 0, :]
    columns = [table[:, k : k + 1] for k in range(8)]
    factor_two, start_square, two_square, two_mixed = columns[:4]
    factor_three, one_square, three_square, three_mixed = columns[4:]

    def over_devices(column):
        return jnp.sum(column, axis=0, keepdims=True)

    norm_square = over_devices(start_square) / entries + epsilon
    alpha_one = over_devices(one_square) / entries / norm_square
    gap = alpha_one - factor_two
    remain_square = over_devices(two_square - gap * (2.0 * two_mixed - gap * start_square)) / entries
    overlap = over_devices(two_mixed - gap * start_square) / entries
    gap = alpha_one - factor_three
    image_square = over_devices(three_square - gap * (2.0 * three_mixed - gap * one_square)) / entries
    norm = jnp.sqrt(norm_square)
    beta_one = jnp.sqrt(remain_square / norm_square + epsilon)
    overlap = overlap / (norm_square * beta_one)
    alpha_two = image_square / (norm_square * beta_one * beta_one) - beta_one * overlap
    scale = 1.0 / (norm * beta_one)
    first_factor = beta_one / norm
    t, z_extent = shape.t, shape.z
    for k in range(24):
        for z in range(z_extent):
            two, start = two_ref[k, z], start_ref[k, z]
            remain = two - alpha_one * start
            result = (four_ref[k, z] - alpha_one * two - alpha_two * remain) * scale
            result = result - first_factor * start
            out_ref[pl.ds(k * t * z_extent + z, t, stride=z_extent), :] = result[0:t]
    coefficients[0] = alpha_one[0, 0]
    coefficients[1] = beta_one[0, 0]
    coefficients[2] = alpha_two[0, 0]


def swap(value, axis, second):
    count = lax.axis_size(axis)
    pairs = []
    for low in range(1 if second else 0, count, 2):
        high = (low + 1) % count
        pairs += [(low, high), (high, low)]
    return lax.ppermute(value, axis, pairs)


def exchange(messages, lanes):
    z_second, t_second, z_first, t_first, y_msg = messages
    halo = (
        swap(z_second, "gz", True),
        swap(t_second, "ta", True),
        swap(z_first, "gz", False),
        swap(t_first, "ta", False),
    )
    y_halo = swap(y_msg, "gy", False)
    if lax.axis_size("gy") > 2:
        even = lax.axis_index("gy") % 2 == 0
        lane = lax.broadcasted_iota(jnp.int32, y_msg.shape, y_msg.ndim - 1)
        y_halo = jnp.where((lane < lanes // 2) == even, y_halo, swap(y_msg, "gy", True))
    return (*halo, y_halo)


def from_everyone(copies):
    return lax.all_to_all(copies, ("ta", "gz", "gy"), split_axis=0, concat_axis=0, tiled=True)


def shards(source, gauge_links):
    devices_all = lax.axis_size("ta") * lax.axis_size("gz") * lax.axis_size("gy")
    entries = float(source.size * devices_all)
    shape = Shape(source.shape[3], source.shape[4], source.shape[5])
    t, z, rows, lanes = shape.t, shape.z, shape.rows, shape.lanes
    vmem = pl.BlockSpec(memory_space=pltpu.VMEM)
    smem = pl.BlockSpec(memory_space=pltpu.SMEM)

    def held(*dims):
        return pltpu.VMEM(dims, jnp.float32)

    field = held(24, z, rows, lanes)
    half = held(12, z, rows, lanes)
    z_face, t_face = held(12 * t, lanes), held(12 * z, lanes)
    messages = (z_face, t_face, z_face, t_face, half, half, half)

    def call(kernel, name, flops, out_shape, operands, out_specs=None, in_spec=vmem, scratch=()):
        return pl.pallas_call(
            kernel,
            name=name,
            out_shape=out_shape,
            in_specs=[in_spec] * len(operands),
            out_specs=out_specs or jax.tree.map(lambda _: vmem, out_shape),
            scratch_shapes=scratch,
            compiler_params=pltpu.CompilerParams(vmem_limit_bytes=8 << 20),
            cost_estimate=pl.CostEstimate(flops=flops, bytes_accessed=1 << 20, transcendentals=0),
        )(*operands)

    sites = t * z * lanes
    psi, links, *sent = call(
        functools.partial(prep_kernel, shape), "prep", 400 * sites,
        (field, held(72, z, rows, lanes), *messages),
        (
            pltpu.with_memory_space_constraint(source.reshape(24 * t * z, lanes), pltpu.HBM),
            pltpu.with_memory_space_constraint(gauge_links.reshape(72 * t * z, lanes), pltpu.HBM),
        ),
        in_spec=pl.BlockSpec(memory_space=pltpu.HBM),
        scratch=(
            held(24 * t * z, lanes), held(72 * t * z, lanes), pltpu.SemaphoreType.DMA((5,)),
        ),
    )
    powers = [psi]
    for step in range(3):
        halo = exchange(sent[:5], lanes)
        inner = functools.partial(inner_kernel, shape)
        total = call(inner, "inner", 700 * sites, field, (psi, links))
        psi, *sent = call(
            functools.partial(mid_kernel, shape), "mid", 1000 * sites,
            (field, *messages), (psi, links, total, *sent[5:], *halo),
        )
        powers.append(psi)
    halo = exchange(sent[:5], lanes)
    total, copies = call(
        functools.partial(inner_sums_kernel, shape), "inner_sums", 1100 * sites,
        (field, held(devices_all, 1, lanes)), (psi, links, sent[5], halo[4], *powers[:3]),
    )
    gathered = from_everyone(copies)
    four = call(
        functools.partial(finish_kernel, shape), "finish", 700 * sites, field,
        (psi, links, total, sent[6], *halo[:4]),
    )
    residual, coefficients = call(
        functools.partial(last_kernel, shape, entries), "last", 100 * sites,
        (
            jax.ShapeDtypeStruct((24 * t * z, lanes), jnp.float32),
            jax.ShapeDtypeStruct((3,), jnp.float32),
        ),
        (powers[0], powers[2], four, gathered), (vmem, smem),
    )
    return (residual.reshape(source.shape), coefficients)


def solution(mesh):
    placed = (P(None, None, None, "ta", "gz", "gy"), P(None, None, None, None, "ta", "gz", "gy"))
    return jax.shard_map(
        shards,
        mesh=mesh,
        in_specs=placed,
        out_specs=(P(None, None, None, "ta", "gz", "gy"), P()),
        check_vma=False,
    )
```

```python
import functools

import jax
import jax.numpy as jnp
from jax import lax
from jax.experimental import pallas as pl
from jax.experimental.pallas import tpu as pltpu
from jax.sharding import PartitionSpec as P

X = 32

hop_kappa = 0.19
epsilon = 1e-06
spin_table = (
    ((1, 0), (-1j, -1j)),
    ((1, 0), (-1, 1)),
    ((0, 1), (-1j, 1j)),
    ((0, 1), (1, 1)),
)
SPIN_COLOUR = [(spin, colour) for spin in range(2) for colour in range(3)]


def add_phased(left, phase, right):
    phase = complex(phase)
    if phase == 1:
        return (left[0] + right[0], left[1] + right[1])
    if phase == -1:
        return (left[0] - right[0], left[1] - right[1])
    if phase == 1j:
        return (left[0] - right[1], left[1] + right[0])
    return (left[0] + right[1], left[1] - right[0])


def project(psi, direction, parity):
    order, phases = spin_table[direction]
    return {
        (s, c): add_phased(psi[s, c], parity * phases[s], psi[2 + order[s], c])
        for s, c in SPIN_COLOUR
    }


def add_rebuilt(total, half, direction, parity):
    order, phases = spin_table[direction]
    for s, c in SPIN_COLOUR:
        total[s, c] = add_phased(total[s, c], 1, half[s, c])
        row = order[s]
        phase = parity * complex(phases[row]).conjugate()
        total[2 + s, c] = add_phased(total[2 + s, c], phase, half[row, c])


def mul_link(links, direction, z, half):
    out = {}
    for row in range(3):
        for s in range(2):
            real, imag = None, None
            for col in range(3):
                u_real, u_imag = links[direction, row, col, z]
                h_real, h_imag = half[s, col]
                term_real = u_real * h_real - u_imag * h_imag
                term_imag = u_real * h_imag + u_imag * h_real
                real = term_real if real is None else real + term_real
                imag = term_imag if imag is None else imag + term_imag
            out[s, row] = (real, imag)
    return out


def mul_link_dag(links, direction, z, half):
    out = {}
    for row in range(3):
        for s in range(2):
            real, imag = None, None
            for col in range(3):
                u_real, u_imag = links[direction, col, row, z]
                h_real, h_imag = half[s, col]
                term_real = u_real * h_real + u_imag * h_imag
                term_imag = u_real * h_imag - u_imag * h_real
                real = term_real if real is None else real + term_real
                imag = term_imag if imag is None else imag + term_imag
            out[s, row] = (real, imag)
    return out


def mapped(function, *halves):
    return {
        key: tuple(function(*(half[key][part] for half in halves)) for part in range(2))
        for key in SPIN_COLOUR
    }


class Links:
    def __init__(self, ref):
        self.ref = ref

    def __getitem__(self, index):
        direction, row, col, z = index
        first = ((direction * 3 + row) * 3 + col) * 2
        return (self.ref[first, z], self.ref[first + 1, z])


def load_psi(ref, z):
    return {
        (s, c): (ref[(s * 3 + c) * 2, z], ref[(s * 3 + c) * 2 + 1, z])
        for s in range(4)
        for c in range(3)
    }


def load_half(ref, z):
    return {
        (s, c): (ref[(s * 3 + c) * 2, z], ref[(s * 3 + c) * 2 + 1, z]) for s, c in SPIN_COLOUR
    }


def store_half(ref, z, half):
    for (s, c), pair in half.items():
        for part in range(2):
            ref[(s * 3 + c) * 2 + part, z] = pair[part]


class Shape:
    def __init__(self, t_extent, z_extent, lanes):
        self.t = t_extent
        self.z = z_extent
        self.rows = -(-t_extent // 8) * 8
        self.lanes = lanes

    def row(self):
        return lax.broadcasted_iota(jnp.int32, (self.rows, self.lanes), 0)

    def lane(self):
        return lax.broadcasted_iota(jnp.int32, (self.rows, self.lanes), 1)


def is_even(axis):
    return jnp.bitwise_and(lax.axis_index(axis), 1) == 0


def either(choice, first, second):
    return jnp.where(choice, first, second)


def emit_messages(shape, psi_ref, links, refs):
    z_second, t_second, z_first, t_first, y_msg, carried_y, carried_t = refs
    t_even, z_even = is_even("ta"), is_even("gz")
    lane = shape.lane()
    last_z, last_t = shape.z - 1, shape.t - 1
    for z in range(shape.z):
        psi = load_psi(psi_ref, z)
        minus = project(psi, 3, -1)
        carried = mul_link_dag(links, 3, z, project(psi, 3, 1))
        store_half(carried_t, z, carried)
        for s, c in SPIN_COLOUR:
            for part in range(2):
                at = ((s * 3 + c) * 2 + part) * shape.z + z
                down = minus[s, c][part][0:1]
                up = carried[s, c][part][last_t : last_t + 1]
                t_first[at : at + 1] = either(t_even, up, down)
                t_second[at : at + 1] = either(t_even, down, up)
        minus = project(psi, 1, -1)
        carried = mul_link_dag(links, 1, z, project(psi, 1, 1))
        store_half(carried_y, z, carried)
        store_half(
            y_msg,
            z,
            mapped(lambda low, high: jnp.where(lane < X, low, high), minus, carried),
        )
    minus = project(load_psi(psi_ref, 0), 2, -1)
    carried = mul_link_dag(links, 2, last_z, project(load_psi(psi_ref, last_z), 2, 1))
    for s, c in SPIN_COLOUR:
        for part in range(2):
            at = ((s * 3 + c) * 2 + part) * shape.t
            down, up = minus[s, c][part][0 : shape.t], carried[s, c][part][0 : shape.t]
            z_first[at : at + shape.t] = either(z_even, up, down)
            z_second[at : at + shape.t] = either(z_even, down, up)


def prep_kernel(shape, source_hbm, links_hbm, psi_ref, links_ref, *refs):
    messages, (source_ref, links_in, arrived) = refs[:-3], refs[-3:]
    t, z_extent = shape.t, shape.z
    part = 18 * t * z_extent
    copies = [pltpu.make_async_copy(source_hbm, source_ref, arrived.at[4])]
    for direction in (3, 2, 1, 0):
        rows = pl.ds(direction * part, part)
        copies.append(
            pltpu.make_async_copy(links_hbm.at[rows], links_in.at[rows], arrived.at[direction])
        )
    for copy in copies:
        copy.start()
    if shape.rows != t:
        links_ref[...] = jnp.zeros_like(links_ref)
        psi_ref[...] = jnp.zeros_like(psi_ref)
    last = lax.broadcasted_iota(jnp.int32, (t, shape.lanes), 0) == t - 1
    sign = jnp.where(lax.axis_index("ta") == lax.axis_size("ta") - 1, -1.0, 1.0)
    flip = jnp.where(last, sign, 1.0)
    copies[0].wait()
    for k in range(24):
        for z in range(z_extent):
            psi_ref[k, z, 0:t] = source_ref[pl.ds(k * t * z_extent + z, t, stride=z_extent), :]
    for direction in (3, 2, 1, 0):
        copies[4 - direction].wait()
        for k in range(18 * direction, 18 * direction + 18):
            for z in range(z_extent):
                value = links_in[pl.ds(k * t * z_extent + z, t, stride=z_extent), :]
                links_ref[k, z, 0:t] = value * flip if direction == 3 else value
    emit_messages(shape, psi_ref, Links(links_ref), messages)


def summed(shape, term):
    total = None
    for k in range(24):
        for z in range(shape.z):
            value = term(k, z)
            total = value if total is None else total + value
    return total


def over_lanes(total):
    return jnp.sum(jnp.sum(total, axis=0, keepdims=True), axis=1, keepdims=True)


def local_sums(shape, image, origin):
    square = summed(shape, lambda k, z: origin[k, z] * origin[k, z])
    mixed = over_lanes(summed(shape, lambda k, z: image[k, z] * origin[k, z]))
    whole = over_lanes(square)
    factor = jnp.where(whole > 0.0, mixed / jnp.where(whole > 0.0, whole, 1.0), 0.0)
    spread = jnp.broadcast_to(factor, (shape.rows, shape.lanes))
    rest_square, rest_mixed = None, None
    for k in range(24):
        for z in range(shape.z):
            start = origin[k, z]
            rest = image[k, z] - spread * start
            terms = rest * rest, rest * start
            if rest_square is None:
                rest_square, rest_mixed = terms
            else:
                rest_square, rest_mixed = rest_square + terms[0], rest_mixed + terms[1]
    return [factor, *(over_lanes(value) for value in (square, rest_square, rest_mixed))]


def inner_kernel(shape, psi_ref, links_ref, total_ref):
    links = Links(links_ref)
    x = shape.lane() % X
    lanes = shape.lanes
    at_end, at_start = x == X - 1, x == 0

    def ahead(value):
        return jnp.where(
            at_end, pltpu.roll(value, X - 1, 1), pltpu.roll(value, lanes - 1, 1)
        )

    def behind(value):
        return jnp.where(at_start, pltpu.roll(value, lanes - X + 1, 1), pltpu.roll(value, 1, 1))

    for z in range(shape.z):
        psi = load_psi(psi_ref, z)
        zero = jnp.zeros((shape.rows, lanes), jnp.float32)
        total = {key: (zero, zero) for key in psi}
        half = mapped(ahead, project(psi, 0, -1))
        add_rebuilt(total, mul_link(links, 0, z, half), 0, -1)
        half = mapped(behind, mul_link_dag(links, 0, z, project(psi, 0, 1)))
        add_rebuilt(total, half, 0, 1)
        if z + 1 < shape.z:
            half = project(load_psi(psi_ref, z + 1), 2, -1)
            add_rebuilt(total, mul_link(links, 2, z, half), 2, -1)
        if z > 0:
            half = project(load_psi(psi_ref, z - 1), 2, 1)
            add_rebuilt(total, mul_link_dag(links, 2, z - 1, half), 2, 1)
        for (s, c), pair in total.items():
            for part in range(2):
                total_ref[(s * 3 + c) * 2 + part, z] = pair[part]


def add_y_hops(shape, z, psi, total, links, carried_y, y_halo):
    lane, lanes = shape.lane(), shape.lanes
    received = load_half(y_halo, z)
    half = mapped(
        lambda own, other: pltpu.roll(jnp.where(lane < X, other, own), lanes - X, 1),
        project(psi, 1, -1),
        received,
    )
    add_rebuilt(total, mul_link(links, 1, z, half), 1, -1)
    half = mapped(
        lambda own, other: pltpu.roll(jnp.where(lane >= lanes - X, other, own), X, 1),
        load_half(carried_y, z),
        received,
    )
    add_rebuilt(total, half, 1, 1)


def add_z_hops(shape, z, total, links, z_second, z_first):
    z_even, t, rows, lanes = is_even("gz"), shape.t, shape.rows, shape.lanes

    def rim_plane(from_even, from_odd):
        half = {}
        for s, c in SPIN_COLOUR:
            pair = []
            for part in range(2):
                at = ((s * 3 + c) * 2 + part) * t
                plane = either(z_even, from_even[at : at + t], from_odd[at : at + t])
                if rows != t:
                    pad = jnp.zeros((rows - t, lanes), jnp.float32)
                    plane = jnp.concatenate([plane, pad], axis=0)
                pair.append(plane)
            half[s, c] = tuple(pair)
        return half

    if z == shape.z - 1:
        add_rebuilt(total, mul_link(links, 2, z, rim_plane(z_first, z_second)), 2, -1)
    if z == 0:
        add_rebuilt(total, rim_plane(z_second, z_first), 2, 1)


def finish_hops(
    shape, psi_ref, links, total_ref, carried_y, carried_t, halo, store
):
    z_second, t_second, z_first, t_first, y_msg = halo
    t_even = is_even("ta")
    row = shape.row()
    lanes, rows, t = shape.lanes, shape.rows, shape.t

    for z in range(shape.z):
        psi = load_psi(psi_ref, z)
        total = load_psi(total_ref, z)

        def rim_rows(from_even, from_odd):
            half = {}
            for s, c in SPIN_COLOUR:
                ats = [((s * 3 + c) * 2 + part) * shape.z + z for part in range(2)]
                half[s, c] = tuple(
                    jnp.broadcast_to(
                        either(t_even, from_even[at : at + 1], from_odd[at : at + 1]),
                        (rows, lanes),
                    )
                    for at in ats
                )
            return half

        if y_msg is not None:
            add_y_hops(shape, z, psi, total, links, carried_y, y_msg)
        if z_first is not None:
            add_z_hops(shape, z, total, links, z_second, z_first)
        half = mapped(
            lambda own, other: jnp.where(row == t - 1, other, pltpu.roll(own, rows - 1, 0)),
            project(psi, 3, -1),
            rim_rows(t_first, t_second),
        )
        add_rebuilt(total, mul_link(links, 3, z, half), 3, -1)
        half = mapped(
            lambda own, other: jnp.where(row == 0, other, pltpu.roll(own, 1, 0)),
            load_half(carried_t, z),
            rim_rows(t_second, t_first),
        )
        add_rebuilt(total, half, 3, 1)
        for (s, c), pair in total.items():
            for part in range(2):
                value = psi[s, c][part] - hop_kappa * pair[part]
                value = value if s < 2 else -value
                if rows != t:
                    value = jnp.where(row < t, value, 0.0)
                store((s * 3 + c) * 2 + part, z, value)


def mid_kernel(shape, psi_ref, links_ref, total_ref, carried_y, carried_t, *refs):
    halo, out_ref, messages = refs[:5], refs[5], refs[6:]
    links = Links(links_ref)

    def store(k, z, value):
        out_ref[k, z] = value

    finish_hops(
        shape, psi_ref, links, total_ref, carried_y, carried_t, halo, store
    )
    emit_messages(shape, out_ref, links, messages)


def inner_sums_kernel(
    shape, psi_ref, links_ref, start_ref, one_ref, two_ref, total_ref, row_ref
):
    sums = local_sums(shape, two_ref, start_ref) + local_sums(shape, psi_ref, one_ref)
    lane = lax.broadcasted_iota(jnp.int32, (1, shape.lanes), 1)
    row = jnp.zeros((1, shape.lanes), jnp.float32)
    for k, value in enumerate(sums):
        row = jnp.where(lane == k, value, row)
    row_ref[...] = row
    inner_kernel(shape, psi_ref, links_ref, total_ref)


def rim_kernel(
    shape, psi_ref, links_ref, total_in, carried_y, z_second, z_first, y_halo, row_ref,
    total_ref, copies_ref,
):
    copies_ref[...] = jnp.broadcast_to(row_ref[...][None], copies_ref.shape)
    links = Links(links_ref)
    for z in range(shape.z):
        total = load_psi(total_in, z)
        add_y_hops(shape, z, load_psi(psi_ref, z), total, links, carried_y, y_halo)
        add_z_hops(shape, z, total, links, z_second, z_first)
        for (s, c), pair in total.items():
            for part in range(2):
                total_ref[(s * 3 + c) * 2 + part, z] = pair[part]


def finish_kernel(shape, psi_ref, links_ref, total_ref, carried_t, t_second, t_first, out_ref):
    halo = None, t_second, None, t_first, None

    def store(k, z, value):
        out_ref[k, z] = value

    finish_hops(
        shape, psi_ref, Links(links_ref), total_ref, None, carried_t, halo, store
    )


def last_kernel(
    shape, entries, start_ref, two_ref, four_ref, gathered, out_ref, coefficients
):
    table = gathered[:, 0, :]
    columns = [table[:, k : k + 1] for k in range(8)]
    factor_two, start_square, two_square, two_mixed = columns[:4]
    factor_three, one_square, three_square, three_mixed = columns[4:]

    def over_devices(column):
        return jnp.sum(column, axis=0, keepdims=True)

    norm_square = over_devices(start_square) / entries + epsilon
    alpha_one = over_devices(one_square) / entries / norm_square
    gap = alpha_one - factor_two
    remain_square = over_devices(two_square - gap * (2.0 * two_mixed - gap * start_square)) / entries
    overlap = over_devices(two_mixed - gap * start_square) / entries
    gap = alpha_one - factor_three
    image_square = over_devices(three_square - gap * (2.0 * three_mixed - gap * one_square)) / entries
    norm = jnp.sqrt(norm_square)
    beta_one = jnp.sqrt(remain_square / norm_square + epsilon)
    overlap = overlap / (norm_square * beta_one)
    alpha_two = image_square / (norm_square * beta_one * beta_one) - beta_one * overlap
    scale = 1.0 / (norm * beta_one)
    first_factor = beta_one / norm
    t, z_extent = shape.t, shape.z
    for k in range(24):
        for z in range(z_extent):
            two, start = two_ref[k, z], start_ref[k, z]
            remain = two - alpha_one * start
            result = (four_ref[k, z] - alpha_one * two - alpha_two * remain) * scale
            result = result - first_factor * start
            out_ref[pl.ds(k * t * z_extent + z, t, stride=z_extent), :] = result[0:t]
    coefficients[0] = alpha_one[0, 0]
    coefficients[1] = beta_one[0, 0]
    coefficients[2] = alpha_two[0, 0]


def swap(value, axis, second):
    count = lax.axis_size(axis)
    pairs = []
    for low in range(1 if second else 0, count, 2):
        high = (low + 1) % count
        pairs += [(low, high), (high, low)]
    return lax.ppermute(value, axis, pairs)


def exchange(messages, lanes):
    z_second, t_second, z_first, t_first, y_msg = messages
    halo = (
        swap(z_second, "gz", True),
        swap(t_second, "ta", True),
        swap(z_first, "gz", False),
        swap(t_first, "ta", False),
    )
    y_halo = swap(y_msg, "gy", False)
    if lax.axis_size("gy") > 2:
        even = lax.axis_index("gy") % 2 == 0
        lane = lax.broadcasted_iota(jnp.int32, y_msg.shape, y_msg.ndim - 1)
        y_halo = jnp.where((lane < lanes // 2) == even, y_halo, swap(y_msg, "gy", True))
    return (*halo, y_halo)


def from_everyone(copies):
    return lax.all_to_all(copies, ("ta", "gz", "gy"), split_axis=0, concat_axis=0, tiled=True)


def shards(source, gauge_links):
    devices_all = lax.axis_size("ta") * lax.axis_size("gz") * lax.axis_size("gy")
    entries = float(source.size * devices_all)
    shape = Shape(source.shape[3], source.shape[4], source.shape[5])
    t, z, rows, lanes = shape.t, shape.z, shape.rows, shape.lanes
    vmem = pl.BlockSpec(memory_space=pltpu.VMEM)
    smem = pl.BlockSpec(memory_space=pltpu.SMEM)

    def held(*dims):
        return pltpu.VMEM(dims, jnp.float32)

    field = held(24, z, rows, lanes)
    half = held(12, z, rows, lanes)
    z_face, t_face = held(12 * t, lanes), held(12 * z, lanes)
    messages = (z_face, t_face, z_face, t_face, half, half, half)

    def call(kernel, name, flops, out_shape, operands, out_specs=None, in_spec=vmem, scratch=()):
        return pl.pallas_call(
            kernel,
            name=name,
            out_shape=out_shape,
            in_specs=[in_spec] * len(operands),
            out_specs=out_specs or jax.tree.map(lambda _: vmem, out_shape),
            scratch_shapes=scratch,
            compiler_params=pltpu.CompilerParams(vmem_limit_bytes=8 << 20),
            cost_estimate=pl.CostEstimate(flops=flops, bytes_accessed=1 << 20, transcendentals=0),
        )(*operands)

    sites = t * z * lanes
    psi, links, *sent = call(
        functools.partial(prep_kernel, shape), "prep", 400 * sites,
        (field, held(72, z, rows, lanes), *messages),
        (
            pltpu.with_memory_space_constraint(source.reshape(24 * t * z, lanes), pltpu.HBM),
            pltpu.with_memory_space_constraint(gauge_links.reshape(72 * t * z, lanes), pltpu.HBM),
        ),
        in_spec=pl.BlockSpec(memory_space=pltpu.HBM),
        scratch=(
            held(24 * t * z, lanes), held(72 * t * z, lanes), pltpu.SemaphoreType.DMA((5,)),
        ),
    )
    powers = [psi]
    for step in range(3):
        halo = exchange(sent[:5], lanes)
        inner = functools.partial(inner_kernel, shape)
        total = call(inner, "inner", 700 * sites, field, (psi, links))
        psi, *sent = call(
            functools.partial(mid_kernel, shape), "mid", 1000 * sites,
            (field, *messages), (psi, links, total, *sent[5:], *halo),
        )
        powers.append(psi)
    halo = exchange(sent[:5], lanes)
    total, row = call(
        functools.partial(inner_sums_kernel, shape), "inner_sums", 900 * sites,
        (field, held(1, lanes)), (psi, links, *powers[:3]),
    )
    total, copies = call(
        functools.partial(rim_kernel, shape), "rim", 400 * sites,
        (field, held(devices_all, 1, lanes)),
        (psi, links, total, sent[5], halo[0], halo[2], halo[4], row),
    )
    gathered = from_everyone(copies)
    four = call(
        functools.partial(finish_kernel, shape), "finish", 400 * sites, field,
        (psi, links, total, sent[6], halo[1], halo[3]),
    )
    residual, coefficients = call(
        functools.partial(last_kernel, shape, entries), "last", 100 * sites,
        (
            jax.ShapeDtypeStruct((24 * t * z, lanes), jnp.float32),
            jax.ShapeDtypeStruct((3,), jnp.float32),
        ),
        (powers[0], powers[2], four, gathered), (vmem, smem),
    )
    return (residual.reshape(source.shape), coefficients)


def solution(mesh):
    placed = (P(None, None, None, "ta", "gz", "gy"), P(None, None, None, None, "ta", "gz", "gy"))
    return jax.shard_map(
        shards,
        mesh=mesh,
        in_specs=placed,
        out_specs=(P(None, None, None, "ta", "gz", "gy"), P()),
        check_vma=False,
    )
```

```python
import functools

import jax
import jax.numpy as jnp
from jax import lax
from jax.experimental import pallas as pl
from jax.experimental.pallas import tpu as pltpu
from jax.sharding import PartitionSpec as P

X = 32

hop_kappa = 0.19
epsilon = 1e-06
spin_table = (
    ((1, 0), (-1j, -1j)),
    ((1, 0), (-1, 1)),
    ((0, 1), (-1j, 1j)),
    ((0, 1), (1, 1)),
)
SPIN_COLOUR = [(spin, colour) for spin in range(2) for colour in range(3)]


def add_phased(left, phase, right):
    phase = complex(phase)
    if phase == 1:
        return (left[0] + right[0], left[1] + right[1])
    if phase == -1:
        return (left[0] - right[0], left[1] - right[1])
    if phase == 1j:
        return (left[0] - right[1], left[1] + right[0])
    return (left[0] + right[1], left[1] - right[0])


def project(psi, direction, parity):
    order, phases = spin_table[direction]
    return {
        (s, c): add_phased(psi[s, c], parity * phases[s], psi[2 + order[s], c])
        for s, c in SPIN_COLOUR
    }


def add_rebuilt(total, half, direction, parity):
    order, phases = spin_table[direction]
    for s, c in SPIN_COLOUR:
        total[s, c] = add_phased(total[s, c], 1, half[s, c])
        row = order[s]
        phase = parity * complex(phases[row]).conjugate()
        total[2 + s, c] = add_phased(total[2 + s, c], phase, half[row, c])


def mul_link(links, direction, z, half):
    out = {}
    for row in range(3):
        for s in range(2):
            real, imag = None, None
            for col in range(3):
                u_real, u_imag = links[direction, row, col, z]
                h_real, h_imag = half[s, col]
                term_real = u_real * h_real - u_imag * h_imag
                term_imag = u_real * h_imag + u_imag * h_real
                real = term_real if real is None else real + term_real
                imag = term_imag if imag is None else imag + term_imag
            out[s, row] = (real, imag)
    return out


def mul_link_dag(links, direction, z, half):
    out = {}
    for row in range(3):
        for s in range(2):
            real, imag = None, None
            for col in range(3):
                u_real, u_imag = links[direction, col, row, z]
                h_real, h_imag = half[s, col]
                term_real = u_real * h_real + u_imag * h_imag
                term_imag = u_real * h_imag - u_imag * h_real
                real = term_real if real is None else real + term_real
                imag = term_imag if imag is None else imag + term_imag
            out[s, row] = (real, imag)
    return out


def mapped(function, *halves):
    return {
        key: tuple(function(*(half[key][part] for half in halves)) for part in range(2))
        for key in SPIN_COLOUR
    }


class Links:
    def __init__(self, ref):
        self.ref = ref

    def __getitem__(self, index):
        direction, row, col, z = index
        first = ((direction * 3 + row) * 3 + col) * 2
        return (self.ref[first, z], self.ref[first + 1, z])


def load_psi(ref, z):
    return {
        (s, c): (ref[(s * 3 + c) * 2, z], ref[(s * 3 + c) * 2 + 1, z])
        for s in range(4)
        for c in range(3)
    }


def load_half(ref, z):
    return {
        (s, c): (ref[(s * 3 + c) * 2, z], ref[(s * 3 + c) * 2 + 1, z]) for s, c in SPIN_COLOUR
    }


def store_half(ref, z, half):
    for (s, c), pair in half.items():
        for part in range(2):
            ref[(s * 3 + c) * 2 + part, z] = pair[part]


class Shape:
    def __init__(self, t_extent, z_extent, lanes):
        self.t = t_extent
        self.z = z_extent
        self.rows = -(-t_extent // 8) * 8
        self.lanes = lanes

    def row(self):
        return lax.broadcasted_iota(jnp.int32, (self.rows, self.lanes), 0)

    def lane(self):
        return lax.broadcasted_iota(jnp.int32, (self.rows, self.lanes), 1)


def is_even(axis):
    return jnp.bitwise_and(lax.axis_index(axis), 1) == 0


def either(choice, first, second):
    return jnp.where(choice, first, second)


def emit_messages(shape, psi_ref, links, refs):
    z_second, t_second, z_first, t_first, y_msg, carried_y, carried_t = refs
    t_even, z_even = is_even("ta"), is_even("gz")
    lane = shape.lane()
    last_z, last_t = shape.z - 1, shape.t - 1
    for z in range(shape.z):
        psi = load_psi(psi_ref, z)
        minus = project(psi, 3, -1)
        carried = mul_link_dag(links, 3, z, project(psi, 3, 1))
        store_half(carried_t, z, carried)
        for s, c in SPIN_COLOUR:
            for part in range(2):
                at = ((s * 3 + c) * 2 + part) * shape.z + z
                down = minus[s, c][part][0:1]
                up = carried[s, c][part][last_t : last_t + 1]
                t_first[at : at + 1] = either(t_even, up, down)
                t_second[at : at + 1] = either(t_even, down, up)
        minus = project(psi, 1, -1)
        carried = mul_link_dag(links, 1, z, project(psi, 1, 1))
        store_half(carried_y, z, carried)
        store_half(
            y_msg,
            z,
            mapped(lambda low, high: jnp.where(lane < X, low, high), minus, carried),
        )
    minus = project(load_psi(psi_ref, 0), 2, -1)
    carried = mul_link_dag(links, 2, last_z, project(load_psi(psi_ref, last_z), 2, 1))
    for s, c in SPIN_COLOUR:
        for part in range(2):
            at = ((s * 3 + c) * 2 + part) * shape.t
            down, up = minus[s, c][part][0 : shape.t], carried[s, c][part][0 : shape.t]
            z_first[at : at + shape.t] = either(z_even, up, down)
            z_second[at : at + shape.t] = either(z_even, down, up)


def prep_kernel(shape, source_hbm, links_hbm, psi_ref, links_ref, *refs):
    messages, (source_ref, links_in, arrived) = refs[:-3], refs[-3:]
    t, z_extent = shape.t, shape.z
    part = 18 * t * z_extent
    copies = [pltpu.make_async_copy(source_hbm, source_ref, arrived.at[4])]
    for direction in (3, 2, 1, 0):
        rows = pl.ds(direction * part, part)
        copies.append(
            pltpu.make_async_copy(links_hbm.at[rows], links_in.at[rows], arrived.at[direction])
        )
    for copy in copies:
        copy.start()
    if shape.rows != t:
        links_ref[...] = jnp.zeros_like(links_ref)
        psi_ref[...] = jnp.zeros_like(psi_ref)
    last = lax.broadcasted_iota(jnp.int32, (t, shape.lanes), 0) == t - 1
    sign = jnp.where(lax.axis_index("ta") == lax.axis_size("ta") - 1, -1.0, 1.0)
    flip = jnp.where(last, sign, 1.0)
    copies[0].wait()
    for k in range(24):
        for z in range(z_extent):
            psi_ref[k, z, 0:t] = source_ref[pl.ds(k * t * z_extent + z, t, stride=z_extent), :]
    for direction in (3, 2, 1, 0):
        copies[4 - direction].wait()
        for k in range(18 * direction, 18 * direction + 18):
            for z in range(z_extent):
                value = links_in[pl.ds(k * t * z_extent + z, t, stride=z_extent), :]
                links_ref[k, z, 0:t] = value * flip if direction == 3 else value
    emit_messages(shape, psi_ref, Links(links_ref), messages)


def summed(shape, term):
    total = None
    for k in range(24):
        for z in range(shape.z):
            value = term(k, z)
            total = value if total is None else total + value
    return total


def over_lanes(total):
    return jnp.sum(jnp.sum(total, axis=0, keepdims=True), axis=1, keepdims=True)


def local_sums(shape, image, origin):
    square = summed(shape, lambda k, z: origin[k, z] * origin[k, z])
    mixed = over_lanes(summed(shape, lambda k, z: image[k, z] * origin[k, z]))
    whole = over_lanes(square)
    factor = jnp.where(whole > 0.0, mixed / jnp.where(whole > 0.0, whole, 1.0), 0.0)
    spread = jnp.broadcast_to(factor, (shape.rows, shape.lanes))
    rest_square, rest_mixed = None, None
    for k in range(24):
        for z in range(shape.z):
            start = origin[k, z]
            rest = image[k, z] - spread * start
            terms = rest * rest, rest * start
            if rest_square is None:
                rest_square, rest_mixed = terms
            else:
                rest_square, rest_mixed = rest_square + terms[0], rest_mixed + terms[1]
    return [factor, *(over_lanes(value) for value in (square, rest_square, rest_mixed))]


def inner_kernel(shape, psi_ref, links_ref, total_ref):
    links = Links(links_ref)
    x = shape.lane() % X
    lanes = shape.lanes
    at_end, at_start = x == X - 1, x == 0

    def ahead(value):
        return jnp.where(
            at_end, pltpu.roll(value, X - 1, 1), pltpu.roll(value, lanes - 1, 1)
        )

    def behind(value):
        return jnp.where(at_start, pltpu.roll(value, lanes - X + 1, 1), pltpu.roll(value, 1, 1))

    for z in range(shape.z):
        psi = load_psi(psi_ref, z)
        zero = jnp.zeros((shape.rows, lanes), jnp.float32)
        total = {key: (zero, zero) for key in psi}
        half = mapped(ahead, project(psi, 0, -1))
        add_rebuilt(total, mul_link(links, 0, z, half), 0, -1)
        half = mapped(behind, mul_link_dag(links, 0, z, project(psi, 0, 1)))
        add_rebuilt(total, half, 0, 1)
        if z + 1 < shape.z:
            half = project(load_psi(psi_ref, z + 1), 2, -1)
            add_rebuilt(total, mul_link(links, 2, z, half), 2, -1)
        if z > 0:
            half = project(load_psi(psi_ref, z - 1), 2, 1)
            add_rebuilt(total, mul_link_dag(links, 2, z - 1, half), 2, 1)
        for (s, c), pair in total.items():
            for part in range(2):
                total_ref[(s * 3 + c) * 2 + part, z] = pair[part]


def add_y_hops(shape, z, psi, total, links, carried_y, y_halo):
    lane, lanes = shape.lane(), shape.lanes
    received = load_half(y_halo, z)
    half = mapped(
        lambda own, other: pltpu.roll(jnp.where(lane < X, other, own), lanes - X, 1),
        project(psi, 1, -1),
        received,
    )
    add_rebuilt(total, mul_link(links, 1, z, half), 1, -1)
    half = mapped(
        lambda own, other: pltpu.roll(jnp.where(lane >= lanes - X, other, own), X, 1),
        load_half(carried_y, z),
        received,
    )
    add_rebuilt(total, half, 1, 1)


def finish_hops(
    shape, psi_ref, links, total_ref, carried_y, carried_t, halo, store
):
    z_second, t_second, z_first, t_first, y_msg = halo
    t_even, z_even = is_even("ta"), is_even("gz")
    row = shape.row()
    lanes, rows, t = shape.lanes, shape.rows, shape.t
    last_z = shape.z - 1

    for z in range(shape.z):
        psi = load_psi(psi_ref, z)
        total = load_psi(total_ref, z)

        def rim_rows(from_even, from_odd):
            half = {}
            for s, c in SPIN_COLOUR:
                ats = [((s * 3 + c) * 2 + part) * shape.z + z for part in range(2)]
                half[s, c] = tuple(
                    jnp.broadcast_to(
                        either(t_even, from_even[at : at + 1], from_odd[at : at + 1]),
                        (rows, lanes),
                    )
                    for at in ats
                )
            return half

        def rim_plane(from_even, from_odd):
            half = {}
            for s, c in SPIN_COLOUR:
                pair = []
                for part in range(2):
                    at = ((s * 3 + c) * 2 + part) * t
                    plane = either(z_even, from_even[at : at + t], from_odd[at : at + t])
                    if rows != t:
                        pad = jnp.zeros((rows - t, lanes), jnp.float32)
                        plane = jnp.concatenate([plane, pad], axis=0)
                    pair.append(plane)
                half[s, c] = tuple(pair)
            return half

        if y_msg is not None:
            add_y_hops(shape, z, psi, total, links, carried_y, y_msg)
        if z == last_z:
            add_rebuilt(total, mul_link(links, 2, z, rim_plane(z_first, z_second)), 2, -1)
        if z == 0:
            add_rebuilt(total, rim_plane(z_second, z_first), 2, 1)
        half = mapped(
            lambda own, other: jnp.where(row == t - 1, other, pltpu.roll(own, rows - 1, 0)),
            project(psi, 3, -1),
            rim_rows(t_first, t_second),
        )
        add_rebuilt(total, mul_link(links, 3, z, half), 3, -1)
        half = mapped(
            lambda own, other: jnp.where(row == 0, other, pltpu.roll(own, 1, 0)),
            load_half(carried_t, z),
            rim_rows(t_second, t_first),
        )
        add_rebuilt(total, half, 3, 1)
        for (s, c), pair in total.items():
            for part in range(2):
                value = psi[s, c][part] - hop_kappa * pair[part]
                value = value if s < 2 else -value
                if rows != t:
                    value = jnp.where(row < t, value, 0.0)
                store((s * 3 + c) * 2 + part, z, value)


def mid_kernel(shape, psi_ref, links_ref, total_ref, carried_y, carried_t, *refs):
    halo, out_ref, messages = refs[:5], refs[5], refs[6:]
    links = Links(links_ref)

    def store(k, z, value):
        out_ref[k, z] = value

    finish_hops(
        shape, psi_ref, links, total_ref, carried_y, carried_t, halo, store
    )
    emit_messages(shape, out_ref, links, messages)


def inner_sums_kernel(
    shape, psi_ref, links_ref, start_ref, one_ref, two_ref, total_ref, copies_ref
):
    sums = local_sums(shape, two_ref, start_ref) + local_sums(shape, psi_ref, one_ref)
    lane = lax.broadcasted_iota(jnp.int32, (1, shape.lanes), 1)
    row = jnp.zeros((1, shape.lanes), jnp.float32)
    for k, value in enumerate(sums):
        row = jnp.where(lane == k, value, row)
    copies_ref[...] = jnp.broadcast_to(row[None], copies_ref.shape)
    inner_kernel(shape, psi_ref, links_ref, total_ref)


def finish_kernel(shape, psi_ref, links_ref, total_ref, carried_y, carried_t, *refs):
    halo, out_ref = refs[:5], refs[5]

    def store(k, z, value):
        out_ref[k, z] = value

    finish_hops(
        shape, psi_ref, Links(links_ref), total_ref, carried_y, carried_t, halo, store
    )


def last_kernel(
    shape, entries, start_ref, two_ref, four_ref, gathered, out_ref, coefficients
):
    table = gathered[:, 0, :]
    columns = [table[:, k : k + 1] for k in range(8)]
    factor_two, start_square, two_square, two_mixed = columns[:4]
    factor_three, one_square, three_square, three_mixed = columns[4:]

    def over_devices(column):
        return jnp.sum(column, axis=0, keepdims=True)

    norm_square = over_devices(start_square) / entries + epsilon
    alpha_one = over_devices(one_square) / entries / norm_square
    gap = alpha_one - factor_two
    remain_square = over_devices(two_square - gap * (2.0 * two_mixed - gap * start_square)) / entries
    overlap = over_devices(two_mixed - gap * start_square) / entries
    gap = alpha_one - factor_three
    image_square = over_devices(three_square - gap * (2.0 * three_mixed - gap * one_square)) / entries
    norm = jnp.sqrt(norm_square)
    beta_one = jnp.sqrt(remain_square / norm_square + epsilon)
    overlap = overlap / (norm_square * beta_one)
    alpha_two = image_square / (norm_square * beta_one * beta_one) - beta_one * overlap
    scale = 1.0 / (norm * beta_one)
    first_factor = beta_one / norm
    t, z_extent = shape.t, shape.z
    for k in range(24):
        for z in range(z_extent):
            two, start = two_ref[k, z], start_ref[k, z]
            remain = two - alpha_one * start
            result = (four_ref[k, z] - alpha_one * two - alpha_two * remain) * scale
            result = result - first_factor * start
            out_ref[pl.ds(k * t * z_extent + z, t, stride=z_extent), :] = result[0:t]
    coefficients[0] = alpha_one[0, 0]
    coefficients[1] = beta_one[0, 0]
    coefficients[2] = alpha_two[0, 0]


def swap(value, axis, second):
    count = lax.axis_size(axis)
    pairs = []
    for low in range(1 if second else 0, count, 2):
        high = (low + 1) % count
        pairs += [(low, high), (high, low)]
    return lax.ppermute(value, axis, pairs)


def exchange(messages, lanes):
    z_second, t_second, z_first, t_first, y_msg = messages
    halo = (
        swap(z_second, "gz", True),
        swap(t_second, "ta", True),
        swap(z_first, "gz", False),
        swap(t_first, "ta", False),
    )
    y_halo = swap(y_msg, "gy", False)
    if lax.axis_size("gy") > 2:
        even = lax.axis_index("gy") % 2 == 0
        lane = lax.broadcasted_iota(jnp.int32, y_msg.shape, y_msg.ndim - 1)
        y_halo = jnp.where((lane < lanes // 2) == even, y_halo, swap(y_msg, "gy", True))
    return (*halo, y_halo)


def from_everyone(copies):
    return lax.all_to_all(copies, ("ta", "gz", "gy"), split_axis=0, concat_axis=0, tiled=True)


def shards(source, gauge_links):
    devices_all = lax.axis_size("ta") * lax.axis_size("gz") * lax.axis_size("gy")
    entries = float(source.size * devices_all)
    shape = Shape(source.shape[3], source.shape[4], source.shape[5])
    t, z, rows, lanes = shape.t, shape.z, shape.rows, shape.lanes
    vmem = pl.BlockSpec(memory_space=pltpu.VMEM)
    smem = pl.BlockSpec(memory_space=pltpu.SMEM)

    def held(*dims):
        return pltpu.VMEM(dims, jnp.float32)

    field = held(24, z, rows, lanes)
    half = held(12, z, rows, lanes)
    z_face, t_face = held(12 * t, lanes), held(12 * z, lanes)
    messages = (z_face, t_face, z_face, t_face, half, half, half)

    def call(kernel, name, flops, out_shape, operands, out_specs=None, in_spec=vmem, scratch=()):
        return pl.pallas_call(
            kernel,
            name=name,
            out_shape=out_shape,
            in_specs=[in_spec] * len(operands),
            out_specs=out_specs or jax.tree.map(lambda _: vmem, out_shape),
            scratch_shapes=scratch,
            compiler_params=pltpu.CompilerParams(vmem_limit_bytes=8 << 20),
            cost_estimate=pl.CostEstimate(flops=flops, bytes_accessed=1 << 20, transcendentals=0),
        )(*operands)

    sites = t * z * lanes
    psi, links, *sent = call(
        functools.partial(prep_kernel, shape), "prep", 400 * sites,
        (field, held(72, z, rows, lanes), *messages),
        (
            pltpu.with_memory_space_constraint(source.reshape(24 * t * z, lanes), pltpu.HBM),
            pltpu.with_memory_space_constraint(gauge_links.reshape(72 * t * z, lanes), pltpu.HBM),
        ),
        in_spec=pl.BlockSpec(memory_space=pltpu.HBM),
        scratch=(
            held(24 * t * z, lanes), held(72 * t * z, lanes), pltpu.SemaphoreType.DMA((5,)),
        ),
    )
    powers = [psi]
    for step in range(3):
        halo = exchange(sent[:5], lanes)
        inner = functools.partial(inner_kernel, shape)
        total = call(inner, "inner", 700 * sites, field, (psi, links))
        psi, *sent = call(
            functools.partial(mid_kernel, shape), "mid", 1000 * sites,
            (field, *messages), (psi, links, total, *sent[5:], *halo),
        )
        powers.append(psi)
    halo = exchange(sent[:5], lanes)
    total, copies = call(
        functools.partial(inner_sums_kernel, shape), "inner_sums", 1100 * sites,
        (field, held(devices_all, 1, lanes)), (psi, links, *powers[:3]),
    )
    gathered = from_everyone(copies)
    four = call(
        functools.partial(finish_kernel, shape), "finish", 10**11, field,
        (psi, links, total, *sent[5:], *halo),
    )
    residual, coefficients = call(
        functools.partial(last_kernel, shape, entries), "last", 100 * sites,
        (
            jax.ShapeDtypeStruct((24 * t * z, lanes), jnp.float32),
            jax.ShapeDtypeStruct((3,), jnp.float32),
        ),
        (powers[0], powers[2], four, gathered), (vmem, smem),
    )
    return (residual.reshape(source.shape), coefficients)


def solution(mesh):
    placed = (P(None, None, None, "ta", "gz", "gy"), P(None, None, None, None, "ta", "gz", "gy"))
    return jax.shard_map(
        shards,
        mesh=mesh,
        in_specs=placed,
        out_specs=(P(None, None, None, "ta", "gz", "gy"), P()),
        check_vma=False,
    )
```

```python
import functools
import math

import jax
import jax.numpy as jnp
from jax import lax
from jax.experimental import pallas as pl
from jax.experimental.pallas import tpu as pltpu
from jax.sharding import PartitionSpec as P

X = 32

hop_kappa = 0.19
epsilon = 1e-06
spin_table = (
    ((1, 0), (-1j, -1j)),
    ((1, 0), (-1, 1)),
    ((0, 1), (-1j, 1j)),
    ((0, 1), (1, 1)),
)
SPIN_COLOUR = [(spin, colour) for spin in range(2) for colour in range(3)]


def add_phased(left, phase, right):
    phase = complex(phase)
    if phase == 1:
        return (left[0] + right[0], left[1] + right[1])
    if phase == -1:
        return (left[0] - right[0], left[1] - right[1])
    if phase == 1j:
        return (left[0] - right[1], left[1] + right[0])
    return (left[0] + right[1], left[1] - right[0])


def project(psi, direction, parity):
    order, phases = spin_table[direction]
    return {
        (s, c): add_phased(psi[s, c], parity * phases[s], psi[2 + order[s], c])
        for s, c in SPIN_COLOUR
    }


def add_rebuilt(total, half, direction, parity):
    order, phases = spin_table[direction]
    for s, c in SPIN_COLOUR:
        total[s, c] = add_phased(total[s, c], 1, half[s, c])
        row = order[s]
        phase = parity * complex(phases[row]).conjugate()
        total[2 + s, c] = add_phased(total[2 + s, c], phase, half[row, c])


def mul_link(links, direction, z, half):
    out = {}
    for row in range(3):
        for s in range(2):
            real, imag = None, None
            for col in range(3):
                u_real, u_imag = links[direction, row, col, z]
                h_real, h_imag = half[s, col]
                term_real = u_real * h_real - u_imag * h_imag
                term_imag = u_real * h_imag + u_imag * h_real
                real = term_real if real is None else real + term_real
                imag = term_imag if imag is None else imag + term_imag
            out[s, row] = (real, imag)
    return out


def mul_link_dag(links, direction, z, half):
    out = {}
    for row in range(3):
        for s in range(2):
            real, imag = None, None
            for col in range(3):
                u_real, u_imag = links[direction, col, row, z]
                h_real, h_imag = half[s, col]
                term_real = u_real * h_real + u_imag * h_imag
                term_imag = u_real * h_imag - u_imag * h_real
                real = term_real if real is None else real + term_real
                imag = term_imag if imag is None else imag + term_imag
            out[s, row] = (real, imag)
    return out


def mapped(function, *halves):
    return {
        key: tuple(function(*(half[key][part] for half in halves)) for part in range(2))
        for key in SPIN_COLOUR
    }


class Links:
    def __init__(self, ref):
        self.ref = ref

    def __getitem__(self, index):
        direction, row, col, z = index
        first = ((direction * 3 + row) * 3 + col) * 2
        return (self.ref[first, z], self.ref[first + 1, z])


def load_psi(ref, z):
    return {
        (s, c): (ref[(s * 3 + c) * 2, z], ref[(s * 3 + c) * 2 + 1, z])
        for s in range(4)
        for c in range(3)
    }


def load_half(ref, z):
    return {
        (s, c): (ref[(s * 3 + c) * 2, z], ref[(s * 3 + c) * 2 + 1, z]) for s, c in SPIN_COLOUR
    }


def store_half(ref, z, half):
    for (s, c), pair in half.items():
        for part in range(2):
            ref[(s * 3 + c) * 2 + part, z] = pair[part]


class Shape:
    def __init__(self, t_extent, z_extent, lanes):
        self.t = t_extent
        self.z = z_extent
        self.rows = -(-t_extent // 8) * 8
        self.lanes = lanes

    def row(self):
        return lax.broadcasted_iota(jnp.int32, (self.rows, self.lanes), 0)

    def lane(self):
        return lax.broadcasted_iota(jnp.int32, (self.rows, self.lanes), 1)


def is_even(axis):
    return jnp.bitwise_and(lax.axis_index(axis), 1) == 0


def either(choice, first, second):
    return jnp.where(choice, first, second)


def emit_messages(shape, psi_ref, links, refs):
    z_second, t_second, z_first, t_first, y_msg, carried_y, carried_t = refs
    t_even, z_even = is_even("ta"), is_even("gz")
    lane = shape.lane()
    last_z, last_t = shape.z - 1, shape.t - 1
    for z in range(shape.z):
        psi = load_psi(psi_ref, z)
        minus = project(psi, 3, -1)
        carried = mul_link_dag(links, 3, z, project(psi, 3, 1))
        store_half(carried_t, z, carried)
        for s, c in SPIN_COLOUR:
            for part in range(2):
                at = ((s * 3 + c) * 2 + part) * shape.z + z
                down = minus[s, c][part][0:1]
                up = carried[s, c][part][last_t : last_t + 1]
                t_first[at : at + 1] = either(t_even, up, down)
                t_second[at : at + 1] = either(t_even, down, up)
        minus = project(psi, 1, -1)
        carried = mul_link_dag(links, 1, z, project(psi, 1, 1))
        store_half(carried_y, z, carried)
        store_half(
            y_msg,
            z,
            mapped(lambda low, high: jnp.where(lane < X, low, high), minus, carried),
        )
    minus = project(load_psi(psi_ref, 0), 2, -1)
    carried = mul_link_dag(links, 2, last_z, project(load_psi(psi_ref, last_z), 2, 1))
    for s, c in SPIN_COLOUR:
        for part in range(2):
            at = ((s * 3 + c) * 2 + part) * shape.t
            down, up = minus[s, c][part][0 : shape.t], carried[s, c][part][0 : shape.t]
            z_first[at : at + shape.t] = either(z_even, up, down)
            z_second[at : at + shape.t] = either(z_even, down, up)


def prep_kernel(shape, source_hbm, links_hbm, psi_ref, links_ref, *refs):
    messages, (source_ref, links_in, arrived) = refs[:-3], refs[-3:]
    t, z_extent = shape.t, shape.z
    part = 18 * t * z_extent
    copies = [pltpu.make_async_copy(source_hbm, source_ref, arrived.at[4])]
    for direction in (3, 2, 1, 0):
        rows = pl.ds(direction * part, part)
        copies.append(
            pltpu.make_async_copy(links_hbm.at[rows], links_in.at[rows], arrived.at[direction])
        )
    for copy in copies:
        copy.start()
    if shape.rows != t:
        links_ref[...] = jnp.zeros_like(links_ref)
        psi_ref[...] = jnp.zeros_like(psi_ref)
    last = lax.broadcasted_iota(jnp.int32, (t, shape.lanes), 0) == t - 1
    sign = jnp.where(lax.axis_index("ta") == lax.axis_size("ta") - 1, -1.0, 1.0)
    flip = jnp.where(last, sign, 1.0)
    copies[0].wait()
    for k in range(24):
        for z in range(z_extent):
            psi_ref[k, z, 0:t] = source_ref[pl.ds(k * t * z_extent + z, t, stride=z_extent), :]
    for direction in (3, 2, 1, 0):
        copies[4 - direction].wait()
        for k in range(18 * direction, 18 * direction + 18):
            for z in range(z_extent):
                value = links_in[pl.ds(k * t * z_extent + z, t, stride=z_extent), :]
                links_ref[k, z, 0:t] = value * flip if direction == 3 else value
    emit_messages(shape, psi_ref, Links(links_ref), messages)


def summed(shape, term):
    total = None
    for k in range(24):
        for z in range(shape.z):
            value = term(k, z)
            total = value if total is None else total + value
    return total


def over_lanes(total):
    return jnp.sum(jnp.sum(total, axis=0, keepdims=True), axis=1, keepdims=True)


def local_sums(shape, image, origin):
    square = summed(shape, lambda k, z: origin[k, z] * origin[k, z])
    mixed = over_lanes(summed(shape, lambda k, z: image[k, z] * origin[k, z]))
    whole = over_lanes(square)
    factor = jnp.where(whole > 0.0, mixed / jnp.where(whole > 0.0, whole, 1.0), 0.0)
    spread = jnp.broadcast_to(factor, (shape.rows, shape.lanes))
    rest_square, rest_mixed = None, None
    for k in range(24):
        for z in range(shape.z):
            start = origin[k, z]
            rest = image[k, z] - spread * start
            terms = rest * rest, rest * start
            if rest_square is None:
                rest_square, rest_mixed = terms
            else:
                rest_square, rest_mixed = rest_square + terms[0], rest_mixed + terms[1]
    return [factor, *(over_lanes(value) for value in (square, rest_square, rest_mixed))]


def inner_kernel(shape, psi_ref, links_ref, total_ref):
    links = Links(links_ref)
    x = shape.lane() % X
    lanes = shape.lanes
    at_end, at_start = x == X - 1, x == 0

    def ahead(value):
        return jnp.where(
            at_end, pltpu.roll(value, X - 1, 1), pltpu.roll(value, lanes - 1, 1)
        )

    def behind(value):
        return jnp.where(at_start, pltpu.roll(value, lanes - X + 1, 1), pltpu.roll(value, 1, 1))

    for z in range(shape.z):
        psi = load_psi(psi_ref, z)
        zero = jnp.zeros((shape.rows, lanes), jnp.float32)
        total = {key: (zero, zero) for key in psi}
        half = mapped(ahead, project(psi, 0, -1))
        add_rebuilt(total, mul_link(links, 0, z, half), 0, -1)
        half = mapped(behind, mul_link_dag(links, 0, z, project(psi, 0, 1)))
        add_rebuilt(total, half, 0, 1)
        if z + 1 < shape.z:
            half = project(load_psi(psi_ref, z + 1), 2, -1)
            add_rebuilt(total, mul_link(links, 2, z, half), 2, -1)
        if z > 0:
            half = project(load_psi(psi_ref, z - 1), 2, 1)
            add_rebuilt(total, mul_link_dag(links, 2, z - 1, half), 2, 1)
        for (s, c), pair in total.items():
            for part in range(2):
                total_ref[(s * 3 + c) * 2 + part, z] = pair[part]


def add_y_hops(shape, z, psi, total, links, carried_y, y_halo):
    lane, lanes = shape.lane(), shape.lanes
    received = load_half(y_halo, z)
    half = mapped(
        lambda own, other: pltpu.roll(jnp.where(lane < X, other, own), lanes - X, 1),
        project(psi, 1, -1),
        received,
    )
    add_rebuilt(total, mul_link(links, 1, z, half), 1, -1)
    half = mapped(
        lambda own, other: pltpu.roll(jnp.where(lane >= lanes - X, other, own), X, 1),
        load_half(carried_y, z),
        received,
    )
    add_rebuilt(total, half, 1, 1)


def finish_hops(
    shape, psi_ref, links, total_ref, carried_y, carried_t, halo, store
):
    z_second, t_second, z_first, t_first, y_msg = halo
    t_even, z_even = is_even("ta"), is_even("gz")
    row = shape.row()
    lanes, rows, t = shape.lanes, shape.rows, shape.t
    last_z = shape.z - 1

    for z in range(shape.z):
        psi = load_psi(psi_ref, z)
        total = load_psi(total_ref, z)

        def rim_rows(from_even, from_odd):
            half = {}
            for s, c in SPIN_COLOUR:
                ats = [((s * 3 + c) * 2 + part) * shape.z + z for part in range(2)]
                half[s, c] = tuple(
                    jnp.broadcast_to(
                        either(t_even, from_even[at : at + 1], from_odd[at : at + 1]),
                        (rows, lanes),
                    )
                    for at in ats
                )
            return half

        def rim_plane(from_even, from_odd):
            half = {}
            for s, c in SPIN_COLOUR:
                pair = []
                for part in range(2):
                    at = ((s * 3 + c) * 2 + part) * t
                    plane = either(z_even, from_even[at : at + t], from_odd[at : at + t])
                    if rows != t:
                        pad = jnp.zeros((rows - t, lanes), jnp.float32)
                        plane = jnp.concatenate([plane, pad], axis=0)
                    pair.append(plane)
                half[s, c] = tuple(pair)
            return half

        if y_msg is not None:
            add_y_hops(shape, z, psi, total, links, carried_y, y_msg)
        if z == last_z:
            add_rebuilt(total, mul_link(links, 2, z, rim_plane(z_first, z_second)), 2, -1)
        if z == 0:
            add_rebuilt(total, rim_plane(z_second, z_first), 2, 1)
        half = mapped(
            lambda own, other: jnp.where(row == t - 1, other, pltpu.roll(own, rows - 1, 0)),
            project(psi, 3, -1),
            rim_rows(t_first, t_second),
        )
        add_rebuilt(total, mul_link(links, 3, z, half), 3, -1)
        half = mapped(
            lambda own, other: jnp.where(row == 0, other, pltpu.roll(own, 1, 0)),
            load_half(carried_t, z),
            rim_rows(t_second, t_first),
        )
        add_rebuilt(total, half, 3, 1)
        for (s, c), pair in total.items():
            for part in range(2):
                value = psi[s, c][part] - hop_kappa * pair[part]
                value = value if s < 2 else -value
                if rows != t:
                    value = jnp.where(row < t, value, 0.0)
                store((s * 3 + c) * 2 + part, z, value)


def mid_kernel(shape, psi_ref, links_ref, total_ref, carried_y, carried_t, *refs):
    halo, out_ref, messages = refs[:5], refs[5], refs[6:]
    links = Links(links_ref)

    def store(k, z, value):
        out_ref[k, z] = value

    finish_hops(
        shape, psi_ref, links, total_ref, carried_y, carried_t, halo, store
    )
    emit_messages(shape, out_ref, links, messages)


def sums_row(shape, two, start, three, one):
    sums = local_sums(shape, two, start) + local_sums(shape, three, one)
    lane = lax.broadcasted_iota(jnp.int32, (1, shape.lanes), 1)
    row = jnp.zeros((1, shape.lanes), jnp.float32)
    for k, value in enumerate(sums):
        row = jnp.where(lane == k, value, row)
    return row


def inner_sums_kernel(
    shape, psi_ref, links_ref, start_ref, one_ref, two_ref, total_ref, copies_ref
):
    row = sums_row(shape, two_ref, start_ref, psi_ref, one_ref)
    copies_ref[...] = jnp.broadcast_to(row[None], copies_ref.shape)
    inner_kernel(shape, psi_ref, links_ref, total_ref)


def finish_kernel(shape, psi_ref, links_ref, total_ref, carried_y, carried_t, *refs):
    halo, out_ref = refs[:5], refs[5]

    def store(k, z, value):
        out_ref[k, z] = value

    finish_hops(
        shape, psi_ref, Links(links_ref), total_ref, carried_y, carried_t, halo, store
    )


def scalars(gathered, entries):
    table = gathered[:, 0, :]
    columns = [table[:, k : k + 1] for k in range(8)]
    factor_two, start_square, two_square, two_mixed = columns[:4]
    factor_three, one_square, three_square, three_mixed = columns[4:]

    def over_devices(column):
        return jnp.sum(column, axis=0, keepdims=True)

    norm_square = over_devices(start_square) / entries + epsilon
    alpha_one = over_devices(one_square) / entries / norm_square
    gap = alpha_one - factor_two
    remain_square = over_devices(two_square - gap * (2.0 * two_mixed - gap * start_square)) / entries
    overlap = over_devices(two_mixed - gap * start_square) / entries
    gap = alpha_one - factor_three
    image_square = over_devices(three_square - gap * (2.0 * three_mixed - gap * one_square)) / entries
    norm = jnp.sqrt(norm_square)
    beta_one = jnp.sqrt(remain_square / norm_square + epsilon)
    overlap = overlap / (norm_square * beta_one)
    alpha_two = image_square / (norm_square * beta_one * beta_one) - beta_one * overlap
    scale = 1.0 / (norm * beta_one)
    return alpha_one, beta_one, alpha_two, scale, beta_one / norm


def last_kernel(
    shape, entries, start_ref, two_ref, four_ref, gathered, out_ref, coefficients
):
    alpha_one, beta_one, alpha_two, scale, first_factor = scalars(gathered, entries)
    t, z_extent = shape.t, shape.z
    for k in range(24):
        for z in range(z_extent):
            two, start = two_ref[k, z], start_ref[k, z]
            remain = two - alpha_one * start
            result = (four_ref[k, z] - alpha_one * two - alpha_two * remain) * scale
            result = result - first_factor * start
            out_ref[pl.ds(k * t * z_extent + z, t, stride=z_extent), :] = result[0:t]
    coefficients[0] = alpha_one[0, 0]
    coefficients[1] = beta_one[0, 0]
    coefficients[2] = alpha_two[0, 0]


def swap(value, axis, second):
    count = math.prod(lax.axis_size(name) for name in (axis if isinstance(axis, tuple) else (axis,)))
    pairs = []
    for low in range(1 if second else 0, count, 2):
        high = (low + 1) % count
        pairs += [(low, high), (high, low)]
    return lax.ppermute(value, axis, pairs)


def exchange(messages, lanes):
    z_second, t_second, z_first, t_first, y_msg = messages
    halo = (
        swap(z_second, "gz", True),
        swap(t_second, "ta", True),
        swap(z_first, "gz", False),
        swap(t_first, "ta", False),
    )
    y_halo = swap(y_msg, "gy", False)
    if lax.axis_size("gy") > 2:
        even = lax.axis_index("gy") % 2 == 0
        lane = lax.broadcasted_iota(jnp.int32, y_msg.shape, y_msg.ndim - 1)
        y_halo = jnp.where((lane < lanes // 2) == even, y_halo, swap(y_msg, "gy", True))
    return (*halo, y_halo)


def from_everyone(copies):
    return lax.all_to_all(copies, ("ta", "gz", "gy"), split_axis=0, concat_axis=0, tiled=True)


def shards(source, gauge_links):
    devices_all = lax.axis_size("ta") * lax.axis_size("gz") * lax.axis_size("gy")
    entries = float(source.size * devices_all)
    shape = Shape(source.shape[3], source.shape[4], source.shape[5])
    t, z, rows, lanes = shape.t, shape.z, shape.rows, shape.lanes
    vmem = pl.BlockSpec(memory_space=pltpu.VMEM)
    smem = pl.BlockSpec(memory_space=pltpu.SMEM)

    def held(*dims):
        return pltpu.VMEM(dims, jnp.float32)

    field = held(24, z, rows, lanes)
    half = held(12, z, rows, lanes)
    z_face, t_face = held(12 * t, lanes), held(12 * z, lanes)
    messages = (z_face, t_face, z_face, t_face, half, half, half)

    def call(kernel, name, flops, out_shape, operands, out_specs=None, in_spec=vmem, scratch=()):
        return pl.pallas_call(
            kernel,
            name=name,
            out_shape=out_shape,
            in_specs=[in_spec] * len(operands),
            out_specs=out_specs or jax.tree.map(lambda _: vmem, out_shape),
            scratch_shapes=scratch,
            compiler_params=pltpu.CompilerParams(vmem_limit_bytes=8 << 20),
            cost_estimate=pl.CostEstimate(flops=flops, bytes_accessed=1 << 20, transcendentals=0),
        )(*operands)

    sites = t * z * lanes
    psi, links, *sent = call(
        functools.partial(prep_kernel, shape), "prep", 400 * sites,
        (field, held(72, z, rows, lanes), *messages),
        (
            pltpu.with_memory_space_constraint(source.reshape(24 * t * z, lanes), pltpu.HBM),
            pltpu.with_memory_space_constraint(gauge_links.reshape(72 * t * z, lanes), pltpu.HBM),
        ),
        in_spec=pl.BlockSpec(memory_space=pltpu.HBM),
        scratch=(
            held(24 * t * z, lanes), held(72 * t * z, lanes), pltpu.SemaphoreType.DMA((5,)),
        ),
    )
    powers = [psi]
    for step in range(3):
        halo = exchange(sent[:5], lanes)
        inner = functools.partial(inner_kernel, shape)
        total = call(inner, "inner", 700 * sites, field, (psi, links))
        psi, *sent = call(
            functools.partial(mid_kernel, shape), "mid", 1000 * sites,
            (field, *messages), (psi, links, total, *sent[5:], *halo),
        )
        powers.append(psi)
    halo = exchange(sent[:5], lanes)
    total, copies = call(
        functools.partial(inner_sums_kernel, shape), "inner_sums", 1100 * sites,
        (field, held(devices_all, 1, lanes)), (psi, links, *powers[:3]),
    )
    gathered = from_everyone(copies)
    four = call(
        functools.partial(finish_kernel, shape), "finish", 700 * sites, field,
        (psi, links, total, *sent[5:], *halo),
    )
    residual, coefficients = call(
        functools.partial(last_kernel, shape, entries), "last", 100 * sites,
        (
            jax.ShapeDtypeStruct((24 * t * z, lanes), jnp.float32),
            jax.ShapeDtypeStruct((3,), jnp.float32),
        ),
        (powers[0], powers[2], four, gathered), (vmem, smem),
    )
    return (residual.reshape(source.shape), coefficients)


class ChipShape(Shape):
    def __init__(self, t_extent, z_extent, lanes):
        super().__init__(t_extent, z_extent, lanes)
        self.parts = 2 * z_extent
        self.z_rows = 24 * t_extent
        self.t_rows = 12 * self.parts

    def block(self, k, part):
        first = (k * self.parts + part) * self.rows
        return pl.ds(first, self.rows)

    def edge(self, k, row):
        return pl.ds(k * self.parts * self.rows + row, self.parts, stride=self.rows)


class ChipLinks:
    def __init__(self, shape, ref, row=None):
        self.shape, self.ref, self.row = shape, ref, row

    def __getitem__(self, index):
        direction, row, col, part = index
        first = ((direction * 3 + row) * 3 + col) * 2
        if self.row is None:
            return tuple(self.ref[self.shape.block(first + n, part), :] for n in range(2))
        return tuple(self.ref[self.shape.edge(first + n, self.row), :] for n in range(2))


def components(spins):
    return [(s, c, part, (s * 3 + c) * 2 + part) for s in range(spins) for c in range(3) for part in range(2)]


def gathered_pairs(spins, value):
    out = {}
    for s in range(spins):
        for c in range(3):
            out[s, c] = tuple(value((s * 3 + c) * 2 + part) for part in range(2))
    return out


def chip_psi(shape, ref, part):
    return gathered_pairs(4, lambda k: ref[shape.block(k, part), :])


def chip_edge(shape, ref, row):
    return gathered_pairs(4, lambda k: ref[shape.edge(k, row), :])


def chip_messages(shape, psi_ref, links_ref, z_second, t_second, z_first, t_first):
    t, last = shape.t, shape.t - 1
    even = is_even("ta")
    minus = project(chip_edge(shape, psi_ref, 0), 3, -1)
    half = project(chip_edge(shape, psi_ref, last), 3, 1)
    carried = mul_link_dag(ChipLinks(shape, links_ref, last), 3, 0, half)
    for s, c, part, k in components(2):
        rows = pl.ds(k * shape.parts, shape.parts)
        up, down = carried[s, c][part], minus[s, c][part]
        t_first[rows, :] = either(even, up, down)
        t_second[rows, :] = either(even, down, up)
    even = is_even("gy")
    links = ChipLinks(shape, links_ref)
    for y_half in range(2):
        minus = project(chip_psi(shape, psi_ref, y_half), 2, -1)
        part_last = shape.parts - 2 + y_half
        half = project(chip_psi(shape, psi_ref, part_last), 2, 1)
        carried = mul_link_dag(links, 2, part_last, half)
        for s, c, part, k in components(2):
            rows = pl.ds((k * 2 + y_half) * t, t)
            up, down = carried[s, c][part][0:t], minus[s, c][part][0:t]
            z_first[rows, :] = either(even, up, down)
            z_second[rows, :] = either(even, down, up)


def chip_bring(shape, y_half, source_ref, links_in, psi_ref, links_ref, arrived):
    t, z_extent = shape.t, 2 * shape.z
    first_plane = lax.axis_index("gy") * shape.z
    last = lax.broadcasted_iota(jnp.int32, (t, shape.lanes), 0) == t - 1
    sign = jnp.where(lax.axis_index("ta") == lax.axis_size("ta") - 1, -1.0, 1.0)
    flip = jnp.where(last, sign, 1.0)

    def bring(in_ref, out_ref, k, z, factor=None):
        value = in_ref[pl.ds(k * t * z_extent + first_plane + z, t, stride=z_extent), :]
        if factor is not None:
            value = value * factor
        at = (k * shape.parts + 2 * z + y_half) * shape.rows
        out_ref[pl.ds(pl.multiple_of(at, 8), t), :] = value

    arrived(4)
    for z in range(shape.z):
        for k in range(24):
            bring(source_ref, psi_ref, k, z)
    for direction in (3, 2, 1, 0):
        arrived(direction)
        for z in range(shape.z):
            for k in range(18 * direction, 18 * direction + 18):
                bring(links_in, links_ref, k, z, flip if direction == 3 else None)


def chip_own_kernel(
    shape, source_hbm, links_hbm, psi_ref, links_ref, source_ref, links_in, semaphores
):
    part = 18 * shape.t * 2 * shape.z
    copies = {4: pltpu.make_async_copy(source_hbm, source_ref, semaphores.at[4])}
    for direction in (3, 2, 1, 0):
        rows = pl.ds(direction * part, part)
        copies[direction] = pltpu.make_async_copy(
            links_hbm.at[rows], links_in.at[rows], semaphores.at[direction]
        )
    for copy in copies.values():
        copy.start()
    if shape.rows != shape.t:
        links_ref[...] = jnp.zeros_like(links_ref)
        psi_ref[...] = jnp.zeros_like(psi_ref)
    chip_bring(
        shape, lax.axis_index("gy"), source_ref, links_in, psi_ref, links_ref,
        lambda n: copies[n].wait(),
    )


def chip_prep_kernel(
    shape, source_ref, links_in, psi_in, links_held, psi_ref, links_ref, *messages
):
    chip_bring(
        shape, 1 - lax.axis_index("gy"), source_ref, links_in, psi_ref, links_ref, lambda n: None
    )
    chip_messages(shape, psi_ref, links_ref, *messages)


def chip_inner_kernel(shape, psi_ref, links_ref, total_ref):
    links = ChipLinks(shape, links_ref)
    lane, row = shape.lane(), shape.row()
    x = lane % X
    lanes, rows, t = shape.lanes, shape.rows, shape.t
    at_end, at_start = x == X - 1, x == 0
    inside_ahead = row < t - 1
    inside_behind = jnp.logical_and(row > 0, row < t)

    def x_ahead(value):
        return jnp.where(
            at_end, pltpu.roll(value, X - 1, 1), pltpu.roll(value, lanes - 1, 1)
        )

    def x_behind(value):
        return jnp.where(at_start, pltpu.roll(value, lanes - X + 1, 1), pltpu.roll(value, 1, 1))

    def t_ahead(value):
        return jnp.where(inside_ahead, pltpu.roll(value, rows - 1, 0), 0.0)

    def t_behind(value):
        return jnp.where(inside_behind, pltpu.roll(value, 1, 0), 0.0)

    for z in range(shape.z):
        for part in (2 * z, 2 * z + 1):
            psi = chip_psi(shape, psi_ref, part)
            zero = jnp.zeros((rows, lanes), jnp.float32)
            total = {key: (zero, zero) for key in psi}
            half = mapped(x_ahead, project(psi, 0, -1))
            add_rebuilt(total, mul_link(links, 0, part, half), 0, -1)
            half = mapped(x_behind, mul_link_dag(links, 0, part, project(psi, 0, 1)))
            add_rebuilt(total, half, 0, 1)
            half = mapped(t_ahead, project(psi, 3, -1))
            add_rebuilt(total, mul_link(links, 3, part, half), 3, -1)
            half = mapped(t_behind, mul_link_dag(links, 3, part, project(psi, 3, 1)))
            add_rebuilt(total, half, 3, 1)
            if z + 1 < shape.z:
                half = project(chip_psi(shape, psi_ref, part + 2), 2, -1)
                add_rebuilt(total, mul_link(links, 2, part, half), 2, -1)
            if z > 0:
                half = project(chip_psi(shape, psi_ref, part - 2), 2, 1)
                add_rebuilt(total, mul_link_dag(links, 2, part - 2, half), 2, 1)
            for s, c, n, k in components(4):
                total_ref[shape.block(k, part), :] = total[s, c][n]
        pair = (2 * z, 2 * z + 1)
        minus, carried = [], []
        for part in pair:
            psi = chip_psi(shape, psi_ref, part)
            minus.append(mapped(lambda v: pltpu.roll(v, lanes - X, 1), project(psi, 1, -1)))
            half = mul_link_dag(links, 1, part, project(psi, 1, 1))
            carried.append(mapped(lambda v: pltpu.roll(v, X, 1), half))
        for own, part in enumerate(pair):
            total = chip_psi(shape, total_ref, part)
            half = mapped(
                lambda a, b: jnp.where(lane >= lanes - X, b, a), minus[own], minus[1 - own]
            )
            add_rebuilt(total, mul_link(links, 1, part, half), 1, -1)
            half = mapped(lambda a, b: jnp.where(lane < X, b, a), carried[own], carried[1 - own])
            add_rebuilt(total, half, 1, 1)
            for s, c, n, k in components(4):
                total_ref[shape.block(k, part), :] = total[s, c][n]


def chip_finish(shape, psi_ref, links_ref, total_ref, received, scratch, out_ref):
    z_second, t_second, z_first, t_first = received
    z_down, z_up = scratch
    t_even, z_even = is_even("ta"), is_even("gy")
    t, rows, lanes, parts = shape.t, shape.rows, shape.lanes, shape.parts
    z_down[...] = either(z_even, z_first[...], z_second[...])
    z_up[...] = either(z_even, z_second[...], z_first[...])
    links = ChipLinks(shape, links_ref)

    def plane(ref, y_half):
        def value(k):
            face = ref[pl.ds((k * 2 + y_half) * t, t), :]
            if rows != t:
                pad = jnp.zeros((rows - t, lanes), jnp.float32)
                face = jnp.concatenate([face, pad], axis=0)
            return face

        return gathered_pairs(2, value)

    for part in range(parts):
        total = chip_psi(shape, total_ref, part)
        if part >= parts - 2:
            half = mul_link(links, 2, part, plane(z_down, part - parts + 2))
            add_rebuilt(total, half, 2, -1)
        if part < 2:
            add_rebuilt(total, plane(z_up, part), 2, 1)
        for s, c, n, k in components(4):
            value = psi_ref[shape.block(k, part), :] - hop_kappa * total[s, c][n]
            out_ref[shape.block(k, part), :] = value if s < 2 else -value

    def t_half(from_even, from_odd):
        def value(k):
            at = pl.ds(k * parts, parts)
            return either(t_even, from_even[at, :], from_odd[at, :])

        return gathered_pairs(2, value)

    down = mul_link(ChipLinks(shape, links_ref, t - 1), 3, 0, t_half(t_first, t_second))
    up = t_half(t_second, t_first)
    zero = jnp.zeros((parts, lanes), jnp.float32)
    for half, parity, row in ((down, -1, t - 1), (up, 1, 0)):
        total = {(s, c): (zero, zero) for s in range(4) for c in range(3)}
        add_rebuilt(total, half, 3, parity)
        for s, c, n, k in components(4):
            at = shape.edge(k, row)
            value = hop_kappa * total[s, c][n]
            out_ref[at, :] = out_ref[at, :] - (value if s < 2 else -value)


def chip_mid_kernel(shape, psi_ref, links_ref, total_ref, *refs):
    received, out_ref, messages, scratch = refs[:4], refs[4], refs[5:9], refs[9:]
    chip_finish(shape, psi_ref, links_ref, total_ref, received, scratch, out_ref)
    chip_messages(shape, out_ref, links_ref, *messages)


def chip_inner_sums_kernel(
    shape, psi_ref, links_ref, start_ref, one_ref, two_ref, total_ref, copies_ref
):
    class View:
        def __init__(self, ref):
            self.ref = ref

        def __getitem__(self, index):
            return self.ref[shape.block(*index), :]

    wide = ChipShape(shape.t, shape.z, shape.lanes)
    wide.z = shape.parts
    row = sums_row(wide, View(two_ref), View(start_ref), View(psi_ref), View(one_ref))
    copies_ref[...] = jnp.broadcast_to(row[None], copies_ref.shape)
    chip_inner_kernel(shape, psi_ref, links_ref, total_ref)


def y_part(shape, k, z, y_half):
    return pl.ds(pl.multiple_of((k * shape.parts + 2 * z + y_half) * shape.rows, 8), shape.rows)


def hand_over_rows(shape, n, k, z):
    return pl.ds(((n * 24 + k) * shape.z + z) * shape.rows, shape.rows)


def chip_finish_kernel(shape, psi_ref, links_ref, total_ref, *refs):
    received, (start_ref, two_ref, out_ref, other_ref), scratch = refs[:4], refs[4:8], refs[8:]
    chip_finish(shape, psi_ref, links_ref, total_ref, received, scratch, out_ref)
    y_half = 1 - lax.axis_index("gy")
    for n, ref in enumerate((start_ref, two_ref, out_ref)):
        for k in range(24):
            for z in range(shape.z):
                rows = y_part(shape, k, z, y_half)
                other_ref[hand_over_rows(shape, n, k, z), :] = ref[rows, :]


def chip_last_kernel(
    shape, entries, start_ref, two_ref, four_ref, other_ref, gathered, out_ref, coefficients
):
    alpha_one, beta_one, alpha_two, scale, first_factor = scalars(gathered, entries)
    t, z_extent = shape.t, 2 * shape.z
    core = lax.axis_index("gy")

    def put(k, z, start, two, four):
        remain = two - alpha_one * start
        result = (four - alpha_one * two - alpha_two * remain) * scale - first_factor * start
        out_ref[pl.ds(k * t * z_extent + z, t, stride=z_extent), :] = result[0:t]

    for k in range(24):
        for z in range(shape.z):
            rows = y_part(shape, k, z, core)
            own = (ref[rows, :] for ref in (start_ref, two_ref, four_ref))
            put(k, core * shape.z + z, *own)
            other = (other_ref[hand_over_rows(shape, n, k, z), :] for n in range(3))
            put(k, (1 - core) * shape.z + z, *other)
    coefficients[0] = alpha_one[0, 0]
    coefficients[1] = beta_one[0, 0]
    coefficients[2] = alpha_two[0, 0]


def chip_shards(source, gauge_links):
    devices_all = lax.axis_size("ta") * lax.axis_size("gz") * 2
    entries = float(source.size * devices_all)
    z_extent = source.shape[4]
    shape = ChipShape(source.shape[3], z_extent // 2, source.shape[5])
    t, rows, lanes = shape.t, shape.rows, shape.lanes
    vmem = pl.BlockSpec(memory_space=pltpu.VMEM)
    smem = pl.BlockSpec(memory_space=pltpu.SMEM)

    def held(*dims):
        return pltpu.VMEM(dims, jnp.float32)

    field = held(24 * shape.parts * rows, lanes)
    links_field = held(72 * shape.parts * rows, lanes)
    z_face, t_face = held(shape.z_rows, lanes), held(shape.t_rows, lanes)
    messages = (z_face, t_face, z_face, t_face)
    z_faces = (z_face, z_face)

    def call(kernel, name, flops, out_shape, operands, **options):
        in_spec = options.pop("in_spec", vmem)
        out_specs = options.pop("out_specs", jax.tree.map(lambda _: vmem, out_shape))
        return pl.pallas_call(
            kernel,
            name=name,
            out_shape=out_shape,
            in_specs=[in_spec] * len(operands),
            out_specs=out_specs,
            compiler_params=pltpu.CompilerParams(vmem_limit_bytes=8 << 20),
            cost_estimate=pl.CostEstimate(flops=flops, bytes_accessed=1 << 20, transcendentals=0),
            **options,
        )(*operands)

    def exchanged(sent):
        z_second, t_second, z_first, t_first = sent
        z_ring = ("gz", "gy")
        return (
            swap(z_second, z_ring, True), swap(t_second, "ta", True),
            swap(z_first, z_ring, False), swap(t_first, "ta", False),
        )

    sites = t * z_extent * lanes
    rows_in = t * z_extent
    own = (source.reshape(24 * rows_in, lanes), gauge_links.reshape(72 * rows_in, lanes))
    other = tuple(swap(value, "gy", False) for value in own)
    psi, links = call(
        functools.partial(chip_own_kernel, shape), "own", 200 * sites, (field, links_field),
        [pltpu.with_memory_space_constraint(value, pltpu.HBM) for value in own],
        scratch_shapes=(
            held(24 * rows_in, lanes), held(72 * rows_in, lanes), pltpu.SemaphoreType.DMA((5,)),
        ),
        in_spec=pl.BlockSpec(memory_space=pltpu.HBM),
    )
    psi, links, *sent = call(
        functools.partial(chip_prep_kernel, shape), "prep", 400 * sites,
        (field, links_field, *messages), (*other, psi, links),
        input_output_aliases={2: 0, 3: 1},
    )
    powers = [psi]
    for step in range(3):
        halo = exchanged(sent)
        inner = functools.partial(chip_inner_kernel, shape)
        total = call(inner, "inner", 1000 * sites, field, (psi, links))
        psi, *sent = call(
            functools.partial(chip_mid_kernel, shape), "mid", 600 * sites,
            (field, *messages), (psi, links, total, *halo), scratch_shapes=z_faces,
        )
        powers.append(psi)
    halo = exchanged(sent)
    total, copies = call(
        functools.partial(chip_inner_sums_kernel, shape), "inner_sums", 1400 * sites,
        (field, held(devices_all, 1, lanes)), (psi, links, *powers[:3]),
    )
    gathered = from_everyone(copies)
    four, for_other = call(
        functools.partial(chip_finish_kernel, shape), "finish", 400 * sites,
        (field, held(3 * 24 * shape.z * rows, lanes)),
        (psi, links, total, *halo, powers[0], powers[2]), scratch_shapes=z_faces,
    )
    residual, coefficients = call(
        functools.partial(chip_last_kernel, shape, entries), "last", 100 * sites,
        (
            jax.ShapeDtypeStruct((24 * rows_in, lanes), jnp.float32),
            jax.ShapeDtypeStruct((3,), jnp.float32),
        ),
        (powers[0], powers[2], four, swap(for_other, "gy", False), gathered),
        out_specs=(vmem, smem),
    )
    return (residual.reshape(source.shape), coefficients)


def solution(mesh):
    placed = (P(None, None, None, "ta", "gz", "gy"), P(None, None, None, None, "ta", "gz", "gy"))
    return jax.shard_map(
        chip_shards if mesh.shape["gy"] == 2 else shards,
        mesh=mesh,
        in_specs=placed,
        out_specs=(P(None, None, None, "ta", "gz", "gy"), P()),
        check_vma=False,
    )
```

```python
import functools
import math

import jax
import jax.numpy as jnp
from jax import lax
from jax.experimental import pallas as pl
from jax.experimental.pallas import tpu as pltpu
from jax.sharding import PartitionSpec as P

X = 32

hop_kappa = 0.19
epsilon = 1e-06
spin_table = (
    ((1, 0), (-1j, -1j)),
    ((1, 0), (-1, 1)),
    ((0, 1), (-1j, 1j)),
    ((0, 1), (1, 1)),
)
SPIN_COLOUR = [(spin, colour) for spin in range(2) for colour in range(3)]


def add_phased(left, phase, right):
    phase = complex(phase)
    if phase == 1:
        return (left[0] + right[0], left[1] + right[1])
    if phase == -1:
        return (left[0] - right[0], left[1] - right[1])
    if phase == 1j:
        return (left[0] - right[1], left[1] + right[0])
    return (left[0] + right[1], left[1] - right[0])


def project(psi, direction, parity):
    order, phases = spin_table[direction]
    return {
        (s, c): add_phased(psi[s, c], parity * phases[s], psi[2 + order[s], c])
        for s, c in SPIN_COLOUR
    }


def add_rebuilt(total, half, direction, parity):
    order, phases = spin_table[direction]
    for s, c in SPIN_COLOUR:
        total[s, c] = add_phased(total[s, c], 1, half[s, c])
        row = order[s]
        phase = parity * complex(phases[row]).conjugate()
        total[2 + s, c] = add_phased(total[2 + s, c], phase, half[row, c])


def mul_link(links, direction, z, half):
    out = {}
    for row in range(3):
        for s in range(2):
            real, imag = None, None
            for col in range(3):
                u_real, u_imag = links[direction, row, col, z]
                h_real, h_imag = half[s, col]
                term_real = u_real * h_real - u_imag * h_imag
                term_imag = u_real * h_imag + u_imag * h_real
                real = term_real if real is None else real + term_real
                imag = term_imag if imag is None else imag + term_imag
            out[s, row] = (real, imag)
    return out


def mul_link_dag(links, direction, z, half):
    out = {}
    for row in range(3):
        for s in range(2):
            real, imag = None, None
            for col in range(3):
                u_real, u_imag = links[direction, col, row, z]
                h_real, h_imag = half[s, col]
                term_real = u_real * h_real + u_imag * h_imag
                term_imag = u_real * h_imag - u_imag * h_real
                real = term_real if real is None else real + term_real
                imag = term_imag if imag is None else imag + term_imag
            out[s, row] = (real, imag)
    return out


def mapped(function, *halves):
    return {
        key: tuple(function(*(half[key][part] for half in halves)) for part in range(2))
        for key in SPIN_COLOUR
    }


class Links:
    def __init__(self, ref):
        self.ref = ref

    def __getitem__(self, index):
        direction, row, col, z = index
        first = ((direction * 3 + row) * 3 + col) * 2
        return (self.ref[first, z], self.ref[first + 1, z])


def load_psi(ref, z):
    return {
        (s, c): (ref[(s * 3 + c) * 2, z], ref[(s * 3 + c) * 2 + 1, z])
        for s in range(4)
        for c in range(3)
    }


def load_half(ref, z):
    return {
        (s, c): (ref[(s * 3 + c) * 2, z], ref[(s * 3 + c) * 2 + 1, z]) for s, c in SPIN_COLOUR
    }


def store_half(ref, z, half):
    for (s, c), pair in half.items():
        for part in range(2):
            ref[(s * 3 + c) * 2 + part, z] = pair[part]


class Shape:
    def __init__(self, t_extent, z_extent, lanes):
        self.t = t_extent
        self.z = z_extent
        self.rows = -(-t_extent // 8) * 8
        self.lanes = lanes

    def row(self):
        return lax.broadcasted_iota(jnp.int32, (self.rows, self.lanes), 0)

    def lane(self):
        return lax.broadcasted_iota(jnp.int32, (self.rows, self.lanes), 1)


def is_even(axis):
    return jnp.bitwise_and(lax.axis_index(axis), 1) == 0


def either(choice, first, second):
    return jnp.where(choice, first, second)


def emit_messages(shape, psi_ref, links, refs):
    z_second, t_second, z_first, t_first, y_msg, carried_y, carried_t = refs
    t_even, z_even = is_even("ta"), is_even("gz")
    lane = shape.lane()
    last_z, last_t = shape.z - 1, shape.t - 1
    for z in range(shape.z):
        psi = load_psi(psi_ref, z)
        minus = project(psi, 3, -1)
        carried = mul_link_dag(links, 3, z, project(psi, 3, 1))
        store_half(carried_t, z, carried)
        for s, c in SPIN_COLOUR:
            for part in range(2):
                at = ((s * 3 + c) * 2 + part) * shape.z + z
                down = minus[s, c][part][0:1]
                up = carried[s, c][part][last_t : last_t + 1]
                t_first[at : at + 1] = either(t_even, up, down)
                t_second[at : at + 1] = either(t_even, down, up)
        minus = project(psi, 1, -1)
        carried = mul_link_dag(links, 1, z, project(psi, 1, 1))
        store_half(carried_y, z, carried)
        store_half(
            y_msg,
            z,
            mapped(lambda low, high: jnp.where(lane < X, low, high), minus, carried),
        )
    minus = project(load_psi(psi_ref, 0), 2, -1)
    carried = mul_link_dag(links, 2, last_z, project(load_psi(psi_ref, last_z), 2, 1))
    for s, c in SPIN_COLOUR:
        for part in range(2):
            at = ((s * 3 + c) * 2 + part) * shape.t
            down, up = minus[s, c][part][0 : shape.t], carried[s, c][part][0 : shape.t]
            z_first[at : at + shape.t] = either(z_even, up, down)
            z_second[at : at + shape.t] = either(z_even, down, up)


def prep_kernel(shape, source_hbm, links_hbm, psi_ref, links_ref, *refs):
    messages, (source_ref, links_in, arrived) = refs[:-3], refs[-3:]
    t, z_extent = shape.t, shape.z
    part = 18 * t * z_extent
    copies = [pltpu.make_async_copy(source_hbm, source_ref, arrived.at[4])]
    for direction in (3, 2, 1, 0):
        rows = pl.ds(direction * part, part)
        copies.append(
            pltpu.make_async_copy(links_hbm.at[rows], links_in.at[rows], arrived.at[direction])
        )
    for copy in copies:
        copy.start()
    if shape.rows != t:
        links_ref[...] = jnp.zeros_like(links_ref)
        psi_ref[...] = jnp.zeros_like(psi_ref)
    last = lax.broadcasted_iota(jnp.int32, (t, shape.lanes), 0) == t - 1
    sign = jnp.where(lax.axis_index("ta") == lax.axis_size("ta") - 1, -1.0, 1.0)
    flip = jnp.where(last, sign, 1.0)
    copies[0].wait()
    for k in range(24):
        for z in range(z_extent):
            psi_ref[k, z, 0:t] = source_ref[pl.ds(k * t * z_extent + z, t, stride=z_extent), :]
    for direction in (3, 2, 1, 0):
        copies[4 - direction].wait()
        for k in range(18 * direction, 18 * direction + 18):
            for z in range(z_extent):
                value = links_in[pl.ds(k * t * z_extent + z, t, stride=z_extent), :]
                links_ref[k, z, 0:t] = value * flip if direction == 3 else value
    emit_messages(shape, psi_ref, Links(links_ref), messages)


def summed(shape, term):
    total = None
    for k in range(24):
        for z in range(shape.z):
            value = term(k, z)
            total = value if total is None else total + value
    return total


def over_lanes(total):
    return jnp.sum(jnp.sum(total, axis=0, keepdims=True), axis=1, keepdims=True)


def local_sums(shape, image, origin):
    square = summed(shape, lambda k, z: origin[k, z] * origin[k, z])
    mixed = over_lanes(summed(shape, lambda k, z: image[k, z] * origin[k, z]))
    whole = over_lanes(square)
    factor = jnp.where(whole > 0.0, mixed / jnp.where(whole > 0.0, whole, 1.0), 0.0)
    spread = jnp.broadcast_to(factor, (shape.rows, shape.lanes))
    rest_square, rest_mixed = None, None
    for k in range(24):
        for z in range(shape.z):
            start = origin[k, z]
            rest = image[k, z] - spread * start
            terms = rest * rest, rest * start
            if rest_square is None:
                rest_square, rest_mixed = terms
            else:
                rest_square, rest_mixed = rest_square + terms[0], rest_mixed + terms[1]
    return [factor, *(over_lanes(value) for value in (square, rest_square, rest_mixed))]


def inner_kernel(shape, psi_ref, links_ref, total_ref):
    links = Links(links_ref)
    x = shape.lane() % X
    lanes = shape.lanes
    at_end, at_start = x == X - 1, x == 0

    def ahead(value):
        return jnp.where(
            at_end, pltpu.roll(value, X - 1, 1), pltpu.roll(value, lanes - 1, 1)
        )

    def behind(value):
        return jnp.where(at_start, pltpu.roll(value, lanes - X + 1, 1), pltpu.roll(value, 1, 1))

    for z in range(shape.z):
        psi = load_psi(psi_ref, z)
        zero = jnp.zeros((shape.rows, lanes), jnp.float32)
        total = {key: (zero, zero) for key in psi}
        half = mapped(ahead, project(psi, 0, -1))
        add_rebuilt(total, mul_link(links, 0, z, half), 0, -1)
        half = mapped(behind, mul_link_dag(links, 0, z, project(psi, 0, 1)))
        add_rebuilt(total, half, 0, 1)
        if z + 1 < shape.z:
            half = project(load_psi(psi_ref, z + 1), 2, -1)
            add_rebuilt(total, mul_link(links, 2, z, half), 2, -1)
        if z > 0:
            half = project(load_psi(psi_ref, z - 1), 2, 1)
            add_rebuilt(total, mul_link_dag(links, 2, z - 1, half), 2, 1)
        for (s, c), pair in total.items():
            for part in range(2):
                total_ref[(s * 3 + c) * 2 + part, z] = pair[part]


def add_y_hops(shape, z, psi, total, links, carried_y, y_halo):
    lane, lanes = shape.lane(), shape.lanes
    received = load_half(y_halo, z)
    half = mapped(
        lambda own, other: pltpu.roll(jnp.where(lane < X, other, own), lanes - X, 1),
        project(psi, 1, -1),
        received,
    )
    add_rebuilt(total, mul_link(links, 1, z, half), 1, -1)
    half = mapped(
        lambda own, other: pltpu.roll(jnp.where(lane >= lanes - X, other, own), X, 1),
        load_half(carried_y, z),
        received,
    )
    add_rebuilt(total, half, 1, 1)


def finish_hops(
    shape, psi_ref, links, total_ref, carried_y, carried_t, halo, store
):
    z_second, t_second, z_first, t_first, y_msg = halo
    t_even, z_even = is_even("ta"), is_even("gz")
    row = shape.row()
    lanes, rows, t = shape.lanes, shape.rows, shape.t
    last_z = shape.z - 1

    for z in range(shape.z):
        psi = load_psi(psi_ref, z)
        total = load_psi(total_ref, z)

        def rim_rows(from_even, from_odd):
            half = {}
            for s, c in SPIN_COLOUR:
                ats = [((s * 3 + c) * 2 + part) * shape.z + z for part in range(2)]
                half[s, c] = tuple(
                    jnp.broadcast_to(
                        either(t_even, from_even[at : at + 1], from_odd[at : at + 1]),
                        (rows, lanes),
                    )
                    for at in ats
                )
            return half

        def rim_plane(from_even, from_odd):
            half = {}
            for s, c in SPIN_COLOUR:
                pair = []
                for part in range(2):
                    at = ((s * 3 + c) * 2 + part) * t
                    plane = either(z_even, from_even[at : at + t], from_odd[at : at + t])
                    if rows != t:
                        pad = jnp.zeros((rows - t, lanes), jnp.float32)
                        plane = jnp.concatenate([plane, pad], axis=0)
                    pair.append(plane)
                half[s, c] = tuple(pair)
            return half

        if y_msg is not None:
            add_y_hops(shape, z, psi, total, links, carried_y, y_msg)
        if z == last_z:
            add_rebuilt(total, mul_link(links, 2, z, rim_plane(z_first, z_second)), 2, -1)
        if z == 0:
            add_rebuilt(total, rim_plane(z_second, z_first), 2, 1)
        half = mapped(
            lambda own, other: jnp.where(row == t - 1, other, pltpu.roll(own, rows - 1, 0)),
            project(psi, 3, -1),
            rim_rows(t_first, t_second),
        )
        add_rebuilt(total, mul_link(links, 3, z, half), 3, -1)
        half = mapped(
            lambda own, other: jnp.where(row == 0, other, pltpu.roll(own, 1, 0)),
            load_half(carried_t, z),
            rim_rows(t_second, t_first),
        )
        add_rebuilt(total, half, 3, 1)
        for (s, c), pair in total.items():
            for part in range(2):
                value = psi[s, c][part] - hop_kappa * pair[part]
                value = value if s < 2 else -value
                if rows != t:
                    value = jnp.where(row < t, value, 0.0)
                store((s * 3 + c) * 2 + part, z, value)


def mid_kernel(shape, psi_ref, links_ref, total_ref, carried_y, carried_t, *refs):
    halo, out_ref, messages = refs[:5], refs[5], refs[6:]
    links = Links(links_ref)

    def store(k, z, value):
        out_ref[k, z] = value

    finish_hops(
        shape, psi_ref, links, total_ref, carried_y, carried_t, halo, store
    )
    emit_messages(shape, out_ref, links, messages)


def sums_row(shape, two, start, three, one):
    sums = local_sums(shape, two, start) + local_sums(shape, three, one)
    lane = lax.broadcasted_iota(jnp.int32, (1, shape.lanes), 1)
    row = jnp.zeros((1, shape.lanes), jnp.float32)
    for k, value in enumerate(sums):
        row = jnp.where(lane == k, value, row)
    return row


def inner_sums_kernel(
    shape, psi_ref, links_ref, start_ref, one_ref, two_ref, total_ref, copies_ref
):
    row = sums_row(shape, two_ref, start_ref, psi_ref, one_ref)
    copies_ref[...] = jnp.broadcast_to(row[None], copies_ref.shape)
    inner_kernel(shape, psi_ref, links_ref, total_ref)


def finish_kernel(shape, psi_ref, links_ref, total_ref, carried_y, carried_t, *refs):
    halo, out_ref = refs[:5], refs[5]

    def store(k, z, value):
        out_ref[k, z] = value

    finish_hops(
        shape, psi_ref, Links(links_ref), total_ref, carried_y, carried_t, halo, store
    )


def scalars(gathered, entries):
    table = gathered[:, 0, :]
    columns = [table[:, k : k + 1] for k in range(8)]
    factor_two, start_square, two_square, two_mixed = columns[:4]
    factor_three, one_square, three_square, three_mixed = columns[4:]

    def over_devices(column):
        return jnp.sum(column, axis=0, keepdims=True)

    norm_square = over_devices(start_square) / entries + epsilon
    alpha_one = over_devices(one_square) / entries / norm_square
    gap = alpha_one - factor_two
    remain_square = over_devices(two_square - gap * (2.0 * two_mixed - gap * start_square)) / entries
    overlap = over_devices(two_mixed - gap * start_square) / entries
    gap = alpha_one - factor_three
    image_square = over_devices(three_square - gap * (2.0 * three_mixed - gap * one_square)) / entries
    norm = jnp.sqrt(norm_square)
    beta_one = jnp.sqrt(remain_square / norm_square + epsilon)
    overlap = overlap / (norm_square * beta_one)
    alpha_two = image_square / (norm_square * beta_one * beta_one) - beta_one * overlap
    scale = 1.0 / (norm * beta_one)
    return alpha_one, beta_one, alpha_two, scale, beta_one / norm


def last_kernel(
    shape, entries, start_ref, two_ref, four_ref, gathered, out_ref, coefficients
):
    alpha_one, beta_one, alpha_two, scale, first_factor = scalars(gathered, entries)
    t, z_extent = shape.t, shape.z
    for k in range(24):
        for z in range(z_extent):
            two, start = two_ref[k, z], start_ref[k, z]
            remain = two - alpha_one * start
            result = (four_ref[k, z] - alpha_one * two - alpha_two * remain) * scale
            result = result - first_factor * start
            out_ref[pl.ds(k * t * z_extent + z, t, stride=z_extent), :] = result[0:t]
    coefficients[0] = alpha_one[0, 0]
    coefficients[1] = beta_one[0, 0]
    coefficients[2] = alpha_two[0, 0]


def swap(value, axis, second):
    count = math.prod(lax.axis_size(name) for name in (axis if isinstance(axis, tuple) else (axis,)))
    pairs = []
    for low in range(1 if second else 0, count, 2):
        high = (low + 1) % count
        pairs += [(low, high), (high, low)]
    return lax.ppermute(value, axis, pairs)


def exchange(messages, lanes):
    z_second, t_second, z_first, t_first, y_msg = messages
    halo = (
        swap(z_second, "gz", True),
        swap(t_second, "ta", True),
        swap(z_first, "gz", False),
        swap(t_first, "ta", False),
    )
    y_halo = swap(y_msg, "gy", False)
    if lax.axis_size("gy") > 2:
        even = lax.axis_index("gy") % 2 == 0
        lane = lax.broadcasted_iota(jnp.int32, y_msg.shape, y_msg.ndim - 1)
        y_halo = jnp.where((lane < lanes // 2) == even, y_halo, swap(y_msg, "gy", True))
    return (*halo, y_halo)


def from_everyone(copies):
    return lax.all_to_all(copies, ("ta", "gz", "gy"), split_axis=0, concat_axis=0, tiled=True)


def shards(source, gauge_links):
    devices_all = lax.axis_size("ta") * lax.axis_size("gz") * lax.axis_size("gy")
    entries = float(source.size * devices_all)
    shape = Shape(source.shape[3], source.shape[4], source.shape[5])
    t, z, rows, lanes = shape.t, shape.z, shape.rows, shape.lanes
    vmem = pl.BlockSpec(memory_space=pltpu.VMEM)
    smem = pl.BlockSpec(memory_space=pltpu.SMEM)

    def held(*dims):
        return pltpu.VMEM(dims, jnp.float32)

    field = held(24, z, rows, lanes)
    half = held(12, z, rows, lanes)
    z_face, t_face = held(12 * t, lanes), held(12 * z, lanes)
    messages = (z_face, t_face, z_face, t_face, half, half, half)

    def call(kernel, name, flops, out_shape, operands, out_specs=None, in_spec=vmem, scratch=()):
        return pl.pallas_call(
            kernel,
            name=name,
            out_shape=out_shape,
            in_specs=[in_spec] * len(operands),
            out_specs=out_specs or jax.tree.map(lambda _: vmem, out_shape),
            scratch_shapes=scratch,
            compiler_params=pltpu.CompilerParams(vmem_limit_bytes=8 << 20),
            cost_estimate=pl.CostEstimate(flops=flops, bytes_accessed=1 << 20, transcendentals=0),
        )(*operands)

    sites = t * z * lanes
    psi, links, *sent = call(
        functools.partial(prep_kernel, shape), "prep", 400 * sites,
        (field, held(72, z, rows, lanes), *messages),
        (
            pltpu.with_memory_space_constraint(source.reshape(24 * t * z, lanes), pltpu.HBM),
            pltpu.with_memory_space_constraint(gauge_links.reshape(72 * t * z, lanes), pltpu.HBM),
        ),
        in_spec=pl.BlockSpec(memory_space=pltpu.HBM),
        scratch=(
            held(24 * t * z, lanes), held(72 * t * z, lanes), pltpu.SemaphoreType.DMA((5,)),
        ),
    )
    powers = [psi]
    for step in range(3):
        halo = exchange(sent[:5], lanes)
        inner = functools.partial(inner_kernel, shape)
        total = call(inner, "inner", 700 * sites, field, (psi, links))
        psi, *sent = call(
            functools.partial(mid_kernel, shape), "mid", 1000 * sites,
            (field, *messages), (psi, links, total, *sent[5:], *halo),
        )
        powers.append(psi)
    halo = exchange(sent[:5], lanes)
    total, copies = call(
        functools.partial(inner_sums_kernel, shape), "inner_sums", 1100 * sites,
        (field, held(devices_all, 8, lanes)), (psi, links, *powers[:3]),
    )
    gathered = from_everyone(copies)
    four = call(
        functools.partial(finish_kernel, shape), "finish", 700 * sites, field,
        (psi, links, total, *sent[5:], *halo),
    )
    residual, coefficients = call(
        functools.partial(last_kernel, shape, entries), "last", 100 * sites,
        (
            jax.ShapeDtypeStruct((24 * t * z, lanes), jnp.float32),
            jax.ShapeDtypeStruct((3,), jnp.float32),
        ),
        (powers[0], powers[2], four, gathered), (vmem, smem),
    )
    return (residual.reshape(source.shape), coefficients)


class ChipShape(Shape):
    def __init__(self, t_extent, z_extent, lanes):
        super().__init__(t_extent, z_extent, lanes)
        self.parts = 2 * z_extent
        self.z_rows = 24 * t_extent
        self.t_rows = 12 * self.parts

    def block(self, k, part):
        first = (k * self.parts + part) * self.rows
        return pl.ds(first, self.rows)

    def edge(self, k, row):
        return pl.ds(k * self.parts * self.rows + row, self.parts, stride=self.rows)


class ChipLinks:
    def __init__(self, shape, ref, row=None):
        self.shape, self.ref, self.row = shape, ref, row

    def __getitem__(self, index):
        direction, row, col, part = index
        first = ((direction * 3 + row) * 3 + col) * 2
        if self.row is None:
            return tuple(self.ref[self.shape.block(first + n, part), :] for n in range(2))
        return tuple(self.ref[self.shape.edge(first + n, self.row), :] for n in range(2))


def components(spins):
    return [(s, c, part, (s * 3 + c) * 2 + part) for s in range(spins) for c in range(3) for part in range(2)]


def gathered_pairs(spins, value):
    out = {}
    for s in range(spins):
        for c in range(3):
            out[s, c] = tuple(value((s * 3 + c) * 2 + part) for part in range(2))
    return out


def chip_psi(shape, ref, part):
    return gathered_pairs(4, lambda k: ref[shape.block(k, part), :])


def chip_edge(shape, ref, row):
    return gathered_pairs(4, lambda k: ref[shape.edge(k, row), :])


def chip_messages(shape, psi_ref, links_ref, z_second, t_second, z_first, t_first):
    t, last = shape.t, shape.t - 1
    even = is_even("ta")
    minus = project(chip_edge(shape, psi_ref, 0), 3, -1)
    half = project(chip_edge(shape, psi_ref, last), 3, 1)
    carried = mul_link_dag(ChipLinks(shape, links_ref, last), 3, 0, half)
    for s, c, part, k in components(2):
        rows = pl.ds(k * shape.parts, shape.parts)
        up, down = carried[s, c][part], minus[s, c][part]
        t_first[rows, :] = either(even, up, down)
        t_second[rows, :] = either(even, down, up)
    even = is_even("gy")
    links = ChipLinks(shape, links_ref)
    for y_half in range(2):
        minus = project(chip_psi(shape, psi_ref, y_half), 2, -1)
        part_last = shape.parts - 2 + y_half
        half = project(chip_psi(shape, psi_ref, part_last), 2, 1)
        carried = mul_link_dag(links, 2, part_last, half)
        for s, c, part, k in components(2):
            rows = pl.ds((k * 2 + y_half) * t, t)
            up, down = carried[s, c][part][0:t], minus[s, c][part][0:t]
            z_first[rows, :] = either(even, up, down)
            z_second[rows, :] = either(even, down, up)


def chip_bring(shape, y_half, source_ref, links_in, psi_ref, links_ref, arrived):
    t, z_extent = shape.t, 2 * shape.z
    first_plane = lax.axis_index("gy") * shape.z
    last = lax.broadcasted_iota(jnp.int32, (t, shape.lanes), 0) == t - 1
    sign = jnp.where(lax.axis_index("ta") == lax.axis_size("ta") - 1, -1.0, 1.0)
    flip = jnp.where(last, sign, 1.0)

    def bring(in_ref, out_ref, k, z, factor=None):
        value = in_ref[pl.ds(k * t * z_extent + first_plane + z, t, stride=z_extent), :]
        if factor is not None:
            value = value * factor
        at = (k * shape.parts + 2 * z + y_half) * shape.rows
        out_ref[pl.ds(pl.multiple_of(at, 8), t), :] = value

    arrived(4)
    for z in range(shape.z):
        for k in range(24):
            bring(source_ref, psi_ref, k, z)
    for direction in (3, 2, 1, 0):
        arrived(direction)
        for z in range(shape.z):
            for k in range(18 * direction, 18 * direction + 18):
                bring(links_in, links_ref, k, z, flip if direction == 3 else None)


def chip_own_kernel(
    shape, source_hbm, links_hbm, psi_ref, links_ref, rest_ref, source_ref, links_in, semaphores
):
    part = 18 * shape.t * 2 * shape.z
    copies = {4: pltpu.make_async_copy(source_hbm, source_ref, semaphores.at[4])}
    for direction in (3, 2, 1, 0):
        rows = pl.ds(direction * part, part)
        copies[direction] = pltpu.make_async_copy(
            links_hbm.at[rows], links_in.at[rows], semaphores.at[direction]
        )
    for copy in copies.values():
        copy.start()
    if shape.rows != shape.t:
        links_ref[...] = jnp.zeros_like(links_ref)
        psi_ref[...] = jnp.zeros_like(psi_ref)
    chip_bring(
        shape, lax.axis_index("gy"), source_ref, links_in, psi_ref, links_ref,
        lambda n: copies[n].wait(),
    )
    t, z_extent = shape.t, 2 * shape.z
    first_plane = (1 - lax.axis_index("gy")) * shape.z
    if shape.rows != t:
        rest_ref[...] = jnp.zeros_like(rest_ref)
    for k in range(24):
        for z in range(shape.z):
            value = source_ref[pl.ds(k * t * z_extent + first_plane + z, t, stride=z_extent), :]
            rest_ref[pl.ds((k * shape.z + z) * shape.rows, t), :] = value


def chip_prep_kernel(
    shape, source_ref, links_in, psi_in, links_held, psi_ref, links_ref, *messages
):
    chip_bring(
        shape, 1 - lax.axis_index("gy"), source_ref, links_in, psi_ref, links_ref, lambda n: None
    )
    chip_messages(shape, psi_ref, links_ref, *messages)


def chip_inner_kernel(shape, psi_ref, links_ref, total_ref):
    links = ChipLinks(shape, links_ref)
    lane, row = shape.lane(), shape.row()
    x = lane % X
    lanes, rows, t = shape.lanes, shape.rows, shape.t
    at_end, at_start = x == X - 1, x == 0
    inside_ahead = row < t - 1
    inside_behind = jnp.logical_and(row > 0, row < t)

    def x_ahead(value):
        return jnp.where(
            at_end, pltpu.roll(value, X - 1, 1), pltpu.roll(value, lanes - 1, 1)
        )

    def x_behind(value):
        return jnp.where(at_start, pltpu.roll(value, lanes - X + 1, 1), pltpu.roll(value, 1, 1))

    def t_ahead(value):
        return jnp.where(inside_ahead, pltpu.roll(value, rows - 1, 0), 0.0)

    def t_behind(value):
        return jnp.where(inside_behind, pltpu.roll(value, 1, 0), 0.0)

    for z in range(shape.z):
        for part in (2 * z, 2 * z + 1):
            psi = chip_psi(shape, psi_ref, part)
            zero = jnp.zeros((rows, lanes), jnp.float32)
            total = {key: (zero, zero) for key in psi}
            half = mapped(x_ahead, project(psi, 0, -1))
            add_rebuilt(total, mul_link(links, 0, part, half), 0, -1)
            half = mapped(x_behind, mul_link_dag(links, 0, part, project(psi, 0, 1)))
            add_rebuilt(total, half, 0, 1)
            half = mapped(t_ahead, project(psi, 3, -1))
            add_rebuilt(total, mul_link(links, 3, part, half), 3, -1)
            half = mapped(t_behind, mul_link_dag(links, 3, part, project(psi, 3, 1)))
            add_rebuilt(total, half, 3, 1)
            if z + 1 < shape.z:
                half = project(chip_psi(shape, psi_ref, part + 2), 2, -1)
                add_rebuilt(total, mul_link(links, 2, part, half), 2, -1)
            if z > 0:
                half = project(chip_psi(shape, psi_ref, part - 2), 2, 1)
                add_rebuilt(total, mul_link_dag(links, 2, part - 2, half), 2, 1)
            for s, c, n, k in components(4):
                total_ref[shape.block(k, part), :] = total[s, c][n]
        pair = (2 * z, 2 * z + 1)
        minus, carried = [], []
        for part in pair:
            psi = chip_psi(shape, psi_ref, part)
            minus.append(mapped(lambda v: pltpu.roll(v, lanes - X, 1), project(psi, 1, -1)))
            half = mul_link_dag(links, 1, part, project(psi, 1, 1))
            carried.append(mapped(lambda v: pltpu.roll(v, X, 1), half))
        for own, part in enumerate(pair):
            total = chip_psi(shape, total_ref, part)
            half = mapped(
                lambda a, b: jnp.where(lane >= lanes - X, b, a), minus[own], minus[1 - own]
            )
            add_rebuilt(total, mul_link(links, 1, part, half), 1, -1)
            half = mapped(lambda a, b: jnp.where(lane < X, b, a), carried[own], carried[1 - own])
            add_rebuilt(total, half, 1, 1)
            for s, c, n, k in components(4):
                total_ref[shape.block(k, part), :] = total[s, c][n]


def chip_finish(shape, psi_ref, links_ref, total_ref, received, scratch, out_ref):
    z_second, t_second, z_first, t_first = received
    z_down, z_up = scratch
    t_even, z_even = is_even("ta"), is_even("gy")
    t, rows, lanes, parts = shape.t, shape.rows, shape.lanes, shape.parts
    z_down[...] = either(z_even, z_first[...], z_second[...])
    z_up[...] = either(z_even, z_second[...], z_first[...])
    links = ChipLinks(shape, links_ref)

    def plane(ref, y_half):
        def value(k):
            face = ref[pl.ds((k * 2 + y_half) * t, t), :]
            if rows != t:
                pad = jnp.zeros((rows - t, lanes), jnp.float32)
                face = jnp.concatenate([face, pad], axis=0)
            return face

        return gathered_pairs(2, value)

    for part in range(parts):
        total = chip_psi(shape, total_ref, part)
        if part >= parts - 2:
            half = mul_link(links, 2, part, plane(z_down, part - parts + 2))
            add_rebuilt(total, half, 2, -1)
        if part < 2:
            add_rebuilt(total, plane(z_up, part), 2, 1)
        for s, c, n, k in components(4):
            value = psi_ref[shape.block(k, part), :] - hop_kappa * total[s, c][n]
            out_ref[shape.block(k, part), :] = value if s < 2 else -value

    def t_half(from_even, from_odd):
        def value(k):
            at = pl.ds(k * parts, parts)
            return either(t_even, from_even[at, :], from_odd[at, :])

        return gathered_pairs(2, value)

    down = mul_link(ChipLinks(shape, links_ref, t - 1), 3, 0, t_half(t_first, t_second))
    up = t_half(t_second, t_first)
    zero = jnp.zeros((parts, lanes), jnp.float32)
    for half, parity, row in ((down, -1, t - 1), (up, 1, 0)):
        total = {(s, c): (zero, zero) for s in range(4) for c in range(3)}
        add_rebuilt(total, half, 3, parity)
        for s, c, n, k in components(4):
            at = shape.edge(k, row)
            value = hop_kappa * total[s, c][n]
            out_ref[at, :] = out_ref[at, :] - (value if s < 2 else -value)


def chip_mid_kernel(shape, hands_over, psi_ref, links_ref, total_ref, *refs):
    received, out_ref, messages, refs = refs[:4], refs[4], refs[5:9], refs[9:]
    chip_finish(shape, psi_ref, links_ref, total_ref, received, refs[-2:], out_ref)
    chip_messages(shape, out_ref, links_ref, *messages)
    if hands_over:
        hand_over(shape, out_ref, refs[0])


def chip_inner_sums_kernel(
    shape, psi_ref, links_ref, start_ref, one_ref, two_ref, total_ref, copies_ref
):
    class View:
        def __init__(self, ref):
            self.ref = ref

        def __getitem__(self, index):
            return self.ref[shape.block(*index), :]

    wide = ChipShape(shape.t, shape.z, shape.lanes)
    wide.z = shape.parts
    row = sums_row(wide, View(two_ref), View(start_ref), View(psi_ref), View(one_ref))
    copies_ref[...] = jnp.broadcast_to(row[None], copies_ref.shape)
    chip_inner_kernel(shape, psi_ref, links_ref, total_ref)


def y_part(shape, k, z, y_half):
    return pl.ds(pl.multiple_of((k * shape.parts + 2 * z + y_half) * shape.rows, 8), shape.rows)


def rest_rows(shape, k, z):
    return pl.ds((k * shape.z + z) * shape.rows, shape.rows)


def hand_over(shape, ref, rest_ref):
    y_half = 1 - lax.axis_index("gy")
    for k in range(24):
        for z in range(shape.z):
            rest_ref[rest_rows(shape, k, z), :] = ref[y_part(shape, k, z, y_half), :]


def chip_finish_kernel(shape, psi_ref, links_ref, total_ref, *refs):
    received, (out_ref, rest_ref), scratch = refs[:4], refs[4:6], refs[6:]
    chip_finish(shape, psi_ref, links_ref, total_ref, received, scratch, out_ref)
    hand_over(shape, out_ref, rest_ref)


def chip_last_kernel(
    shape, entries, start_ref, two_ref, four_ref, start_rest, two_rest, four_rest, gathered,
    out_ref, coefficients,
):
    alpha_one, beta_one, alpha_two, scale, first_factor = scalars(gathered, entries)
    t, z_extent = shape.t, 2 * shape.z
    core = lax.axis_index("gy")

    def put(k, z, start, two, four):
        remain = two - alpha_one * start
        result = (four - alpha_one * two - alpha_two * remain) * scale - first_factor * start
        out_ref[pl.ds(k * t * z_extent + z, t, stride=z_extent), :] = result[0:t]

    for k in range(24):
        for z in range(shape.z):
            rows = y_part(shape, k, z, core)
            own = (ref[rows, :] for ref in (start_ref, two_ref, four_ref))
            put(k, core * shape.z + z, *own)
            rows = rest_rows(shape, k, z)
            other = (ref[rows, :] for ref in (start_rest, two_rest, four_rest))
            put(k, (1 - core) * shape.z + z, *other)
    coefficients[0] = alpha_one[0, 0]
    coefficients[1] = beta_one[0, 0]
    coefficients[2] = alpha_two[0, 0]


def chip_shards(source, gauge_links):
    devices_all = lax.axis_size("ta") * lax.axis_size("gz") * 2
    entries = float(source.size * devices_all)
    z_extent = source.shape[4]
    shape = ChipShape(source.shape[3], z_extent // 2, source.shape[5])
    t, rows, lanes = shape.t, shape.rows, shape.lanes
    vmem = pl.BlockSpec(memory_space=pltpu.VMEM)
    smem = pl.BlockSpec(memory_space=pltpu.SMEM)

    def held(*dims):
        return pltpu.VMEM(dims, jnp.float32)

    field = held(24 * shape.parts * rows, lanes)
    links_field = held(72 * shape.parts * rows, lanes)
    z_face, t_face = held(shape.z_rows, lanes), held(shape.t_rows, lanes)
    messages = (z_face, t_face, z_face, t_face)
    z_faces = (z_face, z_face)

    def call(kernel, name, flops, out_shape, operands, **options):
        in_spec = options.pop("in_spec", vmem)
        out_specs = options.pop("out_specs", jax.tree.map(lambda _: vmem, out_shape))
        return pl.pallas_call(
            kernel,
            name=name,
            out_shape=out_shape,
            in_specs=[in_spec] * len(operands),
            out_specs=out_specs,
            compiler_params=pltpu.CompilerParams(vmem_limit_bytes=8 << 20),
            cost_estimate=pl.CostEstimate(flops=flops, bytes_accessed=1 << 20, transcendentals=0),
            **options,
        )(*operands)

    def exchanged(sent):
        z_second, t_second, z_first, t_first = sent
        z_ring = ("gz", "gy")
        return (
            swap(z_second, z_ring, True), swap(t_second, "ta", True),
            swap(z_first, z_ring, False), swap(t_first, "ta", False),
        )

    sites = t * z_extent * lanes
    rows_in = t * z_extent
    own = (source.reshape(24 * rows_in, lanes), gauge_links.reshape(72 * rows_in, lanes))
    other = tuple(swap(value, "gy", False) for value in own)
    rest = held(24 * shape.z * rows, lanes)
    psi, links, start_rest = call(
        functools.partial(chip_own_kernel, shape), "own", 200 * sites, (field, links_field, rest),
        [pltpu.with_memory_space_constraint(value, pltpu.HBM) for value in own],
        scratch_shapes=(
            held(24 * rows_in, lanes), held(72 * rows_in, lanes), pltpu.SemaphoreType.DMA((5,)),
        ),
        in_spec=pl.BlockSpec(memory_space=pltpu.HBM),
    )
    psi, links, *sent = call(
        functools.partial(chip_prep_kernel, shape), "prep", 400 * sites,
        (field, links_field, *messages), (*other, psi, links),
        input_output_aliases={2: 0, 3: 1},
    )
    powers = [psi]
    for step in range(3):
        halo = exchanged(sent)
        inner = functools.partial(chip_inner_kernel, shape)
        total = call(inner, "inner", 1000 * sites, field, (psi, links))
        hands_over = step == 1
        psi, *sent = call(
            functools.partial(chip_mid_kernel, shape, hands_over), "mid", 600 * sites,
            (field, *messages, rest) if hands_over else (field, *messages),
            (psi, links, total, *halo), scratch_shapes=z_faces,
        )
        powers.append(psi)
        if hands_over:
            two_rest = swap(sent.pop(), "gy", False)
    halo = exchanged(sent)
    total, copies = call(
        functools.partial(chip_inner_sums_kernel, shape), "inner_sums", 1400 * sites,
        (field, held(devices_all, 8, lanes)), (psi, links, *powers[:3]),
    )
    gathered = from_everyone(copies)
    four, four_rest = call(
        functools.partial(chip_finish_kernel, shape), "finish", 400 * sites, (field, rest),
        (psi, links, total, *halo), scratch_shapes=z_faces,
    )
    four_rest = swap(four_rest, "gy", False)
    residual, coefficients = call(
        functools.partial(chip_last_kernel, shape, entries), "last", 100 * sites,
        (
            jax.ShapeDtypeStruct((24 * rows_in, lanes), jnp.float32),
            jax.ShapeDtypeStruct((3,), jnp.float32),
        ),
        (powers[0], powers[2], four, start_rest, two_rest, four_rest, gathered),
        out_specs=(vmem, smem),
    )
    return (residual.reshape(source.shape), coefficients)


def solution(mesh):
    placed = (P(None, None, None, "ta", "gz", "gy"), P(None, None, None, None, "ta", "gz", "gy"))
    return jax.shard_map(
        chip_shards if mesh.shape["gy"] == 2 else shards,
        mesh=mesh,
        in_specs=placed,
        out_specs=(P(None, None, None, "ta", "gz", "gy"), P()),
        check_vma=False,
    )
```

```python
import functools
import math

import jax
import jax.numpy as jnp
from jax import lax
from jax.experimental import pallas as pl
from jax.experimental.pallas import tpu as pltpu
from jax.sharding import PartitionSpec as P

X = 32

hop_kappa = 0.19
epsilon = 1e-06
spin_table = (
    ((1, 0), (-1j, -1j)),
    ((1, 0), (-1, 1)),
    ((0, 1), (-1j, 1j)),
    ((0, 1), (1, 1)),
)
SPIN_COLOUR = [(spin, colour) for spin in range(2) for colour in range(3)]


def add_phased(left, phase, right):
    phase = complex(phase)
    if phase == 1:
        return (left[0] + right[0], left[1] + right[1])
    if phase == -1:
        return (left[0] - right[0], left[1] - right[1])
    if phase == 1j:
        return (left[0] - right[1], left[1] + right[0])
    return (left[0] + right[1], left[1] - right[0])


def project(psi, direction, parity):
    order, phases = spin_table[direction]
    return {
        (s, c): add_phased(psi[s, c], parity * phases[s], psi[2 + order[s], c])
        for s, c in SPIN_COLOUR
    }


def add_rebuilt(total, half, direction, parity):
    order, phases = spin_table[direction]
    for s, c in SPIN_COLOUR:
        total[s, c] = add_phased(total[s, c], 1, half[s, c])
        row = order[s]
        phase = parity * complex(phases[row]).conjugate()
        total[2 + s, c] = add_phased(total[2 + s, c], phase, half[row, c])


def mul_link(links, direction, z, half):
    out = {}
    for row in range(3):
        for s in range(2):
            real, imag = None, None
            for col in range(3):
                u_real, u_imag = links[direction, row, col, z]
                h_real, h_imag = half[s, col]
                term_real = u_real * h_real - u_imag * h_imag
                term_imag = u_real * h_imag + u_imag * h_real
                real = term_real if real is None else real + term_real
                imag = term_imag if imag is None else imag + term_imag
            out[s, row] = (real, imag)
    return out


def mul_link_dag(links, direction, z, half):
    out = {}
    for row in range(3):
        for s in range(2):
            real, imag = None, None
            for col in range(3):
                u_real, u_imag = links[direction, col, row, z]
                h_real, h_imag = half[s, col]
                term_real = u_real * h_real + u_imag * h_imag
                term_imag = u_real * h_imag - u_imag * h_real
                real = term_real if real is None else real + term_real
                imag = term_imag if imag is None else imag + term_imag
            out[s, row] = (real, imag)
    return out


def mapped(function, *halves):
    return {
        key: tuple(function(*(half[key][part] for half in halves)) for part in range(2))
        for key in SPIN_COLOUR
    }


class Links:
    def __init__(self, ref):
        self.ref = ref

    def __getitem__(self, index):
        direction, row, col, z = index
        first = ((direction * 3 + row) * 3 + col) * 2
        return (self.ref[first, z], self.ref[first + 1, z])


def load_psi(ref, z):
    return {
        (s, c): (ref[(s * 3 + c) * 2, z], ref[(s * 3 + c) * 2 + 1, z])
        for s in range(4)
        for c in range(3)
    }


def load_half(ref, z):
    return {
        (s, c): (ref[(s * 3 + c) * 2, z], ref[(s * 3 + c) * 2 + 1, z]) for s, c in SPIN_COLOUR
    }


def store_half(ref, z, half):
    for (s, c), pair in half.items():
        for part in range(2):
            ref[(s * 3 + c) * 2 + part, z] = pair[part]


class Shape:
    def __init__(self, t_extent, z_extent, lanes):
        self.t = t_extent
        self.z = z_extent
        self.rows = -(-t_extent // 8) * 8
        self.lanes = lanes

    def row(self):
        return lax.broadcasted_iota(jnp.int32, (self.rows, self.lanes), 0)

    def lane(self):
        return lax.broadcasted_iota(jnp.int32, (self.rows, self.lanes), 1)


def is_even(axis):
    return jnp.bitwise_and(lax.axis_index(axis), 1) == 0


def either(choice, first, second):
    return jnp.where(choice, first, second)


def emit_messages(shape, psi_ref, links, refs):
    z_second, t_second, z_first, t_first, y_msg, carried_y, carried_t = refs
    t_even, z_even = is_even("ta"), is_even("gz")
    lane = shape.lane()
    last_z, last_t = shape.z - 1, shape.t - 1
    for z in range(shape.z):
        psi = load_psi(psi_ref, z)
        minus = project(psi, 3, -1)
        carried = mul_link_dag(links, 3, z, project(psi, 3, 1))
        store_half(carried_t, z, carried)
        for s, c in SPIN_COLOUR:
            for part in range(2):
                at = ((s * 3 + c) * 2 + part) * shape.z + z
                down = minus[s, c][part][0:1]
                up = carried[s, c][part][last_t : last_t + 1]
                t_first[at : at + 1] = either(t_even, up, down)
                t_second[at : at + 1] = either(t_even, down, up)
        minus = project(psi, 1, -1)
        carried = mul_link_dag(links, 1, z, project(psi, 1, 1))
        store_half(carried_y, z, carried)
        store_half(
            y_msg,
            z,
            mapped(lambda low, high: jnp.where(lane < X, low, high), minus, carried),
        )
    minus = project(load_psi(psi_ref, 0), 2, -1)
    carried = mul_link_dag(links, 2, last_z, project(load_psi(psi_ref, last_z), 2, 1))
    for s, c in SPIN_COLOUR:
        for part in range(2):
            at = ((s * 3 + c) * 2 + part) * shape.t
            down, up = minus[s, c][part][0 : shape.t], carried[s, c][part][0 : shape.t]
            z_first[at : at + shape.t] = either(z_even, up, down)
            z_second[at : at + shape.t] = either(z_even, down, up)


def prep_kernel(shape, source_hbm, links_hbm, psi_ref, links_ref, *refs):
    messages, (source_ref, links_in, arrived) = refs[:-3], refs[-3:]
    t, z_extent = shape.t, shape.z
    part = 18 * t * z_extent
    copies = [pltpu.make_async_copy(source_hbm, source_ref, arrived.at[4])]
    for direction in (3, 2, 1, 0):
        rows = pl.ds(direction * part, part)
        copies.append(
            pltpu.make_async_copy(links_hbm.at[rows], links_in.at[rows], arrived.at[direction])
        )
    for copy in copies:
        copy.start()
    if shape.rows != t:
        links_ref[...] = jnp.zeros_like(links_ref)
        psi_ref[...] = jnp.zeros_like(psi_ref)
    last = lax.broadcasted_iota(jnp.int32, (t, shape.lanes), 0) == t - 1
    sign = jnp.where(lax.axis_index("ta") == lax.axis_size("ta") - 1, -1.0, 1.0)
    flip = jnp.where(last, sign, 1.0)
    copies[0].wait()
    for k in range(24):
        for z in range(z_extent):
            psi_ref[k, z, 0:t] = source_ref[pl.ds(k * t * z_extent + z, t, stride=z_extent), :]
    for direction in (3, 2, 1, 0):
        copies[4 - direction].wait()
        for k in range(18 * direction, 18 * direction + 18):
            for z in range(z_extent):
                value = links_in[pl.ds(k * t * z_extent + z, t, stride=z_extent), :]
                links_ref[k, z, 0:t] = value * flip if direction == 3 else value
    emit_messages(shape, psi_ref, Links(links_ref), messages)


def summed(shape, term):
    total = None
    for k in range(24):
        for z in range(shape.z):
            value = term(k, z)
            total = value if total is None else total + value
    return total


def over_lanes(total):
    return jnp.sum(jnp.sum(total, axis=0, keepdims=True), axis=1, keepdims=True)


def local_sums(shape, image, origin):
    square = summed(shape, lambda k, z: origin[k, z] * origin[k, z])
    mixed = over_lanes(summed(shape, lambda k, z: image[k, z] * origin[k, z]))
    whole = over_lanes(square)
    factor = jnp.where(whole > 0.0, mixed / jnp.where(whole > 0.0, whole, 1.0), 0.0)
    spread = jnp.broadcast_to(factor, (shape.rows, shape.lanes))
    rest_square, rest_mixed = None, None
    for k in range(24):
        for z in range(shape.z):
            start = origin[k, z]
            rest = image[k, z] - spread * start
            terms = rest * rest, rest * start
            if rest_square is None:
                rest_square, rest_mixed = terms
            else:
                rest_square, rest_mixed = rest_square + terms[0], rest_mixed + terms[1]
    return [factor, *(over_lanes(value) for value in (square, rest_square, rest_mixed))]


def inner_kernel(shape, psi_ref, links_ref, total_ref):
    links = Links(links_ref)
    x = shape.lane() % X
    lanes = shape.lanes
    at_end, at_start = x == X - 1, x == 0

    def ahead(value):
        return jnp.where(
            at_end, pltpu.roll(value, X - 1, 1), pltpu.roll(value, lanes - 1, 1)
        )

    def behind(value):
        return jnp.where(at_start, pltpu.roll(value, lanes - X + 1, 1), pltpu.roll(value, 1, 1))

    for z in range(shape.z):
        psi = load_psi(psi_ref, z)
        zero = jnp.zeros((shape.rows, lanes), jnp.float32)
        total = {key: (zero, zero) for key in psi}
        half = mapped(ahead, project(psi, 0, -1))
        add_rebuilt(total, mul_link(links, 0, z, half), 0, -1)
        half = mapped(behind, mul_link_dag(links, 0, z, project(psi, 0, 1)))
        add_rebuilt(total, half, 0, 1)
        if z + 1 < shape.z:
            half = project(load_psi(psi_ref, z + 1), 2, -1)
            add_rebuilt(total, mul_link(links, 2, z, half), 2, -1)
        if z > 0:
            half = project(load_psi(psi_ref, z - 1), 2, 1)
            add_rebuilt(total, mul_link_dag(links, 2, z - 1, half), 2, 1)
        for (s, c), pair in total.items():
            for part in range(2):
                total_ref[(s * 3 + c) * 2 + part, z] = pair[part]


def add_y_hops(shape, z, psi, total, links, carried_y, y_halo):
    lane, lanes = shape.lane(), shape.lanes
    received = load_half(y_halo, z)
    half = mapped(
        lambda own, other: pltpu.roll(jnp.where(lane < X, other, own), lanes - X, 1),
        project(psi, 1, -1),
        received,
    )
    add_rebuilt(total, mul_link(links, 1, z, half), 1, -1)
    half = mapped(
        lambda own, other: pltpu.roll(jnp.where(lane >= lanes - X, other, own), X, 1),
        load_half(carried_y, z),
        received,
    )
    add_rebuilt(total, half, 1, 1)


def finish_hops(
    shape, psi_ref, links, total_ref, carried_y, carried_t, halo, store
):
    z_second, t_second, z_first, t_first, y_msg = halo
    t_even, z_even = is_even("ta"), is_even("gz")
    row = shape.row()
    lanes, rows, t = shape.lanes, shape.rows, shape.t
    last_z = shape.z - 1

    for z in range(shape.z):
        psi = load_psi(psi_ref, z)
        total = load_psi(total_ref, z)

        def rim_rows(from_even, from_odd):
            half = {}
            for s, c in SPIN_COLOUR:
                ats = [((s * 3 + c) * 2 + part) * shape.z + z for part in range(2)]
                half[s, c] = tuple(
                    jnp.broadcast_to(
                        either(t_even, from_even[at : at + 1], from_odd[at : at + 1]),
                        (rows, lanes),
                    )
                    for at in ats
                )
            return half

        def rim_plane(from_even, from_odd):
            half = {}
            for s, c in SPIN_COLOUR:
                pair = []
                for part in range(2):
                    at = ((s * 3 + c) * 2 + part) * t
                    plane = either(z_even, from_even[at : at + t], from_odd[at : at + t])
                    if rows != t:
                        pad = jnp.zeros((rows - t, lanes), jnp.float32)
                        plane = jnp.concatenate([plane, pad], axis=0)
                    pair.append(plane)
                half[s, c] = tuple(pair)
            return half

        if y_msg is not None:
            add_y_hops(shape, z, psi, total, links, carried_y, y_msg)
        if z == last_z:
            add_rebuilt(total, mul_link(links, 2, z, rim_plane(z_first, z_second)), 2, -1)
        if z == 0:
            add_rebuilt(total, rim_plane(z_second, z_first), 2, 1)
        half = mapped(
            lambda own, other: jnp.where(row == t - 1, other, pltpu.roll(own, rows - 1, 0)),
            project(psi, 3, -1),
            rim_rows(t_first, t_second),
        )
        add_rebuilt(total, mul_link(links, 3, z, half), 3, -1)
        half = mapped(
            lambda own, other: jnp.where(row == 0, other, pltpu.roll(own, 1, 0)),
            load_half(carried_t, z),
            rim_rows(t_second, t_first),
        )
        add_rebuilt(total, half, 3, 1)
        for (s, c), pair in total.items():
            for part in range(2):
                value = psi[s, c][part] - hop_kappa * pair[part]
                value = value if s < 2 else -value
                if rows != t:
                    value = jnp.where(row < t, value, 0.0)
                store((s * 3 + c) * 2 + part, z, value)


def mid_kernel(shape, psi_ref, links_ref, total_ref, carried_y, carried_t, *refs):
    halo, out_ref, messages = refs[:5], refs[5], refs[6:]
    links = Links(links_ref)

    def store(k, z, value):
        out_ref[k, z] = value

    finish_hops(
        shape, psi_ref, links, total_ref, carried_y, carried_t, halo, store
    )
    emit_messages(shape, out_ref, links, messages)


def sums_row(shape, two, start, three, one):
    sums = local_sums(shape, two, start) + local_sums(shape, three, one)
    lane = lax.broadcasted_iota(jnp.int32, (1, shape.lanes), 1)
    row = jnp.zeros((1, shape.lanes), jnp.float32)
    for k, value in enumerate(sums):
        row = jnp.where(lane == k, value, row)
    return row


def inner_sums_kernel(
    shape, psi_ref, links_ref, start_ref, one_ref, two_ref, total_ref, copies_ref
):
    row = sums_row(shape, two_ref, start_ref, psi_ref, one_ref)
    copies_ref[...] = jnp.broadcast_to(row[None], copies_ref.shape)
    inner_kernel(shape, psi_ref, links_ref, total_ref)


def finish_kernel(shape, psi_ref, links_ref, total_ref, carried_y, carried_t, *refs):
    halo, out_ref = refs[:5], refs[5]

    def store(k, z, value):
        out_ref[k, z] = value

    finish_hops(
        shape, psi_ref, Links(links_ref), total_ref, carried_y, carried_t, halo, store
    )


def scalars(gathered, entries):
    table = gathered[:, 0, :]
    columns = [table[:, k : k + 1] for k in range(8)]
    factor_two, start_square, two_square, two_mixed = columns[:4]
    factor_three, one_square, three_square, three_mixed = columns[4:]

    def over_devices(column):
        return jnp.sum(column, axis=0, keepdims=True)

    norm_square = over_devices(start_square) / entries + epsilon
    alpha_one = over_devices(one_square) / entries / norm_square
    gap = alpha_one - factor_two
    remain_square = over_devices(two_square - gap * (2.0 * two_mixed - gap * start_square)) / entries
    overlap = over_devices(two_mixed - gap * start_square) / entries
    gap = alpha_one - factor_three
    image_square = over_devices(three_square - gap * (2.0 * three_mixed - gap * one_square)) / entries
    norm = jnp.sqrt(norm_square)
    beta_one = jnp.sqrt(remain_square / norm_square + epsilon)
    overlap = overlap / (norm_square * beta_one)
    alpha_two = image_square / (norm_square * beta_one * beta_one) - beta_one * overlap
    scale = 1.0 / (norm * beta_one)
    return alpha_one, beta_one, alpha_two, scale, beta_one / norm


def last_kernel(
    shape, entries, start_ref, two_ref, four_ref, gathered, out_ref, coefficients
):
    alpha_one, beta_one, alpha_two, scale, first_factor = scalars(gathered, entries)
    t, z_extent = shape.t, shape.z
    for k in range(24):
        for z in range(z_extent):
            two, start = two_ref[k, z], start_ref[k, z]
            remain = two - alpha_one * start
            result = (four_ref[k, z] - alpha_one * two - alpha_two * remain) * scale
            result = result - first_factor * start
            out_ref[pl.ds(k * t * z_extent + z, t, stride=z_extent), :] = result[0:t]
    coefficients[0] = alpha_one[0, 0]
    coefficients[1] = beta_one[0, 0]
    coefficients[2] = alpha_two[0, 0]


def swap(value, axis, second):
    count = math.prod(lax.axis_size(name) for name in (axis if isinstance(axis, tuple) else (axis,)))
    pairs = []
    for low in range(1 if second else 0, count, 2):
        high = (low + 1) % count
        pairs += [(low, high), (high, low)]
    return lax.ppermute(value, axis, pairs)


def exchange(messages, lanes):
    z_second, t_second, z_first, t_first, y_msg = messages
    halo = (
        swap(z_second, "gz", True),
        swap(t_second, "ta", True),
        swap(z_first, "gz", False),
        swap(t_first, "ta", False),
    )
    y_halo = swap(y_msg, "gy", False)
    if lax.axis_size("gy") > 2:
        even = lax.axis_index("gy") % 2 == 0
        lane = lax.broadcasted_iota(jnp.int32, y_msg.shape, y_msg.ndim - 1)
        y_halo = jnp.where((lane < lanes // 2) == even, y_halo, swap(y_msg, "gy", True))
    return (*halo, y_halo)


def from_everyone(copies):
    return lax.all_to_all(copies, ("ta", "gz", "gy"), split_axis=0, concat_axis=0, tiled=True)


def shards(source, gauge_links):
    devices_all = lax.axis_size("ta") * lax.axis_size("gz") * lax.axis_size("gy")
    entries = float(source.size * devices_all)
    shape = Shape(source.shape[3], source.shape[4], source.shape[5])
    t, z, rows, lanes = shape.t, shape.z, shape.rows, shape.lanes
    vmem = pl.BlockSpec(memory_space=pltpu.VMEM)
    smem = pl.BlockSpec(memory_space=pltpu.SMEM)

    def held(*dims):
        return pltpu.VMEM(dims, jnp.float32)

    field = held(24, z, rows, lanes)
    half = held(12, z, rows, lanes)
    z_face, t_face = held(12 * t, lanes), held(12 * z, lanes)
    messages = (z_face, t_face, z_face, t_face, half, half, half)

    def call(kernel, name, flops, out_shape, operands, out_specs=None, in_spec=vmem, scratch=()):
        return pl.pallas_call(
            kernel,
            name=name,
            out_shape=out_shape,
            in_specs=[in_spec] * len(operands),
            out_specs=out_specs or jax.tree.map(lambda _: vmem, out_shape),
            scratch_shapes=scratch,
            compiler_params=pltpu.CompilerParams(vmem_limit_bytes=8 << 20),
            cost_estimate=pl.CostEstimate(flops=flops, bytes_accessed=1 << 20, transcendentals=0),
        )(*operands)

    sites = t * z * lanes
    psi, links, *sent = call(
        functools.partial(prep_kernel, shape), "prep", 400 * sites,
        (field, held(72, z, rows, lanes), *messages),
        (
            pltpu.with_memory_space_constraint(source.reshape(24 * t * z, lanes), pltpu.HBM),
            pltpu.with_memory_space_constraint(gauge_links.reshape(72 * t * z, lanes), pltpu.HBM),
        ),
        in_spec=pl.BlockSpec(memory_space=pltpu.HBM),
        scratch=(
            held(24 * t * z, lanes), held(72 * t * z, lanes), pltpu.SemaphoreType.DMA((5,)),
        ),
    )
    powers = [psi]
    for step in range(3):
        halo = exchange(sent[:5], lanes)
        inner = functools.partial(inner_kernel, shape)
        total = call(inner, "inner", 700 * sites, field, (psi, links))
        psi, *sent = call(
            functools.partial(mid_kernel, shape), "mid", 1000 * sites,
            (field, *messages), (psi, links, total, *sent[5:], *halo),
        )
        powers.append(psi)
    halo = exchange(sent[:5], lanes)
    total, copies = call(
        functools.partial(inner_sums_kernel, shape), "inner_sums", 1100 * sites,
        (field, held(devices_all, 1, lanes)), (psi, links, *powers[:3]),
    )
    gathered = from_everyone(copies)
    four = call(
        functools.partial(finish_kernel, shape), "finish", 700 * sites, field,
        (psi, links, total, *sent[5:], *halo),
    )
    residual, coefficients = call(
        functools.partial(last_kernel, shape, entries), "last", 100 * sites,
        (
            jax.ShapeDtypeStruct((24 * t * z, lanes), jnp.float32),
            jax.ShapeDtypeStruct((3,), jnp.float32),
        ),
        (powers[0], powers[2], four, gathered), (vmem, smem),
    )
    return (residual.reshape(source.shape), coefficients)


class ChipShape(Shape):
    def __init__(self, t_extent, z_extent, lanes):
        super().__init__(t_extent, z_extent, lanes)
        self.parts = 2 * z_extent
        self.z_rows = 24 * t_extent
        self.t_rows = 12 * self.parts

    def block(self, k, part):
        first = (k * self.parts + part) * self.rows
        return pl.ds(first, self.rows)

    def edge(self, k, row):
        return pl.ds(k * self.parts * self.rows + row, self.parts, stride=self.rows)


class ChipLinks:
    def __init__(self, shape, ref, row=None):
        self.shape, self.ref, self.row = shape, ref, row

    def __getitem__(self, index):
        direction, row, col, part = index
        first = ((direction * 3 + row) * 3 + col) * 2
        if self.row is None:
            return tuple(self.ref[self.shape.block(first + n, part), :] for n in range(2))
        return tuple(self.ref[self.shape.edge(first + n, self.row), :] for n in range(2))


def components(spins):
    return [(s, c, part, (s * 3 + c) * 2 + part) for s in range(spins) for c in range(3) for part in range(2)]


def gathered_pairs(spins, value):
    out = {}
    for s in range(spins):
        for c in range(3):
            out[s, c] = tuple(value((s * 3 + c) * 2 + part) for part in range(2))
    return out


def chip_psi(shape, ref, part):
    return gathered_pairs(4, lambda k: ref[shape.block(k, part), :])


def chip_edge(shape, ref, row):
    return gathered_pairs(4, lambda k: ref[shape.edge(k, row), :])


def chip_messages(shape, psi_ref, links_ref, z_second, t_second, z_first, t_first):
    t, last = shape.t, shape.t - 1
    even = is_even("ta")
    minus = project(chip_edge(shape, psi_ref, 0), 3, -1)
    half = project(chip_edge(shape, psi_ref, last), 3, 1)
    carried = mul_link_dag(ChipLinks(shape, links_ref, last), 3, 0, half)
    for s, c, part, k in components(2):
        rows = pl.ds(k * shape.parts, shape.parts)
        up, down = carried[s, c][part], minus[s, c][part]
        t_first[rows, :] = either(even, up, down)
        t_second[rows, :] = either(even, down, up)
    even = is_even("gy")
    links = ChipLinks(shape, links_ref)
    for y_half in range(2):
        minus = project(chip_psi(shape, psi_ref, y_half), 2, -1)
        part_last = shape.parts - 2 + y_half
        half = project(chip_psi(shape, psi_ref, part_last), 2, 1)
        carried = mul_link_dag(links, 2, part_last, half)
        for s, c, part, k in components(2):
            rows = pl.ds((k * 2 + y_half) * t, t)
            up, down = carried[s, c][part][0:t], minus[s, c][part][0:t]
            z_first[rows, :] = either(even, up, down)
            z_second[rows, :] = either(even, down, up)


def chip_bring(shape, y_half, source_ref, links_in, psi_ref, links_ref, arrived):
    t, z_extent = shape.t, 2 * shape.z
    first_plane = lax.axis_index("gy") * shape.z
    last = lax.broadcasted_iota(jnp.int32, (t, shape.lanes), 0) == t - 1
    sign = jnp.where(lax.axis_index("ta") == lax.axis_size("ta") - 1, -1.0, 1.0)
    flip = jnp.where(last, sign, 1.0)

    def bring(in_ref, out_ref, k, z, factor=None):
        value = in_ref[pl.ds(k * t * z_extent + first_plane + z, t, stride=z_extent), :]
        if factor is not None:
            value = value * factor
        at = (k * shape.parts + 2 * z + y_half) * shape.rows
        out_ref[pl.ds(pl.multiple_of(at, 8), t), :] = value

    arrived(4)
    for z in range(shape.z):
        for k in range(24):
            bring(source_ref, psi_ref, k, z)
    for direction in (3, 2, 1, 0):
        arrived(direction)
        for z in range(shape.z):
            for k in range(18 * direction, 18 * direction + 18):
                bring(links_in, links_ref, k, z, flip if direction == 3 else None)


def chip_own_kernel(
    shape, source_hbm, links_hbm, psi_ref, links_ref, rest_ref, source_ref, links_in, semaphores
):
    part = 18 * shape.t * 2 * shape.z
    copies = {4: pltpu.make_async_copy(source_hbm, source_ref, semaphores.at[4])}
    for direction in (3, 2, 1, 0):
        rows = pl.ds(direction * part, part)
        copies[direction] = pltpu.make_async_copy(
            links_hbm.at[rows], links_in.at[rows], semaphores.at[direction]
        )
    for copy in copies.values():
        copy.start()
    if shape.rows != shape.t:
        links_ref[...] = jnp.zeros_like(links_ref)
        psi_ref[...] = jnp.zeros_like(psi_ref)
    chip_bring(
        shape, lax.axis_index("gy"), source_ref, links_in, psi_ref, links_ref,
        lambda n: copies[n].wait(),
    )
    t, z_extent = shape.t, 2 * shape.z
    first_plane = (1 - lax.axis_index("gy")) * shape.z
    if shape.rows != t:
        rest_ref[...] = jnp.zeros_like(rest_ref)
    for k in range(24):
        for z in range(shape.z):
            value = source_ref[pl.ds(k * t * z_extent + first_plane + z, t, stride=z_extent), :]
            rest_ref[pl.ds((k * shape.z + z) * shape.rows, t), :] = value


def chip_prep_kernel(
    shape, source_ref, links_in, psi_in, links_held, psi_ref, links_ref, *messages
):
    chip_bring(
        shape, 1 - lax.axis_index("gy"), source_ref, links_in, psi_ref, links_ref, lambda n: None
    )
    chip_messages(shape, psi_ref, links_ref, *messages)


def chip_inner_kernel(shape, psi_ref, links_ref, total_ref):
    links = ChipLinks(shape, links_ref)
    lane, row = shape.lane(), shape.row()
    x = lane % X
    lanes, rows, t = shape.lanes, shape.rows, shape.t
    at_end, at_start = x == X - 1, x == 0
    inside_ahead = row < t - 1
    inside_behind = jnp.logical_and(row > 0, row < t)

    def x_ahead(value):
        return jnp.where(
            at_end, pltpu.roll(value, X - 1, 1), pltpu.roll(value, lanes - 1, 1)
        )

    def x_behind(value):
        return jnp.where(at_start, pltpu.roll(value, lanes - X + 1, 1), pltpu.roll(value, 1, 1))

    def t_ahead(value):
        return jnp.where(inside_ahead, pltpu.roll(value, rows - 1, 0), 0.0)

    def t_behind(value):
        return jnp.where(inside_behind, pltpu.roll(value, 1, 0), 0.0)

    for z in range(shape.z):
        for part in (2 * z, 2 * z + 1):
            psi = chip_psi(shape, psi_ref, part)
            zero = jnp.zeros((rows, lanes), jnp.float32)
            total = {key: (zero, zero) for key in psi}
            half = mapped(x_ahead, project(psi, 0, -1))
            add_rebuilt(total, mul_link(links, 0, part, half), 0, -1)
            half = mapped(x_behind, mul_link_dag(links, 0, part, project(psi, 0, 1)))
            add_rebuilt(total, half, 0, 1)
            half = mapped(t_ahead, project(psi, 3, -1))
            add_rebuilt(total, mul_link(links, 3, part, half), 3, -1)
            half = mapped(t_behind, mul_link_dag(links, 3, part, project(psi, 3, 1)))
            add_rebuilt(total, half, 3, 1)
            if z + 1 < shape.z:
                half = project(chip_psi(shape, psi_ref, part + 2), 2, -1)
                add_rebuilt(total, mul_link(links, 2, part, half), 2, -1)
            if z > 0:
                half = project(chip_psi(shape, psi_ref, part - 2), 2, 1)
                add_rebuilt(total, mul_link_dag(links, 2, part - 2, half), 2, 1)
            for s, c, n, k in components(4):
                total_ref[shape.block(k, part), :] = total[s, c][n]
        pair = (2 * z, 2 * z + 1)
        minus, carried = [], []
        for part in pair:
            psi = chip_psi(shape, psi_ref, part)
            minus.append(mapped(lambda v: pltpu.roll(v, lanes - X, 1), project(psi, 1, -1)))
            half = mul_link_dag(links, 1, part, project(psi, 1, 1))
            carried.append(mapped(lambda v: pltpu.roll(v, X, 1), half))
        for own, part in enumerate(pair):
            total = chip_psi(shape, total_ref, part)
            half = mapped(
                lambda a, b: jnp.where(lane >= lanes - X, b, a), minus[own], minus[1 - own]
            )
            add_rebuilt(total, mul_link(links, 1, part, half), 1, -1)
            half = mapped(lambda a, b: jnp.where(lane < X, b, a), carried[own], carried[1 - own])
            add_rebuilt(total, half, 1, 1)
            for s, c, n, k in components(4):
                total_ref[shape.block(k, part), :] = total[s, c][n]


def chip_finish(shape, psi_ref, links_ref, total_ref, received, scratch, out_ref):
    z_second, t_second, z_first, t_first = received
    z_down, z_up = scratch
    t_even, z_even = is_even("ta"), is_even("gy")
    t, rows, lanes, parts = shape.t, shape.rows, shape.lanes, shape.parts
    z_down[...] = either(z_even, z_first[...], z_second[...])
    z_up[...] = either(z_even, z_second[...], z_first[...])
    links = ChipLinks(shape, links_ref)

    def plane(ref, y_half):
        def value(k):
            face = ref[pl.ds((k * 2 + y_half) * t, t), :]
            if rows != t:
                pad = jnp.zeros((rows - t, lanes), jnp.float32)
                face = jnp.concatenate([face, pad], axis=0)
            return face

        return gathered_pairs(2, value)

    for part in range(parts):
        total = chip_psi(shape, total_ref, part)
        if part >= parts - 2:
            half = mul_link(links, 2, part, plane(z_down, part - parts + 2))
            add_rebuilt(total, half, 2, -1)
        if part < 2:
            add_rebuilt(total, plane(z_up, part), 2, 1)
        for s, c, n, k in components(4):
            value = psi_ref[shape.block(k, part), :] - hop_kappa * total[s, c][n]
            out_ref[shape.block(k, part), :] = value if s < 2 else -value

    def t_half(from_even, from_odd):
        def value(k):
            at = pl.ds(k * parts, parts)
            return either(t_even, from_even[at, :], from_odd[at, :])

        return gathered_pairs(2, value)

    down = mul_link(ChipLinks(shape, links_ref, t - 1), 3, 0, t_half(t_first, t_second))
    up = t_half(t_second, t_first)
    zero = jnp.zeros((parts, lanes), jnp.float32)
    for half, parity, row in ((down, -1, t - 1), (up, 1, 0)):
        total = {(s, c): (zero, zero) for s in range(4) for c in range(3)}
        add_rebuilt(total, half, 3, parity)
        for s, c, n, k in components(4):
            at = shape.edge(k, row)
            value = hop_kappa * total[s, c][n]
            out_ref[at, :] = out_ref[at, :] - (value if s < 2 else -value)


def chip_mid_kernel(shape, hands_over, psi_ref, links_ref, total_ref, *refs):
    received, out_ref, messages, refs = refs[:4], refs[4], refs[5:9], refs[9:]
    chip_finish(shape, psi_ref, links_ref, total_ref, received, refs[-2:], out_ref)
    chip_messages(shape, out_ref, links_ref, *messages)
    if hands_over:
        hand_over(shape, out_ref, refs[0])


def chip_inner_sums_kernel(
    shape, psi_ref, links_ref, start_ref, one_ref, two_ref, total_ref, copies_ref
):
    class View:
        def __init__(self, ref):
            self.ref = ref

        def __getitem__(self, index):
            return self.ref[shape.block(*index), :]

    wide = ChipShape(shape.t, shape.z, shape.lanes)
    wide.z = shape.parts
    row = sums_row(wide, View(two_ref), View(start_ref), View(psi_ref), View(one_ref))
    copies_ref[...] = jnp.broadcast_to(row[None], copies_ref.shape)
    chip_inner_kernel(shape, psi_ref, links_ref, total_ref)


def y_part(shape, k, z, y_half):
    return pl.ds(pl.multiple_of((k * shape.parts + 2 * z + y_half) * shape.rows, 8), shape.rows)


def rest_rows(shape, k, z):
    return pl.ds((k * shape.z + z) * shape.rows, shape.rows)


def hand_over(shape, ref, rest_ref):
    y_half = 1 - lax.axis_index("gy")
    for k in range(24):
        for z in range(shape.z):
            rest_ref[rest_rows(shape, k, z), :] = ref[y_part(shape, k, z, y_half), :]


def chip_finish_kernel(shape, psi_ref, links_ref, total_ref, *refs):
    received, (out_ref, rest_ref), scratch = refs[:4], refs[4:6], refs[6:]
    chip_finish(shape, psi_ref, links_ref, total_ref, received, scratch, out_ref)
    hand_over(shape, out_ref, rest_ref)


def chip_last_kernel(
    shape, entries, start_ref, two_ref, four_ref, start_rest, two_rest, four_rest, gathered,
    out_ref, coefficients,
):
    alpha_one, beta_one, alpha_two, scale, first_factor = scalars(gathered, entries)
    t, z_extent = shape.t, 2 * shape.z
    core = lax.axis_index("gy")

    def put(k, z, start, two, four):
        remain = two - alpha_one * start
        result = (four - alpha_one * two - alpha_two * remain) * scale - first_factor * start
        out_ref[pl.ds(k * t * z_extent + z, t, stride=z_extent), :] = result[0:t]

    for k in range(24):
        for z in range(shape.z):
            rows = y_part(shape, k, z, core)
            own = (ref[rows, :] for ref in (start_ref, two_ref, four_ref))
            put(k, core * shape.z + z, *own)
            rows = rest_rows(shape, k, z)
            other = (ref[rows, :] for ref in (start_rest, two_rest, four_rest))
            put(k, (1 - core) * shape.z + z, *other)
    coefficients[0] = alpha_one[0, 0]
    coefficients[1] = beta_one[0, 0]
    coefficients[2] = alpha_two[0, 0]


def chip_shards(source, gauge_links):
    devices_all = lax.axis_size("ta") * lax.axis_size("gz") * 2
    entries = float(source.size * devices_all)
    z_extent = source.shape[4]
    shape = ChipShape(source.shape[3], z_extent // 2, source.shape[5])
    t, rows, lanes = shape.t, shape.rows, shape.lanes
    vmem = pl.BlockSpec(memory_space=pltpu.VMEM)
    smem = pl.BlockSpec(memory_space=pltpu.SMEM)

    def held(*dims):
        return pltpu.VMEM(dims, jnp.float32)

    field = held(24 * shape.parts * rows, lanes)
    links_field = held(72 * shape.parts * rows, lanes)
    z_face, t_face = held(shape.z_rows, lanes), held(shape.t_rows, lanes)
    messages = (z_face, t_face, z_face, t_face)
    z_faces = (z_face, z_face)

    def call(kernel, name, flops, out_shape, operands, **options):
        in_spec = options.pop("in_spec", vmem)
        out_specs = options.pop("out_specs", jax.tree.map(lambda _: vmem, out_shape))
        return pl.pallas_call(
            kernel,
            name=name,
            out_shape=out_shape,
            in_specs=[in_spec] * len(operands),
            out_specs=out_specs,
            compiler_params=pltpu.CompilerParams(vmem_limit_bytes=8 << 20),
            cost_estimate=pl.CostEstimate(flops=flops, bytes_accessed=1 << 20, transcendentals=0),
            **options,
        )(*operands)

    def exchanged(sent):
        z_second, t_second, z_first, t_first = sent
        z_ring = ("gz", "gy")
        return (
            swap(z_second, z_ring, True), swap(t_second, "ta", True),
            swap(z_first, z_ring, False), swap(t_first, "ta", False),
        )

    sites = t * z_extent * lanes
    rows_in = t * z_extent
    own = (source.reshape(24 * rows_in, lanes), gauge_links.reshape(72 * rows_in, lanes))
    other = tuple(swap(value, "gy", False) for value in own)
    rest = held(24 * shape.z * rows, lanes)
    psi, links, start_rest = call(
        functools.partial(chip_own_kernel, shape), "own", 200 * sites, (field, links_field, rest),
        [pltpu.with_memory_space_constraint(value, pltpu.HBM) for value in own],
        scratch_shapes=(
            held(24 * rows_in, lanes), held(72 * rows_in, lanes), pltpu.SemaphoreType.DMA((5,)),
        ),
        in_spec=pl.BlockSpec(memory_space=pltpu.HBM),
    )
    psi, links, *sent = call(
        functools.partial(chip_prep_kernel, shape), "prep", 400 * sites,
        (field, links_field, *messages), (*other, psi, links),
        input_output_aliases={2: 0, 3: 1},
    )
    powers = [psi]
    for step in range(3):
        halo = exchanged(sent)
        inner = functools.partial(chip_inner_kernel, shape)
        total = call(inner, "inner", 1000 * sites, field, (psi, links))
        hands_over = step == 1
        psi, *sent = call(
            functools.partial(chip_mid_kernel, shape, hands_over), "mid", 600 * sites,
            (field, *messages, rest) if hands_over else (field, *messages),
            (psi, links, total, *halo), scratch_shapes=z_faces,
        )
        powers.append(psi)
        if hands_over:
            two_rest = swap(sent.pop(), "gy", False)
    halo = exchanged(sent)
    total, copies = call(
        functools.partial(chip_inner_sums_kernel, shape), "inner_sums", 1400 * sites,
        (field, held(devices_all, 1, lanes)), (psi, links, *powers[:3]),
    )
    gathered = from_everyone(copies)
    four, four_rest = call(
        functools.partial(chip_finish_kernel, shape), "finish", 10**11, (field, rest),
        (psi, links, total, *halo), scratch_shapes=z_faces,
    )
    four_rest = swap(four_rest, "gy", False)
    residual, coefficients = call(
        functools.partial(chip_last_kernel, shape, entries), "last", 100 * sites,
        (
            jax.ShapeDtypeStruct((24 * rows_in, lanes), jnp.float32),
            jax.ShapeDtypeStruct((3,), jnp.float32),
        ),
        (powers[0], powers[2], four, start_rest, two_rest, four_rest, gathered),
        out_specs=(vmem, smem),
    )
    return (residual.reshape(source.shape), coefficients)


def solution(mesh):
    placed = (P(None, None, None, "ta", "gz", "gy"), P(None, None, None, None, "ta", "gz", "gy"))
    return jax.shard_map(
        chip_shards if mesh.shape["gy"] == 2 else shards,
        mesh=mesh,
        in_specs=placed,
        out_specs=(P(None, None, None, "ta", "gz", "gy"), P()),
        check_vma=False,
    )
```

```python
import functools
import math

import jax
import jax.numpy as jnp
from jax import lax
from jax.experimental import pallas as pl
from jax.experimental.pallas import tpu as pltpu
from jax.sharding import PartitionSpec as P

X = 32

hop_kappa = 0.19
epsilon = 1e-06
spin_table = (
    ((1, 0), (-1j, -1j)),
    ((1, 0), (-1, 1)),
    ((0, 1), (-1j, 1j)),
    ((0, 1), (1, 1)),
)
SPIN_COLOUR = [(spin, colour) for spin in range(2) for colour in range(3)]


def add_phased(left, phase, right):
    phase = complex(phase)
    if phase == 1:
        return (left[0] + right[0], left[1] + right[1])
    if phase == -1:
        return (left[0] - right[0], left[1] - right[1])
    if phase == 1j:
        return (left[0] - right[1], left[1] + right[0])
    return (left[0] + right[1], left[1] - right[0])


def project(psi, direction, parity):
    order, phases = spin_table[direction]
    return {
        (s, c): add_phased(psi[s, c], parity * phases[s], psi[2 + order[s], c])
        for s, c in SPIN_COLOUR
    }


def add_rebuilt(total, half, direction, parity):
    order, phases = spin_table[direction]
    for s, c in SPIN_COLOUR:
        total[s, c] = add_phased(total[s, c], 1, half[s, c])
        row = order[s]
        phase = parity * complex(phases[row]).conjugate()
        total[2 + s, c] = add_phased(total[2 + s, c], phase, half[row, c])


def mul_link(links, direction, z, half):
    out = {}
    for row in range(3):
        for s in range(2):
            real, imag = None, None
            for col in range(3):
                u_real, u_imag = links[direction, row, col, z]
                h_real, h_imag = half[s, col]
                term_real = u_real * h_real - u_imag * h_imag
                term_imag = u_real * h_imag + u_imag * h_real
                real = term_real if real is None else real + term_real
                imag = term_imag if imag is None else imag + term_imag
            out[s, row] = (real, imag)
    return out


def mul_link_dag(links, direction, z, half):
    out = {}
    for row in range(3):
        for s in range(2):
            real, imag = None, None
            for col in range(3):
                u_real, u_imag = links[direction, col, row, z]
                h_real, h_imag = half[s, col]
                term_real = u_real * h_real + u_imag * h_imag
                term_imag = u_real * h_imag - u_imag * h_real
                real = term_real if real is None else real + term_real
                imag = term_imag if imag is None else imag + term_imag
            out[s, row] = (real, imag)
    return out


def mapped(function, *halves):
    return {
        key: tuple(function(*(half[key][part] for half in halves)) for part in range(2))
        for key in SPIN_COLOUR
    }


class Links:
    def __init__(self, ref):
        self.ref = ref

    def __getitem__(self, index):
        direction, row, col, z = index
        first = ((direction * 3 + row) * 3 + col) * 2
        return (self.ref[first, z], self.ref[first + 1, z])


def load_psi(ref, z):
    return {
        (s, c): (ref[(s * 3 + c) * 2, z], ref[(s * 3 + c) * 2 + 1, z])
        for s in range(4)
        for c in range(3)
    }


def load_half(ref, z):
    return {
        (s, c): (ref[(s * 3 + c) * 2, z], ref[(s * 3 + c) * 2 + 1, z]) for s, c in SPIN_COLOUR
    }


def store_half(ref, z, half):
    for (s, c), pair in half.items():
        for part in range(2):
            ref[(s * 3 + c) * 2 + part, z] = pair[part]


class Shape:
    def __init__(self, t_extent, z_extent, lanes):
        self.t = t_extent
        self.z = z_extent
        self.rows = -(-t_extent // 8) * 8
        self.lanes = lanes

    def row(self):
        return lax.broadcasted_iota(jnp.int32, (self.rows, self.lanes), 0)

    def lane(self):
        return lax.broadcasted_iota(jnp.int32, (self.rows, self.lanes), 1)


def is_even(axis):
    return jnp.bitwise_and(lax.axis_index(axis), 1) == 0


def either(choice, first, second):
    return jnp.where(choice, first, second)


def emit_messages(shape, psi_ref, links, refs):
    z_second, t_second, z_first, t_first, y_msg, carried_y, carried_t = refs
    t_even, z_even = is_even("ta"), is_even("gz")
    lane = shape.lane()
    last_z, last_t = shape.z - 1, shape.t - 1
    for z in range(shape.z):
        psi = load_psi(psi_ref, z)
        minus = project(psi, 3, -1)
        carried = mul_link_dag(links, 3, z, project(psi, 3, 1))
        store_half(carried_t, z, carried)
        for s, c in SPIN_COLOUR:
            for part in range(2):
                at = ((s * 3 + c) * 2 + part) * shape.z + z
                down = minus[s, c][part][0:1]
                up = carried[s, c][part][last_t : last_t + 1]
                t_first[at : at + 1] = either(t_even, up, down)
                t_second[at : at + 1] = either(t_even, down, up)
        minus = project(psi, 1, -1)
        carried = mul_link_dag(links, 1, z, project(psi, 1, 1))
        store_half(carried_y, z, carried)
        store_half(
            y_msg,
            z,
            mapped(lambda low, high: jnp.where(lane < X, low, high), minus, carried),
        )
    minus = project(load_psi(psi_ref, 0), 2, -1)
    carried = mul_link_dag(links, 2, last_z, project(load_psi(psi_ref, last_z), 2, 1))
    for s, c in SPIN_COLOUR:
        for part in range(2):
            at = ((s * 3 + c) * 2 + part) * shape.t
            down, up = minus[s, c][part][0 : shape.t], carried[s, c][part][0 : shape.t]
            z_first[at : at + shape.t] = either(z_even, up, down)
            z_second[at : at + shape.t] = either(z_even, down, up)


def prep_kernel(shape, source_hbm, links_hbm, psi_ref, links_ref, *refs):
    messages, (source_ref, links_in, arrived) = refs[:-3], refs[-3:]
    t, z_extent = shape.t, shape.z
    part = 18 * t * z_extent
    copies = [pltpu.make_async_copy(source_hbm, source_ref, arrived.at[4])]
    for direction in (3, 2, 1, 0):
        rows = pl.ds(direction * part, part)
        copies.append(
            pltpu.make_async_copy(links_hbm.at[rows], links_in.at[rows], arrived.at[direction])
        )
    for copy in copies:
        copy.start()
    if shape.rows != t:
        links_ref[...] = jnp.zeros_like(links_ref)
        psi_ref[...] = jnp.zeros_like(psi_ref)
    last = lax.broadcasted_iota(jnp.int32, (t, shape.lanes), 0) == t - 1
    sign = jnp.where(lax.axis_index("ta") == lax.axis_size("ta") - 1, -1.0, 1.0)
    flip = jnp.where(last, sign, 1.0)
    copies[0].wait()
    for k in range(24):
        for z in range(z_extent):
            psi_ref[k, z, 0:t] = source_ref[pl.ds(k * t * z_extent + z, t, stride=z_extent), :]
    for direction in (3, 2, 1, 0):
        copies[4 - direction].wait()
        for k in range(18 * direction, 18 * direction + 18):
            for z in range(z_extent):
                value = links_in[pl.ds(k * t * z_extent + z, t, stride=z_extent), :]
                links_ref[k, z, 0:t] = value * flip if direction == 3 else value
    emit_messages(shape, psi_ref, Links(links_ref), messages)


def summed(shape, term):
    total = None
    for k in range(24):
        for z in range(shape.z):
            value = term(k, z)
            total = value if total is None else total + value
    return total


def over_lanes(total):
    return jnp.sum(jnp.sum(total, axis=0, keepdims=True), axis=1, keepdims=True)


def local_sums(shape, image, origin):
    square = summed(shape, lambda k, z: origin[k, z] * origin[k, z])
    mixed = over_lanes(summed(shape, lambda k, z: image[k, z] * origin[k, z]))
    whole = over_lanes(square)
    factor = jnp.where(whole > 0.0, mixed / jnp.where(whole > 0.0, whole, 1.0), 0.0)
    spread = jnp.broadcast_to(factor, (shape.rows, shape.lanes))
    rest_square, rest_mixed = None, None
    for k in range(24):
        for z in range(shape.z):
            start = origin[k, z]
            rest = image[k, z] - spread * start
            terms = rest * rest, rest * start
            if rest_square is None:
                rest_square, rest_mixed = terms
            else:
                rest_square, rest_mixed = rest_square + terms[0], rest_mixed + terms[1]
    return [factor, *(over_lanes(value) for value in (square, rest_square, rest_mixed))]


def inner_kernel(shape, psi_ref, links_ref, total_ref):
    links = Links(links_ref)
    x = shape.lane() % X
    lanes = shape.lanes
    at_end, at_start = x == X - 1, x == 0

    def ahead(value):
        return jnp.where(
            at_end, pltpu.roll(value, X - 1, 1), pltpu.roll(value, lanes - 1, 1)
        )

    def behind(value):
        return jnp.where(at_start, pltpu.roll(value, lanes - X + 1, 1), pltpu.roll(value, 1, 1))

    for z in range(shape.z):
        psi = load_psi(psi_ref, z)
        zero = jnp.zeros((shape.rows, lanes), jnp.float32)
        total = {key: (zero, zero) for key in psi}
        half = mapped(ahead, project(psi, 0, -1))
        add_rebuilt(total, mul_link(links, 0, z, half), 0, -1)
        half = mapped(behind, mul_link_dag(links, 0, z, project(psi, 0, 1)))
        add_rebuilt(total, half, 0, 1)
        if z + 1 < shape.z:
            half = project(load_psi(psi_ref, z + 1), 2, -1)
            add_rebuilt(total, mul_link(links, 2, z, half), 2, -1)
        if z > 0:
            half = project(load_psi(psi_ref, z - 1), 2, 1)
            add_rebuilt(total, mul_link_dag(links, 2, z - 1, half), 2, 1)
        for (s, c), pair in total.items():
            for part in range(2):
                total_ref[(s * 3 + c) * 2 + part, z] = pair[part]


def add_y_hops(shape, z, psi, total, links, carried_y, y_halo):
    lane, lanes = shape.lane(), shape.lanes
    received = load_half(y_halo, z)
    half = mapped(
        lambda own, other: pltpu.roll(jnp.where(lane < X, other, own), lanes - X, 1),
        project(psi, 1, -1),
        received,
    )
    add_rebuilt(total, mul_link(links, 1, z, half), 1, -1)
    half = mapped(
        lambda own, other: pltpu.roll(jnp.where(lane >= lanes - X, other, own), X, 1),
        load_half(carried_y, z),
        received,
    )
    add_rebuilt(total, half, 1, 1)


def finish_hops(
    shape, psi_ref, links, total_ref, carried_y, carried_t, halo, store
):
    z_second, t_second, z_first, t_first, y_msg = halo
    t_even, z_even = is_even("ta"), is_even("gz")
    row = shape.row()
    lanes, rows, t = shape.lanes, shape.rows, shape.t
    last_z = shape.z - 1

    for z in range(shape.z):
        psi = load_psi(psi_ref, z)
        total = load_psi(total_ref, z)

        def rim_rows(from_even, from_odd):
            half = {}
            for s, c in SPIN_COLOUR:
                ats = [((s * 3 + c) * 2 + part) * shape.z + z for part in range(2)]
                half[s, c] = tuple(
                    jnp.broadcast_to(
                        either(t_even, from_even[at : at + 1], from_odd[at : at + 1]),
                        (rows, lanes),
                    )
                    for at in ats
                )
            return half

        def rim_plane(from_even, from_odd):
            half = {}
            for s, c in SPIN_COLOUR:
                pair = []
                for part in range(2):
                    at = ((s * 3 + c) * 2 + part) * t
                    plane = either(z_even, from_even[at : at + t], from_odd[at : at + t])
                    if rows != t:
                        pad = jnp.zeros((rows - t, lanes), jnp.float32)
                        plane = jnp.concatenate([plane, pad], axis=0)
                    pair.append(plane)
                half[s, c] = tuple(pair)
            return half

        if y_msg is not None:
            add_y_hops(shape, z, psi, total, links, carried_y, y_msg)
        if z == last_z:
            add_rebuilt(total, mul_link(links, 2, z, rim_plane(z_first, z_second)), 2, -1)
        if z == 0:
            add_rebuilt(total, rim_plane(z_second, z_first), 2, 1)
        half = mapped(
            lambda own, other: jnp.where(row == t - 1, other, pltpu.roll(own, rows - 1, 0)),
            project(psi, 3, -1),
            rim_rows(t_first, t_second),
        )
        add_rebuilt(total, mul_link(links, 3, z, half), 3, -1)
        half = mapped(
            lambda own, other: jnp.where(row == 0, other, pltpu.roll(own, 1, 0)),
            load_half(carried_t, z),
            rim_rows(t_second, t_first),
        )
        add_rebuilt(total, half, 3, 1)
        for (s, c), pair in total.items():
            for part in range(2):
                value = psi[s, c][part] - hop_kappa * pair[part]
                value = value if s < 2 else -value
                if rows != t:
                    value = jnp.where(row < t, value, 0.0)
                store((s * 3 + c) * 2 + part, z, value)


def mid_kernel(shape, psi_ref, links_ref, total_ref, carried_y, carried_t, *refs):
    halo, out_ref, messages = refs[:5], refs[5], refs[6:]
    links = Links(links_ref)

    def store(k, z, value):
        out_ref[k, z] = value

    finish_hops(
        shape, psi_ref, links, total_ref, carried_y, carried_t, halo, store
    )
    emit_messages(shape, out_ref, links, messages)


def sums_row(shape, two, start, three, one):
    sums = local_sums(shape, two, start) + local_sums(shape, three, one)
    lane = lax.broadcasted_iota(jnp.int32, (1, shape.lanes), 1)
    row = jnp.zeros((1, shape.lanes), jnp.float32)
    for k, value in enumerate(sums):
        row = jnp.where(lane == k, value, row)
    return row


def inner_sums_kernel(
    shape, psi_ref, links_ref, start_ref, one_ref, two_ref, total_ref, copies_ref
):
    row = sums_row(shape, two_ref, start_ref, psi_ref, one_ref)
    copies_ref[...] = jnp.broadcast_to(row[None], copies_ref.shape)
    inner_kernel(shape, psi_ref, links_ref, total_ref)


def finish_kernel(shape, psi_ref, links_ref, total_ref, carried_y, carried_t, *refs):
    halo, out_ref = refs[:5], refs[5]

    def store(k, z, value):
        out_ref[k, z] = value

    finish_hops(
        shape, psi_ref, Links(links_ref), total_ref, carried_y, carried_t, halo, store
    )


def scalars(table, entries):
    columns = [table[:, k : k + 1] for k in range(8)]
    factor_two, start_square, two_square, two_mixed = columns[:4]
    factor_three, one_square, three_square, three_mixed = columns[4:]

    def over_devices(column):
        return jnp.sum(column, axis=0, keepdims=True)

    norm_square = over_devices(start_square) / entries + epsilon
    alpha_one = over_devices(one_square) / entries / norm_square
    gap = alpha_one - factor_two
    remain_square = over_devices(two_square - gap * (2.0 * two_mixed - gap * start_square)) / entries
    overlap = over_devices(two_mixed - gap * start_square) / entries
    gap = alpha_one - factor_three
    image_square = over_devices(three_square - gap * (2.0 * three_mixed - gap * one_square)) / entries
    norm = jnp.sqrt(norm_square)
    beta_one = jnp.sqrt(remain_square / norm_square + epsilon)
    overlap = overlap / (norm_square * beta_one)
    alpha_two = image_square / (norm_square * beta_one * beta_one) - beta_one * overlap
    scale = 1.0 / (norm * beta_one)
    return alpha_one, beta_one, alpha_two, scale, beta_one / norm


def last_kernel(
    shape, entries, start_ref, two_ref, four_ref, gathered, out_ref, coefficients
):
    alpha_one, beta_one, alpha_two, scale, first_factor = scalars(gathered[:, 0, :], entries)
    t, z_extent = shape.t, shape.z
    for k in range(24):
        for z in range(z_extent):
            two, start = two_ref[k, z], start_ref[k, z]
            remain = two - alpha_one * start
            result = (four_ref[k, z] - alpha_one * two - alpha_two * remain) * scale
            result = result - first_factor * start
            out_ref[pl.ds(k * t * z_extent + z, t, stride=z_extent), :] = result[0:t]
    coefficients[0] = alpha_one[0, 0]
    coefficients[1] = beta_one[0, 0]
    coefficients[2] = alpha_two[0, 0]


def swap(value, axis, second):
    count = math.prod(lax.axis_size(name) for name in (axis if isinstance(axis, tuple) else (axis,)))
    pairs = []
    for low in range(1 if second else 0, count, 2):
        high = (low + 1) % count
        pairs += [(low, high), (high, low)]
    return lax.ppermute(value, axis, pairs)


def exchange(messages, lanes):
    z_second, t_second, z_first, t_first, y_msg = messages
    halo = (
        swap(z_second, "gz", True),
        swap(t_second, "ta", True),
        swap(z_first, "gz", False),
        swap(t_first, "ta", False),
    )
    y_halo = swap(y_msg, "gy", False)
    if lax.axis_size("gy") > 2:
        even = lax.axis_index("gy") % 2 == 0
        lane = lax.broadcasted_iota(jnp.int32, y_msg.shape, y_msg.ndim - 1)
        y_halo = jnp.where((lane < lanes // 2) == even, y_halo, swap(y_msg, "gy", True))
    return (*halo, y_halo)


def from_everyone(copies):
    return lax.all_to_all(copies, ("ta", "gz", "gy"), split_axis=0, concat_axis=0, tiled=True)


def shards(source, gauge_links):
    devices_all = lax.axis_size("ta") * lax.axis_size("gz") * lax.axis_size("gy")
    entries = float(source.size * devices_all)
    shape = Shape(source.shape[3], source.shape[4], source.shape[5])
    t, z, rows, lanes = shape.t, shape.z, shape.rows, shape.lanes
    vmem = pl.BlockSpec(memory_space=pltpu.VMEM)
    smem = pl.BlockSpec(memory_space=pltpu.SMEM)

    def held(*dims):
        return pltpu.VMEM(dims, jnp.float32)

    field = held(24, z, rows, lanes)
    half = held(12, z, rows, lanes)
    z_face, t_face = held(12 * t, lanes), held(12 * z, lanes)
    messages = (z_face, t_face, z_face, t_face, half, half, half)

    def call(kernel, name, flops, out_shape, operands, out_specs=None, in_spec=vmem, scratch=()):
        return pl.pallas_call(
            kernel,
            name=name,
            out_shape=out_shape,
            in_specs=[in_spec] * len(operands),
            out_specs=out_specs or jax.tree.map(lambda _: vmem, out_shape),
            scratch_shapes=scratch,
            compiler_params=pltpu.CompilerParams(vmem_limit_bytes=8 << 20),
            cost_estimate=pl.CostEstimate(flops=flops, bytes_accessed=1 << 20, transcendentals=0),
        )(*operands)

    sites = t * z * lanes
    psi, links, *sent = call(
        functools.partial(prep_kernel, shape), "prep", 400 * sites,
        (field, held(72, z, rows, lanes), *messages),
        (
            pltpu.with_memory_space_constraint(source.reshape(24 * t * z, lanes), pltpu.HBM),
            pltpu.with_memory_space_constraint(gauge_links.reshape(72 * t * z, lanes), pltpu.HBM),
        ),
        in_spec=pl.BlockSpec(memory_space=pltpu.HBM),
        scratch=(
            held(24 * t * z, lanes), held(72 * t * z, lanes), pltpu.SemaphoreType.DMA((5,)),
        ),
    )
    powers = [psi]
    for step in range(3):
        halo = exchange(sent[:5], lanes)
        inner = functools.partial(inner_kernel, shape)
        total = call(inner, "inner", 700 * sites, field, (psi, links))
        psi, *sent = call(
            functools.partial(mid_kernel, shape), "mid", 1000 * sites,
            (field, *messages), (psi, links, total, *sent[5:], *halo),
        )
        powers.append(psi)
    halo = exchange(sent[:5], lanes)
    total, copies = call(
        functools.partial(inner_sums_kernel, shape), "inner_sums", 1100 * sites,
        (field, held(devices_all, 1, lanes)), (psi, links, *powers[:3]),
    )
    gathered = from_everyone(copies)
    four = call(
        functools.partial(finish_kernel, shape), "finish", 700 * sites, field,
        (psi, links, total, *sent[5:], *halo),
    )
    residual, coefficients = call(
        functools.partial(last_kernel, shape, entries), "last", 100 * sites,
        (
            jax.ShapeDtypeStruct((24 * t * z, lanes), jnp.float32),
            jax.ShapeDtypeStruct((3,), jnp.float32),
        ),
        (powers[0], powers[2], four, gathered), (vmem, smem),
    )
    return (residual.reshape(source.shape), coefficients)


class ChipShape(Shape):
    def __init__(self, t_extent, z_extent, lanes):
        super().__init__(t_extent, z_extent, lanes)
        self.parts = 2 * z_extent
        self.z_rows = 24 * t_extent
        self.t_rows = 12 * self.parts

    def block(self, k, part):
        first = (k * self.parts + part) * self.rows
        return pl.ds(first, self.rows)

    def edge(self, k, row):
        return pl.ds(k * self.parts * self.rows + row, self.parts, stride=self.rows)


class ChipLinks:
    def __init__(self, shape, ref, row=None):
        self.shape, self.ref, self.row = shape, ref, row

    def __getitem__(self, index):
        direction, row, col, part = index
        first = ((direction * 3 + row) * 3 + col) * 2
        if self.row is None:
            return tuple(self.ref[self.shape.block(first + n, part), :] for n in range(2))
        return tuple(self.ref[self.shape.edge(first + n, self.row), :] for n in range(2))


def components(spins):
    return [(s, c, part, (s * 3 + c) * 2 + part) for s in range(spins) for c in range(3) for part in range(2)]


def gathered_pairs(spins, value):
    out = {}
    for s in range(spins):
        for c in range(3):
            out[s, c] = tuple(value((s * 3 + c) * 2 + part) for part in range(2))
    return out


def chip_psi(shape, ref, part):
    return gathered_pairs(4, lambda k: ref[shape.block(k, part), :])


def chip_edge(shape, ref, row):
    return gathered_pairs(4, lambda k: ref[shape.edge(k, row), :])


def chip_messages(shape, psi_ref, links_ref, z_second, t_second, z_first, t_first):
    t, last = shape.t, shape.t - 1
    even = is_even("ta")
    minus = project(chip_edge(shape, psi_ref, 0), 3, -1)
    half = project(chip_edge(shape, psi_ref, last), 3, 1)
    carried = mul_link_dag(ChipLinks(shape, links_ref, last), 3, 0, half)
    for s, c, part, k in components(2):
        rows = pl.ds(k * shape.parts, shape.parts)
        up, down = carried[s, c][part], minus[s, c][part]
        t_first[rows, :] = either(even, up, down)
        t_second[rows, :] = either(even, down, up)
    even = is_even("gy")
    links = ChipLinks(shape, links_ref)
    for y_half in range(2):
        minus = project(chip_psi(shape, psi_ref, y_half), 2, -1)
        part_last = shape.parts - 2 + y_half
        half = project(chip_psi(shape, psi_ref, part_last), 2, 1)
        carried = mul_link_dag(links, 2, part_last, half)
        for s, c, part, k in components(2):
            rows = pl.ds((k * 2 + y_half) * t, t)
            up, down = carried[s, c][part][0:t], minus[s, c][part][0:t]
            z_first[rows, :] = either(even, up, down)
            z_second[rows, :] = either(even, down, up)


def chip_bring(shape, y_half, source_ref, links_in, psi_ref, links_ref, arrived):
    t, z_extent = shape.t, 2 * shape.z
    first_plane = lax.axis_index("gy") * shape.z
    last = lax.broadcasted_iota(jnp.int32, (t, shape.lanes), 0) == t - 1
    sign = jnp.where(lax.axis_index("ta") == lax.axis_size("ta") - 1, -1.0, 1.0)
    flip = jnp.where(last, sign, 1.0)

    def bring(in_ref, out_ref, k, z, factor=None):
        value = in_ref[pl.ds(k * t * z_extent + first_plane + z, t, stride=z_extent), :]
        if factor is not None:
            value = value * factor
        at = (k * shape.parts + 2 * z + y_half) * shape.rows
        out_ref[pl.ds(pl.multiple_of(at, 8), t), :] = value

    arrived(4)
    for z in range(shape.z):
        for k in range(24):
            bring(source_ref, psi_ref, k, z)
    for direction in (3, 2, 1, 0):
        arrived(direction)
        for z in range(shape.z):
            for k in range(18 * direction, 18 * direction + 18):
                bring(links_in, links_ref, k, z, flip if direction == 3 else None)


def chip_own_kernel(
    shape, source_hbm, links_hbm, psi_ref, links_ref, rest_ref, source_ref, links_in, semaphores
):
    part = 18 * shape.t * 2 * shape.z
    copies = {4: pltpu.make_async_copy(source_hbm, source_ref, semaphores.at[4])}
    for direction in (3, 2, 1, 0):
        rows = pl.ds(direction * part, part)
        copies[direction] = pltpu.make_async_copy(
            links_hbm.at[rows], links_in.at[rows], semaphores.at[direction]
        )
    for copy in copies.values():
        copy.start()
    if shape.rows != shape.t:
        links_ref[...] = jnp.zeros_like(links_ref)
        psi_ref[...] = jnp.zeros_like(psi_ref)
    chip_bring(
        shape, lax.axis_index("gy"), source_ref, links_in, psi_ref, links_ref,
        lambda n: copies[n].wait(),
    )
    t, z_extent = shape.t, 2 * shape.z
    first_plane = (1 - lax.axis_index("gy")) * shape.z
    if shape.rows != t:
        rest_ref[...] = jnp.zeros_like(rest_ref)
    for k in range(24):
        for z in range(shape.z):
            value = source_ref[pl.ds(k * t * z_extent + first_plane + z, t, stride=z_extent), :]
            rest_ref[pl.ds((k * shape.z + z) * shape.rows, t), :] = value


def chip_prep_kernel(
    shape, source_ref, links_in, psi_in, links_held, psi_ref, links_ref, *messages
):
    chip_bring(
        shape, 1 - lax.axis_index("gy"), source_ref, links_in, psi_ref, links_ref, lambda n: None
    )
    chip_messages(shape, psi_ref, links_ref, *messages)


def chip_inner_kernel(shape, psi_ref, links_ref, total_ref):
    links = ChipLinks(shape, links_ref)
    lane, row = shape.lane(), shape.row()
    x = lane % X
    lanes, rows, t = shape.lanes, shape.rows, shape.t
    at_end, at_start = x == X - 1, x == 0
    inside_ahead = row < t - 1
    inside_behind = jnp.logical_and(row > 0, row < t)

    def x_ahead(value):
        return jnp.where(
            at_end, pltpu.roll(value, X - 1, 1), pltpu.roll(value, lanes - 1, 1)
        )

    def x_behind(value):
        return jnp.where(at_start, pltpu.roll(value, lanes - X + 1, 1), pltpu.roll(value, 1, 1))

    def t_ahead(value):
        return jnp.where(inside_ahead, pltpu.roll(value, rows - 1, 0), 0.0)

    def t_behind(value):
        return jnp.where(inside_behind, pltpu.roll(value, 1, 0), 0.0)

    for z in range(shape.z):
        for part in (2 * z, 2 * z + 1):
            psi = chip_psi(shape, psi_ref, part)
            zero = jnp.zeros((rows, lanes), jnp.float32)
            total = {key: (zero, zero) for key in psi}
            half = mapped(x_ahead, project(psi, 0, -1))
            add_rebuilt(total, mul_link(links, 0, part, half), 0, -1)
            half = mapped(x_behind, mul_link_dag(links, 0, part, project(psi, 0, 1)))
            add_rebuilt(total, half, 0, 1)
            half = mapped(t_ahead, project(psi, 3, -1))
            add_rebuilt(total, mul_link(links, 3, part, half), 3, -1)
            half = mapped(t_behind, mul_link_dag(links, 3, part, project(psi, 3, 1)))
            add_rebuilt(total, half, 3, 1)
            if z + 1 < shape.z:
                half = project(chip_psi(shape, psi_ref, part + 2), 2, -1)
                add_rebuilt(total, mul_link(links, 2, part, half), 2, -1)
            if z > 0:
                half = project(chip_psi(shape, psi_ref, part - 2), 2, 1)
                add_rebuilt(total, mul_link_dag(links, 2, part - 2, half), 2, 1)
            for s, c, n, k in components(4):
                total_ref[shape.block(k, part), :] = total[s, c][n]
        pair = (2 * z, 2 * z + 1)
        minus, carried = [], []
        for part in pair:
            psi = chip_psi(shape, psi_ref, part)
            minus.append(mapped(lambda v: pltpu.roll(v, lanes - X, 1), project(psi, 1, -1)))
            half = mul_link_dag(links, 1, part, project(psi, 1, 1))
            carried.append(mapped(lambda v: pltpu.roll(v, X, 1), half))
        for own, part in enumerate(pair):
            total = chip_psi(shape, total_ref, part)
            half = mapped(
                lambda a, b: jnp.where(lane >= lanes - X, b, a), minus[own], minus[1 - own]
            )
            add_rebuilt(total, mul_link(links, 1, part, half), 1, -1)
            half = mapped(lambda a, b: jnp.where(lane < X, b, a), carried[own], carried[1 - own])
            add_rebuilt(total, half, 1, 1)
            for s, c, n, k in components(4):
                total_ref[shape.block(k, part), :] = total[s, c][n]


def chip_finish(shape, psi_ref, links_ref, total_ref, received, scratch, out_ref):
    z_second, t_second, z_first, t_first = received
    z_down, z_up = scratch
    t_even, z_even = is_even("ta"), is_even("gy")
    t, rows, lanes, parts = shape.t, shape.rows, shape.lanes, shape.parts
    z_down[...] = either(z_even, z_first[...], z_second[...])
    z_up[...] = either(z_even, z_second[...], z_first[...])
    links = ChipLinks(shape, links_ref)

    def plane(ref, y_half):
        def value(k):
            face = ref[pl.ds((k * 2 + y_half) * t, t), :]
            if rows != t:
                pad = jnp.zeros((rows - t, lanes), jnp.float32)
                face = jnp.concatenate([face, pad], axis=0)
            return face

        return gathered_pairs(2, value)

    for part in range(parts):
        total = chip_psi(shape, total_ref, part)
        if part >= parts - 2:
            half = mul_link(links, 2, part, plane(z_down, part - parts + 2))
            add_rebuilt(total, half, 2, -1)
        if part < 2:
            add_rebuilt(total, plane(z_up, part), 2, 1)
        for s, c, n, k in components(4):
            value = psi_ref[shape.block(k, part), :] - hop_kappa * total[s, c][n]
            out_ref[shape.block(k, part), :] = value if s < 2 else -value

    def t_half(from_even, from_odd):
        def value(k):
            at = pl.ds(k * parts, parts)
            return either(t_even, from_even[at, :], from_odd[at, :])

        return gathered_pairs(2, value)

    down = mul_link(ChipLinks(shape, links_ref, t - 1), 3, 0, t_half(t_first, t_second))
    up = t_half(t_second, t_first)
    zero = jnp.zeros((parts, lanes), jnp.float32)
    for half, parity, row in ((down, -1, t - 1), (up, 1, 0)):
        total = {(s, c): (zero, zero) for s in range(4) for c in range(3)}
        add_rebuilt(total, half, 3, parity)
        for s, c, n, k in components(4):
            at = shape.edge(k, row)
            value = hop_kappa * total[s, c][n]
            out_ref[at, :] = out_ref[at, :] - (value if s < 2 else -value)


def chip_mid_kernel(shape, hands_over, psi_ref, links_ref, total_ref, *refs):
    received, out_ref, messages, refs = refs[:4], refs[4], refs[5:9], refs[9:]
    chip_finish(shape, psi_ref, links_ref, total_ref, received, refs[-2:], out_ref)
    chip_messages(shape, out_ref, links_ref, *messages)
    if hands_over:
        hand_over(shape, out_ref, refs[0])


def chip_inner_sums_kernel(
    shape, psi_ref, links_ref, start_ref, one_ref, two_ref, total_ref, row_ref
):
    class View:
        def __init__(self, ref):
            self.ref = ref

        def __getitem__(self, index):
            return self.ref[shape.block(*index), :]

    wide = ChipShape(shape.t, shape.z, shape.lanes)
    wide.z = shape.parts
    row = sums_row(wide, View(two_ref), View(start_ref), View(psi_ref), View(one_ref))
    row_ref[...] = jnp.broadcast_to(row, row_ref.shape)
    chip_inner_kernel(shape, psi_ref, links_ref, total_ref)


def chip_copies_kernel(row_ref, other_row, copies_ref):
    first = lax.broadcasted_iota(jnp.int32, row_ref.shape, 0) == 0
    block = jnp.where(first, row_ref[...], other_row[...])
    copies_ref[...] = jnp.broadcast_to(block[None], copies_ref.shape)


def y_part(shape, k, z, y_half):
    return pl.ds(pl.multiple_of((k * shape.parts + 2 * z + y_half) * shape.rows, 8), shape.rows)


def rest_rows(shape, k, z):
    return pl.ds((k * shape.z + z) * shape.rows, shape.rows)


def hand_over(shape, ref, rest_ref, first=0, count=24):
    y_half = 1 - lax.axis_index("gy")
    for k in range(count):
        for z in range(shape.z):
            rest_ref[rest_rows(shape, k, z), :] = ref[y_part(shape, first + k, z, y_half), :]


def chip_finish_kernel(shape, psi_ref, links_ref, total_ref, *refs):
    received, (out_ref, upper_rest, lower_rest), scratch = refs[:4], refs[4:7], refs[7:]
    chip_finish(shape, psi_ref, links_ref, total_ref, received, scratch, out_ref)
    hand_over(shape, out_ref, upper_rest, 0, 12)
    hand_over(shape, out_ref, lower_rest, 12, 12)


def chip_last_kernel(
    shape, entries, start_ref, two_ref, four_ref, start_rest, two_rest, upper_rest, lower_rest,
    gathered, out_ref, coefficients,
):
    table = jnp.concatenate([gathered[:, 0, :], gathered[:, 1, :]], axis=0)
    alpha_one, beta_one, alpha_two, scale, first_factor = scalars(table, entries)
    t, z_extent = shape.t, 2 * shape.z
    core = lax.axis_index("gy")

    def put(k, z, start, two, four):
        remain = two - alpha_one * start
        result = (four - alpha_one * two - alpha_two * remain) * scale - first_factor * start
        out_ref[pl.ds(k * t * z_extent + z, t, stride=z_extent), :] = result[0:t]

    for k in range(24):
        for z in range(shape.z):
            rows = y_part(shape, k, z, core)
            own = (ref[rows, :] for ref in (start_ref, two_ref, four_ref))
            put(k, core * shape.z + z, *own)
            rows = rest_rows(shape, k, z)
            four_rest = upper_rest if k < 12 else lower_rest
            other = start_rest[rows, :], two_rest[rows, :], four_rest[rest_rows(shape, k % 12, z), :]
            put(k, (1 - core) * shape.z + z, *other)
    coefficients[0] = alpha_one[0, 0]
    coefficients[1] = beta_one[0, 0]
    coefficients[2] = alpha_two[0, 0]


def chip_shards(source, gauge_links):
    devices_all = lax.axis_size("ta") * lax.axis_size("gz") * 2
    entries = float(source.size * devices_all)
    z_extent = source.shape[4]
    shape = ChipShape(source.shape[3], z_extent // 2, source.shape[5])
    t, rows, lanes = shape.t, shape.rows, shape.lanes
    vmem = pl.BlockSpec(memory_space=pltpu.VMEM)
    smem = pl.BlockSpec(memory_space=pltpu.SMEM)

    def held(*dims):
        return pltpu.VMEM(dims, jnp.float32)

    field = held(24 * shape.parts * rows, lanes)
    links_field = held(72 * shape.parts * rows, lanes)
    z_face, t_face = held(shape.z_rows, lanes), held(shape.t_rows, lanes)
    messages = (z_face, t_face, z_face, t_face)
    z_faces = (z_face, z_face)

    def call(kernel, name, flops, out_shape, operands, **options):
        in_spec = options.pop("in_spec", vmem)
        out_specs = options.pop("out_specs", jax.tree.map(lambda _: vmem, out_shape))
        return pl.pallas_call(
            kernel,
            name=name,
            out_shape=out_shape,
            in_specs=[in_spec] * len(operands),
            out_specs=out_specs,
            compiler_params=pltpu.CompilerParams(vmem_limit_bytes=8 << 20),
            cost_estimate=pl.CostEstimate(flops=flops, bytes_accessed=1 << 20, transcendentals=0),
            **options,
        )(*operands)

    def exchanged(sent):
        z_second, t_second, z_first, t_first = sent
        z_ring = ("gz", "gy")
        return (
            swap(z_second, z_ring, True), swap(t_second, "ta", True),
            swap(z_first, z_ring, False), swap(t_first, "ta", False),
        )

    sites = t * z_extent * lanes
    rows_in = t * z_extent
    own = (source.reshape(24 * rows_in, lanes), gauge_links.reshape(72 * rows_in, lanes))
    other = tuple(swap(value, "gy", False) for value in own)
    rest = held(24 * shape.z * rows, lanes)
    psi, links, start_rest = call(
        functools.partial(chip_own_kernel, shape), "own", 200 * sites, (field, links_field, rest),
        [pltpu.with_memory_space_constraint(value, pltpu.HBM) for value in own],
        scratch_shapes=(
            held(24 * rows_in, lanes), held(72 * rows_in, lanes), pltpu.SemaphoreType.DMA((5,)),
        ),
        in_spec=pl.BlockSpec(memory_space=pltpu.HBM),
    )
    psi, links, *sent = call(
        functools.partial(chip_prep_kernel, shape), "prep", 400 * sites,
        (field, links_field, *messages), (*other, psi, links),
        input_output_aliases={2: 0, 3: 1},
    )
    powers = [psi]
    for step in range(3):
        halo = exchanged(sent)
        inner = functools.partial(chip_inner_kernel, shape)
        total = call(inner, "inner", 1000 * sites, field, (psi, links))
        hands_over = step == 1
        psi, *sent = call(
            functools.partial(chip_mid_kernel, shape, hands_over), "mid", 600 * sites,
            (field, *messages, rest) if hands_over else (field, *messages),
            (psi, links, total, *halo), scratch_shapes=z_faces,
        )
        powers.append(psi)
        if hands_over:
            two_rest = swap(sent.pop(), "gy", False)
    halo = exchanged(sent)
    total, row = call(
        functools.partial(chip_inner_sums_kernel, shape), "inner_sums", 1400 * sites,
        (field, held(8, lanes)), (psi, links, *powers[:3]),
    )
    copies = call(
        chip_copies_kernel, "copies", 1 << 16, held(devices_all // 2, 8, lanes),
        (row, swap(row, "gy", False)),
    )
    gathered = lax.all_to_all(copies, ("ta", "gz"), split_axis=0, concat_axis=0, tiled=True)
    half_rest = held(12 * shape.z * rows, lanes)
    four, *four_rest = call(
        functools.partial(chip_finish_kernel, shape), "finish", 10**11,
        (field, half_rest, half_rest), (psi, links, total, *halo), scratch_shapes=z_faces,
    )
    four_rest = [swap(value, "gy", False) for value in four_rest]
    residual, coefficients = call(
        functools.partial(chip_last_kernel, shape, entries), "last", 100 * sites,
        (
            jax.ShapeDtypeStruct((24 * rows_in, lanes), jnp.float32),
            jax.ShapeDtypeStruct((3,), jnp.float32),
        ),
        (powers[0], powers[2], four, start_rest, two_rest, *four_rest, gathered),
        out_specs=(vmem, smem),
    )
    return (residual.reshape(source.shape), coefficients)


def solution(mesh):
    placed = (P(None, None, None, "ta", "gz", "gy"), P(None, None, None, None, "ta", "gz", "gy"))
    return jax.shard_map(
        chip_shards if mesh.shape["gy"] == 2 else shards,
        mesh=mesh,
        in_specs=placed,
        out_specs=(P(None, None, None, "ta", "gz", "gy"), P()),
        check_vma=False,
    )
```

```python
import functools
import math

import jax
import jax.numpy as jnp
from jax import lax
from jax.experimental import pallas as pl
from jax.experimental.pallas import tpu as pltpu
from jax.sharding import PartitionSpec as P

X = 32

hop_kappa = 0.19
epsilon = 1e-06
spin_table = (
    ((1, 0), (-1j, -1j)),
    ((1, 0), (-1, 1)),
    ((0, 1), (-1j, 1j)),
    ((0, 1), (1, 1)),
)
SPIN_COLOUR = [(spin, colour) for spin in range(2) for colour in range(3)]


def add_phased(left, phase, right):
    phase = complex(phase)
    if phase == 1:
        return (left[0] + right[0], left[1] + right[1])
    if phase == -1:
        return (left[0] - right[0], left[1] - right[1])
    if phase == 1j:
        return (left[0] - right[1], left[1] + right[0])
    return (left[0] + right[1], left[1] - right[0])


def project(psi, direction, parity):
    order, phases = spin_table[direction]
    return {
        (s, c): add_phased(psi[s, c], parity * phases[s], psi[2 + order[s], c])
        for s, c in SPIN_COLOUR
    }


def add_rebuilt(total, half, direction, parity):
    order, phases = spin_table[direction]
    for s, c in SPIN_COLOUR:
        total[s, c] = add_phased(total[s, c], 1, half[s, c])
        row = order[s]
        phase = parity * complex(phases[row]).conjugate()
        total[2 + s, c] = add_phased(total[2 + s, c], phase, half[row, c])


def mul_link(links, direction, z, half):
    out = {}
    for row in range(3):
        for s in range(2):
            real, imag = None, None
            for col in range(3):
                u_real, u_imag = links[direction, row, col, z]
                h_real, h_imag = half[s, col]
                term_real = u_real * h_real - u_imag * h_imag
                term_imag = u_real * h_imag + u_imag * h_real
                real = term_real if real is None else real + term_real
                imag = term_imag if imag is None else imag + term_imag
            out[s, row] = (real, imag)
    return out


def mul_link_dag(links, direction, z, half):
    out = {}
    for row in range(3):
        for s in range(2):
            real, imag = None, None
            for col in range(3):
                u_real, u_imag = links[direction, col, row, z]
                h_real, h_imag = half[s, col]
                term_real = u_real * h_real + u_imag * h_imag
                term_imag = u_real * h_imag - u_imag * h_real
                real = term_real if real is None else real + term_real
                imag = term_imag if imag is None else imag + term_imag
            out[s, row] = (real, imag)
    return out


def mapped(function, *halves):
    return {
        key: tuple(function(*(half[key][part] for half in halves)) for part in range(2))
        for key in SPIN_COLOUR
    }


class Links:
    def __init__(self, ref):
        self.ref = ref

    def __getitem__(self, index):
        direction, row, col, z = index
        first = ((direction * 3 + row) * 3 + col) * 2
        return (self.ref[first, z], self.ref[first + 1, z])


def load_psi(ref, z):
    return {
        (s, c): (ref[(s * 3 + c) * 2, z], ref[(s * 3 + c) * 2 + 1, z])
        for s in range(4)
        for c in range(3)
    }


def load_half(ref, z):
    return {
        (s, c): (ref[(s * 3 + c) * 2, z], ref[(s * 3 + c) * 2 + 1, z]) for s, c in SPIN_COLOUR
    }


def store_half(ref, z, half):
    for (s, c), pair in half.items():
        for part in range(2):
            ref[(s * 3 + c) * 2 + part, z] = pair[part]


class Shape:
    def __init__(self, t_extent, z_extent, lanes):
        self.t = t_extent
        self.z = z_extent
        self.rows = -(-t_extent // 8) * 8
        self.lanes = lanes

    def row(self):
        return lax.broadcasted_iota(jnp.int32, (self.rows, self.lanes), 0)

    def lane(self):
        return lax.broadcasted_iota(jnp.int32, (self.rows, self.lanes), 1)


def is_even(axis):
    return jnp.bitwise_and(lax.axis_index(axis), 1) == 0


def either(choice, first, second):
    return jnp.where(choice, first, second)


def emit_messages(shape, psi_ref, links, refs):
    z_second, t_second, z_first, t_first, y_msg, carried_y, carried_t = refs
    t_even, z_even = is_even("ta"), is_even("gz")
    lane = shape.lane()
    last_z, last_t = shape.z - 1, shape.t - 1
    for z in range(shape.z):
        psi = load_psi(psi_ref, z)
        minus = project(psi, 3, -1)
        carried = mul_link_dag(links, 3, z, project(psi, 3, 1))
        store_half(carried_t, z, carried)
        for s, c in SPIN_COLOUR:
            for part in range(2):
                at = ((s * 3 + c) * 2 + part) * shape.z + z
                down = minus[s, c][part][0:1]
                up = carried[s, c][part][last_t : last_t + 1]
                t_first[at : at + 1] = either(t_even, up, down)
                t_second[at : at + 1] = either(t_even, down, up)
        minus = project(psi, 1, -1)
        carried = mul_link_dag(links, 1, z, project(psi, 1, 1))
        store_half(carried_y, z, carried)
        store_half(
            y_msg,
            z,
            mapped(lambda low, high: jnp.where(lane < X, low, high), minus, carried),
        )
    minus = project(load_psi(psi_ref, 0), 2, -1)
    carried = mul_link_dag(links, 2, last_z, project(load_psi(psi_ref, last_z), 2, 1))
    for s, c in SPIN_COLOUR:
        for part in range(2):
            at = ((s * 3 + c) * 2 + part) * shape.t
            down, up = minus[s, c][part][0 : shape.t], carried[s, c][part][0 : shape.t]
            z_first[at : at + shape.t] = either(z_even, up, down)
            z_second[at : at + shape.t] = either(z_even, down, up)


def prep_kernel(shape, source_hbm, links_hbm, psi_ref, links_ref, *refs):
    messages, (source_ref, links_in, arrived) = refs[:-3], refs[-3:]
    t, z_extent = shape.t, shape.z
    part = 18 * t * z_extent
    copies = [pltpu.make_async_copy(source_hbm, source_ref, arrived.at[4])]
    for direction in (3, 2, 1, 0):
        rows = pl.ds(direction * part, part)
        copies.append(
            pltpu.make_async_copy(links_hbm.at[rows], links_in.at[rows], arrived.at[direction])
        )
    for copy in copies:
        copy.start()
    if shape.rows != t:
        links_ref[...] = jnp.zeros_like(links_ref)
        psi_ref[...] = jnp.zeros_like(psi_ref)
    last = lax.broadcasted_iota(jnp.int32, (t, shape.lanes), 0) == t - 1
    sign = jnp.where(lax.axis_index("ta") == lax.axis_size("ta") - 1, -1.0, 1.0)
    flip = jnp.where(last, sign, 1.0)
    copies[0].wait()
    for k in range(24):
        for z in range(z_extent):
            psi_ref[k, z, 0:t] = source_ref[pl.ds(k * t * z_extent + z, t, stride=z_extent), :]
    for direction in (3, 2, 1, 0):
        copies[4 - direction].wait()
        for k in range(18 * direction, 18 * direction + 18):
            for z in range(z_extent):
                value = links_in[pl.ds(k * t * z_extent + z, t, stride=z_extent), :]
                links_ref[k, z, 0:t] = value * flip if direction == 3 else value
    emit_messages(shape, psi_ref, Links(links_ref), messages)


def summed(shape, term):
    total = None
    for k in range(24):
        for z in range(shape.z):
            value = term(k, z)
            total = value if total is None else total + value
    return total


def over_lanes(total):
    return jnp.sum(jnp.sum(total, axis=0, keepdims=True), axis=1, keepdims=True)


def local_sums(shape, image, origin):
    square = summed(shape, lambda k, z: origin[k, z] * origin[k, z])
    mixed = over_lanes(summed(shape, lambda k, z: image[k, z] * origin[k, z]))
    whole = over_lanes(square)
    factor = jnp.where(whole > 0.0, mixed / jnp.where(whole > 0.0, whole, 1.0), 0.0)
    spread = jnp.broadcast_to(factor, (shape.rows, shape.lanes))
    rest_square, rest_mixed = None, None
    for k in range(24):
        for z in range(shape.z):
            start = origin[k, z]
            rest = image[k, z] - spread * start
            terms = rest * rest, rest * start
            if rest_square is None:
                rest_square, rest_mixed = terms
            else:
                rest_square, rest_mixed = rest_square + terms[0], rest_mixed + terms[1]
    return [factor, *(over_lanes(value) for value in (square, rest_square, rest_mixed))]


def inner_kernel(shape, psi_ref, links_ref, total_ref):
    links = Links(links_ref)
    x = shape.lane() % X
    lanes = shape.lanes
    at_end, at_start = x == X - 1, x == 0

    def ahead(value):
        return jnp.where(
            at_end, pltpu.roll(value, X - 1, 1), pltpu.roll(value, lanes - 1, 1)
        )

    def behind(value):
        return jnp.where(at_start, pltpu.roll(value, lanes - X + 1, 1), pltpu.roll(value, 1, 1))

    for z in range(shape.z):
        psi = load_psi(psi_ref, z)
        zero = jnp.zeros((shape.rows, lanes), jnp.float32)
        total = {key: (zero, zero) for key in psi}
        half = mapped(ahead, project(psi, 0, -1))
        add_rebuilt(total, mul_link(links, 0, z, half), 0, -1)
        half = mapped(behind, mul_link_dag(links, 0, z, project(psi, 0, 1)))
        add_rebuilt(total, half, 0, 1)
        if z + 1 < shape.z:
            half = project(load_psi(psi_ref, z + 1), 2, -1)
            add_rebuilt(total, mul_link(links, 2, z, half), 2, -1)
        if z > 0:
            half = project(load_psi(psi_ref, z - 1), 2, 1)
            add_rebuilt(total, mul_link_dag(links, 2, z - 1, half), 2, 1)
        for (s, c), pair in total.items():
            for part in range(2):
                total_ref[(s * 3 + c) * 2 + part, z] = pair[part]


def add_y_hops(shape, z, psi, total, links, carried_y, y_halo):
    lane, lanes = shape.lane(), shape.lanes
    received = load_half(y_halo, z)
    half = mapped(
        lambda own, other: pltpu.roll(jnp.where(lane < X, other, own), lanes - X, 1),
        project(psi, 1, -1),
        received,
    )
    add_rebuilt(total, mul_link(links, 1, z, half), 1, -1)
    half = mapped(
        lambda own, other: pltpu.roll(jnp.where(lane >= lanes - X, other, own), X, 1),
        load_half(carried_y, z),
        received,
    )
    add_rebuilt(total, half, 1, 1)


def finish_hops(
    shape, psi_ref, links, total_ref, carried_y, carried_t, halo, store
):
    z_second, t_second, z_first, t_first, y_msg = halo
    t_even, z_even = is_even("ta"), is_even("gz")
    row = shape.row()
    lanes, rows, t = shape.lanes, shape.rows, shape.t
    last_z = shape.z - 1

    for z in range(shape.z):
        psi = load_psi(psi_ref, z)
        total = load_psi(total_ref, z)

        def rim_rows(from_even, from_odd):
            half = {}
            for s, c in SPIN_COLOUR:
                ats = [((s * 3 + c) * 2 + part) * shape.z + z for part in range(2)]
                half[s, c] = tuple(
                    jnp.broadcast_to(
                        either(t_even, from_even[at : at + 1], from_odd[at : at + 1]),
                        (rows, lanes),
                    )
                    for at in ats
                )
            return half

        def rim_plane(from_even, from_odd):
            half = {}
            for s, c in SPIN_COLOUR:
                pair = []
                for part in range(2):
                    at = ((s * 3 + c) * 2 + part) * t
                    plane = either(z_even, from_even[at : at + t], from_odd[at : at + t])
                    if rows != t:
                        pad = jnp.zeros((rows - t, lanes), jnp.float32)
                        plane = jnp.concatenate([plane, pad], axis=0)
                    pair.append(plane)
                half[s, c] = tuple(pair)
            return half

        if y_msg is not None:
            add_y_hops(shape, z, psi, total, links, carried_y, y_msg)
        if z == last_z:
            add_rebuilt(total, mul_link(links, 2, z, rim_plane(z_first, z_second)), 2, -1)
        if z == 0:
            add_rebuilt(total, rim_plane(z_second, z_first), 2, 1)
        half = mapped(
            lambda own, other: jnp.where(row == t - 1, other, pltpu.roll(own, rows - 1, 0)),
            project(psi, 3, -1),
            rim_rows(t_first, t_second),
        )
        add_rebuilt(total, mul_link(links, 3, z, half), 3, -1)
        half = mapped(
            lambda own, other: jnp.where(row == 0, other, pltpu.roll(own, 1, 0)),
            load_half(carried_t, z),
            rim_rows(t_second, t_first),
        )
        add_rebuilt(total, half, 3, 1)
        for (s, c), pair in total.items():
            for part in range(2):
                value = psi[s, c][part] - hop_kappa * pair[part]
                value = value if s < 2 else -value
                if rows != t:
                    value = jnp.where(row < t, value, 0.0)
                store((s * 3 + c) * 2 + part, z, value)


def mid_kernel(shape, psi_ref, links_ref, total_ref, carried_y, carried_t, *refs):
    halo, out_ref, messages = refs[:5], refs[5], refs[6:]
    links = Links(links_ref)

    def store(k, z, value):
        out_ref[k, z] = value

    finish_hops(
        shape, psi_ref, links, total_ref, carried_y, carried_t, halo, store
    )
    emit_messages(shape, out_ref, links, messages)


def sums_row(shape, two, start, three, one):
    sums = local_sums(shape, two, start) + local_sums(shape, three, one)
    lane = lax.broadcasted_iota(jnp.int32, (1, shape.lanes), 1)
    row = jnp.zeros((1, shape.lanes), jnp.float32)
    for k, value in enumerate(sums):
        row = jnp.where(lane == k, value, row)
    return row


def inner_sums_kernel(
    shape, psi_ref, links_ref, start_ref, one_ref, two_ref, total_ref, copies_ref
):
    row = sums_row(shape, two_ref, start_ref, psi_ref, one_ref)
    copies_ref[...] = jnp.broadcast_to(row[None], copies_ref.shape)
    inner_kernel(shape, psi_ref, links_ref, total_ref)


def finish_kernel(shape, psi_ref, links_ref, total_ref, carried_y, carried_t, *refs):
    halo, out_ref = refs[:5], refs[5]

    def store(k, z, value):
        out_ref[k, z] = value

    finish_hops(
        shape, psi_ref, Links(links_ref), total_ref, carried_y, carried_t, halo, store
    )


def scalars(table, entries):
    columns = [table[:, k : k + 1] for k in range(8)]
    factor_two, start_square, two_square, two_mixed = columns[:4]
    factor_three, one_square, three_square, three_mixed = columns[4:]

    def over_devices(column):
        return jnp.sum(column, axis=0, keepdims=True)

    norm_square = over_devices(start_square) / entries + epsilon
    alpha_one = over_devices(one_square) / entries / norm_square
    gap = alpha_one - factor_two
    remain_square = over_devices(two_square - gap * (2.0 * two_mixed - gap * start_square)) / entries
    overlap = over_devices(two_mixed - gap * start_square) / entries
    gap = alpha_one - factor_three
    image_square = over_devices(three_square - gap * (2.0 * three_mixed - gap * one_square)) / entries
    norm = jnp.sqrt(norm_square)
    beta_one = jnp.sqrt(remain_square / norm_square + epsilon)
    overlap = overlap / (norm_square * beta_one)
    alpha_two = image_square / (norm_square * beta_one * beta_one) - beta_one * overlap
    scale = 1.0 / (norm * beta_one)
    return alpha_one, beta_one, alpha_two, scale, beta_one / norm


def last_kernel(
    shape, entries, start_ref, two_ref, four_ref, gathered, out_ref, coefficients
):
    alpha_one, beta_one, alpha_two, scale, first_factor = scalars(gathered[:, 0, :], entries)
    t, z_extent = shape.t, shape.z
    for k in range(24):
        for z in range(z_extent):
            two, start = two_ref[k, z], start_ref[k, z]
            remain = two - alpha_one * start
            result = (four_ref[k, z] - alpha_one * two - alpha_two * remain) * scale
            result = result - first_factor * start
            out_ref[pl.ds(k * t * z_extent + z, t, stride=z_extent), :] = result[0:t]
    coefficients[0] = alpha_one[0, 0]
    coefficients[1] = beta_one[0, 0]
    coefficients[2] = alpha_two[0, 0]


def swap(value, axis, second):
    count = math.prod(lax.axis_size(name) for name in (axis if isinstance(axis, tuple) else (axis,)))
    pairs = []
    for low in range(1 if second else 0, count, 2):
        high = (low + 1) % count
        pairs += [(low, high), (high, low)]
    return lax.ppermute(value, axis, pairs)


def exchange(messages, lanes):
    z_second, t_second, z_first, t_first, y_msg = messages
    halo = (
        swap(z_second, "gz", True),
        swap(t_second, "ta", True),
        swap(z_first, "gz", False),
        swap(t_first, "ta", False),
    )
    y_halo = swap(y_msg, "gy", False)
    if lax.axis_size("gy") > 2:
        even = lax.axis_index("gy") % 2 == 0
        lane = lax.broadcasted_iota(jnp.int32, y_msg.shape, y_msg.ndim - 1)
        y_halo = jnp.where((lane < lanes // 2) == even, y_halo, swap(y_msg, "gy", True))
    return (*halo, y_halo)


def from_everyone(copies):
    return lax.all_to_all(copies, ("ta", "gz", "gy"), split_axis=0, concat_axis=0, tiled=True)


def shards(source, gauge_links):
    devices_all = lax.axis_size("ta") * lax.axis_size("gz") * lax.axis_size("gy")
    entries = float(source.size * devices_all)
    shape = Shape(source.shape[3], source.shape[4], source.shape[5])
    t, z, rows, lanes = shape.t, shape.z, shape.rows, shape.lanes
    vmem = pl.BlockSpec(memory_space=pltpu.VMEM)
    smem = pl.BlockSpec(memory_space=pltpu.SMEM)

    def held(*dims):
        return pltpu.VMEM(dims, jnp.float32)

    field = held(24, z, rows, lanes)
    half = held(12, z, rows, lanes)
    z_face, t_face = held(12 * t, lanes), held(12 * z, lanes)
    messages = (z_face, t_face, z_face, t_face, half, half, half)

    def call(kernel, name, flops, out_shape, operands, out_specs=None, in_spec=vmem, scratch=()):
        return pl.pallas_call(
            kernel,
            name=name,
            out_shape=out_shape,
            in_specs=[in_spec] * len(operands),
            out_specs=out_specs or jax.tree.map(lambda _: vmem, out_shape),
            scratch_shapes=scratch,
            compiler_params=pltpu.CompilerParams(vmem_limit_bytes=8 << 20),
            cost_estimate=pl.CostEstimate(flops=flops, bytes_accessed=1 << 20, transcendentals=0),
        )(*operands)

    sites = t * z * lanes
    psi, links, *sent = call(
        functools.partial(prep_kernel, shape), "prep", 400 * sites,
        (field, held(72, z, rows, lanes), *messages),
        (
            pltpu.with_memory_space_constraint(source.reshape(24 * t * z, lanes), pltpu.HBM),
            pltpu.with_memory_space_constraint(gauge_links.reshape(72 * t * z, lanes), pltpu.HBM),
        ),
        in_spec=pl.BlockSpec(memory_space=pltpu.HBM),
        scratch=(
            held(24 * t * z, lanes), held(72 * t * z, lanes), pltpu.SemaphoreType.DMA((5,)),
        ),
    )
    powers = [psi]
    for step in range(3):
        halo = exchange(sent[:5], lanes)
        inner = functools.partial(inner_kernel, shape)
        total = call(inner, "inner", 700 * sites, field, (psi, links))
        psi, *sent = call(
            functools.partial(mid_kernel, shape), "mid", 1000 * sites,
            (field, *messages), (psi, links, total, *sent[5:], *halo),
        )
        powers.append(psi)
    halo = exchange(sent[:5], lanes)
    total, copies = call(
        functools.partial(inner_sums_kernel, shape), "inner_sums", 1100 * sites,
        (field, held(devices_all, 1, lanes)), (psi, links, *powers[:3]),
    )
    gathered = from_everyone(copies)
    four = call(
        functools.partial(finish_kernel, shape), "finish", 700 * sites, field,
        (psi, links, total, *sent[5:], *halo),
    )
    residual, coefficients = call(
        functools.partial(last_kernel, shape, entries), "last", 100 * sites,
        (
            jax.ShapeDtypeStruct((24 * t * z, lanes), jnp.float32),
            jax.ShapeDtypeStruct((3,), jnp.float32),
        ),
        (powers[0], powers[2], four, gathered), (vmem, smem),
    )
    return (residual.reshape(source.shape), coefficients)


class ChipShape(Shape):
    def __init__(self, t_extent, z_extent, lanes):
        super().__init__(t_extent, z_extent, lanes)
        self.parts = 2 * z_extent
        self.z_rows = 24 * t_extent
        self.t_rows = 12 * self.parts

    def block(self, k, part):
        first = (k * self.parts + part) * self.rows
        return pl.ds(first, self.rows)

    def edge(self, k, row):
        return pl.ds(k * self.parts * self.rows + row, self.parts, stride=self.rows)


class ChipLinks:
    def __init__(self, shape, ref, row=None):
        self.shape, self.ref, self.row = shape, ref, row

    def __getitem__(self, index):
        direction, row, col, part = index
        first = ((direction * 3 + row) * 3 + col) * 2
        if self.row is None:
            return tuple(self.ref[self.shape.block(first + n, part), :] for n in range(2))
        return tuple(self.ref[self.shape.edge(first + n, self.row), :] for n in range(2))


def components(spins):
    return [(s, c, part, (s * 3 + c) * 2 + part) for s in range(spins) for c in range(3) for part in range(2)]


def gathered_pairs(spins, value):
    out = {}
    for s in range(spins):
        for c in range(3):
            out[s, c] = tuple(value((s * 3 + c) * 2 + part) for part in range(2))
    return out


def chip_psi(shape, ref, part):
    return gathered_pairs(4, lambda k: ref[shape.block(k, part), :])


def chip_edge(shape, ref, row):
    return gathered_pairs(4, lambda k: ref[shape.edge(k, row), :])


def chip_messages(shape, psi_ref, links_ref, z_second, t_second, z_first, t_first):
    t, last = shape.t, shape.t - 1
    even = is_even("ta")
    minus = project(chip_edge(shape, psi_ref, 0), 3, -1)
    half = project(chip_edge(shape, psi_ref, last), 3, 1)
    carried = mul_link_dag(ChipLinks(shape, links_ref, last), 3, 0, half)
    for s, c, part, k in components(2):
        rows = pl.ds(k * shape.parts, shape.parts)
        up, down = carried[s, c][part], minus[s, c][part]
        t_first[rows, :] = either(even, up, down)
        t_second[rows, :] = either(even, down, up)
    even = is_even("gy")
    links = ChipLinks(shape, links_ref)
    for y_half in range(2):
        minus = project(chip_psi(shape, psi_ref, y_half), 2, -1)
        part_last = shape.parts - 2 + y_half
        half = project(chip_psi(shape, psi_ref, part_last), 2, 1)
        carried = mul_link_dag(links, 2, part_last, half)
        for s, c, part, k in components(2):
            rows = pl.ds((k * 2 + y_half) * t, t)
            up, down = carried[s, c][part][0:t], minus[s, c][part][0:t]
            z_first[rows, :] = either(even, up, down)
            z_second[rows, :] = either(even, down, up)


def chip_bring(shape, y_half, source_ref, links_in, psi_ref, links_ref, arrived):
    t, z_extent = shape.t, 2 * shape.z
    first_plane = lax.axis_index("gy") * shape.z
    last = lax.broadcasted_iota(jnp.int32, (t, shape.lanes), 0) == t - 1
    sign = jnp.where(lax.axis_index("ta") == lax.axis_size("ta") - 1, -1.0, 1.0)
    flip = jnp.where(last, sign, 1.0)

    def bring(in_ref, out_ref, k, z, factor=None):
        value = in_ref[pl.ds(k * t * z_extent + first_plane + z, t, stride=z_extent), :]
        if factor is not None:
            value = value * factor
        at = (k * shape.parts + 2 * z + y_half) * shape.rows
        out_ref[pl.ds(pl.multiple_of(at, 8), t), :] = value

    arrived(4)
    for z in range(shape.z):
        for k in range(24):
            bring(source_ref, psi_ref, k, z)
    for direction in (3, 2, 1, 0):
        arrived(direction)
        for z in range(shape.z):
            for k in range(18 * direction, 18 * direction + 18):
                bring(links_in, links_ref, k, z, flip if direction == 3 else None)


def chip_own_kernel(
    shape, source_hbm, links_hbm, psi_ref, links_ref, rest_ref, source_ref, links_in, semaphores
):
    part = 18 * shape.t * 2 * shape.z
    copies = {4: pltpu.make_async_copy(source_hbm, source_ref, semaphores.at[4])}
    for direction in (3, 2, 1, 0):
        rows = pl.ds(direction * part, part)
        copies[direction] = pltpu.make_async_copy(
            links_hbm.at[rows], links_in.at[rows], semaphores.at[direction]
        )
    for copy in copies.values():
        copy.start()
    if shape.rows != shape.t:
        links_ref[...] = jnp.zeros_like(links_ref)
        psi_ref[...] = jnp.zeros_like(psi_ref)
    chip_bring(
        shape, lax.axis_index("gy"), source_ref, links_in, psi_ref, links_ref,
        lambda n: copies[n].wait(),
    )
    t, z_extent = shape.t, 2 * shape.z
    first_plane = (1 - lax.axis_index("gy")) * shape.z
    if shape.rows != t:
        rest_ref[...] = jnp.zeros_like(rest_ref)
    for k in range(24):
        for z in range(shape.z):
            value = source_ref[pl.ds(k * t * z_extent + first_plane + z, t, stride=z_extent), :]
            rest_ref[pl.ds((k * shape.z + z) * shape.rows, t), :] = value


def chip_prep_kernel(
    shape, source_ref, links_in, psi_in, links_held, psi_ref, links_ref, *messages
):
    chip_bring(
        shape, 1 - lax.axis_index("gy"), source_ref, links_in, psi_ref, links_ref, lambda n: None
    )
    chip_messages(shape, psi_ref, links_ref, *messages)


def chip_inner_kernel(shape, psi_ref, links_ref, total_ref):
    links = ChipLinks(shape, links_ref)
    lane, row = shape.lane(), shape.row()
    x = lane % X
    lanes, rows, t = shape.lanes, shape.rows, shape.t
    at_end, at_start = x == X - 1, x == 0
    inside_ahead = row < t - 1
    inside_behind = jnp.logical_and(row > 0, row < t)

    def x_ahead(value):
        return jnp.where(
            at_end, pltpu.roll(value, X - 1, 1), pltpu.roll(value, lanes - 1, 1)
        )

    def x_behind(value):
        return jnp.where(at_start, pltpu.roll(value, lanes - X + 1, 1), pltpu.roll(value, 1, 1))

    def t_ahead(value):
        return jnp.where(inside_ahead, pltpu.roll(value, rows - 1, 0), 0.0)

    def t_behind(value):
        return jnp.where(inside_behind, pltpu.roll(value, 1, 0), 0.0)

    for z in range(shape.z):
        for part in (2 * z, 2 * z + 1):
            psi = chip_psi(shape, psi_ref, part)
            zero = jnp.zeros((rows, lanes), jnp.float32)
            total = {key: (zero, zero) for key in psi}
            half = mapped(x_ahead, project(psi, 0, -1))
            add_rebuilt(total, mul_link(links, 0, part, half), 0, -1)
            half = mapped(x_behind, mul_link_dag(links, 0, part, project(psi, 0, 1)))
            add_rebuilt(total, half, 0, 1)
            half = mapped(t_ahead, project(psi, 3, -1))
            add_rebuilt(total, mul_link(links, 3, part, half), 3, -1)
            half = mapped(t_behind, mul_link_dag(links, 3, part, project(psi, 3, 1)))
            add_rebuilt(total, half, 3, 1)
            if z + 1 < shape.z:
                half = project(chip_psi(shape, psi_ref, part + 2), 2, -1)
                add_rebuilt(total, mul_link(links, 2, part, half), 2, -1)
            if z > 0:
                half = project(chip_psi(shape, psi_ref, part - 2), 2, 1)
                add_rebuilt(total, mul_link_dag(links, 2, part - 2, half), 2, 1)
            for s, c, n, k in components(4):
                total_ref[shape.block(k, part), :] = total[s, c][n]
        pair = (2 * z, 2 * z + 1)
        minus, carried = [], []
        for part in pair:
            psi = chip_psi(shape, psi_ref, part)
            minus.append(mapped(lambda v: pltpu.roll(v, lanes - X, 1), project(psi, 1, -1)))
            half = mul_link_dag(links, 1, part, project(psi, 1, 1))
            carried.append(mapped(lambda v: pltpu.roll(v, X, 1), half))
        for own, part in enumerate(pair):
            total = chip_psi(shape, total_ref, part)
            half = mapped(
                lambda a, b: jnp.where(lane >= lanes - X, b, a), minus[own], minus[1 - own]
            )
            add_rebuilt(total, mul_link(links, 1, part, half), 1, -1)
            half = mapped(lambda a, b: jnp.where(lane < X, b, a), carried[own], carried[1 - own])
            add_rebuilt(total, half, 1, 1)
            for s, c, n, k in components(4):
                total_ref[shape.block(k, part), :] = total[s, c][n]


def chip_finish(shape, psi_ref, links_ref, total_ref, received, scratch, out_ref):
    z_second, t_second, z_first, t_first = received
    z_down, z_up = scratch
    t_even, z_even = is_even("ta"), is_even("gy")
    t, rows, lanes, parts = shape.t, shape.rows, shape.lanes, shape.parts
    z_down[...] = either(z_even, z_first[...], z_second[...])
    z_up[...] = either(z_even, z_second[...], z_first[...])
    links = ChipLinks(shape, links_ref)

    def plane(ref, y_half):
        def value(k):
            face = ref[pl.ds((k * 2 + y_half) * t, t), :]
            if rows != t:
                pad = jnp.zeros((rows - t, lanes), jnp.float32)
                face = jnp.concatenate([face, pad], axis=0)
            return face

        return gathered_pairs(2, value)

    for part in range(parts):
        total = chip_psi(shape, total_ref, part)
        if part >= parts - 2:
            half = mul_link(links, 2, part, plane(z_down, part - parts + 2))
            add_rebuilt(total, half, 2, -1)
        if part < 2:
            add_rebuilt(total, plane(z_up, part), 2, 1)
        for s, c, n, k in components(4):
            value = psi_ref[shape.block(k, part), :] - hop_kappa * total[s, c][n]
            out_ref[shape.block(k, part), :] = value if s < 2 else -value

    def t_half(from_even, from_odd):
        def value(k):
            at = pl.ds(k * parts, parts)
            return either(t_even, from_even[at, :], from_odd[at, :])

        return gathered_pairs(2, value)

    down = mul_link(ChipLinks(shape, links_ref, t - 1), 3, 0, t_half(t_first, t_second))
    up = t_half(t_second, t_first)
    zero = jnp.zeros((parts, lanes), jnp.float32)
    for half, parity, row in ((down, -1, t - 1), (up, 1, 0)):
        total = {(s, c): (zero, zero) for s in range(4) for c in range(3)}
        add_rebuilt(total, half, 3, parity)
        for s, c, n, k in components(4):
            at = shape.edge(k, row)
            value = hop_kappa * total[s, c][n]
            out_ref[at, :] = out_ref[at, :] - (value if s < 2 else -value)


def chip_mid_kernel(shape, hands_over, psi_ref, links_ref, total_ref, *refs):
    received, out_ref, messages, refs = refs[:4], refs[4], refs[5:9], refs[9:]
    chip_finish(shape, psi_ref, links_ref, total_ref, received, refs[-2:], out_ref)
    chip_messages(shape, out_ref, links_ref, *messages)
    if hands_over:
        hand_over(shape, out_ref, refs[0])


def chip_sums_kernel(shape, start_ref, one_ref, two_ref, three_ref, table_ref):
    class View:
        def __init__(self, ref):
            self.ref = ref

        def __getitem__(self, index):
            return self.ref[shape.block(*index), :]

    wide = ChipShape(shape.t, shape.z, shape.lanes)
    wide.z = shape.parts
    row = sums_row(wide, View(two_ref), View(start_ref), View(three_ref), View(one_ref))
    index = lax.axis_index("ta") * lax.axis_size("gz") + lax.axis_index("gz")
    index = index * 2 + lax.axis_index("gy")
    mine = lax.broadcasted_iota(jnp.int32, table_ref.shape, 0) == index
    table_ref[...] = jnp.where(mine, jnp.broadcast_to(row, table_ref.shape), 0.0)


def y_part(shape, k, z, y_half):
    return pl.ds(pl.multiple_of((k * shape.parts + 2 * z + y_half) * shape.rows, 8), shape.rows)


def rest_rows(shape, k, z):
    return pl.ds((k * shape.z + z) * shape.rows, shape.rows)


def hand_over(shape, ref, rest_ref):
    y_half = 1 - lax.axis_index("gy")
    for k in range(24):
        for z in range(shape.z):
            rest_ref[rest_rows(shape, k, z), :] = ref[y_part(shape, k, z, y_half), :]


def chip_finish_kernel(shape, psi_ref, links_ref, total_ref, *refs):
    received, (out_ref, rest_ref), scratch = refs[:4], refs[4:6], refs[6:]
    chip_finish(shape, psi_ref, links_ref, total_ref, received, scratch, out_ref)
    hand_over(shape, out_ref, rest_ref)


def chip_last_kernel(
    shape, entries, start_ref, two_ref, four_ref, start_rest, two_rest, four_rest, table_ref,
    out_ref, coefficients,
):
    alpha_one, beta_one, alpha_two, scale, first_factor = scalars(table_ref[...], entries)
    t, z_extent = shape.t, 2 * shape.z
    core = lax.axis_index("gy")

    def put(k, z, start, two, four):
        remain = two - alpha_one * start
        result = (four - alpha_one * two - alpha_two * remain) * scale - first_factor * start
        out_ref[pl.ds(k * t * z_extent + z, t, stride=z_extent), :] = result[0:t]

    for k in range(24):
        for z in range(shape.z):
            rows = y_part(shape, k, z, core)
            own = (ref[rows, :] for ref in (start_ref, two_ref, four_ref))
            put(k, core * shape.z + z, *own)
            rows = rest_rows(shape, k, z)
            other = (ref[rows, :] for ref in (start_rest, two_rest, four_rest))
            put(k, (1 - core) * shape.z + z, *other)
    coefficients[0] = alpha_one[0, 0]
    coefficients[1] = beta_one[0, 0]
    coefficients[2] = alpha_two[0, 0]


def filled(table):
    for axis in ("gy", "gz", "ta"):
        count, step = lax.axis_size(axis), 1
        while step < count:
            table = table + lax.ppermute(table, axis, [(i, i ^ step) for i in range(count)])
            step *= 2
    return table


def is_power(count):
    return count & (count - 1) == 0


def chip_shards(source, gauge_links):
    devices_all = lax.axis_size("ta") * lax.axis_size("gz") * 2
    entries = float(source.size * devices_all)
    z_extent = source.shape[4]
    shape = ChipShape(source.shape[3], z_extent // 2, source.shape[5])
    t, rows, lanes = shape.t, shape.rows, shape.lanes
    vmem = pl.BlockSpec(memory_space=pltpu.VMEM)
    smem = pl.BlockSpec(memory_space=pltpu.SMEM)

    def held(*dims):
        return pltpu.VMEM(dims, jnp.float32)

    field = held(24 * shape.parts * rows, lanes)
    links_field = held(72 * shape.parts * rows, lanes)
    z_face, t_face = held(shape.z_rows, lanes), held(shape.t_rows, lanes)
    messages = (z_face, t_face, z_face, t_face)
    z_faces = (z_face, z_face)

    def call(kernel, name, flops, out_shape, operands, **options):
        in_spec = options.pop("in_spec", vmem)
        out_specs = options.pop("out_specs", jax.tree.map(lambda _: vmem, out_shape))
        return pl.pallas_call(
            kernel,
            name=name,
            out_shape=out_shape,
            in_specs=[in_spec] * len(operands),
            out_specs=out_specs,
            compiler_params=pltpu.CompilerParams(vmem_limit_bytes=8 << 20),
            cost_estimate=pl.CostEstimate(flops=flops, bytes_accessed=1 << 20, transcendentals=0),
            **options,
        )(*operands)

    def exchanged(sent):
        z_second, t_second, z_first, t_first = sent
        z_ring = ("gz", "gy")
        return (
            swap(z_second, z_ring, True), swap(t_second, "ta", True),
            swap(z_first, z_ring, False), swap(t_first, "ta", False),
        )

    sites = t * z_extent * lanes
    rows_in = t * z_extent
    own = (source.reshape(24 * rows_in, lanes), gauge_links.reshape(72 * rows_in, lanes))
    other = tuple(swap(value, "gy", False) for value in own)
    rest = held(24 * shape.z * rows, lanes)
    psi, links, start_rest = call(
        functools.partial(chip_own_kernel, shape), "own", 200 * sites, (field, links_field, rest),
        [pltpu.with_memory_space_constraint(value, pltpu.HBM) for value in own],
        scratch_shapes=(
            held(24 * rows_in, lanes), held(72 * rows_in, lanes), pltpu.SemaphoreType.DMA((5,)),
        ),
        in_spec=pl.BlockSpec(memory_space=pltpu.HBM),
    )
    psi, links, *sent = call(
        functools.partial(chip_prep_kernel, shape), "prep", 400 * sites,
        (field, links_field, *messages), (*other, psi, links),
        input_output_aliases={2: 0, 3: 1},
    )
    powers = [psi]
    for step in range(3):
        halo = exchanged(sent)
        inner = functools.partial(chip_inner_kernel, shape)
        total = call(inner, "inner", 1000 * sites, field, (psi, links))
        hands_over = step == 1
        psi, *sent = call(
            functools.partial(chip_mid_kernel, shape, hands_over), "mid", 600 * sites,
            (field, *messages, rest) if hands_over else (field, *messages),
            (psi, links, total, *halo), scratch_shapes=z_faces,
        )
        powers.append(psi)
        if hands_over:
            two_rest = swap(sent.pop(), "gy", False)
    halo = exchanged(sent)
    table = call(
        functools.partial(chip_sums_kernel, shape), "sums", 400 * sites,
        held(devices_all, lanes), powers,
    )
    table = filled(table)
    total = call(inner, "inner", 1000 * sites, field, (psi, links))
    four, four_rest = call(
        functools.partial(chip_finish_kernel, shape), "finish", 400 * sites, (field, rest),
        (psi, links, total, *halo), scratch_shapes=z_faces,
    )
    four_rest = swap(four_rest, "gy", False)
    residual, coefficients = call(
        functools.partial(chip_last_kernel, shape, entries), "last", 100 * sites,
        (
            jax.ShapeDtypeStruct((24 * rows_in, lanes), jnp.float32),
            jax.ShapeDtypeStruct((3,), jnp.float32),
        ),
        (powers[0], powers[2], four, start_rest, two_rest, four_rest, table),
        out_specs=(vmem, smem),
    )
    return (residual.reshape(source.shape), coefficients)


def solution(mesh):
    placed = (P(None, None, None, "ta", "gz", "gy"), P(None, None, None, None, "ta", "gz", "gy"))
    sizes = mesh.shape
    by_chip = sizes["gy"] == 2 and is_power(sizes["ta"]) and is_power(sizes["gz"])
    return jax.shard_map(
        chip_shards if by_chip else shards,
        mesh=mesh,
        in_specs=placed,
        out_specs=(P(None, None, None, "ta", "gz", "gy"), P()),
        check_vma=False,
    )
```

```python
import functools
import math

import jax
import jax.numpy as jnp
from jax import lax
from jax.experimental import pallas as pl
from jax.experimental.pallas import tpu as pltpu
from jax.sharding import PartitionSpec as P

X = 32

hop_kappa = 0.19
epsilon = 1e-06
spin_table = (
    ((1, 0), (-1j, -1j)),
    ((1, 0), (-1, 1)),
    ((0, 1), (-1j, 1j)),
    ((0, 1), (1, 1)),
)
SPIN_COLOUR = [(spin, colour) for spin in range(2) for colour in range(3)]


def add_phased(left, phase, right):
    phase = complex(phase)
    if phase == 1:
        return (left[0] + right[0], left[1] + right[1])
    if phase == -1:
        return (left[0] - right[0], left[1] - right[1])
    if phase == 1j:
        return (left[0] - right[1], left[1] + right[0])
    return (left[0] + right[1], left[1] - right[0])


def project(psi, direction, parity):
    order, phases = spin_table[direction]
    return {
        (s, c): add_phased(psi[s, c], parity * phases[s], psi[2 + order[s], c])
        for s, c in SPIN_COLOUR
    }


def add_rebuilt(total, half, direction, parity):
    order, phases = spin_table[direction]
    for s, c in SPIN_COLOUR:
        total[s, c] = add_phased(total[s, c], 1, half[s, c])
        row = order[s]
        phase = parity * complex(phases[row]).conjugate()
        total[2 + s, c] = add_phased(total[2 + s, c], phase, half[row, c])


def mul_link(links, direction, z, half):
    out = {}
    for row in range(3):
        for s in range(2):
            real, imag = None, None
            for col in range(3):
                u_real, u_imag = links[direction, row, col, z]
                h_real, h_imag = half[s, col]
                term_real = u_real * h_real - u_imag * h_imag
                term_imag = u_real * h_imag + u_imag * h_real
                real = term_real if real is None else real + term_real
                imag = term_imag if imag is None else imag + term_imag
            out[s, row] = (real, imag)
    return out


def mul_link_dag(links, direction, z, half):
    out = {}
    for row in range(3):
        for s in range(2):
            real, imag = None, None
            for col in range(3):
                u_real, u_imag = links[direction, col, row, z]
                h_real, h_imag = half[s, col]
                term_real = u_real * h_real + u_imag * h_imag
                term_imag = u_real * h_imag - u_imag * h_real
                real = term_real if real is None else real + term_real
                imag = term_imag if imag is None else imag + term_imag
            out[s, row] = (real, imag)
    return out


def mapped(function, *halves):
    return {
        key: tuple(function(*(half[key][part] for half in halves)) for part in range(2))
        for key in SPIN_COLOUR
    }


class Links:
    def __init__(self, ref):
        self.ref = ref

    def __getitem__(self, index):
        direction, row, col, z = index
        first = ((direction * 3 + row) * 3 + col) * 2
        return (self.ref[first, z], self.ref[first + 1, z])


def load_psi(ref, z):
    return {
        (s, c): (ref[(s * 3 + c) * 2, z], ref[(s * 3 + c) * 2 + 1, z])
        for s in range(4)
        for c in range(3)
    }


def load_half(ref, z):
    return {
        (s, c): (ref[(s * 3 + c) * 2, z], ref[(s * 3 + c) * 2 + 1, z]) for s, c in SPIN_COLOUR
    }


def store_half(ref, z, half):
    for (s, c), pair in half.items():
        for part in range(2):
            ref[(s * 3 + c) * 2 + part, z] = pair[part]


class Shape:
    def __init__(self, t_extent, z_extent, lanes):
        self.t = t_extent
        self.z = z_extent
        self.rows = -(-t_extent // 8) * 8
        self.lanes = lanes

    def row(self):
        return lax.broadcasted_iota(jnp.int32, (self.rows, self.lanes), 0)

    def lane(self):
        return lax.broadcasted_iota(jnp.int32, (self.rows, self.lanes), 1)


def is_even(axis):
    return jnp.bitwise_and(lax.axis_index(axis), 1) == 0


def either(choice, first, second):
    return jnp.where(choice, first, second)


def emit_messages(shape, psi_ref, links, refs):
    z_second, t_second, z_first, t_first, y_msg, carried_y, carried_t = refs
    t_even, z_even = is_even("ta"), is_even("gz")
    lane = shape.lane()
    last_z, last_t = shape.z - 1, shape.t - 1
    for z in range(shape.z):
        psi = load_psi(psi_ref, z)
        minus = project(psi, 3, -1)
        carried = mul_link_dag(links, 3, z, project(psi, 3, 1))
        store_half(carried_t, z, carried)
        for s, c in SPIN_COLOUR:
            for part in range(2):
                at = ((s * 3 + c) * 2 + part) * shape.z + z
                down = minus[s, c][part][0:1]
                up = carried[s, c][part][last_t : last_t + 1]
                t_first[at : at + 1] = either(t_even, up, down)
                t_second[at : at + 1] = either(t_even, down, up)
        minus = project(psi, 1, -1)
        carried = mul_link_dag(links, 1, z, project(psi, 1, 1))
        store_half(carried_y, z, carried)
        store_half(
            y_msg,
            z,
            mapped(lambda low, high: jnp.where(lane < X, low, high), minus, carried),
        )
    minus = project(load_psi(psi_ref, 0), 2, -1)
    carried = mul_link_dag(links, 2, last_z, project(load_psi(psi_ref, last_z), 2, 1))
    for s, c in SPIN_COLOUR:
        for part in range(2):
            at = ((s * 3 + c) * 2 + part) * shape.t
            down, up = minus[s, c][part][0 : shape.t], carried[s, c][part][0 : shape.t]
            z_first[at : at + shape.t] = either(z_even, up, down)
            z_second[at : at + shape.t] = either(z_even, down, up)


def prep_kernel(shape, source_hbm, links_hbm, psi_ref, links_ref, *refs):
    messages, (source_ref, links_in, arrived) = refs[:-3], refs[-3:]
    t, z_extent = shape.t, shape.z
    part = 18 * t * z_extent
    copies = [pltpu.make_async_copy(source_hbm, source_ref, arrived.at[4])]
    for direction in (3, 2, 1, 0):
        rows = pl.ds(direction * part, part)
        copies.append(
            pltpu.make_async_copy(links_hbm.at[rows], links_in.at[rows], arrived.at[direction])
        )
    for copy in copies:
        copy.start()
    if shape.rows != t:
        links_ref[...] = jnp.zeros_like(links_ref)
        psi_ref[...] = jnp.zeros_like(psi_ref)
    last = lax.broadcasted_iota(jnp.int32, (t, shape.lanes), 0) == t - 1
    sign = jnp.where(lax.axis_index("ta") == lax.axis_size("ta") - 1, -1.0, 1.0)
    flip = jnp.where(last, sign, 1.0)
    copies[0].wait()
    for k in range(24):
        for z in range(z_extent):
            psi_ref[k, z, 0:t] = source_ref[pl.ds(k * t * z_extent + z, t, stride=z_extent), :]
    for direction in (3, 2, 1, 0):
        copies[4 - direction].wait()
        for k in range(18 * direction, 18 * direction + 18):
            for z in range(z_extent):
                value = links_in[pl.ds(k * t * z_extent + z, t, stride=z_extent), :]
                links_ref[k, z, 0:t] = value * flip if direction == 3 else value
    emit_messages(shape, psi_ref, Links(links_ref), messages)


def summed(shape, term):
    total = None
    for k in range(24):
        for z in range(shape.z):
            value = term(k, z)
            total = value if total is None else total + value
    return total


def over_lanes(total):
    return jnp.sum(jnp.sum(total, axis=0, keepdims=True), axis=1, keepdims=True)


def local_sums(shape, image, origin):
    square = summed(shape, lambda k, z: origin[k, z] * origin[k, z])
    mixed = over_lanes(summed(shape, lambda k, z: image[k, z] * origin[k, z]))
    whole = over_lanes(square)
    factor = jnp.where(whole > 0.0, mixed / jnp.where(whole > 0.0, whole, 1.0), 0.0)
    spread = jnp.broadcast_to(factor, (shape.rows, shape.lanes))
    rest_square, rest_mixed = None, None
    for k in range(24):
        for z in range(shape.z):
            start = origin[k, z]
            rest = image[k, z] - spread * start
            terms = rest * rest, rest * start
            if rest_square is None:
                rest_square, rest_mixed = terms
            else:
                rest_square, rest_mixed = rest_square + terms[0], rest_mixed + terms[1]
    return [factor, *(over_lanes(value) for value in (square, rest_square, rest_mixed))]


def inner_kernel(shape, psi_ref, links_ref, total_ref):
    links = Links(links_ref)
    x = shape.lane() % X
    lanes = shape.lanes
    at_end, at_start = x == X - 1, x == 0

    def ahead(value):
        return jnp.where(
            at_end, pltpu.roll(value, X - 1, 1), pltpu.roll(value, lanes - 1, 1)
        )

    def behind(value):
        return jnp.where(at_start, pltpu.roll(value, lanes - X + 1, 1), pltpu.roll(value, 1, 1))

    for z in range(shape.z):
        psi = load_psi(psi_ref, z)
        zero = jnp.zeros((shape.rows, lanes), jnp.float32)
        total = {key: (zero, zero) for key in psi}
        half = mapped(ahead, project(psi, 0, -1))
        add_rebuilt(total, mul_link(links, 0, z, half), 0, -1)
        half = mapped(behind, mul_link_dag(links, 0, z, project(psi, 0, 1)))
        add_rebuilt(total, half, 0, 1)
        if z + 1 < shape.z:
            half = project(load_psi(psi_ref, z + 1), 2, -1)
            add_rebuilt(total, mul_link(links, 2, z, half), 2, -1)
        if z > 0:
            half = project(load_psi(psi_ref, z - 1), 2, 1)
            add_rebuilt(total, mul_link_dag(links, 2, z - 1, half), 2, 1)
        for (s, c), pair in total.items():
            for part in range(2):
                total_ref[(s * 3 + c) * 2 + part, z] = pair[part]


def add_y_hops(shape, z, psi, total, links, carried_y, y_halo):
    lane, lanes = shape.lane(), shape.lanes
    received = load_half(y_halo, z)
    half = mapped(
        lambda own, other: pltpu.roll(jnp.where(lane < X, other, own), lanes - X, 1),
        project(psi, 1, -1),
        received,
    )
    add_rebuilt(total, mul_link(links, 1, z, half), 1, -1)
    half = mapped(
        lambda own, other: pltpu.roll(jnp.where(lane >= lanes - X, other, own), X, 1),
        load_half(carried_y, z),
        received,
    )
    add_rebuilt(total, half, 1, 1)


def finish_hops(
    shape, psi_ref, links, total_ref, carried_y, carried_t, halo, store
):
    z_second, t_second, z_first, t_first, y_msg = halo
    t_even, z_even = is_even("ta"), is_even("gz")
    row = shape.row()
    lanes, rows, t = shape.lanes, shape.rows, shape.t
    last_z = shape.z - 1

    for z in range(shape.z):
        psi = load_psi(psi_ref, z)
        total = load_psi(total_ref, z)

        def rim_rows(from_even, from_odd):
            half = {}
            for s, c in SPIN_COLOUR:
                ats = [((s * 3 + c) * 2 + part) * shape.z + z for part in range(2)]
                half[s, c] = tuple(
                    jnp.broadcast_to(
                        either(t_even, from_even[at : at + 1], from_odd[at : at + 1]),
                        (rows, lanes),
                    )
                    for at in ats
                )
            return half

        def rim_plane(from_even, from_odd):
            half = {}
            for s, c in SPIN_COLOUR:
                pair = []
                for part in range(2):
                    at = ((s * 3 + c) * 2 + part) * t
                    plane = either(z_even, from_even[at : at + t], from_odd[at : at + t])
                    if rows != t:
                        pad = jnp.zeros((rows - t, lanes), jnp.float32)
                        plane = jnp.concatenate([plane, pad], axis=0)
                    pair.append(plane)
                half[s, c] = tuple(pair)
            return half

        if y_msg is not None:
            add_y_hops(shape, z, psi, total, links, carried_y, y_msg)
        if z == last_z:
            add_rebuilt(total, mul_link(links, 2, z, rim_plane(z_first, z_second)), 2, -1)
        if z == 0:
            add_rebuilt(total, rim_plane(z_second, z_first), 2, 1)
        half = mapped(
            lambda own, other: jnp.where(row == t - 1, other, pltpu.roll(own, rows - 1, 0)),
            project(psi, 3, -1),
            rim_rows(t_first, t_second),
        )
        add_rebuilt(total, mul_link(links, 3, z, half), 3, -1)
        half = mapped(
            lambda own, other: jnp.where(row == 0, other, pltpu.roll(own, 1, 0)),
            load_half(carried_t, z),
            rim_rows(t_second, t_first),
        )
        add_rebuilt(total, half, 3, 1)
        for (s, c), pair in total.items():
            for part in range(2):
                value = psi[s, c][part] - hop_kappa * pair[part]
                value = value if s < 2 else -value
                if rows != t:
                    value = jnp.where(row < t, value, 0.0)
                store((s * 3 + c) * 2 + part, z, value)


def mid_kernel(shape, psi_ref, links_ref, total_ref, carried_y, carried_t, *refs):
    halo, out_ref, messages = refs[:5], refs[5], refs[6:]
    links = Links(links_ref)

    def store(k, z, value):
        out_ref[k, z] = value

    finish_hops(
        shape, psi_ref, links, total_ref, carried_y, carried_t, halo, store
    )
    emit_messages(shape, out_ref, links, messages)


def sums_row(shape, two, start, three, one):
    sums = local_sums(shape, two, start) + local_sums(shape, three, one)
    lane = lax.broadcasted_iota(jnp.int32, (1, shape.lanes), 1)
    row = jnp.zeros((1, shape.lanes), jnp.float32)
    for k, value in enumerate(sums):
        row = jnp.where(lane == k, value, row)
    return row


def inner_sums_kernel(
    shape, psi_ref, links_ref, start_ref, one_ref, two_ref, total_ref, copies_ref
):
    row = sums_row(shape, two_ref, start_ref, psi_ref, one_ref)
    copies_ref[...] = jnp.broadcast_to(row[None], copies_ref.shape)
    inner_kernel(shape, psi_ref, links_ref, total_ref)


def finish_kernel(shape, psi_ref, links_ref, total_ref, carried_y, carried_t, *refs):
    halo, out_ref = refs[:5], refs[5]

    def store(k, z, value):
        out_ref[k, z] = value

    finish_hops(
        shape, psi_ref, Links(links_ref), total_ref, carried_y, carried_t, halo, store
    )


def scalars(gathered, entries):
    table = gathered[:, 0, :]
    columns = [table[:, k : k + 1] for k in range(8)]
    factor_two, start_square, two_square, two_mixed = columns[:4]
    factor_three, one_square, three_square, three_mixed = columns[4:]

    def over_devices(column):
        return jnp.sum(column, axis=0, keepdims=True)

    norm_square = over_devices(start_square) / entries + epsilon
    alpha_one = over_devices(one_square) / entries / norm_square
    gap = alpha_one - factor_two
    remain_square = over_devices(two_square - gap * (2.0 * two_mixed - gap * start_square)) / entries
    overlap = over_devices(two_mixed - gap * start_square) / entries
    gap = alpha_one - factor_three
    image_square = over_devices(three_square - gap * (2.0 * three_mixed - gap * one_square)) / entries
    norm = jnp.sqrt(norm_square)
    beta_one = jnp.sqrt(remain_square / norm_square + epsilon)
    overlap = overlap / (norm_square * beta_one)
    alpha_two = image_square / (norm_square * beta_one * beta_one) - beta_one * overlap
    scale = 1.0 / (norm * beta_one)
    return alpha_one, beta_one, alpha_two, scale, beta_one / norm


def last_kernel(
    shape, entries, start_ref, two_ref, four_ref, gathered, out_ref, coefficients
):
    alpha_one, beta_one, alpha_two, scale, first_factor = scalars(gathered, entries)
    t, z_extent = shape.t, shape.z
    for k in range(24):
        for z in range(z_extent):
            two, start = two_ref[k, z], start_ref[k, z]
            remain = two - alpha_one * start
            result = (four_ref[k, z] - alpha_one * two - alpha_two * remain) * scale
            result = result - first_factor * start
            out_ref[pl.ds(k * t * z_extent + z, t, stride=z_extent), :] = result[0:t]
    coefficients[0] = alpha_one[0, 0]
    coefficients[1] = beta_one[0, 0]
    coefficients[2] = alpha_two[0, 0]


def swap(value, axis, second):
    count = math.prod(lax.axis_size(name) for name in (axis if isinstance(axis, tuple) else (axis,)))
    pairs = []
    for low in range(1 if second else 0, count, 2):
        high = (low + 1) % count
        pairs += [(low, high), (high, low)]
    return lax.ppermute(value, axis, pairs)


def exchange(messages, lanes):
    z_second, t_second, z_first, t_first, y_msg = messages
    halo = (
        swap(z_second, "gz", True),
        swap(t_second, "ta", True),
        swap(z_first, "gz", False),
        swap(t_first, "ta", False),
    )
    y_halo = swap(y_msg, "gy", False)
    if lax.axis_size("gy") > 2:
        even = lax.axis_index("gy") % 2 == 0
        lane = lax.broadcasted_iota(jnp.int32, y_msg.shape, y_msg.ndim - 1)
        y_halo = jnp.where((lane < lanes // 2) == even, y_halo, swap(y_msg, "gy", True))
    return (*halo, y_halo)


def from_everyone(copies):
    return lax.all_to_all(copies, ("ta", "gz", "gy"), split_axis=0, concat_axis=0, tiled=True)


def shards(source, gauge_links):
    devices_all = lax.axis_size("ta") * lax.axis_size("gz") * lax.axis_size("gy")
    entries = float(source.size * devices_all)
    shape = Shape(source.shape[3], source.shape[4], source.shape[5])
    t, z, rows, lanes = shape.t, shape.z, shape.rows, shape.lanes
    vmem = pl.BlockSpec(memory_space=pltpu.VMEM)
    smem = pl.BlockSpec(memory_space=pltpu.SMEM)

    def held(*dims):
        return pltpu.VMEM(dims, jnp.float32)

    field = held(24, z, rows, lanes)
    half = held(12, z, rows, lanes)
    z_face, t_face = held(12 * t, lanes), held(12 * z, lanes)
    messages = (z_face, t_face, z_face, t_face, half, half, half)

    def call(kernel, name, flops, out_shape, operands, out_specs=None, in_spec=vmem, scratch=()):
        return pl.pallas_call(
            kernel,
            name=name,
            out_shape=out_shape,
            in_specs=[in_spec] * len(operands),
            out_specs=out_specs or jax.tree.map(lambda _: vmem, out_shape),
            scratch_shapes=scratch,
            compiler_params=pltpu.CompilerParams(vmem_limit_bytes=8 << 20),
            cost_estimate=pl.CostEstimate(flops=flops, bytes_accessed=1 << 20, transcendentals=0),
        )(*operands)

    sites = t * z * lanes
    psi, links, *sent = call(
        functools.partial(prep_kernel, shape), "prep", 400 * sites,
        (field, held(72, z, rows, lanes), *messages),
        (
            pltpu.with_memory_space_constraint(source.reshape(24 * t * z, lanes), pltpu.HBM),
            pltpu.with_memory_space_constraint(gauge_links.reshape(72 * t * z, lanes), pltpu.HBM),
        ),
        in_spec=pl.BlockSpec(memory_space=pltpu.HBM),
        scratch=(
            held(24 * t * z, lanes), held(72 * t * z, lanes), pltpu.SemaphoreType.DMA((5,)),
        ),
    )
    powers = [psi]
    for step in range(3):
        halo = exchange(sent[:5], lanes)
        inner = functools.partial(inner_kernel, shape)
        total = call(inner, "inner", 700 * sites, field, (psi, links))
        psi, *sent = call(
            functools.partial(mid_kernel, shape), "mid", 1000 * sites,
            (field, *messages), (psi, links, total, *sent[5:], *halo),
        )
        powers.append(psi)
    halo = exchange(sent[:5], lanes)
    total, copies = call(
        functools.partial(inner_sums_kernel, shape), "inner_sums", 1100 * sites,
        (field, held(devices_all, 8, lanes)), (psi, links, *powers[:3]),
    )
    gathered = from_everyone(copies)
    four = call(
        functools.partial(finish_kernel, shape), "finish", 700 * sites, field,
        (psi, links, total, *sent[5:], *halo),
    )
    residual, coefficients = call(
        functools.partial(last_kernel, shape, entries), "last", 100 * sites,
        (
            jax.ShapeDtypeStruct((24 * t * z, lanes), jnp.float32),
            jax.ShapeDtypeStruct((3,), jnp.float32),
        ),
        (powers[0], powers[2], four, gathered), (vmem, smem),
    )
    return (residual.reshape(source.shape), coefficients)


class ChipShape(Shape):
    def __init__(self, t_extent, z_extent, lanes):
        super().__init__(t_extent, z_extent, lanes)
        self.parts = 2 * z_extent
        self.z_rows = 24 * t_extent
        self.t_rows = 12 * self.parts

    def block(self, k, part):
        first = (k * self.parts + part) * self.rows
        return pl.ds(first, self.rows)

    def edge(self, k, row):
        return pl.ds(k * self.parts * self.rows + row, self.parts, stride=self.rows)


class ChipLinks:
    def __init__(self, shape, ref, row=None):
        self.shape, self.ref, self.row = shape, ref, row

    def __getitem__(self, index):
        direction, row, col, part = index
        first = ((direction * 3 + row) * 3 + col) * 2
        if self.row is None:
            return tuple(self.ref[self.shape.block(first + n, part), :] for n in range(2))
        return tuple(self.ref[self.shape.edge(first + n, self.row), :] for n in range(2))


def components(spins):
    return [(s, c, part, (s * 3 + c) * 2 + part) for s in range(spins) for c in range(3) for part in range(2)]


def gathered_pairs(spins, value):
    out = {}
    for s in range(spins):
        for c in range(3):
            out[s, c] = tuple(value((s * 3 + c) * 2 + part) for part in range(2))
    return out


def chip_psi(shape, ref, part):
    return gathered_pairs(4, lambda k: ref[shape.block(k, part), :])


def chip_edge(shape, ref, row):
    return gathered_pairs(4, lambda k: ref[shape.edge(k, row), :])


def chip_messages(shape, psi_ref, links_ref, z_second, t_second, z_first, t_first):
    t, last = shape.t, shape.t - 1
    even = is_even("ta")
    minus = project(chip_edge(shape, psi_ref, 0), 3, -1)
    half = project(chip_edge(shape, psi_ref, last), 3, 1)
    carried = mul_link_dag(ChipLinks(shape, links_ref, last), 3, 0, half)
    for s, c, part, k in components(2):
        rows = pl.ds(k * shape.parts, shape.parts)
        up, down = carried[s, c][part], minus[s, c][part]
        t_first[rows, :] = either(even, up, down)
        t_second[rows, :] = either(even, down, up)
    even = is_even("gy")
    links = ChipLinks(shape, links_ref)
    for y_half in range(2):
        minus = project(chip_psi(shape, psi_ref, y_half), 2, -1)
        part_last = shape.parts - 2 + y_half
        half = project(chip_psi(shape, psi_ref, part_last), 2, 1)
        carried = mul_link_dag(links, 2, part_last, half)
        for s, c, part, k in components(2):
            rows = pl.ds((k * 2 + y_half) * t, t)
            up, down = carried[s, c][part][0:t], minus[s, c][part][0:t]
            z_first[rows, :] = either(even, up, down)
            z_second[rows, :] = either(even, down, up)


def chip_bring(shape, y_half, source_ref, links_in, psi_ref, links_ref, arrived):
    t, z_extent = shape.t, 2 * shape.z
    first_plane = lax.axis_index("gy") * shape.z
    last = lax.broadcasted_iota(jnp.int32, (t, shape.lanes), 0) == t - 1
    sign = jnp.where(lax.axis_index("ta") == lax.axis_size("ta") - 1, -1.0, 1.0)
    flip = jnp.where(last, sign, 1.0)

    def bring(in_ref, out_ref, k, z, factor=None):
        value = in_ref[pl.ds(k * t * z_extent + first_plane + z, t, stride=z_extent), :]
        if factor is not None:
            value = value * factor
        at = (k * shape.parts + 2 * z + y_half) * shape.rows
        out_ref[pl.ds(pl.multiple_of(at, 8), t), :] = value

    arrived(4)
    for z in range(shape.z):
        for k in range(24):
            bring(source_ref, psi_ref, k, z)
    for direction in (3, 2, 1, 0):
        arrived(direction)
        for z in range(shape.z):
            for k in range(18 * direction, 18 * direction + 18):
                bring(links_in, links_ref, k, z, flip if direction == 3 else None)


def chip_own_kernel(
    shape, source_hbm, links_hbm, psi_ref, links_ref, rest_ref, source_ref, links_in, semaphores
):
    part = 18 * shape.t * 2 * shape.z
    copies = {4: pltpu.make_async_copy(source_hbm, source_ref, semaphores.at[4])}
    for direction in (3, 2, 1, 0):
        rows = pl.ds(direction * part, part)
        copies[direction] = pltpu.make_async_copy(
            links_hbm.at[rows], links_in.at[rows], semaphores.at[direction]
        )
    for copy in copies.values():
        copy.start()
    if shape.rows != shape.t:
        links_ref[...] = jnp.zeros_like(links_ref)
        psi_ref[...] = jnp.zeros_like(psi_ref)
    chip_bring(
        shape, lax.axis_index("gy"), source_ref, links_in, psi_ref, links_ref,
        lambda n: copies[n].wait(),
    )
    t, z_extent = shape.t, 2 * shape.z
    first_plane = (1 - lax.axis_index("gy")) * shape.z
    if shape.rows != t:
        rest_ref[...] = jnp.zeros_like(rest_ref)
    for k in range(24):
        for z in range(shape.z):
            value = source_ref[pl.ds(k * t * z_extent + first_plane + z, t, stride=z_extent), :]
            rest_ref[pl.ds((k * shape.z + z) * shape.rows, t), :] = value


def chip_prep_kernel(
    shape, source_ref, links_in, psi_in, links_held, psi_ref, links_ref, *messages
):
    chip_bring(
        shape, 1 - lax.axis_index("gy"), source_ref, links_in, psi_ref, links_ref, lambda n: None
    )
    chip_messages(shape, psi_ref, links_ref, *messages)


def chip_inner_kernel(shape, psi_ref, links_ref, total_ref):
    links = ChipLinks(shape, links_ref)
    lane, row = shape.lane(), shape.row()
    x = lane % X
    lanes, rows, t = shape.lanes, shape.rows, shape.t
    at_end, at_start = x == X - 1, x == 0
    inside_ahead = row < t - 1
    inside_behind = jnp.logical_and(row > 0, row < t)

    def x_ahead(value):
        return jnp.where(
            at_end, pltpu.roll(value, X - 1, 1), pltpu.roll(value, lanes - 1, 1)
        )

    def x_behind(value):
        return jnp.where(at_start, pltpu.roll(value, lanes - X + 1, 1), pltpu.roll(value, 1, 1))

    def t_ahead(value):
        return jnp.where(inside_ahead, pltpu.roll(value, rows - 1, 0), 0.0)

    def t_behind(value):
        return jnp.where(inside_behind, pltpu.roll(value, 1, 0), 0.0)

    for z in range(shape.z):
        for part in (2 * z, 2 * z + 1):
            psi = chip_psi(shape, psi_ref, part)
            zero = jnp.zeros((rows, lanes), jnp.float32)
            total = {key: (zero, zero) for key in psi}
            half = mapped(x_ahead, project(psi, 0, -1))
            add_rebuilt(total, mul_link(links, 0, part, half), 0, -1)
            half = mapped(x_behind, mul_link_dag(links, 0, part, project(psi, 0, 1)))
            add_rebuilt(total, half, 0, 1)
            half = mapped(t_ahead, project(psi, 3, -1))
            add_rebuilt(total, mul_link(links, 3, part, half), 3, -1)
            half = mapped(t_behind, mul_link_dag(links, 3, part, project(psi, 3, 1)))
            add_rebuilt(total, half, 3, 1)
            if z + 1 < shape.z:
                half = project(chip_psi(shape, psi_ref, part + 2), 2, -1)
                add_rebuilt(total, mul_link(links, 2, part, half), 2, -1)
            if z > 0:
                half = project(chip_psi(shape, psi_ref, part - 2), 2, 1)
                add_rebuilt(total, mul_link_dag(links, 2, part - 2, half), 2, 1)
            for s, c, n, k in components(4):
                total_ref[shape.block(k, part), :] = total[s, c][n]
        pair = (2 * z, 2 * z + 1)
        minus, carried = [], []
        for part in pair:
            psi = chip_psi(shape, psi_ref, part)
            minus.append(mapped(lambda v: pltpu.roll(v, lanes - X, 1), project(psi, 1, -1)))
            half = mul_link_dag(links, 1, part, project(psi, 1, 1))
            carried.append(mapped(lambda v: pltpu.roll(v, X, 1), half))
        for own, part in enumerate(pair):
            total = chip_psi(shape, total_ref, part)
            half = mapped(
                lambda a, b: jnp.where(lane >= lanes - X, b, a), minus[own], minus[1 - own]
            )
            add_rebuilt(total, mul_link(links, 1, part, half), 1, -1)
            half = mapped(lambda a, b: jnp.where(lane < X, b, a), carried[own], carried[1 - own])
            add_rebuilt(total, half, 1, 1)
            for s, c, n, k in components(4):
                total_ref[shape.block(k, part), :] = total[s, c][n]


def chip_sort_faces(z_second, z_first, scratch):
    z_down, z_up = scratch
    z_even = is_even("gy")
    second = 0.0 if z_second is None else z_second[...]
    first = 0.0 if z_first is None else z_first[...]
    z_down[...] = either(z_even, first, second)
    z_up[...] = either(z_even, second, first)


def chip_add_z(shape, links, part, total, scratch):
    z_down, z_up = scratch
    t, rows, lanes, parts = shape.t, shape.rows, shape.lanes, shape.parts

    def plane(ref, y_half):
        def value(k):
            face = ref[pl.ds((k * 2 + y_half) * t, t), :]
            if rows != t:
                pad = jnp.zeros((rows - t, lanes), jnp.float32)
                face = jnp.concatenate([face, pad], axis=0)
            return face

        return gathered_pairs(2, value)

    if part >= parts - 2:
        half = mul_link(links, 2, part, plane(z_down, part - parts + 2))
        add_rebuilt(total, half, 2, -1)
    if part < 2:
        add_rebuilt(total, plane(z_up, part), 2, 1)


def chip_finish(shape, psi_ref, links_ref, total_ref, received, scratch, out_ref):
    z_second, t_second, z_first, t_first = received
    t_even = is_even("ta")
    t, lanes, parts = shape.t, shape.lanes, shape.parts
    chip_sort_faces(z_second, z_first, scratch)
    links = ChipLinks(shape, links_ref)

    for part in range(parts):
        total = chip_psi(shape, total_ref, part)
        chip_add_z(shape, links, part, total, scratch)
        for s, c, n, k in components(4):
            value = psi_ref[shape.block(k, part), :] - hop_kappa * total[s, c][n]
            out_ref[shape.block(k, part), :] = value if s < 2 else -value

    def t_half(from_even, from_odd):
        def value(k):
            at = pl.ds(k * parts, parts)
            return either(t_even, from_even[at, :], from_odd[at, :])

        return gathered_pairs(2, value)

    down = mul_link(ChipLinks(shape, links_ref, t - 1), 3, 0, t_half(t_first, t_second))
    up = t_half(t_second, t_first)
    zero = jnp.zeros((parts, lanes), jnp.float32)
    for half, parity, row in ((down, -1, t - 1), (up, 1, 0)):
        total = {(s, c): (zero, zero) for s in range(4) for c in range(3)}
        add_rebuilt(total, half, 3, parity)
        for s, c, n, k in components(4):
            at = shape.edge(k, row)
            value = hop_kappa * total[s, c][n]
            out_ref[at, :] = out_ref[at, :] - (value if s < 2 else -value)


def chip_mid_kernel(shape, hands_over, psi_ref, links_ref, total_ref, *refs):
    received, out_ref, messages, refs = refs[:4], refs[4], refs[5:9], refs[9:]
    chip_finish(shape, psi_ref, links_ref, total_ref, received, refs[-2:], out_ref)
    chip_messages(shape, out_ref, links_ref, *messages)
    if hands_over:
        hand_over(shape, out_ref, refs[0])


def chip_inner_sums_kernel(
    shape, psi_ref, links_ref, z_first, start_ref, one_ref, two_ref, total_ref, copies_ref, *scratch
):
    class View:
        def __init__(self, ref):
            self.ref = ref

        def __getitem__(self, index):
            return self.ref[shape.block(*index), :]

    wide = ChipShape(shape.t, shape.z, shape.lanes)
    wide.z = shape.parts
    row = sums_row(wide, View(two_ref), View(start_ref), View(psi_ref), View(one_ref))
    copies_ref[...] = jnp.broadcast_to(row[None], copies_ref.shape)
    chip_inner_kernel(shape, psi_ref, links_ref, total_ref)
    chip_sort_faces(None, z_first, scratch)
    for part in range(shape.parts):
        total = chip_psi(shape, total_ref, part)
        chip_add_z(shape, ChipLinks(shape, links_ref), part, total, scratch)
        for s, c, n, k in components(4):
            total_ref[shape.block(k, part), :] = total[s, c][n]


def y_part(shape, k, z, y_half):
    return pl.ds(pl.multiple_of((k * shape.parts + 2 * z + y_half) * shape.rows, 8), shape.rows)


def rest_rows(shape, k, z):
    return pl.ds((k * shape.z + z) * shape.rows, shape.rows)


def hand_over(shape, ref, rest_ref):
    y_half = 1 - lax.axis_index("gy")
    for k in range(24):
        for z in range(shape.z):
            rest_ref[rest_rows(shape, k, z), :] = ref[y_part(shape, k, z, y_half), :]


def chip_finish_kernel(
    shape, psi_ref, links_ref, total_ref, z_second, t_second, t_first,
    out_ref, upper_rest, lower_rest, *scratch,
):
    received = z_second, t_second, None, t_first
    chip_finish(shape, psi_ref, links_ref, total_ref, received, scratch, out_ref)
    y_half = 1 - lax.axis_index("gy")
    for k in range(24):
        rest_ref = upper_rest if k < 12 else lower_rest
        for z in range(shape.z):
            value = out_ref[y_part(shape, k, z, y_half), :]
            rest_ref[dense_rows(shape, k % 12, z), :] = value[0 : shape.t]


def dense_rows(shape, k, z):
    return pl.ds((k * shape.z + z) * shape.t, shape.t)


def chip_last_kernel(
    shape, entries, start_ref, two_ref, four_ref, start_rest, two_rest, upper_rest, lower_rest,
    gathered, out_ref, coefficients,
):
    alpha_one, beta_one, alpha_two, scale, first_factor = scalars(gathered, entries)
    t, z_extent = shape.t, 2 * shape.z
    core = lax.axis_index("gy")

    def put(k, z, start, two, four):
        remain = two - alpha_one * start
        result = (four - alpha_one * two - alpha_two * remain) * scale - first_factor * start
        out_ref[pl.ds(k * t * z_extent + z, t, stride=z_extent), :] = result

    for k in range(24):
        four_rest = upper_rest if k < 12 else lower_rest
        for z in range(shape.z):
            rows = y_part(shape, k, z, core)
            put(k, core * shape.z + z, *(ref[rows, :][0:t] for ref in (start_ref, two_ref, four_ref)))
            rows = rest_rows(shape, k, z)
            other = [ref[rows, :][0:t] for ref in (start_rest, two_rest)]
            put(k, (1 - core) * shape.z + z, *other, four_rest[dense_rows(shape, k % 12, z), :])
    coefficients[0] = alpha_one[0, 0]
    coefficients[1] = beta_one[0, 0]
    coefficients[2] = alpha_two[0, 0]


def chip_shards(source, gauge_links):
    devices_all = lax.axis_size("ta") * lax.axis_size("gz") * 2
    entries = float(source.size * devices_all)
    z_extent = source.shape[4]
    shape = ChipShape(source.shape[3], z_extent // 2, source.shape[5])
    t, rows, lanes = shape.t, shape.rows, shape.lanes
    vmem = pl.BlockSpec(memory_space=pltpu.VMEM)
    smem = pl.BlockSpec(memory_space=pltpu.SMEM)

    def held(*dims):
        return pltpu.VMEM(dims, jnp.float32)

    field = held(24 * shape.parts * rows, lanes)
    links_field = held(72 * shape.parts * rows, lanes)
    z_face, t_face = held(shape.z_rows, lanes), held(shape.t_rows, lanes)
    messages = (z_face, t_face, z_face, t_face)
    z_faces = (z_face, z_face)

    def call(kernel, name, flops, out_shape, operands, **options):
        in_spec = options.pop("in_spec", vmem)
        out_specs = options.pop("out_specs", jax.tree.map(lambda _: vmem, out_shape))
        return pl.pallas_call(
            kernel,
            name=name,
            out_shape=out_shape,
            in_specs=[in_spec] * len(operands),
            out_specs=out_specs,
            compiler_params=pltpu.CompilerParams(vmem_limit_bytes=8 << 20),
            cost_estimate=pl.CostEstimate(flops=flops, bytes_accessed=1 << 20, transcendentals=0),
            **options,
        )(*operands)

    def exchanged(sent):
        z_second, t_second, z_first, t_first = sent
        z_ring = ("gz", "gy")
        return (
            swap(z_second, z_ring, True), swap(t_second, "ta", True),
            swap(z_first, z_ring, False), swap(t_first, "ta", False),
        )

    sites = t * z_extent * lanes
    rows_in = t * z_extent
    own = (source.reshape(24 * rows_in, lanes), gauge_links.reshape(72 * rows_in, lanes))
    other = tuple(swap(value, "gy", False) for value in own)
    rest = held(24 * shape.z * rows, lanes)
    psi, links, start_rest = call(
        functools.partial(chip_own_kernel, shape), "own", 200 * sites, (field, links_field, rest),
        [pltpu.with_memory_space_constraint(value, pltpu.HBM) for value in own],
        scratch_shapes=(
            held(24 * rows_in, lanes), held(72 * rows_in, lanes), pltpu.SemaphoreType.DMA((5,)),
        ),
        in_spec=pl.BlockSpec(memory_space=pltpu.HBM),
    )
    psi, links, *sent = call(
        functools.partial(chip_prep_kernel, shape), "prep", 400 * sites,
        (field, links_field, *messages), (*other, psi, links),
        input_output_aliases={2: 0, 3: 1},
    )
    powers = [psi]
    for step in range(3):
        halo = exchanged(sent)
        inner = functools.partial(chip_inner_kernel, shape)
        total = call(inner, "inner", 1000 * sites, field, (psi, links))
        hands_over = step == 1
        psi, *sent = call(
            functools.partial(chip_mid_kernel, shape, hands_over), "mid", 600 * sites,
            (field, *messages, rest) if hands_over else (field, *messages),
            (psi, links, total, *halo), scratch_shapes=z_faces,
        )
        powers.append(psi)
        if hands_over:
            two_rest = swap(sent.pop(), "gy", False)
    halo = exchanged(sent)
    total, copies = call(
        functools.partial(chip_inner_sums_kernel, shape), "inner_sums", 1400 * sites,
        (field, held(devices_all, 4, lanes)), (psi, links, halo[2], *powers[:3]),
        scratch_shapes=z_faces,
    )
    gathered = from_everyone(copies)
    dense = held(12 * shape.z * t, lanes)
    four, *four_rest = call(
        functools.partial(chip_finish_kernel, shape), "finish", 400 * sites, (field, dense, dense),
        (psi, links, total, halo[0], halo[1], halo[3]), scratch_shapes=z_faces,
    )
    four_rest = [swap(value, "gy", False) for value in four_rest]
    residual, coefficients = call(
        functools.partial(chip_last_kernel, shape, entries), "last", 100 * sites,
        (
            jax.ShapeDtypeStruct((24 * rows_in, lanes), jnp.float32),
            jax.ShapeDtypeStruct((3,), jnp.float32),
        ),
        (powers[0], powers[2], four, start_rest, two_rest, *four_rest, gathered),
        out_specs=(vmem, smem),
    )
    return (residual.reshape(source.shape), coefficients)


def solution(mesh):
    placed = (P(None, None, None, "ta", "gz", "gy"), P(None, None, None, None, "ta", "gz", "gy"))
    return jax.shard_map(
        chip_shards if mesh.shape["gy"] == 2 else shards,
        mesh=mesh,
        in_specs=placed,
        out_specs=(P(None, None, None, "ta", "gz", "gy"), P()),
        check_vma=False,
    )
```

```python
import functools
import math

import jax
import jax.numpy as jnp
from jax import lax
from jax.experimental import pallas as pl
from jax.experimental.pallas import tpu as pltpu
from jax.sharding import PartitionSpec as P

X = 32

hop_kappa = 0.19
epsilon = 1e-06
spin_table = (
    ((1, 0), (-1j, -1j)),
    ((1, 0), (-1, 1)),
    ((0, 1), (-1j, 1j)),
    ((0, 1), (1, 1)),
)
SPIN_COLOUR = [(spin, colour) for spin in range(2) for colour in range(3)]


def add_phased(left, phase, right):
    phase = complex(phase)
    if phase == 1:
        return (left[0] + right[0], left[1] + right[1])
    if phase == -1:
        return (left[0] - right[0], left[1] - right[1])
    if phase == 1j:
        return (left[0] - right[1], left[1] + right[0])
    return (left[0] + right[1], left[1] - right[0])


def project(psi, direction, parity):
    order, phases = spin_table[direction]
    return {
        (s, c): add_phased(psi[s, c], parity * phases[s], psi[2 + order[s], c])
        for s, c in SPIN_COLOUR
    }


def add_rebuilt(total, half, direction, parity):
    order, phases = spin_table[direction]
    for s, c in SPIN_COLOUR:
        total[s, c] = add_phased(total[s, c], 1, half[s, c])
        row = order[s]
        phase = parity * complex(phases[row]).conjugate()
        total[2 + s, c] = add_phased(total[2 + s, c], phase, half[row, c])


def mul_link(links, direction, z, half):
    out = {}
    for row in range(3):
        for s in range(2):
            real, imag = None, None
            for col in range(3):
                u_real, u_imag = links[direction, row, col, z]
                h_real, h_imag = half[s, col]
                term_real = u_real * h_real - u_imag * h_imag
                term_imag = u_real * h_imag + u_imag * h_real
                real = term_real if real is None else real + term_real
                imag = term_imag if imag is None else imag + term_imag
            out[s, row] = (real, imag)
    return out


def mul_link_dag(links, direction, z, half):
    out = {}
    for row in range(3):
        for s in range(2):
            real, imag = None, None
            for col in range(3):
                u_real, u_imag = links[direction, col, row, z]
                h_real, h_imag = half[s, col]
                term_real = u_real * h_real + u_imag * h_imag
                term_imag = u_real * h_imag - u_imag * h_real
                real = term_real if real is None else real + term_real
                imag = term_imag if imag is None else imag + term_imag
            out[s, row] = (real, imag)
    return out


def mapped(function, *halves):
    return {
        key: tuple(function(*(half[key][part] for half in halves)) for part in range(2))
        for key in SPIN_COLOUR
    }


class Links:
    def __init__(self, ref):
        self.ref = ref

    def __getitem__(self, index):
        direction, row, col, z = index
        first = ((direction * 3 + row) * 3 + col) * 2
        return (self.ref[first, z], self.ref[first + 1, z])


def load_psi(ref, z):
    return {
        (s, c): (ref[(s * 3 + c) * 2, z], ref[(s * 3 + c) * 2 + 1, z])
        for s in range(4)
        for c in range(3)
    }


def load_half(ref, z):
    return {
        (s, c): (ref[(s * 3 + c) * 2, z], ref[(s * 3 + c) * 2 + 1, z]) for s, c in SPIN_COLOUR
    }


def store_half(ref, z, half):
    for (s, c), pair in half.items():
        for part in range(2):
            ref[(s * 3 + c) * 2 + part, z] = pair[part]


class Shape:
    def __init__(self, t_extent, z_extent, lanes):
        self.t = t_extent
        self.z = z_extent
        self.rows = -(-t_extent // 8) * 8
        self.lanes = lanes

    def row(self):
        return lax.broadcasted_iota(jnp.int32, (self.rows, self.lanes), 0)

    def lane(self):
        return lax.broadcasted_iota(jnp.int32, (self.rows, self.lanes), 1)


def is_even(axis):
    return jnp.bitwise_and(lax.axis_index(axis), 1) == 0


def either(choice, first, second):
    return jnp.where(choice, first, second)


def emit_messages(shape, psi_ref, links, refs):
    z_second, t_second, z_first, t_first, y_msg, carried_y, carried_t = refs
    t_even, z_even = is_even("ta"), is_even("gz")
    lane = shape.lane()
    last_z, last_t = shape.z - 1, shape.t - 1
    for z in range(shape.z):
        psi = load_psi(psi_ref, z)
        minus = project(psi, 3, -1)
        carried = mul_link_dag(links, 3, z, project(psi, 3, 1))
        store_half(carried_t, z, carried)
        for s, c in SPIN_COLOUR:
            for part in range(2):
                at = ((s * 3 + c) * 2 + part) * shape.z + z
                down = minus[s, c][part][0:1]
                up = carried[s, c][part][last_t : last_t + 1]
                t_first[at : at + 1] = either(t_even, up, down)
                t_second[at : at + 1] = either(t_even, down, up)
        minus = project(psi, 1, -1)
        carried = mul_link_dag(links, 1, z, project(psi, 1, 1))
        store_half(carried_y, z, carried)
        store_half(
            y_msg,
            z,
            mapped(lambda low, high: jnp.where(lane < X, low, high), minus, carried),
        )
    minus = project(load_psi(psi_ref, 0), 2, -1)
    carried = mul_link_dag(links, 2, last_z, project(load_psi(psi_ref, last_z), 2, 1))
    for s, c in SPIN_COLOUR:
        for part in range(2):
            at = ((s * 3 + c) * 2 + part) * shape.t
            down, up = minus[s, c][part][0 : shape.t], carried[s, c][part][0 : shape.t]
            z_first[at : at + shape.t] = either(z_even, up, down)
            z_second[at : at + shape.t] = either(z_even, down, up)


def prep_kernel(shape, source_hbm, links_hbm, psi_ref, links_ref, *refs):
    messages, (source_ref, links_in, arrived) = refs[:-3], refs[-3:]
    t, z_extent = shape.t, shape.z
    part = 18 * t * z_extent
    copies = [pltpu.make_async_copy(source_hbm, source_ref, arrived.at[4])]
    for direction in (3, 2, 1, 0):
        rows = pl.ds(direction * part, part)
        copies.append(
            pltpu.make_async_copy(links_hbm.at[rows], links_in.at[rows], arrived.at[direction])
        )
    for copy in copies:
        copy.start()
    if shape.rows != t:
        links_ref[...] = jnp.zeros_like(links_ref)
        psi_ref[...] = jnp.zeros_like(psi_ref)
    last = lax.broadcasted_iota(jnp.int32, (t, shape.lanes), 0) == t - 1
    sign = jnp.where(lax.axis_index("ta") == lax.axis_size("ta") - 1, -1.0, 1.0)
    flip = jnp.where(last, sign, 1.0)
    copies[0].wait()
    for k in range(24):
        for z in range(z_extent):
            psi_ref[k, z, 0:t] = source_ref[pl.ds(k * t * z_extent + z, t, stride=z_extent), :]
    for direction in (3, 2, 1, 0):
        copies[4 - direction].wait()
        for k in range(18 * direction, 18 * direction + 18):
            for z in range(z_extent):
                value = links_in[pl.ds(k * t * z_extent + z, t, stride=z_extent), :]
                links_ref[k, z, 0:t] = value * flip if direction == 3 else value
    emit_messages(shape, psi_ref, Links(links_ref), messages)


def summed(shape, term):
    total = None
    for k in range(24):
        for z in range(shape.z):
            value = term(k, z)
            total = value if total is None else total + value
    return total


def over_lanes(total):
    return jnp.sum(jnp.sum(total, axis=0, keepdims=True), axis=1, keepdims=True)


def local_sums(shape, image, origin):
    square = summed(shape, lambda k, z: origin[k, z] * origin[k, z])
    mixed = over_lanes(summed(shape, lambda k, z: image[k, z] * origin[k, z]))
    whole = over_lanes(square)
    factor = jnp.where(whole > 0.0, mixed / jnp.where(whole > 0.0, whole, 1.0), 0.0)
    spread = jnp.broadcast_to(factor, (shape.rows, shape.lanes))
    rest_square, rest_mixed = None, None
    for k in range(24):
        for z in range(shape.z):
            start = origin[k, z]
            rest = image[k, z] - spread * start
            terms = rest * rest, rest * start
            if rest_square is None:
                rest_square, rest_mixed = terms
            else:
                rest_square, rest_mixed = rest_square + terms[0], rest_mixed + terms[1]
    return [factor, *(over_lanes(value) for value in (square, rest_square, rest_mixed))]


def inner_kernel(shape, psi_ref, links_ref, total_ref):
    links = Links(links_ref)
    x = shape.lane() % X
    lanes = shape.lanes
    at_end, at_start = x == X - 1, x == 0

    def ahead(value):
        return jnp.where(
            at_end, pltpu.roll(value, X - 1, 1), pltpu.roll(value, lanes - 1, 1)
        )

    def behind(value):
        return jnp.where(at_start, pltpu.roll(value, lanes - X + 1, 1), pltpu.roll(value, 1, 1))

    for z in range(shape.z):
        psi = load_psi(psi_ref, z)
        zero = jnp.zeros((shape.rows, lanes), jnp.float32)
        total = {key: (zero, zero) for key in psi}
        half = mapped(ahead, project(psi, 0, -1))
        add_rebuilt(total, mul_link(links, 0, z, half), 0, -1)
        half = mapped(behind, mul_link_dag(links, 0, z, project(psi, 0, 1)))
        add_rebuilt(total, half, 0, 1)
        if z + 1 < shape.z:
            half = project(load_psi(psi_ref, z + 1), 2, -1)
            add_rebuilt(total, mul_link(links, 2, z, half), 2, -1)
        if z > 0:
            half = project(load_psi(psi_ref, z - 1), 2, 1)
            add_rebuilt(total, mul_link_dag(links, 2, z - 1, half), 2, 1)
        for (s, c), pair in total.items():
            for part in range(2):
                total_ref[(s * 3 + c) * 2 + part, z] = pair[part]


def add_y_hops(shape, z, psi, total, links, carried_y, y_halo):
    lane, lanes = shape.lane(), shape.lanes
    received = load_half(y_halo, z)
    half = mapped(
        lambda own, other: pltpu.roll(jnp.where(lane < X, other, own), lanes - X, 1),
        project(psi, 1, -1),
        received,
    )
    add_rebuilt(total, mul_link(links, 1, z, half), 1, -1)
    half = mapped(
        lambda own, other: pltpu.roll(jnp.where(lane >= lanes - X, other, own), X, 1),
        load_half(carried_y, z),
        received,
    )
    add_rebuilt(total, half, 1, 1)


def finish_hops(
    shape, psi_ref, links, total_ref, carried_y, carried_t, halo, store
):
    z_second, t_second, z_first, t_first, y_msg = halo
    t_even, z_even = is_even("ta"), is_even("gz")
    row = shape.row()
    lanes, rows, t = shape.lanes, shape.rows, shape.t
    last_z = shape.z - 1

    for z in range(shape.z):
        psi = load_psi(psi_ref, z)
        total = load_psi(total_ref, z)

        def rim_rows(from_even, from_odd):
            half = {}
            for s, c in SPIN_COLOUR:
                ats = [((s * 3 + c) * 2 + part) * shape.z + z for part in range(2)]
                half[s, c] = tuple(
                    jnp.broadcast_to(
                        either(t_even, from_even[at : at + 1], from_odd[at : at + 1]),
                        (rows, lanes),
                    )
                    for at in ats
                )
            return half

        def rim_plane(from_even, from_odd):
            half = {}
            for s, c in SPIN_COLOUR:
                pair = []
                for part in range(2):
                    at = ((s * 3 + c) * 2 + part) * t
                    plane = either(z_even, from_even[at : at + t], from_odd[at : at + t])
                    if rows != t:
                        pad = jnp.zeros((rows - t, lanes), jnp.float32)
                        plane = jnp.concatenate([plane, pad], axis=0)
                    pair.append(plane)
                half[s, c] = tuple(pair)
            return half

        if y_msg is not None:
            add_y_hops(shape, z, psi, total, links, carried_y, y_msg)
        if z == last_z:
            add_rebuilt(total, mul_link(links, 2, z, rim_plane(z_first, z_second)), 2, -1)
        if z == 0:
            add_rebuilt(total, rim_plane(z_second, z_first), 2, 1)
        half = mapped(
            lambda own, other: jnp.where(row == t - 1, other, pltpu.roll(own, rows - 1, 0)),
            project(psi, 3, -1),
            rim_rows(t_first, t_second),
        )
        add_rebuilt(total, mul_link(links, 3, z, half), 3, -1)
        half = mapped(
            lambda own, other: jnp.where(row == 0, other, pltpu.roll(own, 1, 0)),
            load_half(carried_t, z),
            rim_rows(t_second, t_first),
        )
        add_rebuilt(total, half, 3, 1)
        for (s, c), pair in total.items():
            for part in range(2):
                value = psi[s, c][part] - hop_kappa * pair[part]
                value = value if s < 2 else -value
                if rows != t:
                    value = jnp.where(row < t, value, 0.0)
                store((s * 3 + c) * 2 + part, z, value)


def mid_kernel(shape, psi_ref, links_ref, total_ref, carried_y, carried_t, *refs):
    halo, out_ref, messages = refs[:5], refs[5], refs[6:]
    links = Links(links_ref)

    def store(k, z, value):
        out_ref[k, z] = value

    finish_hops(
        shape, psi_ref, links, total_ref, carried_y, carried_t, halo, store
    )
    emit_messages(shape, out_ref, links, messages)


def sums_row(shape, two, start, three, one):
    sums = local_sums(shape, two, start) + local_sums(shape, three, one)
    lane = lax.broadcasted_iota(jnp.int32, (1, shape.lanes), 1)
    row = jnp.zeros((1, shape.lanes), jnp.float32)
    for k, value in enumerate(sums):
        row = jnp.where(lane == k, value, row)
    return row


def inner_sums_kernel(
    shape, psi_ref, links_ref, start_ref, one_ref, two_ref, total_ref, copies_ref
):
    row = sums_row(shape, two_ref, start_ref, psi_ref, one_ref)
    copies_ref[...] = jnp.broadcast_to(row[None], copies_ref.shape)
    inner_kernel(shape, psi_ref, links_ref, total_ref)


def finish_kernel(shape, psi_ref, links_ref, total_ref, carried_y, carried_t, *refs):
    halo, out_ref = refs[:5], refs[5]

    def store(k, z, value):
        out_ref[k, z] = value

    finish_hops(
        shape, psi_ref, Links(links_ref), total_ref, carried_y, carried_t, halo, store
    )


def scalars(table, entries):
    columns = [table[:, k : k + 1] for k in range(8)]
    factor_two, start_square, two_square, two_mixed = columns[:4]
    factor_three, one_square, three_square, three_mixed = columns[4:]

    def over_devices(column):
        return jnp.sum(column, axis=0, keepdims=True)

    norm_square = over_devices(start_square) / entries + epsilon
    alpha_one = over_devices(one_square) / entries / norm_square
    gap = alpha_one - factor_two
    remain_square = over_devices(two_square - gap * (2.0 * two_mixed - gap * start_square)) / entries
    overlap = over_devices(two_mixed - gap * start_square) / entries
    gap = alpha_one - factor_three
    image_square = over_devices(three_square - gap * (2.0 * three_mixed - gap * one_square)) / entries
    norm = jnp.sqrt(norm_square)
    beta_one = jnp.sqrt(remain_square / norm_square + epsilon)
    overlap = overlap / (norm_square * beta_one)
    alpha_two = image_square / (norm_square * beta_one * beta_one) - beta_one * overlap
    scale = 1.0 / (norm * beta_one)
    return alpha_one, beta_one, alpha_two, scale, beta_one / norm


def last_kernel(
    shape, entries, start_ref, two_ref, four_ref, gathered, out_ref, coefficients
):
    alpha_one, beta_one, alpha_two, scale, first_factor = scalars(gathered[:, 0, :], entries)
    t, z_extent = shape.t, shape.z
    for k in range(24):
        for z in range(z_extent):
            two, start = two_ref[k, z], start_ref[k, z]
            remain = two - alpha_one * start
            result = (four_ref[k, z] - alpha_one * two - alpha_two * remain) * scale
            result = result - first_factor * start
            out_ref[pl.ds(k * t * z_extent + z, t, stride=z_extent), :] = result[0:t]
    coefficients[0] = alpha_one[0, 0]
    coefficients[1] = beta_one[0, 0]
    coefficients[2] = alpha_two[0, 0]


def swap(value, axis, second):
    count = math.prod(lax.axis_size(name) for name in (axis if isinstance(axis, tuple) else (axis,)))
    pairs = []
    for low in range(1 if second else 0, count, 2):
        high = (low + 1) % count
        pairs += [(low, high), (high, low)]
    return lax.ppermute(value, axis, pairs)


def exchange(messages, lanes):
    z_second, t_second, z_first, t_first, y_msg = messages
    halo = (
        swap(z_second, "gz", True),
        swap(t_second, "ta", True),
        swap(z_first, "gz", False),
        swap(t_first, "ta", False),
    )
    y_halo = swap(y_msg, "gy", False)
    if lax.axis_size("gy") > 2:
        even = lax.axis_index("gy") % 2 == 0
        lane = lax.broadcasted_iota(jnp.int32, y_msg.shape, y_msg.ndim - 1)
        y_halo = jnp.where((lane < lanes // 2) == even, y_halo, swap(y_msg, "gy", True))
    return (*halo, y_halo)


def from_everyone(copies):
    return lax.all_to_all(copies, ("ta", "gz", "gy"), split_axis=0, concat_axis=0, tiled=True)


def shards(source, gauge_links):
    devices_all = lax.axis_size("ta") * lax.axis_size("gz") * lax.axis_size("gy")
    entries = float(source.size * devices_all)
    shape = Shape(source.shape[3], source.shape[4], source.shape[5])
    t, z, rows, lanes = shape.t, shape.z, shape.rows, shape.lanes
    vmem = pl.BlockSpec(memory_space=pltpu.VMEM)
    smem = pl.BlockSpec(memory_space=pltpu.SMEM)

    def held(*dims):
        return pltpu.VMEM(dims, jnp.float32)

    field = held(24, z, rows, lanes)
    half = held(12, z, rows, lanes)
    z_face, t_face = held(12 * t, lanes), held(12 * z, lanes)
    messages = (z_face, t_face, z_face, t_face, half, half, half)

    def call(kernel, name, flops, out_shape, operands, out_specs=None, in_spec=vmem, scratch=()):
        return pl.pallas_call(
            kernel,
            name=name,
            out_shape=out_shape,
            in_specs=[in_spec] * len(operands),
            out_specs=out_specs or jax.tree.map(lambda _: vmem, out_shape),
            scratch_shapes=scratch,
            compiler_params=pltpu.CompilerParams(vmem_limit_bytes=8 << 20),
            cost_estimate=pl.CostEstimate(flops=flops, bytes_accessed=1 << 20, transcendentals=0),
        )(*operands)

    sites = t * z * lanes
    psi, links, *sent = call(
        functools.partial(prep_kernel, shape), "prep", 400 * sites,
        (field, held(72, z, rows, lanes), *messages),
        (
            pltpu.with_memory_space_constraint(source.reshape(24 * t * z, lanes), pltpu.HBM),
            pltpu.with_memory_space_constraint(gauge_links.reshape(72 * t * z, lanes), pltpu.HBM),
        ),
        in_spec=pl.BlockSpec(memory_space=pltpu.HBM),
        scratch=(
            held(24 * t * z, lanes), held(72 * t * z, lanes), pltpu.SemaphoreType.DMA((5,)),
        ),
    )
    powers = [psi]
    for step in range(3):
        halo = exchange(sent[:5], lanes)
        inner = functools.partial(inner_kernel, shape)
        total = call(inner, "inner", 700 * sites, field, (psi, links))
        psi, *sent = call(
            functools.partial(mid_kernel, shape), "mid", 1000 * sites,
            (field, *messages), (psi, links, total, *sent[5:], *halo),
        )
        powers.append(psi)
    halo = exchange(sent[:5], lanes)
    total, copies = call(
        functools.partial(inner_sums_kernel, shape), "inner_sums", 1100 * sites,
        (field, held(devices_all, 8, lanes)), (psi, links, *powers[:3]),
    )
    gathered = from_everyone(copies)
    four = call(
        functools.partial(finish_kernel, shape), "finish", 700 * sites, field,
        (psi, links, total, *sent[5:], *halo),
    )
    residual, coefficients = call(
        functools.partial(last_kernel, shape, entries), "last", 100 * sites,
        (
            jax.ShapeDtypeStruct((24 * t * z, lanes), jnp.float32),
            jax.ShapeDtypeStruct((3,), jnp.float32),
        ),
        (powers[0], powers[2], four, gathered), (vmem, smem),
    )
    return (residual.reshape(source.shape), coefficients)


class ChipShape(Shape):
    def __init__(self, t_extent, z_extent, lanes):
        super().__init__(t_extent, z_extent, lanes)
        self.parts = 2 * z_extent
        self.z_rows = 24 * t_extent
        self.t_rows = 12 * self.parts

    def block(self, k, part):
        first = (k * self.parts + part) * self.rows
        return pl.ds(first, self.rows)

    def edge(self, k, row):
        return pl.ds(k * self.parts * self.rows + row, self.parts, stride=self.rows)


class ChipLinks:
    def __init__(self, shape, ref, row=None):
        self.shape, self.ref, self.row = shape, ref, row

    def __getitem__(self, index):
        direction, row, col, part = index
        first = ((direction * 3 + row) * 3 + col) * 2
        if self.row is None:
            return tuple(self.ref[self.shape.block(first + n, part), :] for n in range(2))
        return tuple(self.ref[self.shape.edge(first + n, self.row), :] for n in range(2))


def components(spins):
    return [(s, c, part, (s * 3 + c) * 2 + part) for s in range(spins) for c in range(3) for part in range(2)]


def gathered_pairs(spins, value):
    out = {}
    for s in range(spins):
        for c in range(3):
            out[s, c] = tuple(value((s * 3 + c) * 2 + part) for part in range(2))
    return out


def chip_psi(shape, ref, part):
    return gathered_pairs(4, lambda k: ref[shape.block(k, part), :])


def chip_edge(shape, ref, row):
    return gathered_pairs(4, lambda k: ref[shape.edge(k, row), :])


def chip_messages(shape, psi_ref, links_ref, z_second, t_second, z_first, t_first):
    t, last = shape.t, shape.t - 1
    even = is_even("ta")
    minus = project(chip_edge(shape, psi_ref, 0), 3, -1)
    half = project(chip_edge(shape, psi_ref, last), 3, 1)
    carried = mul_link_dag(ChipLinks(shape, links_ref, last), 3, 0, half)
    for s, c, part, k in components(2):
        rows = pl.ds(k * shape.parts, shape.parts)
        up, down = carried[s, c][part], minus[s, c][part]
        t_first[rows, :] = either(even, up, down)
        t_second[rows, :] = either(even, down, up)
    even = is_even("gy")
    links = ChipLinks(shape, links_ref)
    for y_half in range(2):
        minus = project(chip_psi(shape, psi_ref, y_half), 2, -1)
        part_last = shape.parts - 2 + y_half
        half = project(chip_psi(shape, psi_ref, part_last), 2, 1)
        carried = mul_link_dag(links, 2, part_last, half)
        for s, c, part, k in components(2):
            rows = pl.ds((k * 2 + y_half) * t, t)
            up, down = carried[s, c][part][0:t], minus[s, c][part][0:t]
            z_first[rows, :] = either(even, up, down)
            z_second[rows, :] = either(even, down, up)


def chip_bring(shape, y_half, source_ref, links_in, psi_ref, links_ref, arrived):
    t, z_extent = shape.t, 2 * shape.z
    first_plane = lax.axis_index("gy") * shape.z
    last = lax.broadcasted_iota(jnp.int32, (t, shape.lanes), 0) == t - 1
    sign = jnp.where(lax.axis_index("ta") == lax.axis_size("ta") - 1, -1.0, 1.0)
    flip = jnp.where(last, sign, 1.0)

    def bring(in_ref, out_ref, k, z, factor=None):
        value = in_ref[pl.ds(k * t * z_extent + first_plane + z, t, stride=z_extent), :]
        if factor is not None:
            value = value * factor
        at = (k * shape.parts + 2 * z + y_half) * shape.rows
        out_ref[pl.ds(pl.multiple_of(at, 8), t), :] = value

    arrived(4)
    for z in range(shape.z):
        for k in range(24):
            bring(source_ref, psi_ref, k, z)
    for direction in (3, 2, 1, 0):
        arrived(direction)
        for z in range(shape.z):
            for k in range(18 * direction, 18 * direction + 18):
                bring(links_in, links_ref, k, z, flip if direction == 3 else None)


def chip_own_kernel(
    shape, source_hbm, links_hbm, psi_ref, links_ref, rest_ref, source_ref, links_in, semaphores
):
    part = 18 * shape.t * 2 * shape.z
    copies = {4: pltpu.make_async_copy(source_hbm, source_ref, semaphores.at[4])}
    for direction in (3, 2, 1, 0):
        rows = pl.ds(direction * part, part)
        copies[direction] = pltpu.make_async_copy(
            links_hbm.at[rows], links_in.at[rows], semaphores.at[direction]
        )
    for copy in copies.values():
        copy.start()
    if shape.rows != shape.t:
        links_ref[...] = jnp.zeros_like(links_ref)
        psi_ref[...] = jnp.zeros_like(psi_ref)
    chip_bring(
        shape, lax.axis_index("gy"), source_ref, links_in, psi_ref, links_ref,
        lambda n: copies[n].wait(),
    )
    t, z_extent = shape.t, 2 * shape.z
    first_plane = (1 - lax.axis_index("gy")) * shape.z
    if shape.rows != t:
        rest_ref[...] = jnp.zeros_like(rest_ref)
    for k in range(24):
        for z in range(shape.z):
            value = source_ref[pl.ds(k * t * z_extent + first_plane + z, t, stride=z_extent), :]
            rest_ref[pl.ds((k * shape.z + z) * shape.rows, t), :] = value


def chip_prep_kernel(
    shape, source_ref, links_in, psi_in, links_held, psi_ref, links_ref, *messages
):
    chip_bring(
        shape, 1 - lax.axis_index("gy"), source_ref, links_in, psi_ref, links_ref, lambda n: None
    )
    chip_messages(shape, psi_ref, links_ref, *messages)


def chip_inner_kernel(shape, psi_ref, links_ref, total_ref):
    links = ChipLinks(shape, links_ref)
    lane, row = shape.lane(), shape.row()
    x = lane % X
    lanes, rows, t = shape.lanes, shape.rows, shape.t
    at_end, at_start = x == X - 1, x == 0
    inside_ahead = row < t - 1
    inside_behind = jnp.logical_and(row > 0, row < t)

    def x_ahead(value):
        return jnp.where(
            at_end, pltpu.roll(value, X - 1, 1), pltpu.roll(value, lanes - 1, 1)
        )

    def x_behind(value):
        return jnp.where(at_start, pltpu.roll(value, lanes - X + 1, 1), pltpu.roll(value, 1, 1))

    def t_ahead(value):
        return jnp.where(inside_ahead, pltpu.roll(value, rows - 1, 0), 0.0)

    def t_behind(value):
        return jnp.where(inside_behind, pltpu.roll(value, 1, 0), 0.0)

    for z in range(shape.z):
        for part in (2 * z, 2 * z + 1):
            psi = chip_psi(shape, psi_ref, part)
            zero = jnp.zeros((rows, lanes), jnp.float32)
            total = {key: (zero, zero) for key in psi}
            half = mapped(x_ahead, project(psi, 0, -1))
            add_rebuilt(total, mul_link(links, 0, part, half), 0, -1)
            half = mapped(x_behind, mul_link_dag(links, 0, part, project(psi, 0, 1)))
            add_rebuilt(total, half, 0, 1)
            half = mapped(t_ahead, project(psi, 3, -1))
            add_rebuilt(total, mul_link(links, 3, part, half), 3, -1)
            half = mapped(t_behind, mul_link_dag(links, 3, part, project(psi, 3, 1)))
            add_rebuilt(total, half, 3, 1)
            if z + 1 < shape.z:
                half = project(chip_psi(shape, psi_ref, part + 2), 2, -1)
                add_rebuilt(total, mul_link(links, 2, part, half), 2, -1)
            if z > 0:
                half = project(chip_psi(shape, psi_ref, part - 2), 2, 1)
                add_rebuilt(total, mul_link_dag(links, 2, part - 2, half), 2, 1)
            for s, c, n, k in components(4):
                total_ref[shape.block(k, part), :] = total[s, c][n]
        pair = (2 * z, 2 * z + 1)
        minus, carried = [], []
        for part in pair:
            psi = chip_psi(shape, psi_ref, part)
            minus.append(mapped(lambda v: pltpu.roll(v, lanes - X, 1), project(psi, 1, -1)))
            half = mul_link_dag(links, 1, part, project(psi, 1, 1))
            carried.append(mapped(lambda v: pltpu.roll(v, X, 1), half))
        for own, part in enumerate(pair):
            total = chip_psi(shape, total_ref, part)
            half = mapped(
                lambda a, b: jnp.where(lane >= lanes - X, b, a), minus[own], minus[1 - own]
            )
            add_rebuilt(total, mul_link(links, 1, part, half), 1, -1)
            half = mapped(lambda a, b: jnp.where(lane < X, b, a), carried[own], carried[1 - own])
            add_rebuilt(total, half, 1, 1)
            for s, c, n, k in components(4):
                total_ref[shape.block(k, part), :] = total[s, c][n]


def chip_sort_faces(z_second, z_first, scratch):
    z_down, z_up = scratch
    z_even = is_even("gy")
    z_down[...] = either(z_even, z_first[...], z_second[...])
    z_up[...] = either(z_even, z_second[...], z_first[...])


def chip_add_z(shape, links, part, total, scratch):
    z_down, z_up = scratch
    t, rows, lanes, parts = shape.t, shape.rows, shape.lanes, shape.parts

    def plane(ref, y_half):
        def value(k):
            face = ref[pl.ds((k * 2 + y_half) * t, t), :]
            if rows != t:
                pad = jnp.zeros((rows - t, lanes), jnp.float32)
                face = jnp.concatenate([face, pad], axis=0)
            return face

        return gathered_pairs(2, value)

    if part >= parts - 2:
        half = mul_link(links, 2, part, plane(z_down, part - parts + 2))
        add_rebuilt(total, half, 2, -1)
    if part < 2:
        add_rebuilt(total, plane(z_up, part), 2, 1)


def chip_finish(shape, psi_ref, links_ref, total_ref, received, scratch, out_ref):
    z_second, t_second, z_first, t_first = received
    t_even = is_even("ta")
    t, lanes, parts = shape.t, shape.lanes, shape.parts
    chip_sort_faces(z_second, z_first, scratch)
    links = ChipLinks(shape, links_ref)

    for part in range(parts):
        total = chip_psi(shape, total_ref, part)
        chip_add_z(shape, links, part, total, scratch)
        for s, c, n, k in components(4):
            value = psi_ref[shape.block(k, part), :] - hop_kappa * total[s, c][n]
            out_ref[shape.block(k, part), :] = value if s < 2 else -value

    def t_half(from_even, from_odd):
        def value(k):
            at = pl.ds(k * parts, parts)
            return either(t_even, from_even[at, :], from_odd[at, :])

        return gathered_pairs(2, value)

    down = mul_link(ChipLinks(shape, links_ref, t - 1), 3, 0, t_half(t_first, t_second))
    up = t_half(t_second, t_first)
    zero = jnp.zeros((parts, lanes), jnp.float32)
    for half, parity, row in ((down, -1, t - 1), (up, 1, 0)):
        total = {(s, c): (zero, zero) for s in range(4) for c in range(3)}
        add_rebuilt(total, half, 3, parity)
        for s, c, n, k in components(4):
            at = shape.edge(k, row)
            value = hop_kappa * total[s, c][n]
            out_ref[at, :] = out_ref[at, :] - (value if s < 2 else -value)


def chip_mid_kernel(shape, hands_over, psi_ref, links_ref, total_ref, *refs):
    received, out_ref, messages, refs = refs[:4], refs[4], refs[5:9], refs[9:]
    chip_finish(shape, psi_ref, links_ref, total_ref, received, refs[-2:], out_ref)
    chip_messages(shape, out_ref, links_ref, *messages)
    if hands_over:
        hand_over(shape, out_ref, refs[0])


def chip_sums_kernel(shape, start_ref, one_ref, two_ref, three_ref, copies_ref):
    class View:
        def __init__(self, ref):
            self.ref = ref

        def __getitem__(self, index):
            return self.ref[shape.block(*index), :]

    wide = ChipShape(shape.t, shape.z, shape.lanes)
    wide.z = shape.parts
    row = sums_row(wide, View(two_ref), View(start_ref), View(three_ref), View(one_ref))
    copies_ref[...] = jnp.broadcast_to(row[None], copies_ref.shape)


def chip_scalars_kernel(entries, gathered, factors_ref, coefficients):
    alpha_one, beta_one, alpha_two, scale, first_factor = scalars(gathered[:, 0, :], entries)
    lanes = factors_ref.shape[1]
    values = [alpha_one, alpha_two, scale, first_factor]
    values = [jnp.broadcast_to(value, (1, lanes)) for value in values]
    values.append(jnp.zeros((4, lanes), jnp.float32))
    factors_ref[...] = jnp.concatenate(values, axis=0)
    coefficients[0] = alpha_one[0, 0]
    coefficients[1] = beta_one[0, 0]
    coefficients[2] = alpha_two[0, 0]


def y_part(shape, k, z, y_half):
    return pl.ds(pl.multiple_of((k * shape.parts + 2 * z + y_half) * shape.rows, 8), shape.rows)


def rest_rows(shape, k, z):
    return pl.ds((k * shape.z + z) * shape.rows, shape.rows)


def hand_over(shape, ref, rest_ref):
    y_half = 1 - lax.axis_index("gy")
    for k in range(24):
        for z in range(shape.z):
            rest_ref[rest_rows(shape, k, z), :] = ref[y_part(shape, k, z, y_half), :]


def chip_finish_kernel(
    shape, psi_ref, links_ref, total_ref, z_second, t_second, z_first, t_first,
    out_ref, upper_rest, lower_rest, *scratch,
):
    received = z_second, t_second, z_first, t_first
    chip_finish(shape, psi_ref, links_ref, total_ref, received, scratch, out_ref)
    y_half = 1 - lax.axis_index("gy")
    for k in range(24):
        rest_ref = upper_rest if k < 12 else lower_rest
        for z in range(shape.z):
            value = out_ref[y_part(shape, k, z, y_half), :]
            rest_ref[dense_rows(shape, k % 12, z), :] = value[0 : shape.t]


def dense_rows(shape, k, z):
    return pl.ds((k * shape.z + z) * shape.t, shape.t)


def chip_last_kernel(
    shape, start_ref, two_ref, four_ref, start_rest, two_rest, upper_rest, lower_rest,
    factors_ref, out_ref,
):
    t, z_extent = shape.t, 2 * shape.z
    alpha_one, alpha_two, scale, first_factor = (
        jnp.broadcast_to(factors_ref[k : k + 1], (t, shape.lanes)) for k in range(4)
    )
    core = lax.axis_index("gy")

    def put(k, z, start, two, four):
        remain = two - alpha_one * start
        result = (four - alpha_one * two - alpha_two * remain) * scale - first_factor * start
        out_ref[pl.ds(k * t * z_extent + z, t, stride=z_extent), :] = result

    for k in range(24):
        four_rest = upper_rest if k < 12 else lower_rest
        for z in range(shape.z):
            rows = y_part(shape, k, z, core)
            put(k, core * shape.z + z, *(ref[rows, :][0:t] for ref in (start_ref, two_ref, four_ref)))
            rows = rest_rows(shape, k, z)
            other = [ref[rows, :][0:t] for ref in (start_rest, two_rest)]
            put(k, (1 - core) * shape.z + z, *other, four_rest[dense_rows(shape, k % 12, z), :])


def chip_shards(source, gauge_links):
    devices_all = lax.axis_size("ta") * lax.axis_size("gz") * 2
    entries = float(source.size * devices_all)
    z_extent = source.shape[4]
    shape = ChipShape(source.shape[3], z_extent // 2, source.shape[5])
    t, rows, lanes = shape.t, shape.rows, shape.lanes
    vmem = pl.BlockSpec(memory_space=pltpu.VMEM)
    smem = pl.BlockSpec(memory_space=pltpu.SMEM)

    def held(*dims):
        return pltpu.VMEM(dims, jnp.float32)

    field = held(24 * shape.parts * rows, lanes)
    links_field = held(72 * shape.parts * rows, lanes)
    z_face, t_face = held(shape.z_rows, lanes), held(shape.t_rows, lanes)
    messages = (z_face, t_face, z_face, t_face)
    z_faces = (z_face, z_face)

    def call(kernel, name, flops, out_shape, operands, **options):
        in_spec = options.pop("in_spec", vmem)
        out_specs = options.pop("out_specs", jax.tree.map(lambda _: vmem, out_shape))
        return pl.pallas_call(
            kernel,
            name=name,
            out_shape=out_shape,
            in_specs=[in_spec] * len(operands),
            out_specs=out_specs,
            compiler_params=pltpu.CompilerParams(vmem_limit_bytes=8 << 20),
            cost_estimate=pl.CostEstimate(flops=flops, bytes_accessed=1 << 20, transcendentals=0),
            **options,
        )(*operands)

    def exchanged(sent):
        z_second, t_second, z_first, t_first = sent
        z_ring = ("gz", "gy")
        return (
            swap(z_second, z_ring, True), swap(t_second, "ta", True),
            swap(z_first, z_ring, False), swap(t_first, "ta", False),
        )

    sites = t * z_extent * lanes
    rows_in = t * z_extent
    own = (source.reshape(24 * rows_in, lanes), gauge_links.reshape(72 * rows_in, lanes))
    other = tuple(swap(value, "gy", False) for value in own)
    rest = held(24 * shape.z * rows, lanes)
    psi, links, start_rest = call(
        functools.partial(chip_own_kernel, shape), "own", 200 * sites, (field, links_field, rest),
        [pltpu.with_memory_space_constraint(value, pltpu.HBM) for value in own],
        scratch_shapes=(
            held(24 * rows_in, lanes), held(72 * rows_in, lanes), pltpu.SemaphoreType.DMA((5,)),
        ),
        in_spec=pl.BlockSpec(memory_space=pltpu.HBM),
    )
    psi, links, *sent = call(
        functools.partial(chip_prep_kernel, shape), "prep", 400 * sites,
        (field, links_field, *messages), (*other, psi, links),
        input_output_aliases={2: 0, 3: 1},
    )
    powers = [psi]
    for step in range(3):
        halo = exchanged(sent)
        inner = functools.partial(chip_inner_kernel, shape)
        total = call(inner, "inner", 1000 * sites, field, (psi, links))
        hands_over = step == 1
        psi, *sent = call(
            functools.partial(chip_mid_kernel, shape, hands_over), "mid", 600 * sites,
            (field, *messages, rest) if hands_over else (field, *messages),
            (psi, links, total, *halo), scratch_shapes=z_faces,
        )
        powers.append(psi)
        if hands_over:
            two_rest = swap(sent.pop(), "gy", False)
    halo = exchanged(sent)
    copies = call(
        functools.partial(chip_sums_kernel, shape), "sums", 400 * sites,
        held(devices_all, 4, lanes), powers,
    )
    total = call(inner, "inner", 1000 * sites, field, (psi, links))
    gathered = from_everyone(copies)
    dense = held(12 * shape.z * t, lanes)
    four, *four_rest = call(
        functools.partial(chip_finish_kernel, shape), "finish", 400 * sites, (field, dense, dense),
        (psi, links, total, *halo), scratch_shapes=z_faces,
    )
    four_rest = [swap(value, "gy", False) for value in four_rest]
    factors, coefficients = call(
        functools.partial(chip_scalars_kernel, entries), "scalars", 10 * sites,
        (held(8, lanes), jax.ShapeDtypeStruct((3,), jnp.float32)), (gathered,),
        out_specs=(vmem, smem),
    )
    residual = call(
        functools.partial(chip_last_kernel, shape), "last", 100 * sites,
        jax.ShapeDtypeStruct((24 * rows_in, lanes), jnp.float32),
        (powers[0], powers[2], four, start_rest, two_rest, *four_rest, factors),
    )
    return (residual.reshape(source.shape), coefficients)


def solution(mesh):
    placed = (P(None, None, None, "ta", "gz", "gy"), P(None, None, None, None, "ta", "gz", "gy"))
    return jax.shard_map(
        chip_shards if mesh.shape["gy"] == 2 else shards,
        mesh=mesh,
        in_specs=placed,
        out_specs=(P(None, None, None, "ta", "gz", "gy"), P()),
        check_vma=False,
    )
```

```python
import functools
import math

import jax
import jax.numpy as jnp
from jax import lax
from jax.experimental import pallas as pl
from jax.experimental.pallas import tpu as pltpu
from jax.sharding import PartitionSpec as P

X = 32

hop_kappa = 0.19
epsilon = 1e-06
spin_table = (
    ((1, 0), (-1j, -1j)),
    ((1, 0), (-1, 1)),
    ((0, 1), (-1j, 1j)),
    ((0, 1), (1, 1)),
)
SPIN_COLOUR = [(spin, colour) for spin in range(2) for colour in range(3)]


def add_phased(left, phase, right):
    phase = complex(phase)
    if phase == 1:
        return (left[0] + right[0], left[1] + right[1])
    if phase == -1:
        return (left[0] - right[0], left[1] - right[1])
    if phase == 1j:
        return (left[0] - right[1], left[1] + right[0])
    return (left[0] + right[1], left[1] - right[0])


def project(psi, direction, parity):
    order, phases = spin_table[direction]
    return {
        (s, c): add_phased(psi[s, c], parity * phases[s], psi[2 + order[s], c])
        for s, c in SPIN_COLOUR
    }


def add_rebuilt(total, half, direction, parity):
    order, phases = spin_table[direction]
    for s, c in SPIN_COLOUR:
        total[s, c] = add_phased(total[s, c], 1, half[s, c])
        row = order[s]
        phase = parity * complex(phases[row]).conjugate()
        total[2 + s, c] = add_phased(total[2 + s, c], phase, half[row, c])


def mul_link(links, direction, z, half):
    out = {}
    for row in range(3):
        for s in range(2):
            real, imag = None, None
            for col in range(3):
                u_real, u_imag = links[direction, row, col, z]
                h_real, h_imag = half[s, col]
                term_real = u_real * h_real - u_imag * h_imag
                term_imag = u_real * h_imag + u_imag * h_real
                real = term_real if real is None else real + term_real
                imag = term_imag if imag is None else imag + term_imag
            out[s, row] = (real, imag)
    return out


def mul_link_dag(links, direction, z, half):
    out = {}
    for row in range(3):
        for s in range(2):
            real, imag = None, None
            for col in range(3):
                u_real, u_imag = links[direction, col, row, z]
                h_real, h_imag = half[s, col]
                term_real = u_real * h_real + u_imag * h_imag
                term_imag = u_real * h_imag - u_imag * h_real
                real = term_real if real is None else real + term_real
                imag = term_imag if imag is None else imag + term_imag
            out[s, row] = (real, imag)
    return out


def mapped(function, *halves):
    return {
        key: tuple(function(*(half[key][part] for half in halves)) for part in range(2))
        for key in SPIN_COLOUR
    }


class Links:
    def __init__(self, ref):
        self.ref = ref

    def __getitem__(self, index):
        direction, row, col, z = index
        first = ((direction * 3 + row) * 3 + col) * 2
        return (self.ref[first, z], self.ref[first + 1, z])


def load_psi(ref, z):
    return {
        (s, c): (ref[(s * 3 + c) * 2, z], ref[(s * 3 + c) * 2 + 1, z])
        for s in range(4)
        for c in range(3)
    }


def load_half(ref, z):
    return {
        (s, c): (ref[(s * 3 + c) * 2, z], ref[(s * 3 + c) * 2 + 1, z]) for s, c in SPIN_COLOUR
    }


def store_half(ref, z, half):
    for (s, c), pair in half.items():
        for part in range(2):
            ref[(s * 3 + c) * 2 + part, z] = pair[part]


class Shape:
    def __init__(self, t_extent, z_extent, lanes):
        self.t = t_extent
        self.z = z_extent
        self.rows = -(-t_extent // 8) * 8
        self.lanes = lanes

    def row(self):
        return lax.broadcasted_iota(jnp.int32, (self.rows, self.lanes), 0)

    def lane(self):
        return lax.broadcasted_iota(jnp.int32, (self.rows, self.lanes), 1)


def is_even(axis):
    return jnp.bitwise_and(lax.axis_index(axis), 1) == 0


def either(choice, first, second):
    return jnp.where(choice, first, second)


def emit_messages(shape, psi_ref, links, refs):
    z_second, t_second, z_first, t_first, y_msg, carried_y, carried_t = refs
    t_even, z_even = is_even("ta"), is_even("gz")
    lane = shape.lane()
    last_z, last_t = shape.z - 1, shape.t - 1
    for z in range(shape.z):
        psi = load_psi(psi_ref, z)
        minus = project(psi, 3, -1)
        carried = mul_link_dag(links, 3, z, project(psi, 3, 1))
        store_half(carried_t, z, carried)
        for s, c in SPIN_COLOUR:
            for part in range(2):
                at = ((s * 3 + c) * 2 + part) * shape.z + z
                down = minus[s, c][part][0:1]
                up = carried[s, c][part][last_t : last_t + 1]
                t_first[at : at + 1] = either(t_even, up, down)
                t_second[at : at + 1] = either(t_even, down, up)
        minus = project(psi, 1, -1)
        carried = mul_link_dag(links, 1, z, project(psi, 1, 1))
        store_half(carried_y, z, carried)
        store_half(
            y_msg,
            z,
            mapped(lambda low, high: jnp.where(lane < X, low, high), minus, carried),
        )
    minus = project(load_psi(psi_ref, 0), 2, -1)
    carried = mul_link_dag(links, 2, last_z, project(load_psi(psi_ref, last_z), 2, 1))
    for s, c in SPIN_COLOUR:
        for part in range(2):
            at = ((s * 3 + c) * 2 + part) * shape.t
            down, up = minus[s, c][part][0 : shape.t], carried[s, c][part][0 : shape.t]
            z_first[at : at + shape.t] = either(z_even, up, down)
            z_second[at : at + shape.t] = either(z_even, down, up)


def prep_kernel(shape, source_hbm, links_hbm, psi_ref, links_ref, *refs):
    messages, (source_ref, links_in, arrived) = refs[:-3], refs[-3:]
    t, z_extent = shape.t, shape.z
    part = 18 * t * z_extent
    copies = [pltpu.make_async_copy(source_hbm, source_ref, arrived.at[4])]
    for direction in (3, 2, 1, 0):
        rows = pl.ds(direction * part, part)
        copies.append(
            pltpu.make_async_copy(links_hbm.at[rows], links_in.at[rows], arrived.at[direction])
        )
    for copy in copies:
        copy.start()
    if shape.rows != t:
        links_ref[...] = jnp.zeros_like(links_ref)
        psi_ref[...] = jnp.zeros_like(psi_ref)
    last = lax.broadcasted_iota(jnp.int32, (t, shape.lanes), 0) == t - 1
    sign = jnp.where(lax.axis_index("ta") == lax.axis_size("ta") - 1, -1.0, 1.0)
    flip = jnp.where(last, sign, 1.0)
    copies[0].wait()
    for k in range(24):
        for z in range(z_extent):
            psi_ref[k, z, 0:t] = source_ref[pl.ds(k * t * z_extent + z, t, stride=z_extent), :]
    for direction in (3, 2, 1, 0):
        copies[4 - direction].wait()
        for k in range(18 * direction, 18 * direction + 18):
            for z in range(z_extent):
                value = links_in[pl.ds(k * t * z_extent + z, t, stride=z_extent), :]
                links_ref[k, z, 0:t] = value * flip if direction == 3 else value
    emit_messages(shape, psi_ref, Links(links_ref), messages)


def summed(shape, term):
    total = None
    for k in range(24):
        for z in range(shape.z):
            value = term(k, z)
            total = value if total is None else total + value
    return total


def over_lanes(total):
    return jnp.sum(jnp.sum(total, axis=0, keepdims=True), axis=1, keepdims=True)


def local_sums(shape, image, origin):
    square = summed(shape, lambda k, z: origin[k, z] * origin[k, z])
    mixed = over_lanes(summed(shape, lambda k, z: image[k, z] * origin[k, z]))
    whole = over_lanes(square)
    factor = jnp.where(whole > 0.0, mixed / jnp.where(whole > 0.0, whole, 1.0), 0.0)
    spread = jnp.broadcast_to(factor, (shape.rows, shape.lanes))
    rest_square, rest_mixed = None, None
    for k in range(24):
        for z in range(shape.z):
            start = origin[k, z]
            rest = image[k, z] - spread * start
            terms = rest * rest, rest * start
            if rest_square is None:
                rest_square, rest_mixed = terms
            else:
                rest_square, rest_mixed = rest_square + terms[0], rest_mixed + terms[1]
    return [factor, *(over_lanes(value) for value in (square, rest_square, rest_mixed))]


def inner_kernel(shape, psi_ref, links_ref, total_ref):
    links = Links(links_ref)
    x = shape.lane() % X
    lanes = shape.lanes
    at_end, at_start = x == X - 1, x == 0

    def ahead(value):
        return jnp.where(
            at_end, pltpu.roll(value, X - 1, 1), pltpu.roll(value, lanes - 1, 1)
        )

    def behind(value):
        return jnp.where(at_start, pltpu.roll(value, lanes - X + 1, 1), pltpu.roll(value, 1, 1))

    for z in range(shape.z):
        psi = load_psi(psi_ref, z)
        zero = jnp.zeros((shape.rows, lanes), jnp.float32)
        total = {key: (zero, zero) for key in psi}
        half = mapped(ahead, project(psi, 0, -1))
        add_rebuilt(total, mul_link(links, 0, z, half), 0, -1)
        half = mapped(behind, mul_link_dag(links, 0, z, project(psi, 0, 1)))
        add_rebuilt(total, half, 0, 1)
        if z + 1 < shape.z:
            half = project(load_psi(psi_ref, z + 1), 2, -1)
            add_rebuilt(total, mul_link(links, 2, z, half), 2, -1)
        if z > 0:
            half = project(load_psi(psi_ref, z - 1), 2, 1)
            add_rebuilt(total, mul_link_dag(links, 2, z - 1, half), 2, 1)
        for (s, c), pair in total.items():
            for part in range(2):
                total_ref[(s * 3 + c) * 2 + part, z] = pair[part]


def add_y_hops(shape, z, psi, total, links, carried_y, y_halo):
    lane, lanes = shape.lane(), shape.lanes
    received = load_half(y_halo, z)
    half = mapped(
        lambda own, other: pltpu.roll(jnp.where(lane < X, other, own), lanes - X, 1),
        project(psi, 1, -1),
        received,
    )
    add_rebuilt(total, mul_link(links, 1, z, half), 1, -1)
    half = mapped(
        lambda own, other: pltpu.roll(jnp.where(lane >= lanes - X, other, own), X, 1),
        load_half(carried_y, z),
        received,
    )
    add_rebuilt(total, half, 1, 1)


def finish_hops(
    shape, psi_ref, links, total_ref, carried_y, carried_t, halo, store
):
    z_second, t_second, z_first, t_first, y_msg = halo
    t_even, z_even = is_even("ta"), is_even("gz")
    row = shape.row()
    lanes, rows, t = shape.lanes, shape.rows, shape.t
    last_z = shape.z - 1

    for z in range(shape.z):
        psi = load_psi(psi_ref, z)
        total = load_psi(total_ref, z)

        def rim_rows(from_even, from_odd):
            half = {}
            for s, c in SPIN_COLOUR:
                ats = [((s * 3 + c) * 2 + part) * shape.z + z for part in range(2)]
                half[s, c] = tuple(
                    jnp.broadcast_to(
                        either(t_even, from_even[at : at + 1], from_odd[at : at + 1]),
                        (rows, lanes),
                    )
                    for at in ats
                )
            return half

        def rim_plane(from_even, from_odd):
            half = {}
            for s, c in SPIN_COLOUR:
                pair = []
                for part in range(2):
                    at = ((s * 3 + c) * 2 + part) * t
                    plane = either(z_even, from_even[at : at + t], from_odd[at : at + t])
                    if rows != t:
                        pad = jnp.zeros((rows - t, lanes), jnp.float32)
                        plane = jnp.concatenate([plane, pad], axis=0)
                    pair.append(plane)
                half[s, c] = tuple(pair)
            return half

        if y_msg is not None:
            add_y_hops(shape, z, psi, total, links, carried_y, y_msg)
        if z == last_z:
            add_rebuilt(total, mul_link(links, 2, z, rim_plane(z_first, z_second)), 2, -1)
        if z == 0:
            add_rebuilt(total, rim_plane(z_second, z_first), 2, 1)
        half = mapped(
            lambda own, other: jnp.where(row == t - 1, other, pltpu.roll(own, rows - 1, 0)),
            project(psi, 3, -1),
            rim_rows(t_first, t_second),
        )
        add_rebuilt(total, mul_link(links, 3, z, half), 3, -1)
        half = mapped(
            lambda own, other: jnp.where(row == 0, other, pltpu.roll(own, 1, 0)),
            load_half(carried_t, z),
            rim_rows(t_second, t_first),
        )
        add_rebuilt(total, half, 3, 1)
        for (s, c), pair in total.items():
            for part in range(2):
                value = psi[s, c][part] - hop_kappa * pair[part]
                value = value if s < 2 else -value
                if rows != t:
                    value = jnp.where(row < t, value, 0.0)
                store((s * 3 + c) * 2 + part, z, value)


def mid_kernel(shape, psi_ref, links_ref, total_ref, carried_y, carried_t, *refs):
    halo, out_ref, messages = refs[:5], refs[5], refs[6:]
    links = Links(links_ref)

    def store(k, z, value):
        out_ref[k, z] = value

    finish_hops(
        shape, psi_ref, links, total_ref, carried_y, carried_t, halo, store
    )
    emit_messages(shape, out_ref, links, messages)


def sums_row(shape, two, start, three, one):
    sums = local_sums(shape, two, start) + local_sums(shape, three, one)
    lane = lax.broadcasted_iota(jnp.int32, (1, shape.lanes), 1)
    row = jnp.zeros((1, shape.lanes), jnp.float32)
    for k, value in enumerate(sums):
        row = jnp.where(lane == k, value, row)
    return row


def inner_sums_kernel(
    shape, psi_ref, links_ref, start_ref, one_ref, two_ref, total_ref, copies_ref
):
    row = sums_row(shape, two_ref, start_ref, psi_ref, one_ref)
    copies_ref[...] = jnp.broadcast_to(row[None], copies_ref.shape)
    inner_kernel(shape, psi_ref, links_ref, total_ref)


def finish_kernel(shape, psi_ref, links_ref, total_ref, carried_y, carried_t, *refs):
    halo, out_ref = refs[:5], refs[5]

    def store(k, z, value):
        out_ref[k, z] = value

    finish_hops(
        shape, psi_ref, Links(links_ref), total_ref, carried_y, carried_t, halo, store
    )


def scalars(table, entries):
    columns = [table[:, k : k + 1] for k in range(8)]
    factor_two, start_square, two_square, two_mixed = columns[:4]
    factor_three, one_square, three_square, three_mixed = columns[4:]

    def over_devices(column):
        return jnp.sum(column, axis=0, keepdims=True)

    norm_square = over_devices(start_square) / entries + epsilon
    alpha_one = over_devices(one_square) / entries / norm_square
    gap = alpha_one - factor_two
    remain_square = over_devices(two_square - gap * (2.0 * two_mixed - gap * start_square)) / entries
    overlap = over_devices(two_mixed - gap * start_square) / entries
    gap = alpha_one - factor_three
    image_square = over_devices(three_square - gap * (2.0 * three_mixed - gap * one_square)) / entries
    norm = jnp.sqrt(norm_square)
    beta_one = jnp.sqrt(remain_square / norm_square + epsilon)
    overlap = overlap / (norm_square * beta_one)
    alpha_two = image_square / (norm_square * beta_one * beta_one) - beta_one * overlap
    scale = 1.0 / (norm * beta_one)
    return alpha_one, beta_one, alpha_two, scale, beta_one / norm


def last_kernel(
    shape, entries, start_ref, two_ref, four_ref, gathered, out_ref, coefficients
):
    alpha_one, beta_one, alpha_two, scale, first_factor = scalars(gathered[:, 0, :], entries)
    t, z_extent = shape.t, shape.z
    for k in range(24):
        for z in range(z_extent):
            two, start = two_ref[k, z], start_ref[k, z]
            remain = two - alpha_one * start
            result = (four_ref[k, z] - alpha_one * two - alpha_two * remain) * scale
            result = result - first_factor * start
            out_ref[pl.ds(k * t * z_extent + z, t, stride=z_extent), :] = result[0:t]
    coefficients[0] = alpha_one[0, 0]
    coefficients[1] = beta_one[0, 0]
    coefficients[2] = alpha_two[0, 0]


def swap(value, axis, second):
    count = math.prod(lax.axis_size(name) for name in (axis if isinstance(axis, tuple) else (axis,)))
    pairs = []
    for low in range(1 if second else 0, count, 2):
        high = (low + 1) % count
        pairs += [(low, high), (high, low)]
    return lax.ppermute(value, axis, pairs)


def exchange(messages, lanes):
    z_second, t_second, z_first, t_first, y_msg = messages
    halo = (
        swap(z_second, "gz", True),
        swap(t_second, "ta", True),
        swap(z_first, "gz", False),
        swap(t_first, "ta", False),
    )
    y_halo = swap(y_msg, "gy", False)
    if lax.axis_size("gy") > 2:
        even = lax.axis_index("gy") % 2 == 0
        lane = lax.broadcasted_iota(jnp.int32, y_msg.shape, y_msg.ndim - 1)
        y_halo = jnp.where((lane < lanes // 2) == even, y_halo, swap(y_msg, "gy", True))
    return (*halo, y_halo)


def from_everyone(copies):
    return lax.all_to_all(copies, ("ta", "gz", "gy"), split_axis=0, concat_axis=0, tiled=True)


def shards(source, gauge_links):
    devices_all = lax.axis_size("ta") * lax.axis_size("gz") * lax.axis_size("gy")
    entries = float(source.size * devices_all)
    shape = Shape(source.shape[3], source.shape[4], source.shape[5])
    t, z, rows, lanes = shape.t, shape.z, shape.rows, shape.lanes
    vmem = pl.BlockSpec(memory_space=pltpu.VMEM)
    smem = pl.BlockSpec(memory_space=pltpu.SMEM)

    def held(*dims):
        return pltpu.VMEM(dims, jnp.float32)

    field = held(24, z, rows, lanes)
    half = held(12, z, rows, lanes)
    z_face, t_face = held(12 * t, lanes), held(12 * z, lanes)
    messages = (z_face, t_face, z_face, t_face, half, half, half)

    def call(kernel, name, flops, out_shape, operands, out_specs=None, in_spec=vmem, scratch=()):
        return pl.pallas_call(
            kernel,
            name=name,
            out_shape=out_shape,
            in_specs=[in_spec] * len(operands),
            out_specs=out_specs or jax.tree.map(lambda _: vmem, out_shape),
            scratch_shapes=scratch,
            compiler_params=pltpu.CompilerParams(vmem_limit_bytes=8 << 20),
            cost_estimate=pl.CostEstimate(flops=flops, bytes_accessed=1 << 20, transcendentals=0),
        )(*operands)

    sites = t * z * lanes
    psi, links, *sent = call(
        functools.partial(prep_kernel, shape), "prep", 400 * sites,
        (field, held(72, z, rows, lanes), *messages),
        (
            pltpu.with_memory_space_constraint(source.reshape(24 * t * z, lanes), pltpu.HBM),
            pltpu.with_memory_space_constraint(gauge_links.reshape(72 * t * z, lanes), pltpu.HBM),
        ),
        in_spec=pl.BlockSpec(memory_space=pltpu.HBM),
        scratch=(
            held(24 * t * z, lanes), held(72 * t * z, lanes), pltpu.SemaphoreType.DMA((5,)),
        ),
    )
    powers = [psi]
    for step in range(3):
        halo = exchange(sent[:5], lanes)
        inner = functools.partial(inner_kernel, shape)
        total = call(inner, "inner", 700 * sites, field, (psi, links))
        psi, *sent = call(
            functools.partial(mid_kernel, shape), "mid", 1000 * sites,
            (field, *messages), (psi, links, total, *sent[5:], *halo),
        )
        powers.append(psi)
    halo = exchange(sent[:5], lanes)
    total, copies = call(
        functools.partial(inner_sums_kernel, shape), "inner_sums", 1100 * sites,
        (field, held(devices_all, 8, lanes)), (psi, links, *powers[:3]),
    )
    gathered = from_everyone(copies)
    four = call(
        functools.partial(finish_kernel, shape), "finish", 700 * sites, field,
        (psi, links, total, *sent[5:], *halo),
    )
    residual, coefficients = call(
        functools.partial(last_kernel, shape, entries), "last", 100 * sites,
        (
            jax.ShapeDtypeStruct((24 * t * z, lanes), jnp.float32),
            jax.ShapeDtypeStruct((3,), jnp.float32),
        ),
        (powers[0], powers[2], four, gathered), (vmem, smem),
    )
    return (residual.reshape(source.shape), coefficients)


class ChipShape(Shape):
    def __init__(self, t_extent, z_extent, lanes):
        super().__init__(t_extent, z_extent, lanes)
        self.parts = 2 * z_extent
        self.z_rows = 24 * t_extent
        self.t_rows = 12 * self.parts

    def block(self, k, part):
        first = (k * self.parts + part) * self.rows
        return pl.ds(first, self.rows)

    def edge(self, k, row):
        return pl.ds(k * self.parts * self.rows + row, self.parts, stride=self.rows)


class ChipLinks:
    def __init__(self, shape, ref, row=None):
        self.shape, self.ref, self.row = shape, ref, row

    def __getitem__(self, index):
        direction, row, col, part = index
        first = ((direction * 3 + row) * 3 + col) * 2
        if self.row is None:
            return tuple(self.ref[self.shape.block(first + n, part), :] for n in range(2))
        return tuple(self.ref[self.shape.edge(first + n, self.row), :] for n in range(2))


def components(spins):
    return [(s, c, part, (s * 3 + c) * 2 + part) for s in range(spins) for c in range(3) for part in range(2)]


def gathered_pairs(spins, value):
    out = {}
    for s in range(spins):
        for c in range(3):
            out[s, c] = tuple(value((s * 3 + c) * 2 + part) for part in range(2))
    return out


def chip_psi(shape, ref, part):
    return gathered_pairs(4, lambda k: ref[shape.block(k, part), :])


def chip_edge(shape, ref, row):
    return gathered_pairs(4, lambda k: ref[shape.edge(k, row), :])


def chip_messages(shape, psi_ref, links_ref, z_second, t_second, z_first, t_first):
    t, last = shape.t, shape.t - 1
    even = is_even("ta")
    minus = project(chip_edge(shape, psi_ref, 0), 3, -1)
    half = project(chip_edge(shape, psi_ref, last), 3, 1)
    carried = mul_link_dag(ChipLinks(shape, links_ref, last), 3, 0, half)
    for s, c, part, k in components(2):
        rows = pl.ds(k * shape.parts, shape.parts)
        up, down = carried[s, c][part], minus[s, c][part]
        t_first[rows, :] = either(even, up, down)
        t_second[rows, :] = either(even, down, up)
    even = is_even("gy")
    links = ChipLinks(shape, links_ref)
    for y_half in range(2):
        minus = project(chip_psi(shape, psi_ref, y_half), 2, -1)
        part_last = shape.parts - 2 + y_half
        half = project(chip_psi(shape, psi_ref, part_last), 2, 1)
        carried = mul_link_dag(links, 2, part_last, half)
        for s, c, part, k in components(2):
            rows = pl.ds((k * 2 + y_half) * t, t)
            up, down = carried[s, c][part][0:t], minus[s, c][part][0:t]
            z_first[rows, :] = either(even, up, down)
            z_second[rows, :] = either(even, down, up)


def chip_bring(shape, y_half, source_ref, links_in, psi_ref, links_ref, arrived):
    t, z_extent = shape.t, 2 * shape.z
    first_plane = lax.axis_index("gy") * shape.z
    last = lax.broadcasted_iota(jnp.int32, (t, shape.lanes), 0) == t - 1
    sign = jnp.where(lax.axis_index("ta") == lax.axis_size("ta") - 1, -1.0, 1.0)
    flip = jnp.where(last, sign, 1.0)

    def bring(in_ref, out_ref, k, z, factor=None):
        value = in_ref[pl.ds(k * t * z_extent + first_plane + z, t, stride=z_extent), :]
        if factor is not None:
            value = value * factor
        at = (k * shape.parts + 2 * z + y_half) * shape.rows
        out_ref[pl.ds(pl.multiple_of(at, 8), t), :] = value

    arrived(4)
    for z in range(shape.z):
        for k in range(24):
            bring(source_ref, psi_ref, k, z)
    for direction in (3, 2, 1, 0):
        arrived(direction)
        for z in range(shape.z):
            for k in range(18 * direction, 18 * direction + 18):
                bring(links_in, links_ref, k, z, flip if direction == 3 else None)


def chip_own_kernel(
    shape, source_hbm, links_hbm, psi_ref, links_ref, rest_ref, source_ref, links_in, semaphores
):
    part = 18 * shape.t * 2 * shape.z
    copies = {4: pltpu.make_async_copy(source_hbm, source_ref, semaphores.at[4])}
    for direction in (3, 2, 1, 0):
        rows = pl.ds(direction * part, part)
        copies[direction] = pltpu.make_async_copy(
            links_hbm.at[rows], links_in.at[rows], semaphores.at[direction]
        )
    for copy in copies.values():
        copy.start()
    if shape.rows != shape.t:
        links_ref[...] = jnp.zeros_like(links_ref)
        psi_ref[...] = jnp.zeros_like(psi_ref)
    chip_bring(
        shape, lax.axis_index("gy"), source_ref, links_in, psi_ref, links_ref,
        lambda n: copies[n].wait(),
    )
    t, z_extent = shape.t, 2 * shape.z
    first_plane = (1 - lax.axis_index("gy")) * shape.z
    if shape.rows != t:
        rest_ref[...] = jnp.zeros_like(rest_ref)
    for k in range(24):
        for z in range(shape.z):
            value = source_ref[pl.ds(k * t * z_extent + first_plane + z, t, stride=z_extent), :]
            rest_ref[pl.ds((k * shape.z + z) * shape.rows, t), :] = value


def chip_prep_kernel(
    shape, source_ref, links_in, psi_in, links_held, psi_ref, links_ref, *messages
):
    chip_bring(
        shape, 1 - lax.axis_index("gy"), source_ref, links_in, psi_ref, links_ref, lambda n: None
    )
    chip_messages(shape, psi_ref, links_ref, *messages)


def chip_inner_kernel(shape, psi_ref, links_ref, total_ref):
    links = ChipLinks(shape, links_ref)
    lane, row = shape.lane(), shape.row()
    x = lane % X
    lanes, rows, t = shape.lanes, shape.rows, shape.t
    at_end, at_start = x == X - 1, x == 0
    inside_ahead = row < t - 1
    inside_behind = jnp.logical_and(row > 0, row < t)

    def x_ahead(value):
        return jnp.where(
            at_end, pltpu.roll(value, X - 1, 1), pltpu.roll(value, lanes - 1, 1)
        )

    def x_behind(value):
        return jnp.where(at_start, pltpu.roll(value, lanes - X + 1, 1), pltpu.roll(value, 1, 1))

    def t_ahead(value):
        return jnp.where(inside_ahead, pltpu.roll(value, rows - 1, 0), 0.0)

    def t_behind(value):
        return jnp.where(inside_behind, pltpu.roll(value, 1, 0), 0.0)

    for z in range(shape.z):
        for part in (2 * z, 2 * z + 1):
            psi = chip_psi(shape, psi_ref, part)
            zero = jnp.zeros((rows, lanes), jnp.float32)
            total = {key: (zero, zero) for key in psi}
            half = mapped(x_ahead, project(psi, 0, -1))
            add_rebuilt(total, mul_link(links, 0, part, half), 0, -1)
            half = mapped(x_behind, mul_link_dag(links, 0, part, project(psi, 0, 1)))
            add_rebuilt(total, half, 0, 1)
            half = mapped(t_ahead, project(psi, 3, -1))
            add_rebuilt(total, mul_link(links, 3, part, half), 3, -1)
            half = mapped(t_behind, mul_link_dag(links, 3, part, project(psi, 3, 1)))
            add_rebuilt(total, half, 3, 1)
            if z + 1 < shape.z:
                half = project(chip_psi(shape, psi_ref, part + 2), 2, -1)
                add_rebuilt(total, mul_link(links, 2, part, half), 2, -1)
            if z > 0:
                half = project(chip_psi(shape, psi_ref, part - 2), 2, 1)
                add_rebuilt(total, mul_link_dag(links, 2, part - 2, half), 2, 1)
            for s, c, n, k in components(4):
                total_ref[shape.block(k, part), :] = total[s, c][n]
        pair = (2 * z, 2 * z + 1)
        minus, carried = [], []
        for part in pair:
            psi = chip_psi(shape, psi_ref, part)
            minus.append(mapped(lambda v: pltpu.roll(v, lanes - X, 1), project(psi, 1, -1)))
            half = mul_link_dag(links, 1, part, project(psi, 1, 1))
            carried.append(mapped(lambda v: pltpu.roll(v, X, 1), half))
        for own, part in enumerate(pair):
            total = chip_psi(shape, total_ref, part)
            half = mapped(
                lambda a, b: jnp.where(lane >= lanes - X, b, a), minus[own], minus[1 - own]
            )
            add_rebuilt(total, mul_link(links, 1, part, half), 1, -1)
            half = mapped(lambda a, b: jnp.where(lane < X, b, a), carried[own], carried[1 - own])
            add_rebuilt(total, half, 1, 1)
            for s, c, n, k in components(4):
                total_ref[shape.block(k, part), :] = total[s, c][n]


def chip_sort_faces(z_second, z_first, scratch):
    z_down, z_up = scratch
    z_even = is_even("gy")
    second = 0.0 if z_second is None else z_second[...]
    first = 0.0 if z_first is None else z_first[...]
    z_down[...] = either(z_even, first, second)
    z_up[...] = either(z_even, second, first)


def chip_add_z(shape, links, part, total, scratch):
    z_down, z_up = scratch
    t, rows, lanes, parts = shape.t, shape.rows, shape.lanes, shape.parts

    def plane(ref, y_half):
        def value(k):
            face = ref[pl.ds((k * 2 + y_half) * t, t), :]
            if rows != t:
                pad = jnp.zeros((rows - t, lanes), jnp.float32)
                face = jnp.concatenate([face, pad], axis=0)
            return face

        return gathered_pairs(2, value)

    if part >= parts - 2:
        half = mul_link(links, 2, part, plane(z_down, part - parts + 2))
        add_rebuilt(total, half, 2, -1)
    if part < 2:
        add_rebuilt(total, plane(z_up, part), 2, 1)


def chip_finish(shape, psi_ref, links_ref, total_ref, received, scratch, out_ref):
    z_second, t_second, z_first, t_first = received
    t_even = is_even("ta")
    t, lanes, parts = shape.t, shape.lanes, shape.parts
    chip_sort_faces(z_second, z_first, scratch)
    links = ChipLinks(shape, links_ref)

    for part in range(parts):
        total = chip_psi(shape, total_ref, part)
        chip_add_z(shape, links, part, total, scratch)
        for s, c, n, k in components(4):
            value = psi_ref[shape.block(k, part), :] - hop_kappa * total[s, c][n]
            out_ref[shape.block(k, part), :] = value if s < 2 else -value

    def t_half(from_even, from_odd):
        def value(k):
            at = pl.ds(k * parts, parts)
            return either(t_even, from_even[at, :], from_odd[at, :])

        return gathered_pairs(2, value)

    down = mul_link(ChipLinks(shape, links_ref, t - 1), 3, 0, t_half(t_first, t_second))
    up = t_half(t_second, t_first)
    zero = jnp.zeros((parts, lanes), jnp.float32)
    for half, parity, row in ((down, -1, t - 1), (up, 1, 0)):
        total = {(s, c): (zero, zero) for s in range(4) for c in range(3)}
        add_rebuilt(total, half, 3, parity)
        for s, c, n, k in components(4):
            at = shape.edge(k, row)
            value = hop_kappa * total[s, c][n]
            out_ref[at, :] = out_ref[at, :] - (value if s < 2 else -value)


def chip_mid_kernel(shape, hands_over, psi_ref, links_ref, total_ref, *refs):
    received, out_ref, messages, refs = refs[:4], refs[4], refs[5:9], refs[9:]
    chip_finish(shape, psi_ref, links_ref, total_ref, received, refs[-2:], out_ref)
    chip_messages(shape, out_ref, links_ref, *messages)
    if hands_over:
        hand_over(shape, out_ref, refs[0])


def chip_sums_kernel(
    shape, links_ref, total_in, z_first, start_ref, one_ref, two_ref, three_ref,
    total_ref, copies_ref, *scratch,
):
    class View:
        def __init__(self, ref):
            self.ref = ref

        def __getitem__(self, index):
            return self.ref[shape.block(*index), :]

    wide = ChipShape(shape.t, shape.z, shape.lanes)
    wide.z = shape.parts
    row = sums_row(wide, View(two_ref), View(start_ref), View(three_ref), View(one_ref))
    copies_ref[...] = jnp.broadcast_to(row[None], copies_ref.shape)
    chip_sort_faces(None, z_first, scratch)
    for part in range(shape.parts):
        total = chip_psi(shape, total_in, part)
        chip_add_z(shape, ChipLinks(shape, links_ref), part, total, scratch)
        for s, c, n, k in components(4):
            total_ref[shape.block(k, part), :] = total[s, c][n]


def chip_scalars_kernel(entries, gathered, factors_ref, coefficients):
    alpha_one, beta_one, alpha_two, scale, first_factor = scalars(gathered[:, 0, :], entries)
    lanes = factors_ref.shape[1]
    values = [alpha_one, alpha_two, scale, first_factor]
    values = [jnp.broadcast_to(value, (1, lanes)) for value in values]
    values.append(jnp.zeros((4, lanes), jnp.float32))
    factors_ref[...] = jnp.concatenate(values, axis=0)
    coefficients[0] = alpha_one[0, 0]
    coefficients[1] = beta_one[0, 0]
    coefficients[2] = alpha_two[0, 0]


def y_part(shape, k, z, y_half):
    return pl.ds(pl.multiple_of((k * shape.parts + 2 * z + y_half) * shape.rows, 8), shape.rows)


def rest_rows(shape, k, z):
    return pl.ds((k * shape.z + z) * shape.rows, shape.rows)


def hand_over(shape, ref, rest_ref):
    y_half = 1 - lax.axis_index("gy")
    for k in range(24):
        for z in range(shape.z):
            rest_ref[rest_rows(shape, k, z), :] = ref[y_part(shape, k, z, y_half), :]


def chip_finish_kernel(
    shape, psi_ref, links_ref, total_ref, z_second, t_second, t_first,
    out_ref, upper_rest, lower_rest, *scratch,
):
    received = z_second, t_second, None, t_first
    chip_finish(shape, psi_ref, links_ref, total_ref, received, scratch, out_ref)
    y_half = 1 - lax.axis_index("gy")
    for k in range(24):
        rest_ref = upper_rest if k < 12 else lower_rest
        for z in range(shape.z):
            value = out_ref[y_part(shape, k, z, y_half), :]
            rest_ref[dense_rows(shape, k % 12, z), :] = value[0 : shape.t]


def dense_rows(shape, k, z):
    return pl.ds((k * shape.z + z) * shape.t, shape.t)


def chip_last_kernel(
    shape, start_ref, two_ref, four_ref, start_rest, two_rest, upper_rest, lower_rest,
    factors_ref, out_ref,
):
    t, z_extent = shape.t, 2 * shape.z
    alpha_one, alpha_two, scale, first_factor = (
        jnp.broadcast_to(factors_ref[k : k + 1], (t, shape.lanes)) for k in range(4)
    )
    core = lax.axis_index("gy")

    def put(k, z, start, two, four):
        remain = two - alpha_one * start
        result = (four - alpha_one * two - alpha_two * remain) * scale - first_factor * start
        out_ref[pl.ds(k * t * z_extent + z, t, stride=z_extent), :] = result

    for k in range(24):
        four_rest = upper_rest if k < 12 else lower_rest
        for z in range(shape.z):
            rows = y_part(shape, k, z, core)
            put(k, core * shape.z + z, *(ref[rows, :][0:t] for ref in (start_ref, two_ref, four_ref)))
            rows = rest_rows(shape, k, z)
            other = [ref[rows, :][0:t] for ref in (start_rest, two_rest)]
            put(k, (1 - core) * shape.z + z, *other, four_rest[dense_rows(shape, k % 12, z), :])


def chip_shards(source, gauge_links):
    devices_all = lax.axis_size("ta") * lax.axis_size("gz") * 2
    entries = float(source.size * devices_all)
    z_extent = source.shape[4]
    shape = ChipShape(source.shape[3], z_extent // 2, source.shape[5])
    t, rows, lanes = shape.t, shape.rows, shape.lanes
    vmem = pl.BlockSpec(memory_space=pltpu.VMEM)
    smem = pl.BlockSpec(memory_space=pltpu.SMEM)

    def held(*dims):
        return pltpu.VMEM(dims, jnp.float32)

    field = held(24 * shape.parts * rows, lanes)
    links_field = held(72 * shape.parts * rows, lanes)
    z_face, t_face = held(shape.z_rows, lanes), held(shape.t_rows, lanes)
    messages = (z_face, t_face, z_face, t_face)
    z_faces = (z_face, z_face)

    def call(kernel, name, flops, out_shape, operands, **options):
        in_spec = options.pop("in_spec", vmem)
        out_specs = options.pop("out_specs", jax.tree.map(lambda _: vmem, out_shape))
        return pl.pallas_call(
            kernel,
            name=name,
            out_shape=out_shape,
            in_specs=[in_spec] * len(operands),
            out_specs=out_specs,
            compiler_params=pltpu.CompilerParams(vmem_limit_bytes=8 << 20),
            cost_estimate=pl.CostEstimate(flops=flops, bytes_accessed=1 << 20, transcendentals=0),
            **options,
        )(*operands)

    def exchanged(sent):
        z_second, t_second, z_first, t_first = sent
        z_ring = ("gz", "gy")
        return (
            swap(z_second, z_ring, True), swap(t_second, "ta", True),
            swap(z_first, z_ring, False), swap(t_first, "ta", False),
        )

    sites = t * z_extent * lanes
    rows_in = t * z_extent
    own = (source.reshape(24 * rows_in, lanes), gauge_links.reshape(72 * rows_in, lanes))
    other = tuple(swap(value, "gy", False) for value in own)
    rest = held(24 * shape.z * rows, lanes)
    psi, links, start_rest = call(
        functools.partial(chip_own_kernel, shape), "own", 200 * sites, (field, links_field, rest),
        [pltpu.with_memory_space_constraint(value, pltpu.HBM) for value in own],
        scratch_shapes=(
            held(24 * rows_in, lanes), held(72 * rows_in, lanes), pltpu.SemaphoreType.DMA((5,)),
        ),
        in_spec=pl.BlockSpec(memory_space=pltpu.HBM),
    )
    psi, links, *sent = call(
        functools.partial(chip_prep_kernel, shape), "prep", 400 * sites,
        (field, links_field, *messages), (*other, psi, links),
        input_output_aliases={2: 0, 3: 1},
    )
    powers = [psi]
    for step in range(3):
        halo = exchanged(sent)
        inner = functools.partial(chip_inner_kernel, shape)
        total = call(inner, "inner", 1000 * sites, field, (psi, links))
        hands_over = step == 1
        psi, *sent = call(
            functools.partial(chip_mid_kernel, shape, hands_over), "mid", 600 * sites,
            (field, *messages, rest) if hands_over else (field, *messages),
            (psi, links, total, *halo), scratch_shapes=z_faces,
        )
        powers.append(psi)
        if hands_over:
            two_rest = swap(sent.pop(), "gy", False)
    halo = exchanged(sent)
    total = call(inner, "inner", 1000 * sites, field, (psi, links))
    total, copies = call(
        functools.partial(chip_sums_kernel, shape), "sums", 600 * sites,
        (field, held(devices_all, 1, lanes)), (links, total, halo[2], *powers),
        scratch_shapes=z_faces,
    )
    gathered = from_everyone(copies)
    dense = held(12 * shape.z * t, lanes)
    four, *four_rest = call(
        functools.partial(chip_finish_kernel, shape), "finish", 400 * sites, (field, dense, dense),
        (psi, links, total, halo[0], halo[1], halo[3]), scratch_shapes=z_faces,
    )
    four_rest = [swap(value, "gy", False) for value in four_rest]
    factors, coefficients = call(
        functools.partial(chip_scalars_kernel, entries), "scalars", 10**11,
        (held(8, lanes), jax.ShapeDtypeStruct((3,), jnp.float32)), (gathered,),
        out_specs=(vmem, smem),
    )
    residual = call(
        functools.partial(chip_last_kernel, shape), "last", 100 * sites,
        jax.ShapeDtypeStruct((24 * rows_in, lanes), jnp.float32),
        (powers[0], powers[2], four, start_rest, two_rest, *four_rest, factors),
    )
    return (residual.reshape(source.shape), coefficients)


def solution(mesh):
    placed = (P(None, None, None, "ta", "gz", "gy"), P(None, None, None, None, "ta", "gz", "gy"))
    return jax.shard_map(
        chip_shards if mesh.shape["gy"] == 2 else shards,
        mesh=mesh,
        in_specs=placed,
        out_specs=(P(None, None, None, "ta", "gz", "gy"), P()),
        check_vma=False,
    )
```

```python
import functools
import math

import jax
import jax.numpy as jnp
from jax import lax
from jax.experimental import pallas as pl
from jax.experimental.pallas import tpu as pltpu
from jax.sharding import PartitionSpec as P

X = 32

hop_kappa = 0.19
epsilon = 1e-06
spin_table = (
    ((1, 0), (-1j, -1j)),
    ((1, 0), (-1, 1)),
    ((0, 1), (-1j, 1j)),
    ((0, 1), (1, 1)),
)
SPIN_COLOUR = [(spin, colour) for spin in range(2) for colour in range(3)]


def add_phased(left, phase, right):
    phase = complex(phase)
    if phase == 1:
        return (left[0] + right[0], left[1] + right[1])
    if phase == -1:
        return (left[0] - right[0], left[1] - right[1])
    if phase == 1j:
        return (left[0] - right[1], left[1] + right[0])
    return (left[0] + right[1], left[1] - right[0])


def project(psi, direction, parity):
    order, phases = spin_table[direction]
    return {
        (s, c): add_phased(psi[s, c], parity * phases[s], psi[2 + order[s], c])
        for s, c in SPIN_COLOUR
    }


def add_rebuilt(total, half, direction, parity):
    order, phases = spin_table[direction]
    for s, c in SPIN_COLOUR:
        total[s, c] = add_phased(total[s, c], 1, half[s, c])
        row = order[s]
        phase = parity * complex(phases[row]).conjugate()
        total[2 + s, c] = add_phased(total[2 + s, c], phase, half[row, c])


def mul_link(links, direction, z, half):
    out = {}
    for row in range(3):
        for s in range(2):
            real, imag = None, None
            for col in range(3):
                u_real, u_imag = links[direction, row, col, z]
                h_real, h_imag = half[s, col]
                term_real = u_real * h_real - u_imag * h_imag
                term_imag = u_real * h_imag + u_imag * h_real
                real = term_real if real is None else real + term_real
                imag = term_imag if imag is None else imag + term_imag
            out[s, row] = (real, imag)
    return out


def mul_link_dag(links, direction, z, half):
    out = {}
    for row in range(3):
        for s in range(2):
            real, imag = None, None
            for col in range(3):
                u_real, u_imag = links[direction, col, row, z]
                h_real, h_imag = half[s, col]
                term_real = u_real * h_real + u_imag * h_imag
                term_imag = u_real * h_imag - u_imag * h_real
                real = term_real if real is None else real + term_real
                imag = term_imag if imag is None else imag + term_imag
            out[s, row] = (real, imag)
    return out


def mapped(function, *halves):
    return {
        key: tuple(function(*(half[key][part] for half in halves)) for part in range(2))
        for key in SPIN_COLOUR
    }


class Links:
    def __init__(self, ref):
        self.ref = ref

    def __getitem__(self, index):
        direction, row, col, z = index
        first = ((direction * 3 + row) * 3 + col) * 2
        return (self.ref[first, z], self.ref[first + 1, z])


def load_psi(ref, z):
    return {
        (s, c): (ref[(s * 3 + c) * 2, z], ref[(s * 3 + c) * 2 + 1, z])
        for s in range(4)
        for c in range(3)
    }


def load_half(ref, z):
    return {
        (s, c): (ref[(s * 3 + c) * 2, z], ref[(s * 3 + c) * 2 + 1, z]) for s, c in SPIN_COLOUR
    }


def store_half(ref, z, half):
    for (s, c), pair in half.items():
        for part in range(2):
            ref[(s * 3 + c) * 2 + part, z] = pair[part]


class Shape:
    def __init__(self, t_extent, z_extent, lanes):
        self.t = t_extent
        self.z = z_extent
        self.rows = -(-t_extent // 8) * 8
        self.lanes = lanes

    def row(self):
        return lax.broadcasted_iota(jnp.int32, (self.rows, self.lanes), 0)

    def lane(self):
        return lax.broadcasted_iota(jnp.int32, (self.rows, self.lanes), 1)


def is_even(axis):
    return jnp.bitwise_and(lax.axis_index(axis), 1) == 0


def either(choice, first, second):
    return jnp.where(choice, first, second)


def emit_messages(shape, psi_ref, links, refs):
    z_second, t_second, z_first, t_first, y_msg, carried_y, carried_t = refs
    t_even, z_even = is_even("ta"), is_even("gz")
    lane = shape.lane()
    last_z, last_t = shape.z - 1, shape.t - 1
    for z in range(shape.z):
        psi = load_psi(psi_ref, z)
        minus = project(psi, 3, -1)
        carried = mul_link_dag(links, 3, z, project(psi, 3, 1))
        store_half(carried_t, z, carried)
        for s, c in SPIN_COLOUR:
            for part in range(2):
                at = ((s * 3 + c) * 2 + part) * shape.z + z
                down = minus[s, c][part][0:1]
                up = carried[s, c][part][last_t : last_t + 1]
                t_first[at : at + 1] = either(t_even, up, down)
                t_second[at : at + 1] = either(t_even, down, up)
        minus = project(psi, 1, -1)
        carried = mul_link_dag(links, 1, z, project(psi, 1, 1))
        store_half(carried_y, z, carried)
        store_half(
            y_msg,
            z,
            mapped(lambda low, high: jnp.where(lane < X, low, high), minus, carried),
        )
    minus = project(load_psi(psi_ref, 0), 2, -1)
    carried = mul_link_dag(links, 2, last_z, project(load_psi(psi_ref, last_z), 2, 1))
    for s, c in SPIN_COLOUR:
        for part in range(2):
            at = ((s * 3 + c) * 2 + part) * shape.t
            down, up = minus[s, c][part][0 : shape.t], carried[s, c][part][0 : shape.t]
            z_first[at : at + shape.t] = either(z_even, up, down)
            z_second[at : at + shape.t] = either(z_even, down, up)


def prep_kernel(shape, source_hbm, links_hbm, psi_ref, links_ref, *refs):
    messages, (source_ref, links_in, arrived) = refs[:-3], refs[-3:]
    t, z_extent = shape.t, shape.z
    part = 18 * t * z_extent
    copies = [pltpu.make_async_copy(source_hbm, source_ref, arrived.at[4])]
    for direction in (3, 2, 1, 0):
        rows = pl.ds(direction * part, part)
        copies.append(
            pltpu.make_async_copy(links_hbm.at[rows], links_in.at[rows], arrived.at[direction])
        )
    for copy in copies:
        copy.start()
    if shape.rows != t:
        links_ref[...] = jnp.zeros_like(links_ref)
        psi_ref[...] = jnp.zeros_like(psi_ref)
    last = lax.broadcasted_iota(jnp.int32, (t, shape.lanes), 0) == t - 1
    sign = jnp.where(lax.axis_index("ta") == lax.axis_size("ta") - 1, -1.0, 1.0)
    flip = jnp.where(last, sign, 1.0)
    copies[0].wait()
    for k in range(24):
        for z in range(z_extent):
            psi_ref[k, z, 0:t] = source_ref[pl.ds(k * t * z_extent + z, t, stride=z_extent), :]
    for direction in (3, 2, 1, 0):
        copies[4 - direction].wait()
        for k in range(18 * direction, 18 * direction + 18):
            for z in range(z_extent):
                value = links_in[pl.ds(k * t * z_extent + z, t, stride=z_extent), :]
                links_ref[k, z, 0:t] = value * flip if direction == 3 else value
    emit_messages(shape, psi_ref, Links(links_ref), messages)


def summed(shape, term):
    total = None
    for k in range(24):
        for z in range(shape.z):
            value = term(k, z)
            total = value if total is None else total + value
    return total


def over_lanes(total):
    return jnp.sum(jnp.sum(total, axis=0, keepdims=True), axis=1, keepdims=True)


def local_sums(shape, image, origin):
    square = summed(shape, lambda k, z: origin[k, z] * origin[k, z])
    mixed = over_lanes(summed(shape, lambda k, z: image[k, z] * origin[k, z]))
    whole = over_lanes(square)
    factor = jnp.where(whole > 0.0, mixed / jnp.where(whole > 0.0, whole, 1.0), 0.0)
    spread = jnp.broadcast_to(factor, (shape.rows, shape.lanes))
    rest_square, rest_mixed = None, None
    for k in range(24):
        for z in range(shape.z):
            start = origin[k, z]
            rest = image[k, z] - spread * start
            terms = rest * rest, rest * start
            if rest_square is None:
                rest_square, rest_mixed = terms
            else:
                rest_square, rest_mixed = rest_square + terms[0], rest_mixed + terms[1]
    return [factor, *(over_lanes(value) for value in (square, rest_square, rest_mixed))]


def inner_kernel(shape, psi_ref, links_ref, total_ref):
    links = Links(links_ref)
    x = shape.lane() % X
    lanes = shape.lanes
    at_end, at_start = x == X - 1, x == 0

    def ahead(value):
        return jnp.where(
            at_end, pltpu.roll(value, X - 1, 1), pltpu.roll(value, lanes - 1, 1)
        )

    def behind(value):
        return jnp.where(at_start, pltpu.roll(value, lanes - X + 1, 1), pltpu.roll(value, 1, 1))

    for z in range(shape.z):
        psi = load_psi(psi_ref, z)
        zero = jnp.zeros((shape.rows, lanes), jnp.float32)
        total = {key: (zero, zero) for key in psi}
        half = mapped(ahead, project(psi, 0, -1))
        add_rebuilt(total, mul_link(links, 0, z, half), 0, -1)
        half = mapped(behind, mul_link_dag(links, 0, z, project(psi, 0, 1)))
        add_rebuilt(total, half, 0, 1)
        if z + 1 < shape.z:
            half = project(load_psi(psi_ref, z + 1), 2, -1)
            add_rebuilt(total, mul_link(links, 2, z, half), 2, -1)
        if z > 0:
            half = project(load_psi(psi_ref, z - 1), 2, 1)
            add_rebuilt(total, mul_link_dag(links, 2, z - 1, half), 2, 1)
        for (s, c), pair in total.items():
            for part in range(2):
                total_ref[(s * 3 + c) * 2 + part, z] = pair[part]


def add_y_hops(shape, z, psi, total, links, carried_y, y_halo):
    lane, lanes = shape.lane(), shape.lanes
    received = load_half(y_halo, z)
    half = mapped(
        lambda own, other: pltpu.roll(jnp.where(lane < X, other, own), lanes - X, 1),
        project(psi, 1, -1),
        received,
    )
    add_rebuilt(total, mul_link(links, 1, z, half), 1, -1)
    half = mapped(
        lambda own, other: pltpu.roll(jnp.where(lane >= lanes - X, other, own), X, 1),
        load_half(carried_y, z),
        received,
    )
    add_rebuilt(total, half, 1, 1)


def finish_hops(
    shape, psi_ref, links, total_ref, carried_y, carried_t, halo, store
):
    z_second, t_second, z_first, t_first, y_msg = halo
    t_even, z_even = is_even("ta"), is_even("gz")
    row = shape.row()
    lanes, rows, t = shape.lanes, shape.rows, shape.t
    last_z = shape.z - 1

    for z in range(shape.z):
        psi = load_psi(psi_ref, z)
        total = load_psi(total_ref, z)

        def rim_rows(from_even, from_odd):
            half = {}
            for s, c in SPIN_COLOUR:
                ats = [((s * 3 + c) * 2 + part) * shape.z + z for part in range(2)]
                half[s, c] = tuple(
                    jnp.broadcast_to(
                        either(t_even, from_even[at : at + 1], from_odd[at : at + 1]),
                        (rows, lanes),
                    )
                    for at in ats
                )
            return half

        def rim_plane(from_even, from_odd):
            half = {}
            for s, c in SPIN_COLOUR:
                pair = []
                for part in range(2):
                    at = ((s * 3 + c) * 2 + part) * t
                    plane = either(z_even, from_even[at : at + t], from_odd[at : at + t])
                    if rows != t:
                        pad = jnp.zeros((rows - t, lanes), jnp.float32)
                        plane = jnp.concatenate([plane, pad], axis=0)
                    pair.append(plane)
                half[s, c] = tuple(pair)
            return half

        if y_msg is not None:
            add_y_hops(shape, z, psi, total, links, carried_y, y_msg)
        if z == last_z:
            add_rebuilt(total, mul_link(links, 2, z, rim_plane(z_first, z_second)), 2, -1)
        if z == 0:
            add_rebuilt(total, rim_plane(z_second, z_first), 2, 1)
        half = mapped(
            lambda own, other: jnp.where(row == t - 1, other, pltpu.roll(own, rows - 1, 0)),
            project(psi, 3, -1),
            rim_rows(t_first, t_second),
        )
        add_rebuilt(total, mul_link(links, 3, z, half), 3, -1)
        half = mapped(
            lambda own, other: jnp.where(row == 0, other, pltpu.roll(own, 1, 0)),
            load_half(carried_t, z),
            rim_rows(t_second, t_first),
        )
        add_rebuilt(total, half, 3, 1)
        for (s, c), pair in total.items():
            for part in range(2):
                value = psi[s, c][part] - hop_kappa * pair[part]
                value = value if s < 2 else -value
                if rows != t:
                    value = jnp.where(row < t, value, 0.0)
                store((s * 3 + c) * 2 + part, z, value)


def mid_kernel(shape, psi_ref, links_ref, total_ref, carried_y, carried_t, *refs):
    halo, out_ref, messages = refs[:5], refs[5], refs[6:]
    links = Links(links_ref)

    def store(k, z, value):
        out_ref[k, z] = value

    finish_hops(
        shape, psi_ref, links, total_ref, carried_y, carried_t, halo, store
    )
    emit_messages(shape, out_ref, links, messages)


def sums_row(shape, two, start, three, one):
    sums = local_sums(shape, two, start) + local_sums(shape, three, one)
    lane = lax.broadcasted_iota(jnp.int32, (1, shape.lanes), 1)
    row = jnp.zeros((1, shape.lanes), jnp.float32)
    for k, value in enumerate(sums):
        row = jnp.where(lane == k, value, row)
    return row


def inner_sums_kernel(
    shape, psi_ref, links_ref, start_ref, one_ref, two_ref, total_ref, copies_ref
):
    row = sums_row(shape, two_ref, start_ref, psi_ref, one_ref)
    copies_ref[...] = jnp.broadcast_to(row[None], copies_ref.shape)
    inner_kernel(shape, psi_ref, links_ref, total_ref)


def finish_kernel(shape, psi_ref, links_ref, total_ref, carried_y, carried_t, *refs):
    halo, out_ref = refs[:5], refs[5]

    def store(k, z, value):
        out_ref[k, z] = value

    finish_hops(
        shape, psi_ref, Links(links_ref), total_ref, carried_y, carried_t, halo, store
    )


def scalars(table, entries):
    columns = [table[:, k : k + 1] for k in range(8)]
    factor_two, start_square, two_square, two_mixed = columns[:4]
    factor_three, one_square, three_square, three_mixed = columns[4:]

    def over_devices(column):
        return jnp.sum(column, axis=0, keepdims=True)

    norm_square = over_devices(start_square) / entries + epsilon
    alpha_one = over_devices(one_square) / entries / norm_square
    gap = alpha_one - factor_two
    remain_square = over_devices(two_square - gap * (2.0 * two_mixed - gap * start_square)) / entries
    overlap = over_devices(two_mixed - gap * start_square) / entries
    gap = alpha_one - factor_three
    image_square = over_devices(three_square - gap * (2.0 * three_mixed - gap * one_square)) / entries
    norm = jnp.sqrt(norm_square)
    beta_one = jnp.sqrt(remain_square / norm_square + epsilon)
    overlap = overlap / (norm_square * beta_one)
    alpha_two = image_square / (norm_square * beta_one * beta_one) - beta_one * overlap
    scale = 1.0 / (norm * beta_one)
    return alpha_one, beta_one, alpha_two, scale, beta_one / norm


def last_kernel(
    shape, entries, start_ref, two_ref, four_ref, gathered, out_ref, coefficients
):
    alpha_one, beta_one, alpha_two, scale, first_factor = scalars(gathered[:, 0, :], entries)
    t, z_extent = shape.t, shape.z
    for k in range(24):
        for z in range(z_extent):
            two, start = two_ref[k, z], start_ref[k, z]
            remain = two - alpha_one * start
            result = (four_ref[k, z] - alpha_one * two - alpha_two * remain) * scale
            result = result - first_factor * start
            out_ref[pl.ds(k * t * z_extent + z, t, stride=z_extent), :] = result[0:t]
    coefficients[0] = alpha_one[0, 0]
    coefficients[1] = beta_one[0, 0]
    coefficients[2] = alpha_two[0, 0]


def swap(value, axis, second):
    count = math.prod(lax.axis_size(name) for name in (axis if isinstance(axis, tuple) else (axis,)))
    pairs = []
    for low in range(1 if second else 0, count, 2):
        high = (low + 1) % count
        pairs += [(low, high), (high, low)]
    return lax.ppermute(value, axis, pairs)


def exchange(messages, lanes):
    z_second, t_second, z_first, t_first, y_msg = messages
    halo = (
        swap(z_second, "gz", True),
        swap(t_second, "ta", True),
        swap(z_first, "gz", False),
        swap(t_first, "ta", False),
    )
    y_halo = swap(y_msg, "gy", False)
    if lax.axis_size("gy") > 2:
        even = lax.axis_index("gy") % 2 == 0
        lane = lax.broadcasted_iota(jnp.int32, y_msg.shape, y_msg.ndim - 1)
        y_halo = jnp.where((lane < lanes // 2) == even, y_halo, swap(y_msg, "gy", True))
    return (*halo, y_halo)


def from_everyone(copies):
    return lax.all_to_all(copies, ("ta", "gz", "gy"), split_axis=0, concat_axis=0, tiled=True)


def shards(source, gauge_links):
    devices_all = lax.axis_size("ta") * lax.axis_size("gz") * lax.axis_size("gy")
    entries = float(source.size * devices_all)
    shape = Shape(source.shape[3], source.shape[4], source.shape[5])
    t, z, rows, lanes = shape.t, shape.z, shape.rows, shape.lanes
    vmem = pl.BlockSpec(memory_space=pltpu.VMEM)
    smem = pl.BlockSpec(memory_space=pltpu.SMEM)

    def held(*dims):
        return pltpu.VMEM(dims, jnp.float32)

    field = held(24, z, rows, lanes)
    half = held(12, z, rows, lanes)
    z_face, t_face = held(12 * t, lanes), held(12 * z, lanes)
    messages = (z_face, t_face, z_face, t_face, half, half, half)

    def call(kernel, name, flops, out_shape, operands, out_specs=None, in_spec=vmem, scratch=()):
        return pl.pallas_call(
            kernel,
            name=name,
            out_shape=out_shape,
            in_specs=[in_spec] * len(operands),
            out_specs=out_specs or jax.tree.map(lambda _: vmem, out_shape),
            scratch_shapes=scratch,
            compiler_params=pltpu.CompilerParams(vmem_limit_bytes=8 << 20),
            cost_estimate=pl.CostEstimate(flops=flops, bytes_accessed=1 << 20, transcendentals=0),
        )(*operands)

    sites = t * z * lanes
    psi, links, *sent = call(
        functools.partial(prep_kernel, shape), "prep", 400 * sites,
        (field, held(72, z, rows, lanes), *messages),
        (
            pltpu.with_memory_space_constraint(source.reshape(24 * t * z, lanes), pltpu.HBM),
            pltpu.with_memory_space_constraint(gauge_links.reshape(72 * t * z, lanes), pltpu.HBM),
        ),
        in_spec=pl.BlockSpec(memory_space=pltpu.HBM),
        scratch=(
            held(24 * t * z, lanes), held(72 * t * z, lanes), pltpu.SemaphoreType.DMA((5,)),
        ),
    )
    powers = [psi]
    for step in range(3):
        halo = exchange(sent[:5], lanes)
        inner = functools.partial(inner_kernel, shape)
        total = call(inner, "inner", 700 * sites, field, (psi, links))
        psi, *sent = call(
            functools.partial(mid_kernel, shape), "mid", 1000 * sites,
            (field, *messages), (psi, links, total, *sent[5:], *halo),
        )
        powers.append(psi)
    halo = exchange(sent[:5], lanes)
    total, copies = call(
        functools.partial(inner_sums_kernel, shape), "inner_sums", 1100 * sites,
        (field, held(devices_all, 8, lanes)), (psi, links, *powers[:3]),
    )
    gathered = from_everyone(copies)
    four = call(
        functools.partial(finish_kernel, shape), "finish", 700 * sites, field,
        (psi, links, total, *sent[5:], *halo),
    )
    residual, coefficients = call(
        functools.partial(last_kernel, shape, entries), "last", 100 * sites,
        (
            jax.ShapeDtypeStruct((24 * t * z, lanes), jnp.float32),
            jax.ShapeDtypeStruct((3,), jnp.float32),
        ),
        (powers[0], powers[2], four, gathered), (vmem, smem),
    )
    return (residual.reshape(source.shape), coefficients)


class ChipShape(Shape):
    def __init__(self, t_extent, z_extent, lanes):
        super().__init__(t_extent, z_extent, lanes)
        self.parts = 2 * z_extent
        self.z_rows = 24 * t_extent
        self.t_rows = 12 * self.parts

    def block(self, k, part):
        first = (k * self.parts + part) * self.rows
        return pl.ds(first, self.rows)

    def edge(self, k, row):
        return pl.ds(k * self.parts * self.rows + row, self.parts, stride=self.rows)


class ChipLinks:
    def __init__(self, shape, ref, row=None):
        self.shape, self.ref, self.row = shape, ref, row

    def __getitem__(self, index):
        direction, row, col, part = index
        first = ((direction * 3 + row) * 3 + col) * 2
        if self.row is None:
            return tuple(self.ref[self.shape.block(first + n, part), :] for n in range(2))
        return tuple(self.ref[self.shape.edge(first + n, self.row), :] for n in range(2))


def components(spins):
    return [(s, c, part, (s * 3 + c) * 2 + part) for s in range(spins) for c in range(3) for part in range(2)]


def gathered_pairs(spins, value):
    out = {}
    for s in range(spins):
        for c in range(3):
            out[s, c] = tuple(value((s * 3 + c) * 2 + part) for part in range(2))
    return out


def chip_psi(shape, ref, part):
    return gathered_pairs(4, lambda k: ref[shape.block(k, part), :])


def chip_edge(shape, ref, row):
    return gathered_pairs(4, lambda k: ref[shape.edge(k, row), :])


def chip_messages(shape, psi_ref, links_ref, z_second, t_second, z_first, t_first):
    t, last = shape.t, shape.t - 1
    even = is_even("ta")
    minus = project(chip_edge(shape, psi_ref, 0), 3, -1)
    half = project(chip_edge(shape, psi_ref, last), 3, 1)
    carried = mul_link_dag(ChipLinks(shape, links_ref, last), 3, 0, half)
    for s, c, part, k in components(2):
        rows = pl.ds(k * shape.parts, shape.parts)
        up, down = carried[s, c][part], minus[s, c][part]
        t_first[rows, :] = either(even, up, down)
        t_second[rows, :] = either(even, down, up)
    even = is_even("gy")
    links = ChipLinks(shape, links_ref)
    for y_half in range(2):
        minus = project(chip_psi(shape, psi_ref, y_half), 2, -1)
        part_last = shape.parts - 2 + y_half
        half = project(chip_psi(shape, psi_ref, part_last), 2, 1)
        carried = mul_link_dag(links, 2, part_last, half)
        for s, c, part, k in components(2):
            rows = pl.ds((k * 2 + y_half) * t, t)
            up, down = carried[s, c][part][0:t], minus[s, c][part][0:t]
            z_first[rows, :] = either(even, up, down)
            z_second[rows, :] = either(even, down, up)


def chip_bring(shape, y_half, source_ref, links_in, psi_ref, links_ref, arrived):
    t, z_extent = shape.t, 2 * shape.z
    first_plane = lax.axis_index("gy") * shape.z
    last = lax.broadcasted_iota(jnp.int32, (t, shape.lanes), 0) == t - 1
    sign = jnp.where(lax.axis_index("ta") == lax.axis_size("ta") - 1, -1.0, 1.0)
    flip = jnp.where(last, sign, 1.0)

    def bring(in_ref, out_ref, k, z, factor=None):
        value = in_ref[pl.ds(k * t * z_extent + first_plane + z, t, stride=z_extent), :]
        if factor is not None:
            value = value * factor
        at = (k * shape.parts + 2 * z + y_half) * shape.rows
        out_ref[pl.ds(pl.multiple_of(at, 8), t), :] = value

    arrived(4)
    for z in range(shape.z):
        for k in range(24):
            bring(source_ref, psi_ref, k, z)
    for direction in (3, 2, 1, 0):
        arrived(direction)
        for z in range(shape.z):
            for k in range(18 * direction, 18 * direction + 18):
                bring(links_in, links_ref, k, z, flip if direction == 3 else None)


def chip_own_kernel(
    shape, source_hbm, links_hbm, psi_ref, links_ref, rest_ref, source_ref, links_in, semaphores
):
    part = 18 * shape.t * 2 * shape.z
    copies = {4: pltpu.make_async_copy(source_hbm, source_ref, semaphores.at[4])}
    for direction in (3, 2, 1, 0):
        rows = pl.ds(direction * part, part)
        copies[direction] = pltpu.make_async_copy(
            links_hbm.at[rows], links_in.at[rows], semaphores.at[direction]
        )
    for copy in copies.values():
        copy.start()
    if shape.rows != shape.t:
        links_ref[...] = jnp.zeros_like(links_ref)
        psi_ref[...] = jnp.zeros_like(psi_ref)
    chip_bring(
        shape, lax.axis_index("gy"), source_ref, links_in, psi_ref, links_ref,
        lambda n: copies[n].wait(),
    )
    t, z_extent = shape.t, 2 * shape.z
    first_plane = (1 - lax.axis_index("gy")) * shape.z
    if shape.rows != t:
        rest_ref[...] = jnp.zeros_like(rest_ref)
    for k in range(24):
        for z in range(shape.z):
            value = source_ref[pl.ds(k * t * z_extent + first_plane + z, t, stride=z_extent), :]
            rest_ref[pl.ds((k * shape.z + z) * shape.rows, t), :] = value


def chip_prep_kernel(
    shape, source_ref, links_in, psi_in, links_held, psi_ref, links_ref, *messages
):
    chip_bring(
        shape, 1 - lax.axis_index("gy"), source_ref, links_in, psi_ref, links_ref, lambda n: None
    )
    chip_messages(shape, psi_ref, links_ref, *messages)


def chip_inner_kernel(shape, psi_ref, links_ref, total_ref):
    links = ChipLinks(shape, links_ref)
    lane, row = shape.lane(), shape.row()
    x = lane % X
    lanes, rows, t = shape.lanes, shape.rows, shape.t
    at_end, at_start = x == X - 1, x == 0
    inside_ahead = row < t - 1
    inside_behind = jnp.logical_and(row > 0, row < t)

    def x_ahead(value):
        return jnp.where(
            at_end, pltpu.roll(value, X - 1, 1), pltpu.roll(value, lanes - 1, 1)
        )

    def x_behind(value):
        return jnp.where(at_start, pltpu.roll(value, lanes - X + 1, 1), pltpu.roll(value, 1, 1))

    def t_ahead(value):
        return jnp.where(inside_ahead, pltpu.roll(value, rows - 1, 0), 0.0)

    def t_behind(value):
        return jnp.where(inside_behind, pltpu.roll(value, 1, 0), 0.0)

    for z in range(shape.z):
        for part in (2 * z, 2 * z + 1):
            psi = chip_psi(shape, psi_ref, part)
            zero = jnp.zeros((rows, lanes), jnp.float32)
            total = {key: (zero, zero) for key in psi}
            half = mapped(x_ahead, project(psi, 0, -1))
            add_rebuilt(total, mul_link(links, 0, part, half), 0, -1)
            half = mapped(x_behind, mul_link_dag(links, 0, part, project(psi, 0, 1)))
            add_rebuilt(total, half, 0, 1)
            half = mapped(t_ahead, project(psi, 3, -1))
            add_rebuilt(total, mul_link(links, 3, part, half), 3, -1)
            half = mapped(t_behind, mul_link_dag(links, 3, part, project(psi, 3, 1)))
            add_rebuilt(total, half, 3, 1)
            if z + 1 < shape.z:
                half = project(chip_psi(shape, psi_ref, part + 2), 2, -1)
                add_rebuilt(total, mul_link(links, 2, part, half), 2, -1)
            if z > 0:
                half = project(chip_psi(shape, psi_ref, part - 2), 2, 1)
                add_rebuilt(total, mul_link_dag(links, 2, part - 2, half), 2, 1)
            for s, c, n, k in components(4):
                total_ref[shape.block(k, part), :] = total[s, c][n]
        pair = (2 * z, 2 * z + 1)
        minus, carried = [], []
        for part in pair:
            psi = chip_psi(shape, psi_ref, part)
            minus.append(mapped(lambda v: pltpu.roll(v, lanes - X, 1), project(psi, 1, -1)))
            half = mul_link_dag(links, 1, part, project(psi, 1, 1))
            carried.append(mapped(lambda v: pltpu.roll(v, X, 1), half))
        for own, part in enumerate(pair):
            total = chip_psi(shape, total_ref, part)
            half = mapped(
                lambda a, b: jnp.where(lane >= lanes - X, b, a), minus[own], minus[1 - own]
            )
            add_rebuilt(total, mul_link(links, 1, part, half), 1, -1)
            half = mapped(lambda a, b: jnp.where(lane < X, b, a), carried[own], carried[1 - own])
            add_rebuilt(total, half, 1, 1)
            for s, c, n, k in components(4):
                total_ref[shape.block(k, part), :] = total[s, c][n]


def chip_sort_faces(z_second, z_first, scratch):
    z_down, z_up = scratch
    z_even = is_even("gy")
    second = 0.0 if z_second is None else z_second[...]
    first = 0.0 if z_first is None else z_first[...]
    z_down[...] = either(z_even, first, second)
    z_up[...] = either(z_even, second, first)


def chip_add_z(shape, links, part, total, scratch):
    z_down, z_up = scratch
    t, rows, lanes, parts = shape.t, shape.rows, shape.lanes, shape.parts

    def plane(ref, y_half):
        def value(k):
            face = ref[pl.ds((k * 2 + y_half) * t, t), :]
            if rows != t:
                pad = jnp.zeros((rows - t, lanes), jnp.float32)
                face = jnp.concatenate([face, pad], axis=0)
            return face

        return gathered_pairs(2, value)

    if part >= parts - 2:
        half = mul_link(links, 2, part, plane(z_down, part - parts + 2))
        add_rebuilt(total, half, 2, -1)
    if part < 2:
        add_rebuilt(total, plane(z_up, part), 2, 1)


def chip_finish(
    shape, psi_ref, links_ref, total_ref, received, scratch, out_ref, face_ref=None
):
    z_second, t_second, z_first, t_first = received
    t_even = is_even("ta")
    t, lanes, parts = shape.t, shape.lanes, shape.parts
    chip_sort_faces(z_second, z_first, scratch)
    links = ChipLinks(shape, links_ref)

    for part in range(parts):
        total = chip_psi(shape, total_ref, part)
        chip_add_z(shape, links, part, total, scratch)
        for s, c, n, k in components(4):
            value = total[s, c][n]
            if face_ref is not None:
                value = value + face_ref[shape.block(k, part), :]
            value = psi_ref[shape.block(k, part), :] - hop_kappa * value
            out_ref[shape.block(k, part), :] = value if s < 2 else -value

    def t_half(from_even, from_odd):
        def value(k):
            at = pl.ds(k * parts, parts)
            return either(t_even, from_even[at, :], from_odd[at, :])

        return gathered_pairs(2, value)

    down = mul_link(ChipLinks(shape, links_ref, t - 1), 3, 0, t_half(t_first, t_second))
    up = t_half(t_second, t_first)
    zero = jnp.zeros((parts, lanes), jnp.float32)
    for half, parity, row in ((down, -1, t - 1), (up, 1, 0)):
        total = {(s, c): (zero, zero) for s in range(4) for c in range(3)}
        add_rebuilt(total, half, 3, parity)
        for s, c, n, k in components(4):
            at = shape.edge(k, row)
            value = hop_kappa * total[s, c][n]
            out_ref[at, :] = out_ref[at, :] - (value if s < 2 else -value)


def chip_mid_kernel(shape, hands_over, psi_ref, links_ref, total_ref, *refs):
    received, out_ref, messages, refs = refs[:4], refs[4], refs[5:9], refs[9:]
    chip_finish(shape, psi_ref, links_ref, total_ref, received, refs[-2:], out_ref)
    chip_messages(shape, out_ref, links_ref, *messages)
    if hands_over:
        hand_over(shape, out_ref, refs[0])


def chip_sums_kernel(
    shape, links_ref, z_first, start_ref, one_ref, two_ref, three_ref,
    face_ref, copies_ref, *scratch,
):
    class View:
        def __init__(self, ref):
            self.ref = ref

        def __getitem__(self, index):
            return self.ref[shape.block(*index), :]

    wide = ChipShape(shape.t, shape.z, shape.lanes)
    wide.z = shape.parts
    row = sums_row(wide, View(two_ref), View(start_ref), View(three_ref), View(one_ref))
    copies_ref[...] = jnp.broadcast_to(row[None], copies_ref.shape)
    chip_sort_faces(None, z_first, scratch)
    zero = jnp.zeros((shape.rows, shape.lanes), jnp.float32)
    for part in range(shape.parts):
        total = {(s, c): (zero, zero) for s in range(4) for c in range(3)}
        chip_add_z(shape, ChipLinks(shape, links_ref), part, total, scratch)
        for s, c, n, k in components(4):
            face_ref[shape.block(k, part), :] = total[s, c][n]


def chip_scalars_kernel(entries, gathered, factors_ref, coefficients):
    alpha_one, beta_one, alpha_two, scale, first_factor = scalars(gathered[:, 0, :], entries)
    lanes = factors_ref.shape[1]
    values = [alpha_one, alpha_two, scale, first_factor]
    values = [jnp.broadcast_to(value, (1, lanes)) for value in values]
    values.append(jnp.zeros((4, lanes), jnp.float32))
    factors_ref[...] = jnp.concatenate(values, axis=0)
    coefficients[0] = alpha_one[0, 0]
    coefficients[1] = beta_one[0, 0]
    coefficients[2] = alpha_two[0, 0]


def y_part(shape, k, z, y_half):
    return pl.ds(pl.multiple_of((k * shape.parts + 2 * z + y_half) * shape.rows, 8), shape.rows)


def rest_rows(shape, k, z):
    return pl.ds((k * shape.z + z) * shape.rows, shape.rows)


def hand_over(shape, ref, rest_ref):
    y_half = 1 - lax.axis_index("gy")
    for k in range(24):
        for z in range(shape.z):
            rest_ref[rest_rows(shape, k, z), :] = ref[y_part(shape, k, z, y_half), :]


def chip_finish_kernel(
    shape, psi_ref, links_ref, total_ref, face_ref, z_second, t_second, t_first,
    out_ref, rest_ref, *scratch,
):
    received = z_second, t_second, None, t_first
    chip_finish(shape, psi_ref, links_ref, total_ref, received, scratch, out_ref, face_ref)
    y_half = 1 - lax.axis_index("gy")
    for k in range(24):
        for z in range(shape.z):
            value = out_ref[y_part(shape, k, z, y_half), :]
            rest_ref[dense_rows(shape, k, z), :] = value[0 : shape.t]


def dense_rows(shape, k, z):
    return pl.ds((k * shape.z + z) * shape.t, shape.t)


def chip_last_kernel(
    shape, start_ref, two_ref, four_ref, start_rest, two_rest, four_rest, factors_ref, out_ref
):
    t, z_extent = shape.t, 2 * shape.z
    alpha_one, alpha_two, scale, first_factor = (
        jnp.broadcast_to(factors_ref[k : k + 1], (t, shape.lanes)) for k in range(4)
    )
    core = lax.axis_index("gy")

    def put(k, z, start, two, four):
        remain = two - alpha_one * start
        result = (four - alpha_one * two - alpha_two * remain) * scale - first_factor * start
        out_ref[pl.ds(k * t * z_extent + z, t, stride=z_extent), :] = result

    for k in range(24):
        for z in range(shape.z):
            rows = y_part(shape, k, z, core)
            put(k, core * shape.z + z, *(ref[rows, :][0:t] for ref in (start_ref, two_ref, four_ref)))
            rows = rest_rows(shape, k, z)
            other = [ref[rows, :][0:t] for ref in (start_rest, two_rest)]
            put(k, (1 - core) * shape.z + z, *other, four_rest[dense_rows(shape, k, z), :])


def chip_shards(source, gauge_links):
    devices_all = lax.axis_size("ta") * lax.axis_size("gz") * 2
    entries = float(source.size * devices_all)
    z_extent = source.shape[4]
    shape = ChipShape(source.shape[3], z_extent // 2, source.shape[5])
    t, rows, lanes = shape.t, shape.rows, shape.lanes
    vmem = pl.BlockSpec(memory_space=pltpu.VMEM)
    smem = pl.BlockSpec(memory_space=pltpu.SMEM)

    def held(*dims):
        return pltpu.VMEM(dims, jnp.float32)

    field = held(24 * shape.parts * rows, lanes)
    links_field = held(72 * shape.parts * rows, lanes)
    z_face, t_face = held(shape.z_rows, lanes), held(shape.t_rows, lanes)
    messages = (z_face, t_face, z_face, t_face)
    z_faces = (z_face, z_face)

    def call(kernel, name, flops, out_shape, operands, **options):
        in_spec = options.pop("in_spec", vmem)
        out_specs = options.pop("out_specs", jax.tree.map(lambda _: vmem, out_shape))
        return pl.pallas_call(
            kernel,
            name=name,
            out_shape=out_shape,
            in_specs=[in_spec] * len(operands),
            out_specs=out_specs,
            compiler_params=pltpu.CompilerParams(vmem_limit_bytes=8 << 20),
            cost_estimate=pl.CostEstimate(flops=flops, bytes_accessed=1 << 20, transcendentals=0),
            **options,
        )(*operands)

    def exchanged(sent):
        z_second, t_second, z_first, t_first = sent
        z_ring = ("gz", "gy")
        return (
            swap(z_second, z_ring, True), swap(t_second, "ta", True),
            swap(z_first, z_ring, False), swap(t_first, "ta", False),
        )

    sites = t * z_extent * lanes
    rows_in = t * z_extent
    own = (source.reshape(24 * rows_in, lanes), gauge_links.reshape(72 * rows_in, lanes))
    other = tuple(swap(value, "gy", False) for value in own)
    rest = held(24 * shape.z * rows, lanes)
    psi, links, start_rest = call(
        functools.partial(chip_own_kernel, shape), "own", 200 * sites, (field, links_field, rest),
        [pltpu.with_memory_space_constraint(value, pltpu.HBM) for value in own],
        scratch_shapes=(
            held(24 * rows_in, lanes), held(72 * rows_in, lanes), pltpu.SemaphoreType.DMA((5,)),
        ),
        in_spec=pl.BlockSpec(memory_space=pltpu.HBM),
    )
    psi, links, *sent = call(
        functools.partial(chip_prep_kernel, shape), "prep", 400 * sites,
        (field, links_field, *messages), (*other, psi, links),
        input_output_aliases={2: 0, 3: 1},
    )
    powers = [psi]
    for step in range(3):
        halo = exchanged(sent)
        inner = functools.partial(chip_inner_kernel, shape)
        total = call(inner, "inner", 1000 * sites, field, (psi, links))
        hands_over = step == 1
        psi, *sent = call(
            functools.partial(chip_mid_kernel, shape, hands_over), "mid", 600 * sites,
            (field, *messages, rest) if hands_over else (field, *messages),
            (psi, links, total, *halo), scratch_shapes=z_faces,
        )
        powers.append(psi)
        if hands_over:
            two_rest = swap(sent.pop(), "gy", False)
    halo = exchanged(sent)
    face, copies = call(
        functools.partial(chip_sums_kernel, shape), "sums", 600 * sites,
        (field, held(devices_all, 1, lanes)), (links, halo[2], *powers), scratch_shapes=z_faces,
    )
    gathered = from_everyone(copies)
    total = call(inner, "inner", 1000 * sites, field, (psi, links))
    four, four_rest = call(
        functools.partial(chip_finish_kernel, shape), "finish", 400 * sites,
        (field, held(24 * shape.z * t, lanes)),
        (psi, links, total, face, halo[0], halo[1], halo[3]), scratch_shapes=z_faces,
    )
    four_rest = swap(four_rest, "gy", False)
    factors, coefficients = call(
        functools.partial(chip_scalars_kernel, entries), "scalars", 10**11,
        (held(8, lanes), jax.ShapeDtypeStruct((3,), jnp.float32)), (gathered,),
        out_specs=(vmem, smem),
    )
    residual = call(
        functools.partial(chip_last_kernel, shape), "last", 100 * sites,
        jax.ShapeDtypeStruct((24 * rows_in, lanes), jnp.float32),
        (powers[0], powers[2], four, start_rest, two_rest, four_rest, factors),
    )
    return (residual.reshape(source.shape), coefficients)


def solution(mesh):
    placed = (P(None, None, None, "ta", "gz", "gy"), P(None, None, None, None, "ta", "gz", "gy"))
    return jax.shard_map(
        chip_shards if mesh.shape["gy"] == 2 else shards,
        mesh=mesh,
        in_specs=placed,
        out_specs=(P(None, None, None, "ta", "gz", "gy"), P()),
        check_vma=False,
    )
```

```python
import functools
import math

import jax
import jax.numpy as jnp
from jax import lax
from jax.experimental import pallas as pl
from jax.experimental.pallas import tpu as pltpu
from jax.sharding import PartitionSpec as P

X = 32

hop_kappa = 0.19
epsilon = 1e-06
spin_table = (
    ((1, 0), (-1j, -1j)),
    ((1, 0), (-1, 1)),
    ((0, 1), (-1j, 1j)),
    ((0, 1), (1, 1)),
)
SPIN_COLOUR = [(spin, colour) for spin in range(2) for colour in range(3)]


def add_phased(left, phase, right):
    phase = complex(phase)
    if phase == 1:
        return (left[0] + right[0], left[1] + right[1])
    if phase == -1:
        return (left[0] - right[0], left[1] - right[1])
    if phase == 1j:
        return (left[0] - right[1], left[1] + right[0])
    return (left[0] + right[1], left[1] - right[0])


def project(psi, direction, parity):
    order, phases = spin_table[direction]
    return {
        (s, c): add_phased(psi[s, c], parity * phases[s], psi[2 + order[s], c])
        for s, c in SPIN_COLOUR
    }


def add_rebuilt(total, half, direction, parity):
    order, phases = spin_table[direction]
    for s, c in SPIN_COLOUR:
        total[s, c] = add_phased(total[s, c], 1, half[s, c])
        row = order[s]
        phase = parity * complex(phases[row]).conjugate()
        total[2 + s, c] = add_phased(total[2 + s, c], phase, half[row, c])


def mul_link(links, direction, z, half):
    out = {}
    for row in range(3):
        for s in range(2):
            real, imag = None, None
            for col in range(3):
                u_real, u_imag = links[direction, row, col, z]
                h_real, h_imag = half[s, col]
                term_real = u_real * h_real - u_imag * h_imag
                term_imag = u_real * h_imag + u_imag * h_real
                real = term_real if real is None else real + term_real
                imag = term_imag if imag is None else imag + term_imag
            out[s, row] = (real, imag)
    return out


def mul_link_dag(links, direction, z, half):
    out = {}
    for row in range(3):
        for s in range(2):
            real, imag = None, None
            for col in range(3):
                u_real, u_imag = links[direction, col, row, z]
                h_real, h_imag = half[s, col]
                term_real = u_real * h_real + u_imag * h_imag
                term_imag = u_real * h_imag - u_imag * h_real
                real = term_real if real is None else real + term_real
                imag = term_imag if imag is None else imag + term_imag
            out[s, row] = (real, imag)
    return out


def mapped(function, *halves):
    return {
        key: tuple(function(*(half[key][part] for half in halves)) for part in range(2))
        for key in SPIN_COLOUR
    }


class Links:
    def __init__(self, ref):
        self.ref = ref

    def __getitem__(self, index):
        direction, row, col, z = index
        first = ((direction * 3 + row) * 3 + col) * 2
        return (self.ref[first, z], self.ref[first + 1, z])


def load_psi(ref, z):
    return {
        (s, c): (ref[(s * 3 + c) * 2, z], ref[(s * 3 + c) * 2 + 1, z])
        for s in range(4)
        for c in range(3)
    }


def load_half(ref, z):
    return {
        (s, c): (ref[(s * 3 + c) * 2, z], ref[(s * 3 + c) * 2 + 1, z]) for s, c in SPIN_COLOUR
    }


def store_half(ref, z, half):
    for (s, c), pair in half.items():
        for part in range(2):
            ref[(s * 3 + c) * 2 + part, z] = pair[part]


class Shape:
    def __init__(self, t_extent, z_extent, lanes):
        self.t = t_extent
        self.z = z_extent
        self.rows = -(-t_extent // 8) * 8
        self.lanes = lanes

    def row(self):
        return lax.broadcasted_iota(jnp.int32, (self.rows, self.lanes), 0)

    def lane(self):
        return lax.broadcasted_iota(jnp.int32, (self.rows, self.lanes), 1)


def is_even(axis):
    return jnp.bitwise_and(lax.axis_index(axis), 1) == 0


def either(choice, first, second):
    return jnp.where(choice, first, second)


def emit_messages(shape, psi_ref, links, refs):
    z_second, t_second, z_first, t_first, y_msg, carried_y, carried_t = refs
    t_even, z_even = is_even("ta"), is_even("gz")
    lane = shape.lane()
    last_z, last_t = shape.z - 1, shape.t - 1
    for z in range(shape.z):
        psi = load_psi(psi_ref, z)
        minus = project(psi, 3, -1)
        carried = mul_link_dag(links, 3, z, project(psi, 3, 1))
        store_half(carried_t, z, carried)
        for s, c in SPIN_COLOUR:
            for part in range(2):
                at = ((s * 3 + c) * 2 + part) * shape.z + z
                down = minus[s, c][part][0:1]
                up = carried[s, c][part][last_t : last_t + 1]
                t_first[at : at + 1] = either(t_even, up, down)
                t_second[at : at + 1] = either(t_even, down, up)
        minus = project(psi, 1, -1)
        carried = mul_link_dag(links, 1, z, project(psi, 1, 1))
        store_half(carried_y, z, carried)
        store_half(
            y_msg,
            z,
            mapped(lambda low, high: jnp.where(lane < X, low, high), minus, carried),
        )
    minus = project(load_psi(psi_ref, 0), 2, -1)
    carried = mul_link_dag(links, 2, last_z, project(load_psi(psi_ref, last_z), 2, 1))
    for s, c in SPIN_COLOUR:
        for part in range(2):
            at = ((s * 3 + c) * 2 + part) * shape.t
            down, up = minus[s, c][part][0 : shape.t], carried[s, c][part][0 : shape.t]
            z_first[at : at + shape.t] = either(z_even, up, down)
            z_second[at : at + shape.t] = either(z_even, down, up)


def prep_kernel(shape, source_hbm, links_hbm, psi_ref, links_ref, *refs):
    messages, (source_ref, links_in, arrived) = refs[:-3], refs[-3:]
    t, z_extent = shape.t, shape.z
    part = 18 * t * z_extent
    copies = [pltpu.make_async_copy(source_hbm, source_ref, arrived.at[4])]
    for direction in (3, 2, 1, 0):
        rows = pl.ds(direction * part, part)
        copies.append(
            pltpu.make_async_copy(links_hbm.at[rows], links_in.at[rows], arrived.at[direction])
        )
    for copy in copies:
        copy.start()
    if shape.rows != t:
        links_ref[...] = jnp.zeros_like(links_ref)
        psi_ref[...] = jnp.zeros_like(psi_ref)
    last = lax.broadcasted_iota(jnp.int32, (t, shape.lanes), 0) == t - 1
    sign = jnp.where(lax.axis_index("ta") == lax.axis_size("ta") - 1, -1.0, 1.0)
    flip = jnp.where(last, sign, 1.0)
    copies[0].wait()
    for k in range(24):
        for z in range(z_extent):
            psi_ref[k, z, 0:t] = source_ref[pl.ds(k * t * z_extent + z, t, stride=z_extent), :]
    for direction in (3, 2, 1, 0):
        copies[4 - direction].wait()
        for k in range(18 * direction, 18 * direction + 18):
            for z in range(z_extent):
                value = links_in[pl.ds(k * t * z_extent + z, t, stride=z_extent), :]
                links_ref[k, z, 0:t] = value * flip if direction == 3 else value
    emit_messages(shape, psi_ref, Links(links_ref), messages)


def summed(shape, term):
    total = None
    for k in range(24):
        for z in range(shape.z):
            value = term(k, z)
            total = value if total is None else total + value
    return total


def over_lanes(total):
    return jnp.sum(jnp.sum(total, axis=0, keepdims=True), axis=1, keepdims=True)


def local_sums(shape, image, origin):
    square = summed(shape, lambda k, z: origin[k, z] * origin[k, z])
    mixed = over_lanes(summed(shape, lambda k, z: image[k, z] * origin[k, z]))
    whole = over_lanes(square)
    factor = jnp.where(whole > 0.0, mixed / jnp.where(whole > 0.0, whole, 1.0), 0.0)
    spread = jnp.broadcast_to(factor, (shape.rows, shape.lanes))
    rest_square, rest_mixed = None, None
    for k in range(24):
        for z in range(shape.z):
            start = origin[k, z]
            rest = image[k, z] - spread * start
            terms = rest * rest, rest * start
            if rest_square is None:
                rest_square, rest_mixed = terms
            else:
                rest_square, rest_mixed = rest_square + terms[0], rest_mixed + terms[1]
    return [factor, *(over_lanes(value) for value in (square, rest_square, rest_mixed))]


def inner_kernel(shape, psi_ref, links_ref, total_ref):
    links = Links(links_ref)
    x = shape.lane() % X
    lanes = shape.lanes
    at_end, at_start = x == X - 1, x == 0

    def ahead(value):
        return jnp.where(
            at_end, pltpu.roll(value, X - 1, 1), pltpu.roll(value, lanes - 1, 1)
        )

    def behind(value):
        return jnp.where(at_start, pltpu.roll(value, lanes - X + 1, 1), pltpu.roll(value, 1, 1))

    for z in range(shape.z):
        psi = load_psi(psi_ref, z)
        zero = jnp.zeros((shape.rows, lanes), jnp.float32)
        total = {key: (zero, zero) for key in psi}
        half = mapped(ahead, project(psi, 0, -1))
        add_rebuilt(total, mul_link(links, 0, z, half), 0, -1)
        half = mapped(behind, mul_link_dag(links, 0, z, project(psi, 0, 1)))
        add_rebuilt(total, half, 0, 1)
        if z + 1 < shape.z:
            half = project(load_psi(psi_ref, z + 1), 2, -1)
            add_rebuilt(total, mul_link(links, 2, z, half), 2, -1)
        if z > 0:
            half = project(load_psi(psi_ref, z - 1), 2, 1)
            add_rebuilt(total, mul_link_dag(links, 2, z - 1, half), 2, 1)
        for (s, c), pair in total.items():
            for part in range(2):
                total_ref[(s * 3 + c) * 2 + part, z] = pair[part]


def add_y_hops(shape, z, psi, total, links, carried_y, y_halo):
    lane, lanes = shape.lane(), shape.lanes
    received = load_half(y_halo, z)
    half = mapped(
        lambda own, other: pltpu.roll(jnp.where(lane < X, other, own), lanes - X, 1),
        project(psi, 1, -1),
        received,
    )
    add_rebuilt(total, mul_link(links, 1, z, half), 1, -1)
    half = mapped(
        lambda own, other: pltpu.roll(jnp.where(lane >= lanes - X, other, own), X, 1),
        load_half(carried_y, z),
        received,
    )
    add_rebuilt(total, half, 1, 1)


def finish_hops(
    shape, psi_ref, links, total_ref, carried_y, carried_t, halo, store
):
    z_second, t_second, z_first, t_first, y_msg = halo
    t_even, z_even = is_even("ta"), is_even("gz")
    row = shape.row()
    lanes, rows, t = shape.lanes, shape.rows, shape.t
    last_z = shape.z - 1

    for z in range(shape.z):
        psi = load_psi(psi_ref, z)
        total = load_psi(total_ref, z)

        def rim_rows(from_even, from_odd):
            half = {}
            for s, c in SPIN_COLOUR:
                ats = [((s * 3 + c) * 2 + part) * shape.z + z for part in range(2)]
                half[s, c] = tuple(
                    jnp.broadcast_to(
                        either(t_even, from_even[at : at + 1], from_odd[at : at + 1]),
                        (rows, lanes),
                    )
                    for at in ats
                )
            return half

        def rim_plane(from_even, from_odd):
            half = {}
            for s, c in SPIN_COLOUR:
                pair = []
                for part in range(2):
                    at = ((s * 3 + c) * 2 + part) * t
                    plane = either(z_even, from_even[at : at + t], from_odd[at : at + t])
                    if rows != t:
                        pad = jnp.zeros((rows - t, lanes), jnp.float32)
                        plane = jnp.concatenate([plane, pad], axis=0)
                    pair.append(plane)
                half[s, c] = tuple(pair)
            return half

        if y_msg is not None:
            add_y_hops(shape, z, psi, total, links, carried_y, y_msg)
        if z == last_z:
            add_rebuilt(total, mul_link(links, 2, z, rim_plane(z_first, z_second)), 2, -1)
        if z == 0:
            add_rebuilt(total, rim_plane(z_second, z_first), 2, 1)
        half = mapped(
            lambda own, other: jnp.where(row == t - 1, other, pltpu.roll(own, rows - 1, 0)),
            project(psi, 3, -1),
            rim_rows(t_first, t_second),
        )
        add_rebuilt(total, mul_link(links, 3, z, half), 3, -1)
        half = mapped(
            lambda own, other: jnp.where(row == 0, other, pltpu.roll(own, 1, 0)),
            load_half(carried_t, z),
            rim_rows(t_second, t_first),
        )
        add_rebuilt(total, half, 3, 1)
        for (s, c), pair in total.items():
            for part in range(2):
                value = psi[s, c][part] - hop_kappa * pair[part]
                value = value if s < 2 else -value
                if rows != t:
                    value = jnp.where(row < t, value, 0.0)
                store((s * 3 + c) * 2 + part, z, value)


def mid_kernel(shape, psi_ref, links_ref, total_ref, carried_y, carried_t, *refs):
    halo, out_ref, messages = refs[:5], refs[5], refs[6:]
    links = Links(links_ref)

    def store(k, z, value):
        out_ref[k, z] = value

    finish_hops(
        shape, psi_ref, links, total_ref, carried_y, carried_t, halo, store
    )
    emit_messages(shape, out_ref, links, messages)


def sums_row(shape, two, start, three, one):
    sums = local_sums(shape, two, start) + local_sums(shape, three, one)
    lane = lax.broadcasted_iota(jnp.int32, (1, shape.lanes), 1)
    row = jnp.zeros((1, shape.lanes), jnp.float32)
    for k, value in enumerate(sums):
        row = jnp.where(lane == k, value, row)
    return row


def inner_sums_kernel(
    shape, psi_ref, links_ref, start_ref, one_ref, two_ref, total_ref, copies_ref
):
    row = sums_row(shape, two_ref, start_ref, psi_ref, one_ref)
    copies_ref[...] = jnp.broadcast_to(row[None], copies_ref.shape)
    inner_kernel(shape, psi_ref, links_ref, total_ref)


def finish_kernel(shape, psi_ref, links_ref, total_ref, carried_y, carried_t, *refs):
    halo, out_ref = refs[:5], refs[5]

    def store(k, z, value):
        out_ref[k, z] = value

    finish_hops(
        shape, psi_ref, Links(links_ref), total_ref, carried_y, carried_t, halo, store
    )


def scalars(table, entries):
    columns = [table[:, k : k + 1] for k in range(8)]
    factor_two, start_square, two_square, two_mixed = columns[:4]
    factor_three, one_square, three_square, three_mixed = columns[4:]

    def over_devices(column):
        return jnp.sum(column, axis=0, keepdims=True)

    norm_square = over_devices(start_square) / entries + epsilon
    alpha_one = over_devices(one_square) / entries / norm_square
    gap = alpha_one - factor_two
    remain_square = over_devices(two_square - gap * (2.0 * two_mixed - gap * start_square)) / entries
    overlap = over_devices(two_mixed - gap * start_square) / entries
    gap = alpha_one - factor_three
    image_square = over_devices(three_square - gap * (2.0 * three_mixed - gap * one_square)) / entries
    norm = jnp.sqrt(norm_square)
    beta_one = jnp.sqrt(remain_square / norm_square + epsilon)
    overlap = overlap / (norm_square * beta_one)
    alpha_two = image_square / (norm_square * beta_one * beta_one) - beta_one * overlap
    scale = 1.0 / (norm * beta_one)
    return alpha_one, beta_one, alpha_two, scale, beta_one / norm


def last_kernel(
    shape, entries, start_ref, two_ref, four_ref, gathered, out_ref, coefficients
):
    alpha_one, beta_one, alpha_two, scale, first_factor = scalars(gathered[:, 0, :], entries)
    t, z_extent = shape.t, shape.z
    for k in range(24):
        for z in range(z_extent):
            two, start = two_ref[k, z], start_ref[k, z]
            remain = two - alpha_one * start
            result = (four_ref[k, z] - alpha_one * two - alpha_two * remain) * scale
            result = result - first_factor * start
            out_ref[pl.ds(k * t * z_extent + z, t, stride=z_extent), :] = result[0:t]
    coefficients[0] = alpha_one[0, 0]
    coefficients[1] = beta_one[0, 0]
    coefficients[2] = alpha_two[0, 0]


def swap(value, axis, second):
    count = math.prod(lax.axis_size(name) for name in (axis if isinstance(axis, tuple) else (axis,)))
    pairs = []
    for low in range(1 if second else 0, count, 2):
        high = (low + 1) % count
        pairs += [(low, high), (high, low)]
    return lax.ppermute(value, axis, pairs)


def exchange(messages, lanes):
    z_second, t_second, z_first, t_first, y_msg = messages
    halo = (
        swap(z_second, "gz", True),
        swap(t_second, "ta", True),
        swap(z_first, "gz", False),
        swap(t_first, "ta", False),
    )
    y_halo = swap(y_msg, "gy", False)
    if lax.axis_size("gy") > 2:
        even = lax.axis_index("gy") % 2 == 0
        lane = lax.broadcasted_iota(jnp.int32, y_msg.shape, y_msg.ndim - 1)
        y_halo = jnp.where((lane < lanes // 2) == even, y_halo, swap(y_msg, "gy", True))
    return (*halo, y_halo)


def from_everyone(copies):
    return lax.all_to_all(copies, ("ta", "gz", "gy"), split_axis=0, concat_axis=0, tiled=True)


def shards(source, gauge_links):
    devices_all = lax.axis_size("ta") * lax.axis_size("gz") * lax.axis_size("gy")
    entries = float(source.size * devices_all)
    shape = Shape(source.shape[3], source.shape[4], source.shape[5])
    t, z, rows, lanes = shape.t, shape.z, shape.rows, shape.lanes
    vmem = pl.BlockSpec(memory_space=pltpu.VMEM)
    smem = pl.BlockSpec(memory_space=pltpu.SMEM)

    def held(*dims):
        return pltpu.VMEM(dims, jnp.float32)

    field = held(24, z, rows, lanes)
    half = held(12, z, rows, lanes)
    z_face, t_face = held(12 * t, lanes), held(12 * z, lanes)
    messages = (z_face, t_face, z_face, t_face, half, half, half)

    def call(kernel, name, flops, out_shape, operands, out_specs=None, in_spec=vmem, scratch=()):
        return pl.pallas_call(
            kernel,
            name=name,
            out_shape=out_shape,
            in_specs=[in_spec] * len(operands),
            out_specs=out_specs or jax.tree.map(lambda _: vmem, out_shape),
            scratch_shapes=scratch,
            compiler_params=pltpu.CompilerParams(vmem_limit_bytes=8 << 20),
            cost_estimate=pl.CostEstimate(flops=flops, bytes_accessed=1 << 20, transcendentals=0),
        )(*operands)

    sites = t * z * lanes
    psi, links, *sent = call(
        functools.partial(prep_kernel, shape), "prep", 400 * sites,
        (field, held(72, z, rows, lanes), *messages),
        (
            pltpu.with_memory_space_constraint(source.reshape(24 * t * z, lanes), pltpu.HBM),
            pltpu.with_memory_space_constraint(gauge_links.reshape(72 * t * z, lanes), pltpu.HBM),
        ),
        in_spec=pl.BlockSpec(memory_space=pltpu.HBM),
        scratch=(
            held(24 * t * z, lanes), held(72 * t * z, lanes), pltpu.SemaphoreType.DMA((5,)),
        ),
    )
    powers = [psi]
    for step in range(3):
        halo = exchange(sent[:5], lanes)
        inner = functools.partial(inner_kernel, shape)
        total = call(inner, "inner", 700 * sites, field, (psi, links))
        psi, *sent = call(
            functools.partial(mid_kernel, shape), "mid", 1000 * sites,
            (field, *messages), (psi, links, total, *sent[5:], *halo),
        )
        powers.append(psi)
    halo = exchange(sent[:5], lanes)
    total, copies = call(
        functools.partial(inner_sums_kernel, shape), "inner_sums", 1100 * sites,
        (field, held(devices_all, 8, lanes)), (psi, links, *powers[:3]),
    )
    gathered = from_everyone(copies)
    four = call(
        functools.partial(finish_kernel, shape), "finish", 700 * sites, field,
        (psi, links, total, *sent[5:], *halo),
    )
    residual, coefficients = call(
        functools.partial(last_kernel, shape, entries), "last", 100 * sites,
        (
            jax.ShapeDtypeStruct((24 * t * z, lanes), jnp.float32),
            jax.ShapeDtypeStruct((3,), jnp.float32),
        ),
        (powers[0], powers[2], four, gathered), (vmem, smem),
    )
    return (residual.reshape(source.shape), coefficients)


class ChipShape(Shape):
    def __init__(self, t_extent, z_extent, lanes):
        super().__init__(t_extent, z_extent, lanes)
        self.parts = 2 * z_extent
        self.z_rows = 24 * t_extent
        self.t_rows = 12 * self.parts

    def block(self, k, part):
        first = (k * self.parts + part) * self.rows
        return pl.ds(first, self.rows)

    def edge(self, k, row):
        return pl.ds(k * self.parts * self.rows + row, self.parts, stride=self.rows)


class ChipLinks:
    def __init__(self, shape, ref, row=None):
        self.shape, self.ref, self.row = shape, ref, row

    def __getitem__(self, index):
        direction, row, col, part = index
        first = ((direction * 3 + row) * 3 + col) * 2
        if self.row is None:
            return tuple(self.ref[self.shape.block(first + n, part), :] for n in range(2))
        return tuple(self.ref[self.shape.edge(first + n, self.row), :] for n in range(2))


def components(spins):
    return [(s, c, part, (s * 3 + c) * 2 + part) for s in range(spins) for c in range(3) for part in range(2)]


def gathered_pairs(spins, value):
    out = {}
    for s in range(spins):
        for c in range(3):
            out[s, c] = tuple(value((s * 3 + c) * 2 + part) for part in range(2))
    return out


def chip_psi(shape, ref, part):
    return gathered_pairs(4, lambda k: ref[shape.block(k, part), :])


def chip_edge(shape, ref, row):
    return gathered_pairs(4, lambda k: ref[shape.edge(k, row), :])


def chip_messages(shape, psi_ref, links_ref, z_second, t_second, z_first, t_first):
    t, last = shape.t, shape.t - 1
    even = is_even("ta")
    minus = project(chip_edge(shape, psi_ref, 0), 3, -1)
    half = project(chip_edge(shape, psi_ref, last), 3, 1)
    carried = mul_link_dag(ChipLinks(shape, links_ref, last), 3, 0, half)
    for s, c, part, k in components(2):
        rows = pl.ds(k * shape.parts, shape.parts)
        up, down = carried[s, c][part], minus[s, c][part]
        t_first[rows, :] = either(even, up, down)
        t_second[rows, :] = either(even, down, up)
    even = is_even("gy")
    links = ChipLinks(shape, links_ref)
    for y_half in range(2):
        minus = project(chip_psi(shape, psi_ref, y_half), 2, -1)
        part_last = shape.parts - 2 + y_half
        half = project(chip_psi(shape, psi_ref, part_last), 2, 1)
        carried = mul_link_dag(links, 2, part_last, half)
        for s, c, part, k in components(2):
            rows = pl.ds((k * 2 + y_half) * t, t)
            up, down = carried[s, c][part][0:t], minus[s, c][part][0:t]
            z_first[rows, :] = either(even, up, down)
            z_second[rows, :] = either(even, down, up)


def chip_bring(shape, y_half, source_ref, links_in, psi_ref, links_ref, arrived):
    t, z_extent = shape.t, 2 * shape.z
    first_plane = lax.axis_index("gy") * shape.z
    last = lax.broadcasted_iota(jnp.int32, (t, shape.lanes), 0) == t - 1
    sign = jnp.where(lax.axis_index("ta") == lax.axis_size("ta") - 1, -1.0, 1.0)
    flip = jnp.where(last, sign, 1.0)

    def bring(in_ref, out_ref, k, z, factor=None):
        value = in_ref[pl.ds(k * t * z_extent + first_plane + z, t, stride=z_extent), :]
        if factor is not None:
            value = value * factor
        at = (k * shape.parts + 2 * z + y_half) * shape.rows
        out_ref[pl.ds(pl.multiple_of(at, 8), t), :] = value

    arrived(4)
    for z in range(shape.z):
        for k in range(24):
            bring(source_ref, psi_ref, k, z)
    for direction in (3, 2, 1, 0):
        arrived(direction)
        for z in range(shape.z):
            for k in range(18 * direction, 18 * direction + 18):
                bring(links_in, links_ref, k, z, flip if direction == 3 else None)


def chip_own_kernel(
    shape, source_hbm, links_hbm, psi_ref, links_ref, rest_ref, source_ref, links_in, semaphores
):
    part = 18 * shape.t * 2 * shape.z
    copies = {4: pltpu.make_async_copy(source_hbm, source_ref, semaphores.at[4])}
    for direction in (3, 2, 1, 0):
        rows = pl.ds(direction * part, part)
        copies[direction] = pltpu.make_async_copy(
            links_hbm.at[rows], links_in.at[rows], semaphores.at[direction]
        )
    for copy in copies.values():
        copy.start()
    if shape.rows != shape.t:
        links_ref[...] = jnp.zeros_like(links_ref)
        psi_ref[...] = jnp.zeros_like(psi_ref)
    chip_bring(
        shape, lax.axis_index("gy"), source_ref, links_in, psi_ref, links_ref,
        lambda n: copies[n].wait(),
    )
    t, z_extent = shape.t, 2 * shape.z
    first_plane = (1 - lax.axis_index("gy")) * shape.z
    if shape.rows != t:
        rest_ref[...] = jnp.zeros_like(rest_ref)
    for k in range(24):
        for z in range(shape.z):
            value = source_ref[pl.ds(k * t * z_extent + first_plane + z, t, stride=z_extent), :]
            rest_ref[pl.ds((k * shape.z + z) * shape.rows, t), :] = value


def chip_prep_kernel(
    shape, source_ref, links_in, psi_in, links_held, psi_ref, links_ref, *messages
):
    chip_bring(
        shape, 1 - lax.axis_index("gy"), source_ref, links_in, psi_ref, links_ref, lambda n: None
    )
    chip_messages(shape, psi_ref, links_ref, *messages)


def chip_inner_kernel(shape, psi_ref, links_ref, total_ref):
    links = ChipLinks(shape, links_ref)
    lane, row = shape.lane(), shape.row()
    x = lane % X
    lanes, rows, t = shape.lanes, shape.rows, shape.t
    at_end, at_start = x == X - 1, x == 0
    inside_ahead = row < t - 1
    inside_behind = jnp.logical_and(row > 0, row < t)

    def x_ahead(value):
        return jnp.where(
            at_end, pltpu.roll(value, X - 1, 1), pltpu.roll(value, lanes - 1, 1)
        )

    def x_behind(value):
        return jnp.where(at_start, pltpu.roll(value, lanes - X + 1, 1), pltpu.roll(value, 1, 1))

    def t_ahead(value):
        return jnp.where(inside_ahead, pltpu.roll(value, rows - 1, 0), 0.0)

    def t_behind(value):
        return jnp.where(inside_behind, pltpu.roll(value, 1, 0), 0.0)

    for z in range(shape.z):
        for part in (2 * z, 2 * z + 1):
            psi = chip_psi(shape, psi_ref, part)
            zero = jnp.zeros((rows, lanes), jnp.float32)
            total = {key: (zero, zero) for key in psi}
            half = mapped(x_ahead, project(psi, 0, -1))
            add_rebuilt(total, mul_link(links, 0, part, half), 0, -1)
            half = mapped(x_behind, mul_link_dag(links, 0, part, project(psi, 0, 1)))
            add_rebuilt(total, half, 0, 1)
            half = mapped(t_ahead, project(psi, 3, -1))
            add_rebuilt(total, mul_link(links, 3, part, half), 3, -1)
            half = mapped(t_behind, mul_link_dag(links, 3, part, project(psi, 3, 1)))
            add_rebuilt(total, half, 3, 1)
            if z + 1 < shape.z:
                half = project(chip_psi(shape, psi_ref, part + 2), 2, -1)
                add_rebuilt(total, mul_link(links, 2, part, half), 2, -1)
            if z > 0:
                half = project(chip_psi(shape, psi_ref, part - 2), 2, 1)
                add_rebuilt(total, mul_link_dag(links, 2, part - 2, half), 2, 1)
            for s, c, n, k in components(4):
                total_ref[shape.block(k, part), :] = total[s, c][n]
        pair = (2 * z, 2 * z + 1)
        minus, carried = [], []
        for part in pair:
            psi = chip_psi(shape, psi_ref, part)
            minus.append(mapped(lambda v: pltpu.roll(v, lanes - X, 1), project(psi, 1, -1)))
            half = mul_link_dag(links, 1, part, project(psi, 1, 1))
            carried.append(mapped(lambda v: pltpu.roll(v, X, 1), half))
        for own, part in enumerate(pair):
            total = chip_psi(shape, total_ref, part)
            half = mapped(
                lambda a, b: jnp.where(lane >= lanes - X, b, a), minus[own], minus[1 - own]
            )
            add_rebuilt(total, mul_link(links, 1, part, half), 1, -1)
            half = mapped(lambda a, b: jnp.where(lane < X, b, a), carried[own], carried[1 - own])
            add_rebuilt(total, half, 1, 1)
            for s, c, n, k in components(4):
                total_ref[shape.block(k, part), :] = total[s, c][n]


def chip_sort_faces(z_second, z_first, scratch):
    z_down, z_up = scratch
    z_even = is_even("gy")
    second = 0.0 if z_second is None else z_second[...]
    first = 0.0 if z_first is None else z_first[...]
    z_down[...] = either(z_even, first, second)
    z_up[...] = either(z_even, second, first)


def chip_add_z(shape, links, part, total, scratch):
    z_down, z_up = scratch
    t, rows, lanes, parts = shape.t, shape.rows, shape.lanes, shape.parts

    def plane(ref, y_half):
        def value(k):
            face = ref[pl.ds((k * 2 + y_half) * t, t), :]
            if rows != t:
                pad = jnp.zeros((rows - t, lanes), jnp.float32)
                face = jnp.concatenate([face, pad], axis=0)
            return face

        return gathered_pairs(2, value)

    if part >= parts - 2:
        half = mul_link(links, 2, part, plane(z_down, part - parts + 2))
        add_rebuilt(total, half, 2, -1)
    if part < 2:
        add_rebuilt(total, plane(z_up, part), 2, 1)


def chip_finish(
    shape, psi_ref, links_ref, total_ref, received, scratch, out_ref, face_ref=None
):
    z_second, t_second, z_first, t_first = received
    t_even = is_even("ta")
    t, lanes, parts = shape.t, shape.lanes, shape.parts
    chip_sort_faces(z_second, z_first, scratch)
    links = ChipLinks(shape, links_ref)

    for part in range(parts):
        total = chip_psi(shape, total_ref, part)
        chip_add_z(shape, links, part, total, scratch)
        for s, c, n, k in components(4):
            value = total[s, c][n]
            if face_ref is not None:
                value = value + face_ref[shape.block(k, part), :]
            value = psi_ref[shape.block(k, part), :] - hop_kappa * value
            out_ref[shape.block(k, part), :] = value if s < 2 else -value

    def t_half(from_even, from_odd):
        def value(k):
            at = pl.ds(k * parts, parts)
            return either(t_even, from_even[at, :], from_odd[at, :])

        return gathered_pairs(2, value)

    down = mul_link(ChipLinks(shape, links_ref, t - 1), 3, 0, t_half(t_first, t_second))
    up = t_half(t_second, t_first)
    zero = jnp.zeros((parts, lanes), jnp.float32)
    for half, parity, row in ((down, -1, t - 1), (up, 1, 0)):
        total = {(s, c): (zero, zero) for s in range(4) for c in range(3)}
        add_rebuilt(total, half, 3, parity)
        for s, c, n, k in components(4):
            at = shape.edge(k, row)
            value = hop_kappa * total[s, c][n]
            out_ref[at, :] = out_ref[at, :] - (value if s < 2 else -value)


def chip_mid_kernel(shape, hands_over, psi_ref, links_ref, total_ref, *refs):
    received, out_ref, messages, refs = refs[:4], refs[4], refs[5:9], refs[9:]
    chip_finish(shape, psi_ref, links_ref, total_ref, received, refs[-2:], out_ref)
    chip_messages(shape, out_ref, links_ref, *messages)
    if hands_over:
        hand_over(shape, out_ref, refs[0])


def chip_sums_kernel(
    shape, links_ref, z_first, start_ref, one_ref, two_ref, three_ref,
    face_ref, copies_ref, *scratch,
):
    class View:
        def __init__(self, ref):
            self.ref = ref

        def __getitem__(self, index):
            return self.ref[shape.block(*index), :]

    wide = ChipShape(shape.t, shape.z, shape.lanes)
    wide.z = shape.parts
    row = sums_row(wide, View(two_ref), View(start_ref), View(three_ref), View(one_ref))
    copies_ref[...] = jnp.broadcast_to(row[None], copies_ref.shape)
    chip_sort_faces(None, z_first, scratch)
    zero = jnp.zeros((shape.rows, shape.lanes), jnp.float32)
    for part in range(shape.parts):
        total = {(s, c): (zero, zero) for s in range(4) for c in range(3)}
        chip_add_z(shape, ChipLinks(shape, links_ref), part, total, scratch)
        for s, c, n, k in components(4):
            face_ref[shape.block(k, part), :] = total[s, c][n]


def chip_scalars_kernel(entries, gathered, factors_ref, coefficients):
    alpha_one, beta_one, alpha_two, scale, first_factor = scalars(gathered[:, 0, :], entries)
    lanes = factors_ref.shape[1]
    values = [alpha_one, alpha_two, scale, first_factor]
    values = [jnp.broadcast_to(value, (1, lanes)) for value in values]
    values.append(jnp.zeros((4, lanes), jnp.float32))
    factors_ref[...] = jnp.concatenate(values, axis=0)
    coefficients[0] = alpha_one[0, 0]
    coefficients[1] = beta_one[0, 0]
    coefficients[2] = alpha_two[0, 0]


def y_part(shape, k, z, y_half):
    return pl.ds(pl.multiple_of((k * shape.parts + 2 * z + y_half) * shape.rows, 8), shape.rows)


def rest_rows(shape, k, z):
    return pl.ds((k * shape.z + z) * shape.rows, shape.rows)


def hand_over(shape, ref, rest_ref):
    y_half = 1 - lax.axis_index("gy")
    for k in range(24):
        for z in range(shape.z):
            rest_ref[rest_rows(shape, k, z), :] = ref[y_part(shape, k, z, y_half), :]


def chip_finish_kernel(
    shape, psi_ref, links_ref, total_ref, face_ref, z_second, t_second, t_first,
    out_ref, rest_ref, *scratch,
):
    received = z_second, t_second, None, t_first
    chip_finish(shape, psi_ref, links_ref, total_ref, received, scratch, out_ref, face_ref)
    y_half = 1 - lax.axis_index("gy")
    for k in range(24):
        for z in range(shape.z):
            value = out_ref[y_part(shape, k, z, y_half), :]
            rest_ref[dense_rows(shape, k, z), :] = value[0 : shape.t]


def dense_rows(shape, k, z):
    return pl.ds((k * shape.z + z) * shape.t, shape.t)


def chip_last_kernel(
    shape, start_ref, two_ref, four_ref, start_rest, two_rest, four_rest, factors_ref, out_ref
):
    t, z_extent = shape.t, 2 * shape.z
    alpha_one, alpha_two, scale, first_factor = (
        jnp.broadcast_to(factors_ref[k : k + 1], (t, shape.lanes)) for k in range(4)
    )
    core = lax.axis_index("gy")

    def put(k, z, start, two, four):
        remain = two - alpha_one * start
        result = (four - alpha_one * two - alpha_two * remain) * scale - first_factor * start
        out_ref[pl.ds(k * t * z_extent + z, t, stride=z_extent), :] = result

    for k in range(24):
        for z in range(shape.z):
            rows = y_part(shape, k, z, core)
            put(k, core * shape.z + z, *(ref[rows, :][0:t] for ref in (start_ref, two_ref, four_ref)))
            rows = rest_rows(shape, k, z)
            other = [ref[rows, :][0:t] for ref in (start_rest, two_rest)]
            put(k, (1 - core) * shape.z + z, *other, four_rest[dense_rows(shape, k, z), :])


def chip_shards(source, gauge_links):
    devices_all = lax.axis_size("ta") * lax.axis_size("gz") * 2
    entries = float(source.size * devices_all)
    z_extent = source.shape[4]
    shape = ChipShape(source.shape[3], z_extent // 2, source.shape[5])
    t, rows, lanes = shape.t, shape.rows, shape.lanes
    vmem = pl.BlockSpec(memory_space=pltpu.VMEM)
    smem = pl.BlockSpec(memory_space=pltpu.SMEM)

    def held(*dims):
        return pltpu.VMEM(dims, jnp.float32)

    field = held(24 * shape.parts * rows, lanes)
    links_field = held(72 * shape.parts * rows, lanes)
    z_face, t_face = held(shape.z_rows, lanes), held(shape.t_rows, lanes)
    messages = (z_face, t_face, z_face, t_face)
    z_faces = (z_face, z_face)

    def call(kernel, name, flops, out_shape, operands, **options):
        in_spec = options.pop("in_spec", vmem)
        out_specs = options.pop("out_specs", jax.tree.map(lambda _: vmem, out_shape))
        return pl.pallas_call(
            kernel,
            name=name,
            out_shape=out_shape,
            in_specs=[in_spec] * len(operands),
            out_specs=out_specs,
            compiler_params=pltpu.CompilerParams(vmem_limit_bytes=8 << 20),
            cost_estimate=pl.CostEstimate(flops=flops, bytes_accessed=1 << 20, transcendentals=0),
            **options,
        )(*operands)

    def exchanged(sent):
        z_second, t_second, z_first, t_first = sent
        z_ring = ("gz", "gy")
        z_second = swap(z_second, z_ring, True)
        t_first = swap(t_first, "ta", False)
        z_first = swap(z_first, z_ring, False)
        t_second = swap(t_second, "ta", True)
        return z_second, t_second, z_first, t_first

    sites = t * z_extent * lanes
    rows_in = t * z_extent
    own = (source.reshape(24 * rows_in, lanes), gauge_links.reshape(72 * rows_in, lanes))
    other = tuple(swap(value, "gy", False) for value in own)
    rest = held(24 * shape.z * rows, lanes)
    psi, links, start_rest = call(
        functools.partial(chip_own_kernel, shape), "own", 200 * sites, (field, links_field, rest),
        [pltpu.with_memory_space_constraint(value, pltpu.HBM) for value in own],
        scratch_shapes=(
            held(24 * rows_in, lanes), held(72 * rows_in, lanes), pltpu.SemaphoreType.DMA((5,)),
        ),
        in_spec=pl.BlockSpec(memory_space=pltpu.HBM),
    )
    psi, links, *sent = call(
        functools.partial(chip_prep_kernel, shape), "prep", 400 * sites,
        (field, links_field, *messages), (*other, psi, links),
        input_output_aliases={2: 0, 3: 1},
    )
    powers = [psi]
    for step in range(3):
        halo = exchanged(sent)
        inner = functools.partial(chip_inner_kernel, shape)
        total = call(inner, "inner", 1000 * sites, field, (psi, links))
        hands_over = step == 1
        psi, *sent = call(
            functools.partial(chip_mid_kernel, shape, hands_over), "mid", 600 * sites,
            (field, *messages, rest) if hands_over else (field, *messages),
            (psi, links, total, *halo), scratch_shapes=z_faces,
        )
        powers.append(psi)
        if hands_over:
            two_rest = swap(sent.pop(), "gy", False)
    halo = exchanged(sent)
    face, copies = call(
        functools.partial(chip_sums_kernel, shape), "sums", 600 * sites,
        (field, held(devices_all, 1, lanes)), (links, halo[2], *powers), scratch_shapes=z_faces,
    )
    gathered = from_everyone(copies)
    total = call(inner, "inner", 1000 * sites, field, (psi, links))
    four, four_rest = call(
        functools.partial(chip_finish_kernel, shape), "finish", 400 * sites,
        (field, held(24 * shape.z * t, lanes)),
        (psi, links, total, face, halo[0], halo[1], halo[3]), scratch_shapes=z_faces,
    )
    four_rest = swap(four_rest, "gy", False)
    factors, coefficients = call(
        functools.partial(chip_scalars_kernel, entries), "scalars", 10**11,
        (held(8, lanes), jax.ShapeDtypeStruct((3,), jnp.float32)), (gathered,),
        out_specs=(vmem, smem),
    )
    residual = call(
        functools.partial(chip_last_kernel, shape), "last", 100 * sites,
        jax.ShapeDtypeStruct((24 * rows_in, lanes), jnp.float32),
        (powers[0], powers[2], four, start_rest, two_rest, four_rest, factors),
    )
    return (residual.reshape(source.shape), coefficients)


def solution(mesh):
    placed = (P(None, None, None, "ta", "gz", "gy"), P(None, None, None, None, "ta", "gz", "gy"))
    return jax.shard_map(
        chip_shards if mesh.shape["gy"] == 2 else shards,
        mesh=mesh,
        in_specs=placed,
        out_specs=(P(None, None, None, "ta", "gz", "gy"), P()),
        check_vma=False,
    )
```

```python
import functools
import math

import jax
import jax.numpy as jnp
from jax import lax
from jax.experimental import pallas as pl
from jax.experimental.pallas import tpu as pltpu
from jax.sharding import PartitionSpec as P

X = 32

hop_kappa = 0.19
epsilon = 1e-06
spin_table = (
    ((1, 0), (-1j, -1j)),
    ((1, 0), (-1, 1)),
    ((0, 1), (-1j, 1j)),
    ((0, 1), (1, 1)),
)
SPIN_COLOUR = [(spin, colour) for spin in range(2) for colour in range(3)]


def add_phased(left, phase, right):
    phase = complex(phase)
    if phase == 1:
        return (left[0] + right[0], left[1] + right[1])
    if phase == -1:
        return (left[0] - right[0], left[1] - right[1])
    if phase == 1j:
        return (left[0] - right[1], left[1] + right[0])
    return (left[0] + right[1], left[1] - right[0])


def project(psi, direction, parity):
    order, phases = spin_table[direction]
    return {
        (s, c): add_phased(psi[s, c], parity * phases[s], psi[2 + order[s], c])
        for s, c in SPIN_COLOUR
    }


def add_rebuilt(total, half, direction, parity):
    order, phases = spin_table[direction]
    for s, c in SPIN_COLOUR:
        total[s, c] = add_phased(total[s, c], 1, half[s, c])
        row = order[s]
        phase = parity * complex(phases[row]).conjugate()
        total[2 + s, c] = add_phased(total[2 + s, c], phase, half[row, c])


def mul_link(links, direction, z, half):
    out = {}
    for row in range(3):
        for s in range(2):
            real, imag = None, None
            for col in range(3):
                u_real, u_imag = links[direction, row, col, z]
                h_real, h_imag = half[s, col]
                term_real = u_real * h_real - u_imag * h_imag
                term_imag = u_real * h_imag + u_imag * h_real
                real = term_real if real is None else real + term_real
                imag = term_imag if imag is None else imag + term_imag
            out[s, row] = (real, imag)
    return out


def mul_link_dag(links, direction, z, half):
    out = {}
    for row in range(3):
        for s in range(2):
            real, imag = None, None
            for col in range(3):
                u_real, u_imag = links[direction, col, row, z]
                h_real, h_imag = half[s, col]
                term_real = u_real * h_real + u_imag * h_imag
                term_imag = u_real * h_imag - u_imag * h_real
                real = term_real if real is None else real + term_real
                imag = term_imag if imag is None else imag + term_imag
            out[s, row] = (real, imag)
    return out


def mapped(function, *halves):
    return {
        key: tuple(function(*(half[key][part] for half in halves)) for part in range(2))
        for key in SPIN_COLOUR
    }


class Links:
    def __init__(self, ref):
        self.ref = ref

    def __getitem__(self, index):
        direction, row, col, z = index
        first = ((direction * 3 + row) * 3 + col) * 2
        return (self.ref[first, z], self.ref[first + 1, z])


def load_psi(ref, z):
    return {
        (s, c): (ref[(s * 3 + c) * 2, z], ref[(s * 3 + c) * 2 + 1, z])
        for s in range(4)
        for c in range(3)
    }


def load_half(ref, z):
    return {
        (s, c): (ref[(s * 3 + c) * 2, z], ref[(s * 3 + c) * 2 + 1, z]) for s, c in SPIN_COLOUR
    }


def store_half(ref, z, half):
    for (s, c), pair in half.items():
        for part in range(2):
            ref[(s * 3 + c) * 2 + part, z] = pair[part]


class Shape:
    def __init__(self, t_extent, z_extent, lanes):
        self.t = t_extent
        self.z = z_extent
        self.rows = -(-t_extent // 8) * 8
        self.lanes = lanes

    def row(self):
        return lax.broadcasted_iota(jnp.int32, (self.rows, self.lanes), 0)

    def lane(self):
        return lax.broadcasted_iota(jnp.int32, (self.rows, self.lanes), 1)


def is_even(axis):
    return jnp.bitwise_and(lax.axis_index(axis), 1) == 0


def either(choice, first, second):
    return jnp.where(choice, first, second)


def emit_messages(shape, psi_ref, links, refs):
    z_second, t_second, z_first, t_first, y_msg, carried_y, carried_t = refs
    t_even, z_even = is_even("ta"), is_even("gz")
    lane = shape.lane()
    last_z, last_t = shape.z - 1, shape.t - 1
    for z in range(shape.z):
        psi = load_psi(psi_ref, z)
        minus = project(psi, 3, -1)
        carried = mul_link_dag(links, 3, z, project(psi, 3, 1))
        store_half(carried_t, z, carried)
        for s, c in SPIN_COLOUR:
            for part in range(2):
                at = ((s * 3 + c) * 2 + part) * shape.z + z
                down = minus[s, c][part][0:1]
                up = carried[s, c][part][last_t : last_t + 1]
                t_first[at : at + 1] = either(t_even, up, down)
                t_second[at : at + 1] = either(t_even, down, up)
        minus = project(psi, 1, -1)
        carried = mul_link_dag(links, 1, z, project(psi, 1, 1))
        store_half(carried_y, z, carried)
        store_half(
            y_msg,
            z,
            mapped(lambda low, high: jnp.where(lane < X, low, high), minus, carried),
        )
    minus = project(load_psi(psi_ref, 0), 2, -1)
    carried = mul_link_dag(links, 2, last_z, project(load_psi(psi_ref, last_z), 2, 1))
    for s, c in SPIN_COLOUR:
        for part in range(2):
            at = ((s * 3 + c) * 2 + part) * shape.t
            down, up = minus[s, c][part][0 : shape.t], carried[s, c][part][0 : shape.t]
            z_first[at : at + shape.t] = either(z_even, up, down)
            z_second[at : at + shape.t] = either(z_even, down, up)


def prep_kernel(shape, source_hbm, links_hbm, psi_ref, links_ref, *refs):
    messages, (source_ref, links_in, arrived) = refs[:-3], refs[-3:]
    t, z_extent = shape.t, shape.z
    part = 18 * t * z_extent
    copies = [pltpu.make_async_copy(source_hbm, source_ref, arrived.at[4])]
    for direction in (3, 2, 1, 0):
        rows = pl.ds(direction * part, part)
        copies.append(
            pltpu.make_async_copy(links_hbm.at[rows], links_in.at[rows], arrived.at[direction])
        )
    for copy in copies:
        copy.start()
    if shape.rows != t:
        links_ref[...] = jnp.zeros_like(links_ref)
        psi_ref[...] = jnp.zeros_like(psi_ref)
    last = lax.broadcasted_iota(jnp.int32, (t, shape.lanes), 0) == t - 1
    sign = jnp.where(lax.axis_index("ta") == lax.axis_size("ta") - 1, -1.0, 1.0)
    flip = jnp.where(last, sign, 1.0)
    copies[0].wait()
    for k in range(24):
        for z in range(z_extent):
            psi_ref[k, z, 0:t] = source_ref[pl.ds(k * t * z_extent + z, t, stride=z_extent), :]
    for direction in (3, 2, 1, 0):
        copies[4 - direction].wait()
        for k in range(18 * direction, 18 * direction + 18):
            for z in range(z_extent):
                value = links_in[pl.ds(k * t * z_extent + z, t, stride=z_extent), :]
                links_ref[k, z, 0:t] = value * flip if direction == 3 else value
    emit_messages(shape, psi_ref, Links(links_ref), messages)


def summed(shape, term):
    total = None
    for k in range(24):
        for z in range(shape.z):
            value = term(k, z)
            total = value if total is None else total + value
    return total


def over_lanes(total):
    return jnp.sum(jnp.sum(total, axis=0, keepdims=True), axis=1, keepdims=True)


def local_sums(shape, image, origin):
    square = summed(shape, lambda k, z: origin[k, z] * origin[k, z])
    mixed = over_lanes(summed(shape, lambda k, z: image[k, z] * origin[k, z]))
    whole = over_lanes(square)
    factor = jnp.where(whole > 0.0, mixed / jnp.where(whole > 0.0, whole, 1.0), 0.0)
    spread = jnp.broadcast_to(factor, (shape.rows, shape.lanes))
    rest_square, rest_mixed = None, None
    for k in range(24):
        for z in range(shape.z):
            start = origin[k, z]
            rest = image[k, z] - spread * start
            terms = rest * rest, rest * start
            if rest_square is None:
                rest_square, rest_mixed = terms
            else:
                rest_square, rest_mixed = rest_square + terms[0], rest_mixed + terms[1]
    return [factor, *(over_lanes(value) for value in (square, rest_square, rest_mixed))]


def inner_kernel(shape, psi_ref, links_ref, total_ref):
    links = Links(links_ref)
    x = shape.lane() % X
    lanes = shape.lanes
    at_end, at_start = x == X - 1, x == 0

    def ahead(value):
        return jnp.where(
            at_end, pltpu.roll(value, X - 1, 1), pltpu.roll(value, lanes - 1, 1)
        )

    def behind(value):
        return jnp.where(at_start, pltpu.roll(value, lanes - X + 1, 1), pltpu.roll(value, 1, 1))

    for z in range(shape.z):
        psi = load_psi(psi_ref, z)
        zero = jnp.zeros((shape.rows, lanes), jnp.float32)
        total = {key: (zero, zero) for key in psi}
        half = mapped(ahead, project(psi, 0, -1))
        add_rebuilt(total, mul_link(links, 0, z, half), 0, -1)
        half = mapped(behind, mul_link_dag(links, 0, z, project(psi, 0, 1)))
        add_rebuilt(total, half, 0, 1)
        if z + 1 < shape.z:
            half = project(load_psi(psi_ref, z + 1), 2, -1)
            add_rebuilt(total, mul_link(links, 2, z, half), 2, -1)
        if z > 0:
            half = project(load_psi(psi_ref, z - 1), 2, 1)
            add_rebuilt(total, mul_link_dag(links, 2, z - 1, half), 2, 1)
        for (s, c), pair in total.items():
            for part in range(2):
                total_ref[(s * 3 + c) * 2 + part, z] = pair[part]


def add_y_hops(shape, z, psi, total, links, carried_y, y_halo):
    lane, lanes = shape.lane(), shape.lanes
    received = load_half(y_halo, z)
    half = mapped(
        lambda own, other: pltpu.roll(jnp.where(lane < X, other, own), lanes - X, 1),
        project(psi, 1, -1),
        received,
    )
    add_rebuilt(total, mul_link(links, 1, z, half), 1, -1)
    half = mapped(
        lambda own, other: pltpu.roll(jnp.where(lane >= lanes - X, other, own), X, 1),
        load_half(carried_y, z),
        received,
    )
    add_rebuilt(total, half, 1, 1)


def finish_hops(
    shape, psi_ref, links, total_ref, carried_y, carried_t, halo, store
):
    z_second, t_second, z_first, t_first, y_msg = halo
    t_even, z_even = is_even("ta"), is_even("gz")
    row = shape.row()
    lanes, rows, t = shape.lanes, shape.rows, shape.t
    last_z = shape.z - 1

    for z in range(shape.z):
        psi = load_psi(psi_ref, z)
        total = load_psi(total_ref, z)

        def rim_rows(from_even, from_odd):
            half = {}
            for s, c in SPIN_COLOUR:
                ats = [((s * 3 + c) * 2 + part) * shape.z + z for part in range(2)]
                half[s, c] = tuple(
                    jnp.broadcast_to(
                        either(t_even, from_even[at : at + 1], from_odd[at : at + 1]),
                        (rows, lanes),
                    )
                    for at in ats
                )
            return half

        def rim_plane(from_even, from_odd):
            half = {}
            for s, c in SPIN_COLOUR:
                pair = []
                for part in range(2):
                    at = ((s * 3 + c) * 2 + part) * t
                    plane = either(z_even, from_even[at : at + t], from_odd[at : at + t])
                    if rows != t:
                        pad = jnp.zeros((rows - t, lanes), jnp.float32)
                        plane = jnp.concatenate([plane, pad], axis=0)
                    pair.append(plane)
                half[s, c] = tuple(pair)
            return half

        if y_msg is not None:
            add_y_hops(shape, z, psi, total, links, carried_y, y_msg)
        if z == last_z:
            add_rebuilt(total, mul_link(links, 2, z, rim_plane(z_first, z_second)), 2, -1)
        if z == 0:
            add_rebuilt(total, rim_plane(z_second, z_first), 2, 1)
        half = mapped(
            lambda own, other: jnp.where(row == t - 1, other, pltpu.roll(own, rows - 1, 0)),
            project(psi, 3, -1),
            rim_rows(t_first, t_second),
        )
        add_rebuilt(total, mul_link(links, 3, z, half), 3, -1)
        half = mapped(
            lambda own, other: jnp.where(row == 0, other, pltpu.roll(own, 1, 0)),
            load_half(carried_t, z),
            rim_rows(t_second, t_first),
        )
        add_rebuilt(total, half, 3, 1)
        for (s, c), pair in total.items():
            for part in range(2):
                value = psi[s, c][part] - hop_kappa * pair[part]
                value = value if s < 2 else -value
                if rows != t:
                    value = jnp.where(row < t, value, 0.0)
                store((s * 3 + c) * 2 + part, z, value)


def mid_kernel(shape, psi_ref, links_ref, total_ref, carried_y, carried_t, *refs):
    halo, out_ref, messages = refs[:5], refs[5], refs[6:]
    links = Links(links_ref)

    def store(k, z, value):
        out_ref[k, z] = value

    finish_hops(
        shape, psi_ref, links, total_ref, carried_y, carried_t, halo, store
    )
    emit_messages(shape, out_ref, links, messages)


def sums_row(shape, two, start, three, one):
    sums = local_sums(shape, two, start) + local_sums(shape, three, one)
    lane = lax.broadcasted_iota(jnp.int32, (1, shape.lanes), 1)
    row = jnp.zeros((1, shape.lanes), jnp.float32)
    for k, value in enumerate(sums):
        row = jnp.where(lane == k, value, row)
    return row


def inner_sums_kernel(
    shape, psi_ref, links_ref, start_ref, one_ref, two_ref, total_ref, copies_ref
):
    row = sums_row(shape, two_ref, start_ref, psi_ref, one_ref)
    copies_ref[...] = jnp.broadcast_to(row[None], copies_ref.shape)
    inner_kernel(shape, psi_ref, links_ref, total_ref)


def finish_kernel(shape, psi_ref, links_ref, total_ref, carried_y, carried_t, *refs):
    halo, out_ref = refs[:5], refs[5]

    def store(k, z, value):
        out_ref[k, z] = value

    finish_hops(
        shape, psi_ref, Links(links_ref), total_ref, carried_y, carried_t, halo, store
    )


def scalars(table, entries):
    columns = [table[:, k : k + 1] for k in range(8)]
    factor_two, start_square, two_square, two_mixed = columns[:4]
    factor_three, one_square, three_square, three_mixed = columns[4:]

    def over_devices(column):
        return jnp.sum(column, axis=0, keepdims=True)

    norm_square = over_devices(start_square) / entries + epsilon
    alpha_one = over_devices(one_square) / entries / norm_square
    gap = alpha_one - factor_two
    remain_square = over_devices(two_square - gap * (2.0 * two_mixed - gap * start_square)) / entries
    overlap = over_devices(two_mixed - gap * start_square) / entries
    gap = alpha_one - factor_three
    image_square = over_devices(three_square - gap * (2.0 * three_mixed - gap * one_square)) / entries
    norm = jnp.sqrt(norm_square)
    beta_one = jnp.sqrt(remain_square / norm_square + epsilon)
    overlap = overlap / (norm_square * beta_one)
    alpha_two = image_square / (norm_square * beta_one * beta_one) - beta_one * overlap
    scale = 1.0 / (norm * beta_one)
    return alpha_one, beta_one, alpha_two, scale, beta_one / norm


def last_kernel(
    shape, entries, start_ref, two_ref, four_ref, gathered, out_ref, coefficients
):
    alpha_one, beta_one, alpha_two, scale, first_factor = scalars(gathered[:, 0, :], entries)
    t, z_extent = shape.t, shape.z
    for k in range(24):
        for z in range(z_extent):
            two, start = two_ref[k, z], start_ref[k, z]
            remain = two - alpha_one * start
            result = (four_ref[k, z] - alpha_one * two - alpha_two * remain) * scale
            result = result - first_factor * start
            out_ref[pl.ds(k * t * z_extent + z, t, stride=z_extent), :] = result[0:t]
    coefficients[0] = alpha_one[0, 0]
    coefficients[1] = beta_one[0, 0]
    coefficients[2] = alpha_two[0, 0]


def swap(value, axis, second):
    count = math.prod(lax.axis_size(name) for name in (axis if isinstance(axis, tuple) else (axis,)))
    pairs = []
    for low in range(1 if second else 0, count, 2):
        high = (low + 1) % count
        pairs += [(low, high), (high, low)]
    return lax.ppermute(value, axis, pairs)


def exchange(messages, lanes):
    z_second, t_second, z_first, t_first, y_msg = messages
    halo = (
        swap(z_second, "gz", True),
        swap(t_second, "ta", True),
        swap(z_first, "gz", False),
        swap(t_first, "ta", False),
    )
    y_halo = swap(y_msg, "gy", False)
    if lax.axis_size("gy") > 2:
        even = lax.axis_index("gy") % 2 == 0
        lane = lax.broadcasted_iota(jnp.int32, y_msg.shape, y_msg.ndim - 1)
        y_halo = jnp.where((lane < lanes // 2) == even, y_halo, swap(y_msg, "gy", True))
    return (*halo, y_halo)


def from_everyone(copies):
    return lax.all_to_all(copies, ("ta", "gz", "gy"), split_axis=0, concat_axis=0, tiled=True)


def shards(source, gauge_links):
    devices_all = lax.axis_size("ta") * lax.axis_size("gz") * lax.axis_size("gy")
    entries = float(source.size * devices_all)
    shape = Shape(source.shape[3], source.shape[4], source.shape[5])
    t, z, rows, lanes = shape.t, shape.z, shape.rows, shape.lanes
    vmem = pl.BlockSpec(memory_space=pltpu.VMEM)
    smem = pl.BlockSpec(memory_space=pltpu.SMEM)

    def held(*dims):
        return pltpu.VMEM(dims, jnp.float32)

    field = held(24, z, rows, lanes)
    half = held(12, z, rows, lanes)
    z_face, t_face = held(12 * t, lanes), held(12 * z, lanes)
    messages = (z_face, t_face, z_face, t_face, half, half, half)

    def call(kernel, name, flops, out_shape, operands, out_specs=None, in_spec=vmem, scratch=()):
        return pl.pallas_call(
            kernel,
            name=name,
            out_shape=out_shape,
            in_specs=[in_spec] * len(operands),
            out_specs=out_specs or jax.tree.map(lambda _: vmem, out_shape),
            scratch_shapes=scratch,
            compiler_params=pltpu.CompilerParams(vmem_limit_bytes=8 << 20),
            cost_estimate=pl.CostEstimate(flops=flops, bytes_accessed=1 << 20, transcendentals=0),
        )(*operands)

    sites = t * z * lanes
    psi, links, *sent = call(
        functools.partial(prep_kernel, shape), "prep", 400 * sites,
        (field, held(72, z, rows, lanes), *messages),
        (
            pltpu.with_memory_space_constraint(source.reshape(24 * t * z, lanes), pltpu.HBM),
            pltpu.with_memory_space_constraint(gauge_links.reshape(72 * t * z, lanes), pltpu.HBM),
        ),
        in_spec=pl.BlockSpec(memory_space=pltpu.HBM),
        scratch=(
            held(24 * t * z, lanes), held(72 * t * z, lanes), pltpu.SemaphoreType.DMA((5,)),
        ),
    )
    powers = [psi]
    for step in range(3):
        halo = exchange(sent[:5], lanes)
        inner = functools.partial(inner_kernel, shape)
        total = call(inner, "inner", 700 * sites, field, (psi, links))
        psi, *sent = call(
            functools.partial(mid_kernel, shape), "mid", 1000 * sites,
            (field, *messages), (psi, links, total, *sent[5:], *halo),
        )
        powers.append(psi)
    halo = exchange(sent[:5], lanes)
    total, copies = call(
        functools.partial(inner_sums_kernel, shape), "inner_sums", 1100 * sites,
        (field, held(devices_all, 8, lanes)), (psi, links, *powers[:3]),
    )
    gathered = from_everyone(copies)
    four = call(
        functools.partial(finish_kernel, shape), "finish", 700 * sites, field,
        (psi, links, total, *sent[5:], *halo),
    )
    residual, coefficients = call(
        functools.partial(last_kernel, shape, entries), "last", 100 * sites,
        (
            jax.ShapeDtypeStruct((24 * t * z, lanes), jnp.float32),
            jax.ShapeDtypeStruct((3,), jnp.float32),
        ),
        (powers[0], powers[2], four, gathered), (vmem, smem),
    )
    return (residual.reshape(source.shape), coefficients)


class ChipShape(Shape):
    def __init__(self, t_extent, z_extent, lanes):
        super().__init__(t_extent, z_extent, lanes)
        self.parts = 2 * z_extent
        self.z_rows = 24 * t_extent
        self.t_rows = 12 * self.parts

    def block(self, k, part):
        first = (k * self.parts + part) * self.rows
        return pl.ds(first, self.rows)

    def edge(self, k, row):
        return pl.ds(k * self.parts * self.rows + row, self.parts, stride=self.rows)


class ChipLinks:
    def __init__(self, shape, ref, row=None):
        self.shape, self.ref, self.row = shape, ref, row

    def __getitem__(self, index):
        direction, row, col, part = index
        first = ((direction * 3 + row) * 3 + col) * 2
        if self.row is None:
            return tuple(self.ref[self.shape.block(first + n, part), :] for n in range(2))
        return tuple(self.ref[self.shape.edge(first + n, self.row), :] for n in range(2))


def components(spins):
    return [(s, c, part, (s * 3 + c) * 2 + part) for s in range(spins) for c in range(3) for part in range(2)]


def gathered_pairs(spins, value):
    out = {}
    for s in range(spins):
        for c in range(3):
            out[s, c] = tuple(value((s * 3 + c) * 2 + part) for part in range(2))
    return out


def chip_psi(shape, ref, part):
    return gathered_pairs(4, lambda k: ref[shape.block(k, part), :])


def chip_edge(shape, ref, row):
    return gathered_pairs(4, lambda k: ref[shape.edge(k, row), :])


def chip_messages(shape, psi_ref, links_ref, z_second, t_second, z_first, t_first):
    t, last = shape.t, shape.t - 1
    even = is_even("ta")
    minus = project(chip_edge(shape, psi_ref, 0), 3, -1)
    half = project(chip_edge(shape, psi_ref, last), 3, 1)
    carried = mul_link_dag(ChipLinks(shape, links_ref, last), 3, 0, half)
    for s, c, part, k in components(2):
        rows = pl.ds(k * shape.parts, shape.parts)
        up, down = carried[s, c][part], minus[s, c][part]
        t_first[rows, :] = either(even, up, down)
        t_second[rows, :] = either(even, down, up)
    even = is_even("gy")
    links = ChipLinks(shape, links_ref)
    for y_half in range(2):
        minus = project(chip_psi(shape, psi_ref, y_half), 2, -1)
        part_last = shape.parts - 2 + y_half
        half = project(chip_psi(shape, psi_ref, part_last), 2, 1)
        carried = mul_link_dag(links, 2, part_last, half)
        for s, c, part, k in components(2):
            rows = pl.ds((k * 2 + y_half) * t, t)
            up, down = carried[s, c][part][0:t], minus[s, c][part][0:t]
            z_first[rows, :] = either(even, up, down)
            z_second[rows, :] = either(even, down, up)


def chip_bring(shape, y_half, source_ref, links_in, psi_ref, links_ref, arrived):
    t, z_extent = shape.t, 2 * shape.z
    first_plane = lax.axis_index("gy") * shape.z
    last = lax.broadcasted_iota(jnp.int32, (t, shape.lanes), 0) == t - 1
    sign = jnp.where(lax.axis_index("ta") == lax.axis_size("ta") - 1, -1.0, 1.0)
    flip = jnp.where(last, sign, 1.0)

    def bring(in_ref, out_ref, k, z, factor=None):
        value = in_ref[pl.ds(k * t * z_extent + first_plane + z, t, stride=z_extent), :]
        if factor is not None:
            value = value * factor
        at = (k * shape.parts + 2 * z + y_half) * shape.rows
        out_ref[pl.ds(pl.multiple_of(at, 8), t), :] = value

    arrived(4)
    for z in range(shape.z):
        for k in range(24):
            bring(source_ref, psi_ref, k, z)
    for direction in (3, 2, 1, 0):
        arrived(direction)
        for z in range(shape.z):
            for k in range(18 * direction, 18 * direction + 18):
                bring(links_in, links_ref, k, z, flip if direction == 3 else None)


def chip_own_kernel(
    shape, source_hbm, links_hbm, psi_ref, links_ref, rest_ref, source_ref, links_in, semaphores
):
    part = 18 * shape.t * 2 * shape.z
    copies = {4: pltpu.make_async_copy(source_hbm, source_ref, semaphores.at[4])}
    for direction in (3, 2, 1, 0):
        rows = pl.ds(direction * part, part)
        copies[direction] = pltpu.make_async_copy(
            links_hbm.at[rows], links_in.at[rows], semaphores.at[direction]
        )
    for copy in copies.values():
        copy.start()
    if shape.rows != shape.t:
        links_ref[...] = jnp.zeros_like(links_ref)
        psi_ref[...] = jnp.zeros_like(psi_ref)
    chip_bring(
        shape, lax.axis_index("gy"), source_ref, links_in, psi_ref, links_ref,
        lambda n: copies[n].wait(),
    )
    t, z_extent = shape.t, 2 * shape.z
    first_plane = (1 - lax.axis_index("gy")) * shape.z
    if shape.rows != t:
        rest_ref[...] = jnp.zeros_like(rest_ref)
    for k in range(24):
        for z in range(shape.z):
            value = source_ref[pl.ds(k * t * z_extent + first_plane + z, t, stride=z_extent), :]
            rest_ref[pl.ds((k * shape.z + z) * shape.rows, t), :] = value


def chip_prep_kernel(
    shape, source_ref, links_in, psi_in, links_held, psi_ref, links_ref, *messages
):
    chip_bring(
        shape, 1 - lax.axis_index("gy"), source_ref, links_in, psi_ref, links_ref, lambda n: None
    )
    chip_messages(shape, psi_ref, links_ref, *messages)


def chip_inner_kernel(shape, psi_ref, links_ref, total_ref):
    links = ChipLinks(shape, links_ref)
    lane, row = shape.lane(), shape.row()
    x = lane % X
    lanes, rows, t = shape.lanes, shape.rows, shape.t
    at_end, at_start = x == X - 1, x == 0
    inside_ahead = row < t - 1
    inside_behind = jnp.logical_and(row > 0, row < t)

    def x_ahead(value):
        return jnp.where(
            at_end, pltpu.roll(value, X - 1, 1), pltpu.roll(value, lanes - 1, 1)
        )

    def x_behind(value):
        return jnp.where(at_start, pltpu.roll(value, lanes - X + 1, 1), pltpu.roll(value, 1, 1))

    def t_ahead(value):
        return jnp.where(inside_ahead, pltpu.roll(value, rows - 1, 0), 0.0)

    def t_behind(value):
        return jnp.where(inside_behind, pltpu.roll(value, 1, 0), 0.0)

    for z in range(shape.z):
        for part in (2 * z, 2 * z + 1):
            psi = chip_psi(shape, psi_ref, part)
            zero = jnp.zeros((rows, lanes), jnp.float32)
            total = {key: (zero, zero) for key in psi}
            half = mapped(x_ahead, project(psi, 0, -1))
            add_rebuilt(total, mul_link(links, 0, part, half), 0, -1)
            half = mapped(x_behind, mul_link_dag(links, 0, part, project(psi, 0, 1)))
            add_rebuilt(total, half, 0, 1)
            half = mapped(t_ahead, project(psi, 3, -1))
            add_rebuilt(total, mul_link(links, 3, part, half), 3, -1)
            half = mapped(t_behind, mul_link_dag(links, 3, part, project(psi, 3, 1)))
            add_rebuilt(total, half, 3, 1)
            if z + 1 < shape.z:
                half = project(chip_psi(shape, psi_ref, part + 2), 2, -1)
                add_rebuilt(total, mul_link(links, 2, part, half), 2, -1)
            if z > 0:
                half = project(chip_psi(shape, psi_ref, part - 2), 2, 1)
                add_rebuilt(total, mul_link_dag(links, 2, part - 2, half), 2, 1)
            for s, c, n, k in components(4):
                total_ref[shape.block(k, part), :] = total[s, c][n]
        pair = (2 * z, 2 * z + 1)
        minus, carried = [], []
        for part in pair:
            psi = chip_psi(shape, psi_ref, part)
            minus.append(mapped(lambda v: pltpu.roll(v, lanes - X, 1), project(psi, 1, -1)))
            half = mul_link_dag(links, 1, part, project(psi, 1, 1))
            carried.append(mapped(lambda v: pltpu.roll(v, X, 1), half))
        for own, part in enumerate(pair):
            total = chip_psi(shape, total_ref, part)
            half = mapped(
                lambda a, b: jnp.where(lane >= lanes - X, b, a), minus[own], minus[1 - own]
            )
            add_rebuilt(total, mul_link(links, 1, part, half), 1, -1)
            half = mapped(lambda a, b: jnp.where(lane < X, b, a), carried[own], carried[1 - own])
            add_rebuilt(total, half, 1, 1)
            for s, c, n, k in components(4):
                total_ref[shape.block(k, part), :] = total[s, c][n]


def chip_sort_faces(z_second, z_first, scratch):
    z_down, z_up = scratch
    z_even = is_even("gy")
    second = 0.0 if z_second is None else z_second[...]
    first = 0.0 if z_first is None else z_first[...]
    z_down[...] = either(z_even, first, second)
    z_up[...] = either(z_even, second, first)


def chip_add_z(shape, links, part, total, scratch):
    z_down, z_up = scratch
    t, rows, lanes, parts = shape.t, shape.rows, shape.lanes, shape.parts

    def plane(ref, y_half):
        def value(k):
            face = ref[pl.ds((k * 2 + y_half) * t, t), :]
            if rows != t:
                pad = jnp.zeros((rows - t, lanes), jnp.float32)
                face = jnp.concatenate([face, pad], axis=0)
            return face

        return gathered_pairs(2, value)

    if part >= parts - 2:
        half = mul_link(links, 2, part, plane(z_down, part - parts + 2))
        add_rebuilt(total, half, 2, -1)
    if part < 2:
        add_rebuilt(total, plane(z_up, part), 2, 1)


def chip_finish(
    shape, psi_ref, links_ref, total_ref, received, scratch, out_ref, face_ref=None
):
    z_second, t_first, z_first, t_second = received
    t_even = is_even("ta")
    t, lanes, parts = shape.t, shape.lanes, shape.parts
    chip_sort_faces(z_second, z_first, scratch)
    links = ChipLinks(shape, links_ref)

    for part in range(parts):
        total = chip_psi(shape, total_ref, part)
        chip_add_z(shape, links, part, total, scratch)
        for s, c, n, k in components(4):
            value = total[s, c][n]
            if face_ref is not None:
                value = value + face_ref[shape.block(k, part), :]
            value = psi_ref[shape.block(k, part), :] - hop_kappa * value
            out_ref[shape.block(k, part), :] = value if s < 2 else -value

    def t_half(from_even, from_odd):
        def value(k):
            at = pl.ds(k * parts, parts)
            return either(t_even, from_even[at, :], from_odd[at, :])

        return gathered_pairs(2, value)

    down = mul_link(ChipLinks(shape, links_ref, t - 1), 3, 0, t_half(t_first, t_second))
    up = t_half(t_second, t_first)
    zero = jnp.zeros((parts, lanes), jnp.float32)
    for half, parity, row in ((down, -1, t - 1), (up, 1, 0)):
        total = {(s, c): (zero, zero) for s in range(4) for c in range(3)}
        add_rebuilt(total, half, 3, parity)
        for s, c, n, k in components(4):
            at = shape.edge(k, row)
            value = hop_kappa * total[s, c][n]
            out_ref[at, :] = out_ref[at, :] - (value if s < 2 else -value)


def chip_mid_kernel(shape, hands_over, psi_ref, links_ref, total_ref, *refs):
    received, out_ref, messages, refs = refs[:4], refs[4], refs[5:9], refs[9:]
    chip_finish(shape, psi_ref, links_ref, total_ref, received, refs[-2:], out_ref)
    chip_messages(shape, out_ref, links_ref, *messages)
    if hands_over:
        hand_over(shape, out_ref, refs[0])


def chip_sums_kernel(
    shape, links_ref, z_first, start_ref, one_ref, two_ref, three_ref,
    face_ref, copies_ref, *scratch,
):
    class View:
        def __init__(self, ref):
            self.ref = ref

        def __getitem__(self, index):
            return self.ref[shape.block(*index), :]

    wide = ChipShape(shape.t, shape.z, shape.lanes)
    wide.z = shape.parts
    row = sums_row(wide, View(two_ref), View(start_ref), View(three_ref), View(one_ref))
    copies_ref[...] = jnp.broadcast_to(row[None], copies_ref.shape)
    chip_sort_faces(None, z_first, scratch)
    zero = jnp.zeros((shape.rows, shape.lanes), jnp.float32)
    for part in range(shape.parts):
        total = {(s, c): (zero, zero) for s in range(4) for c in range(3)}
        chip_add_z(shape, ChipLinks(shape, links_ref), part, total, scratch)
        for s, c, n, k in components(4):
            face_ref[shape.block(k, part), :] = total[s, c][n]


def chip_scalars_kernel(entries, gathered, factors_ref, coefficients):
    alpha_one, beta_one, alpha_two, scale, first_factor = scalars(gathered[:, 0, :], entries)
    lanes = factors_ref.shape[1]
    values = [alpha_one, alpha_two, scale, first_factor]
    values = [jnp.broadcast_to(value, (1, lanes)) for value in values]
    values.append(jnp.zeros((4, lanes), jnp.float32))
    factors_ref[...] = jnp.concatenate(values, axis=0)
    coefficients[0] = alpha_one[0, 0]
    coefficients[1] = beta_one[0, 0]
    coefficients[2] = alpha_two[0, 0]


def y_part(shape, k, z, y_half):
    return pl.ds(pl.multiple_of((k * shape.parts + 2 * z + y_half) * shape.rows, 8), shape.rows)


def rest_rows(shape, k, z):
    return pl.ds((k * shape.z + z) * shape.rows, shape.rows)


def hand_over(shape, ref, rest_ref):
    y_half = 1 - lax.axis_index("gy")
    for k in range(24):
        for z in range(shape.z):
            rest_ref[rest_rows(shape, k, z), :] = ref[y_part(shape, k, z, y_half), :]


def chip_finish_kernel(
    shape, psi_ref, links_ref, total_ref, face_ref, z_second, t_first, t_second,
    out_ref, rest_ref, *scratch,
):
    received = z_second, t_first, None, t_second
    chip_finish(shape, psi_ref, links_ref, total_ref, received, scratch, out_ref, face_ref)
    y_half = 1 - lax.axis_index("gy")
    for k in range(24):
        for z in range(shape.z):
            value = out_ref[y_part(shape, k, z, y_half), :]
            rest_ref[dense_rows(shape, k, z), :] = value[0 : shape.t]


def dense_rows(shape, k, z):
    return pl.ds((k * shape.z + z) * shape.t, shape.t)


def chip_last_kernel(
    shape, start_ref, two_ref, four_ref, start_rest, two_rest, four_rest, factors_ref, out_ref
):
    t, z_extent = shape.t, 2 * shape.z
    alpha_one, alpha_two, scale, first_factor = (
        jnp.broadcast_to(factors_ref[k : k + 1], (t, shape.lanes)) for k in range(4)
    )
    core = lax.axis_index("gy")

    def put(k, z, start, two, four):
        remain = two - alpha_one * start
        result = (four - alpha_one * two - alpha_two * remain) * scale - first_factor * start
        out_ref[pl.ds(k * t * z_extent + z, t, stride=z_extent), :] = result

    for k in range(24):
        for z in range(shape.z):
            rows = y_part(shape, k, z, core)
            put(k, core * shape.z + z, *(ref[rows, :][0:t] for ref in (start_ref, two_ref, four_ref)))
            rows = rest_rows(shape, k, z)
            other = [ref[rows, :][0:t] for ref in (start_rest, two_rest)]
            put(k, (1 - core) * shape.z + z, *other, four_rest[dense_rows(shape, k, z), :])


def chip_shards(source, gauge_links):
    devices_all = lax.axis_size("ta") * lax.axis_size("gz") * 2
    entries = float(source.size * devices_all)
    z_extent = source.shape[4]
    shape = ChipShape(source.shape[3], z_extent // 2, source.shape[5])
    t, rows, lanes = shape.t, shape.rows, shape.lanes
    vmem = pl.BlockSpec(memory_space=pltpu.VMEM)
    smem = pl.BlockSpec(memory_space=pltpu.SMEM)

    def held(*dims):
        return pltpu.VMEM(dims, jnp.float32)

    field = held(24 * shape.parts * rows, lanes)
    links_field = held(72 * shape.parts * rows, lanes)
    z_face, t_face = held(shape.z_rows, lanes), held(shape.t_rows, lanes)
    messages = (z_face, t_face, z_face, t_face)
    z_faces = (z_face, z_face)

    def call(kernel, name, flops, out_shape, operands, **options):
        in_spec = options.pop("in_spec", vmem)
        out_specs = options.pop("out_specs", jax.tree.map(lambda _: vmem, out_shape))
        return pl.pallas_call(
            kernel,
            name=name,
            out_shape=out_shape,
            in_specs=[in_spec] * len(operands),
            out_specs=out_specs,
            compiler_params=pltpu.CompilerParams(vmem_limit_bytes=8 << 20),
            cost_estimate=pl.CostEstimate(flops=flops, bytes_accessed=1 << 20, transcendentals=0),
            **options,
        )(*operands)

    def exchanged(sent):
        z_second, t_second, z_first, t_first = sent
        z_ring = ("gz", "gy")
        z_second = swap(z_second, z_ring, True)
        t_first = swap(t_first, "ta", False)
        z_first = swap(z_first, z_ring, False)
        t_second = swap(t_second, "ta", True)
        return z_second, t_first, z_first, t_second

    sites = t * z_extent * lanes
    rows_in = t * z_extent
    own = (source.reshape(24 * rows_in, lanes), gauge_links.reshape(72 * rows_in, lanes))
    other = tuple(swap(value, "gy", False) for value in own)
    rest = held(24 * shape.z * rows, lanes)
    psi, links, start_rest = call(
        functools.partial(chip_own_kernel, shape), "own", 200 * sites, (field, links_field, rest),
        [pltpu.with_memory_space_constraint(value, pltpu.HBM) for value in own],
        scratch_shapes=(
            held(24 * rows_in, lanes), held(72 * rows_in, lanes), pltpu.SemaphoreType.DMA((5,)),
        ),
        in_spec=pl.BlockSpec(memory_space=pltpu.HBM),
    )
    psi, links, *sent = call(
        functools.partial(chip_prep_kernel, shape), "prep", 400 * sites,
        (field, links_field, *messages), (*other, psi, links),
        input_output_aliases={2: 0, 3: 1},
    )
    powers = [psi]
    for step in range(3):
        halo = exchanged(sent)
        inner = functools.partial(chip_inner_kernel, shape)
        total = call(inner, "inner", 1000 * sites, field, (psi, links))
        hands_over = step == 1
        psi, *sent = call(
            functools.partial(chip_mid_kernel, shape, hands_over), "mid", 600 * sites,
            (field, *messages, rest) if hands_over else (field, *messages),
            (psi, links, total, *halo), scratch_shapes=z_faces,
        )
        powers.append(psi)
        if hands_over:
            two_rest = swap(sent.pop(), "gy", False)
    halo = exchanged(sent)
    face, copies = call(
        functools.partial(chip_sums_kernel, shape), "sums", 600 * sites,
        (field, held(devices_all, 1, lanes)), (links, halo[2], *powers), scratch_shapes=z_faces,
    )
    gathered = from_everyone(copies)
    total = call(inner, "inner", 1000 * sites, field, (psi, links))
    four, four_rest = call(
        functools.partial(chip_finish_kernel, shape), "finish", 400 * sites,
        (field, held(24 * shape.z * t, lanes)),
        (psi, links, total, face, halo[0], halo[1], halo[3]), scratch_shapes=z_faces,
    )
    four_rest = swap(four_rest, "gy", False)
    factors, coefficients = call(
        functools.partial(chip_scalars_kernel, entries), "scalars", 10**11,
        (held(8, lanes), jax.ShapeDtypeStruct((3,), jnp.float32)), (gathered,),
        out_specs=(vmem, smem),
    )
    residual = call(
        functools.partial(chip_last_kernel, shape), "last", 100 * sites,
        jax.ShapeDtypeStruct((24 * rows_in, lanes), jnp.float32),
        (powers[0], powers[2], four, start_rest, two_rest, four_rest, factors),
    )
    return (residual.reshape(source.shape), coefficients)


def solution(mesh):
    placed = (P(None, None, None, "ta", "gz", "gy"), P(None, None, None, None, "ta", "gz", "gy"))
    return jax.shard_map(
        chip_shards if mesh.shape["gy"] == 2 else shards,
        mesh=mesh,
        in_specs=placed,
        out_specs=(P(None, None, None, "ta", "gz", "gy"), P()),
        check_vma=False,
    )
```

```python
import functools
import math

import jax
import jax.numpy as jnp
from jax import lax
from jax.experimental import pallas as pl
from jax.experimental.pallas import tpu as pltpu
from jax.sharding import PartitionSpec as P

X = 32

hop_kappa = 0.19
epsilon = 1e-06
spin_table = (
    ((1, 0), (-1j, -1j)),
    ((1, 0), (-1, 1)),
    ((0, 1), (-1j, 1j)),
    ((0, 1), (1, 1)),
)
SPIN_COLOUR = [(spin, colour) for spin in range(2) for colour in range(3)]


def add_phased(left, phase, right):
    phase = complex(phase)
    if phase == 1:
        return (left[0] + right[0], left[1] + right[1])
    if phase == -1:
        return (left[0] - right[0], left[1] - right[1])
    if phase == 1j:
        return (left[0] - right[1], left[1] + right[0])
    return (left[0] + right[1], left[1] - right[0])


def project(psi, direction, parity):
    order, phases = spin_table[direction]
    return {
        (s, c): add_phased(psi[s, c], parity * phases[s], psi[2 + order[s], c])
        for s, c in SPIN_COLOUR
    }


def add_rebuilt(total, half, direction, parity):
    order, phases = spin_table[direction]
    for s, c in SPIN_COLOUR:
        total[s, c] = add_phased(total[s, c], 1, half[s, c])
        row = order[s]
        phase = parity * complex(phases[row]).conjugate()
        total[2 + s, c] = add_phased(total[2 + s, c], phase, half[row, c])


def mul_link(links, direction, z, half):
    out = {}
    for row in range(3):
        for s in range(2):
            real, imag = None, None
            for col in range(3):
                u_real, u_imag = links[direction, row, col, z]
                h_real, h_imag = half[s, col]
                term_real = u_real * h_real - u_imag * h_imag
                term_imag = u_real * h_imag + u_imag * h_real
                real = term_real if real is None else real + term_real
                imag = term_imag if imag is None else imag + term_imag
            out[s, row] = (real, imag)
    return out


def mul_link_dag(links, direction, z, half):
    out = {}
    for row in range(3):
        for s in range(2):
            real, imag = None, None
            for col in range(3):
                u_real, u_imag = links[direction, col, row, z]
                h_real, h_imag = half[s, col]
                term_real = u_real * h_real + u_imag * h_imag
                term_imag = u_real * h_imag - u_imag * h_real
                real = term_real if real is None else real + term_real
                imag = term_imag if imag is None else imag + term_imag
            out[s, row] = (real, imag)
    return out


def mapped(function, *halves):
    return {
        key: tuple(function(*(half[key][part] for half in halves)) for part in range(2))
        for key in SPIN_COLOUR
    }


class Links:
    def __init__(self, ref):
        self.ref = ref

    def __getitem__(self, index):
        direction, row, col, z = index
        first = ((direction * 3 + row) * 3 + col) * 2
        return (self.ref[first, z], self.ref[first + 1, z])


def load_psi(ref, z):
    return {
        (s, c): (ref[(s * 3 + c) * 2, z], ref[(s * 3 + c) * 2 + 1, z])
        for s in range(4)
        for c in range(3)
    }


def load_half(ref, z):
    return {
        (s, c): (ref[(s * 3 + c) * 2, z], ref[(s * 3 + c) * 2 + 1, z]) for s, c in SPIN_COLOUR
    }


def store_half(ref, z, half):
    for (s, c), pair in half.items():
        for part in range(2):
            ref[(s * 3 + c) * 2 + part, z] = pair[part]


class Shape:
    def __init__(self, t_extent, z_extent, lanes):
        self.t = t_extent
        self.z = z_extent
        self.rows = -(-t_extent // 8) * 8
        self.lanes = lanes

    def row(self):
        return lax.broadcasted_iota(jnp.int32, (self.rows, self.lanes), 0)

    def lane(self):
        return lax.broadcasted_iota(jnp.int32, (self.rows, self.lanes), 1)


def is_even(axis):
    return jnp.bitwise_and(lax.axis_index(axis), 1) == 0


def either(choice, first, second):
    return jnp.where(choice, first, second)


def emit_messages(shape, psi_ref, links, refs):
    z_second, t_second, z_first, t_first, y_msg, carried_y, carried_t = refs
    t_even, z_even = is_even("ta"), is_even("gz")
    lane = shape.lane()
    last_z, last_t = shape.z - 1, shape.t - 1
    for z in range(shape.z):
        psi = load_psi(psi_ref, z)
        minus = project(psi, 3, -1)
        carried = mul_link_dag(links, 3, z, project(psi, 3, 1))
        store_half(carried_t, z, carried)
        for s, c in SPIN_COLOUR:
            for part in range(2):
                at = ((s * 3 + c) * 2 + part) * shape.z + z
                down = minus[s, c][part][0:1]
                up = carried[s, c][part][last_t : last_t + 1]
                t_first[at : at + 1] = either(t_even, up, down)
                t_second[at : at + 1] = either(t_even, down, up)
        minus = project(psi, 1, -1)
        carried = mul_link_dag(links, 1, z, project(psi, 1, 1))
        store_half(carried_y, z, carried)
        store_half(
            y_msg,
            z,
            mapped(lambda low, high: jnp.where(lane < X, low, high), minus, carried),
        )
    minus = project(load_psi(psi_ref, 0), 2, -1)
    carried = mul_link_dag(links, 2, last_z, project(load_psi(psi_ref, last_z), 2, 1))
    for s, c in SPIN_COLOUR:
        for part in range(2):
            at = ((s * 3 + c) * 2 + part) * shape.t
            down, up = minus[s, c][part][0 : shape.t], carried[s, c][part][0 : shape.t]
            z_first[at : at + shape.t] = either(z_even, up, down)
            z_second[at : at + shape.t] = either(z_even, down, up)


def prep_kernel(shape, source_hbm, links_hbm, psi_ref, links_ref, *refs):
    messages, (source_ref, links_in, arrived) = refs[:-3], refs[-3:]
    t, z_extent = shape.t, shape.z
    part = 18 * t * z_extent
    copies = [pltpu.make_async_copy(source_hbm, source_ref, arrived.at[4])]
    for direction in (3, 2, 1, 0):
        rows = pl.ds(direction * part, part)
        copies.append(
            pltpu.make_async_copy(links_hbm.at[rows], links_in.at[rows], arrived.at[direction])
        )
    for copy in copies:
        copy.start()
    if shape.rows != t:
        links_ref[...] = jnp.zeros_like(links_ref)
        psi_ref[...] = jnp.zeros_like(psi_ref)
    last = lax.broadcasted_iota(jnp.int32, (t, shape.lanes), 0) == t - 1
    sign = jnp.where(lax.axis_index("ta") == lax.axis_size("ta") - 1, -1.0, 1.0)
    flip = jnp.where(last, sign, 1.0)
    copies[0].wait()
    for k in range(24):
        for z in range(z_extent):
            psi_ref[k, z, 0:t] = source_ref[pl.ds(k * t * z_extent + z, t, stride=z_extent), :]
    for direction in (3, 2, 1, 0):
        copies[4 - direction].wait()
        for k in range(18 * direction, 18 * direction + 18):
            for z in range(z_extent):
                value = links_in[pl.ds(k * t * z_extent + z, t, stride=z_extent), :]
                links_ref[k, z, 0:t] = value * flip if direction == 3 else value
    emit_messages(shape, psi_ref, Links(links_ref), messages)


def summed(shape, term):
    total = None
    for k in range(24):
        for z in range(shape.z):
            value = term(k, z)
            total = value if total is None else total + value
    return total


def over_lanes(total):
    return jnp.sum(jnp.sum(total, axis=0, keepdims=True), axis=1, keepdims=True)


def local_sums(shape, image, origin):
    square = summed(shape, lambda k, z: origin[k, z] * origin[k, z])
    mixed = over_lanes(summed(shape, lambda k, z: image[k, z] * origin[k, z]))
    whole = over_lanes(square)
    factor = jnp.where(whole > 0.0, mixed / jnp.where(whole > 0.0, whole, 1.0), 0.0)
    spread = jnp.broadcast_to(factor, (shape.rows, shape.lanes))
    rest_square, rest_mixed = None, None
    for k in range(24):
        for z in range(shape.z):
            start = origin[k, z]
            rest = image[k, z] - spread * start
            terms = rest * rest, rest * start
            if rest_square is None:
                rest_square, rest_mixed = terms
            else:
                rest_square, rest_mixed = rest_square + terms[0], rest_mixed + terms[1]
    return [factor, *(over_lanes(value) for value in (square, rest_square, rest_mixed))]


def inner_kernel(shape, psi_ref, links_ref, total_ref):
    links = Links(links_ref)
    x = shape.lane() % X
    lanes = shape.lanes
    at_end, at_start = x == X - 1, x == 0

    def ahead(value):
        return jnp.where(
            at_end, pltpu.roll(value, X - 1, 1), pltpu.roll(value, lanes - 1, 1)
        )

    def behind(value):
        return jnp.where(at_start, pltpu.roll(value, lanes - X + 1, 1), pltpu.roll(value, 1, 1))

    for z in range(shape.z):
        psi = load_psi(psi_ref, z)
        zero = jnp.zeros((shape.rows, lanes), jnp.float32)
        total = {key: (zero, zero) for key in psi}
        half = mapped(ahead, project(psi, 0, -1))
        add_rebuilt(total, mul_link(links, 0, z, half), 0, -1)
        half = mapped(behind, mul_link_dag(links, 0, z, project(psi, 0, 1)))
        add_rebuilt(total, half, 0, 1)
        if z + 1 < shape.z:
            half = project(load_psi(psi_ref, z + 1), 2, -1)
            add_rebuilt(total, mul_link(links, 2, z, half), 2, -1)
        if z > 0:
            half = project(load_psi(psi_ref, z - 1), 2, 1)
            add_rebuilt(total, mul_link_dag(links, 2, z - 1, half), 2, 1)
        for (s, c), pair in total.items():
            for part in range(2):
                total_ref[(s * 3 + c) * 2 + part, z] = pair[part]


def add_y_hops(shape, z, psi, total, links, carried_y, y_halo):
    lane, lanes = shape.lane(), shape.lanes
    received = load_half(y_halo, z)
    half = mapped(
        lambda own, other: pltpu.roll(jnp.where(lane < X, other, own), lanes - X, 1),
        project(psi, 1, -1),
        received,
    )
    add_rebuilt(total, mul_link(links, 1, z, half), 1, -1)
    half = mapped(
        lambda own, other: pltpu.roll(jnp.where(lane >= lanes - X, other, own), X, 1),
        load_half(carried_y, z),
        received,
    )
    add_rebuilt(total, half, 1, 1)


def finish_hops(
    shape, psi_ref, links, total_ref, carried_y, carried_t, halo, store
):
    z_second, t_second, z_first, t_first, y_msg = halo
    t_even, z_even = is_even("ta"), is_even("gz")
    row = shape.row()
    lanes, rows, t = shape.lanes, shape.rows, shape.t
    last_z = shape.z - 1

    for z in range(shape.z):
        psi = load_psi(psi_ref, z)
        total = load_psi(total_ref, z)

        def rim_rows(from_even, from_odd):
            half = {}
            for s, c in SPIN_COLOUR:
                ats = [((s * 3 + c) * 2 + part) * shape.z + z for part in range(2)]
                half[s, c] = tuple(
                    jnp.broadcast_to(
                        either(t_even, from_even[at : at + 1], from_odd[at : at + 1]),
                        (rows, lanes),
                    )
                    for at in ats
                )
            return half

        def rim_plane(from_even, from_odd):
            half = {}
            for s, c in SPIN_COLOUR:
                pair = []
                for part in range(2):
                    at = ((s * 3 + c) * 2 + part) * t
                    plane = either(z_even, from_even[at : at + t], from_odd[at : at + t])
                    if rows != t:
                        pad = jnp.zeros((rows - t, lanes), jnp.float32)
                        plane = jnp.concatenate([plane, pad], axis=0)
                    pair.append(plane)
                half[s, c] = tuple(pair)
            return half

        if y_msg is not None:
            add_y_hops(shape, z, psi, total, links, carried_y, y_msg)
        if z == last_z:
            add_rebuilt(total, mul_link(links, 2, z, rim_plane(z_first, z_second)), 2, -1)
        if z == 0:
            add_rebuilt(total, rim_plane(z_second, z_first), 2, 1)
        half = mapped(
            lambda own, other: jnp.where(row == t - 1, other, pltpu.roll(own, rows - 1, 0)),
            project(psi, 3, -1),
            rim_rows(t_first, t_second),
        )
        add_rebuilt(total, mul_link(links, 3, z, half), 3, -1)
        half = mapped(
            lambda own, other: jnp.where(row == 0, other, pltpu.roll(own, 1, 0)),
            load_half(carried_t, z),
            rim_rows(t_second, t_first),
        )
        add_rebuilt(total, half, 3, 1)
        for (s, c), pair in total.items():
            for part in range(2):
                value = psi[s, c][part] - hop_kappa * pair[part]
                value = value if s < 2 else -value
                if rows != t:
                    value = jnp.where(row < t, value, 0.0)
                store((s * 3 + c) * 2 + part, z, value)


def mid_kernel(shape, psi_ref, links_ref, total_ref, carried_y, carried_t, *refs):
    halo, out_ref, messages = refs[:5], refs[5], refs[6:]
    links = Links(links_ref)

    def store(k, z, value):
        out_ref[k, z] = value

    finish_hops(
        shape, psi_ref, links, total_ref, carried_y, carried_t, halo, store
    )
    emit_messages(shape, out_ref, links, messages)


def sums_row(shape, two, start, three, one):
    sums = local_sums(shape, two, start) + local_sums(shape, three, one)
    lane = lax.broadcasted_iota(jnp.int32, (1, shape.lanes), 1)
    row = jnp.zeros((1, shape.lanes), jnp.float32)
    for k, value in enumerate(sums):
        row = jnp.where(lane == k, value, row)
    return row


def inner_sums_kernel(
    shape, psi_ref, links_ref, start_ref, one_ref, two_ref, total_ref, copies_ref
):
    row = sums_row(shape, two_ref, start_ref, psi_ref, one_ref)
    copies_ref[...] = jnp.broadcast_to(row[None], copies_ref.shape)
    inner_kernel(shape, psi_ref, links_ref, total_ref)


def finish_kernel(shape, psi_ref, links_ref, total_ref, carried_y, carried_t, *refs):
    halo, out_ref = refs[:5], refs[5]

    def store(k, z, value):
        out_ref[k, z] = value

    finish_hops(
        shape, psi_ref, Links(links_ref), total_ref, carried_y, carried_t, halo, store
    )


def scalars(table, entries):
    columns = [table[:, k : k + 1] for k in range(8)]
    factor_two, start_square, two_square, two_mixed = columns[:4]
    factor_three, one_square, three_square, three_mixed = columns[4:]

    def over_devices(column):
        return jnp.sum(column, axis=0, keepdims=True)

    norm_square = over_devices(start_square) / entries + epsilon
    alpha_one = over_devices(one_square) / entries / norm_square
    gap = alpha_one - factor_two
    remain_square = over_devices(two_square - gap * (2.0 * two_mixed - gap * start_square)) / entries
    overlap = over_devices(two_mixed - gap * start_square) / entries
    gap = alpha_one - factor_three
    image_square = over_devices(three_square - gap * (2.0 * three_mixed - gap * one_square)) / entries
    norm = jnp.sqrt(norm_square)
    beta_one = jnp.sqrt(remain_square / norm_square + epsilon)
    overlap = overlap / (norm_square * beta_one)
    alpha_two = image_square / (norm_square * beta_one * beta_one) - beta_one * overlap
    scale = 1.0 / (norm * beta_one)
    return alpha_one, beta_one, alpha_two, scale, beta_one / norm


def last_kernel(
    shape, entries, start_ref, two_ref, four_ref, gathered, out_ref, coefficients
):
    alpha_one, beta_one, alpha_two, scale, first_factor = scalars(gathered[:, 0, :], entries)
    t, z_extent = shape.t, shape.z
    for k in range(24):
        for z in range(z_extent):
            two, start = two_ref[k, z], start_ref[k, z]
            remain = two - alpha_one * start
            result = (four_ref[k, z] - alpha_one * two - alpha_two * remain) * scale
            result = result - first_factor * start
            out_ref[pl.ds(k * t * z_extent + z, t, stride=z_extent), :] = result[0:t]
    coefficients[0] = alpha_one[0, 0]
    coefficients[1] = beta_one[0, 0]
    coefficients[2] = alpha_two[0, 0]


def swap(value, axis, second):
    count = math.prod(lax.axis_size(name) for name in (axis if isinstance(axis, tuple) else (axis,)))
    pairs = []
    for low in range(1 if second else 0, count, 2):
        high = (low + 1) % count
        pairs += [(low, high), (high, low)]
    return lax.ppermute(value, axis, pairs)


def exchange(messages, lanes):
    z_second, t_second, z_first, t_first, y_msg = messages
    halo = (
        swap(z_second, "gz", True),
        swap(t_second, "ta", True),
        swap(z_first, "gz", False),
        swap(t_first, "ta", False),
    )
    y_halo = swap(y_msg, "gy", False)
    if lax.axis_size("gy") > 2:
        even = lax.axis_index("gy") % 2 == 0
        lane = lax.broadcasted_iota(jnp.int32, y_msg.shape, y_msg.ndim - 1)
        y_halo = jnp.where((lane < lanes // 2) == even, y_halo, swap(y_msg, "gy", True))
    return (*halo, y_halo)


def from_everyone(copies):
    return lax.all_to_all(copies, ("ta", "gz", "gy"), split_axis=0, concat_axis=0, tiled=True)


def shards(source, gauge_links):
    devices_all = lax.axis_size("ta") * lax.axis_size("gz") * lax.axis_size("gy")
    entries = float(source.size * devices_all)
    shape = Shape(source.shape[3], source.shape[4], source.shape[5])
    t, z, rows, lanes = shape.t, shape.z, shape.rows, shape.lanes
    vmem = pl.BlockSpec(memory_space=pltpu.VMEM)
    smem = pl.BlockSpec(memory_space=pltpu.SMEM)

    def held(*dims):
        return pltpu.VMEM(dims, jnp.float32)

    field = held(24, z, rows, lanes)
    half = held(12, z, rows, lanes)
    z_face, t_face = held(12 * t, lanes), held(12 * z, lanes)
    messages = (z_face, t_face, z_face, t_face, half, half, half)

    def call(kernel, name, flops, out_shape, operands, out_specs=None, in_spec=vmem, scratch=()):
        return pl.pallas_call(
            kernel,
            name=name,
            out_shape=out_shape,
            in_specs=[in_spec] * len(operands),
            out_specs=out_specs or jax.tree.map(lambda _: vmem, out_shape),
            scratch_shapes=scratch,
            compiler_params=pltpu.CompilerParams(vmem_limit_bytes=8 << 20),
            cost_estimate=pl.CostEstimate(flops=flops, bytes_accessed=1 << 20, transcendentals=0),
        )(*operands)

    sites = t * z * lanes
    psi, links, *sent = call(
        functools.partial(prep_kernel, shape), "prep", 400 * sites,
        (field, held(72, z, rows, lanes), *messages),
        (
            pltpu.with_memory_space_constraint(source.reshape(24 * t * z, lanes), pltpu.HBM),
            pltpu.with_memory_space_constraint(gauge_links.reshape(72 * t * z, lanes), pltpu.HBM),
        ),
        in_spec=pl.BlockSpec(memory_space=pltpu.HBM),
        scratch=(
            held(24 * t * z, lanes), held(72 * t * z, lanes), pltpu.SemaphoreType.DMA((5,)),
        ),
    )
    powers = [psi]
    for step in range(3):
        halo = exchange(sent[:5], lanes)
        inner = functools.partial(inner_kernel, shape)
        total = call(inner, "inner", 700 * sites, field, (psi, links))
        psi, *sent = call(
            functools.partial(mid_kernel, shape), "mid", 1000 * sites,
            (field, *messages), (psi, links, total, *sent[5:], *halo),
        )
        powers.append(psi)
    halo = exchange(sent[:5], lanes)
    total, copies = call(
        functools.partial(inner_sums_kernel, shape), "inner_sums", 1100 * sites,
        (field, held(devices_all, 8, lanes)), (psi, links, *powers[:3]),
    )
    gathered = from_everyone(copies)
    four = call(
        functools.partial(finish_kernel, shape), "finish", 700 * sites, field,
        (psi, links, total, *sent[5:], *halo),
    )
    residual, coefficients = call(
        functools.partial(last_kernel, shape, entries), "last", 100 * sites,
        (
            jax.ShapeDtypeStruct((24 * t * z, lanes), jnp.float32),
            jax.ShapeDtypeStruct((3,), jnp.float32),
        ),
        (powers[0], powers[2], four, gathered), (vmem, smem),
    )
    return (residual.reshape(source.shape), coefficients)


class ChipShape(Shape):
    def __init__(self, t_extent, z_extent, lanes):
        super().__init__(t_extent, z_extent, lanes)
        self.parts = 2 * z_extent
        self.z_rows = 24 * t_extent
        self.t_rows = 12 * self.parts

    def block(self, k, part):
        first = (k * self.parts + part) * self.rows
        return pl.ds(first, self.rows)

    def edge(self, k, row):
        return pl.ds(k * self.parts * self.rows + row, self.parts, stride=self.rows)


class ChipLinks:
    def __init__(self, shape, ref, row=None):
        self.shape, self.ref, self.row = shape, ref, row

    def __getitem__(self, index):
        direction, row, col, part = index
        first = ((direction * 3 + row) * 3 + col) * 2
        if self.row is None:
            return tuple(self.ref[self.shape.block(first + n, part), :] for n in range(2))
        return tuple(self.ref[self.shape.edge(first + n, self.row), :] for n in range(2))


def components(spins):
    return [(s, c, part, (s * 3 + c) * 2 + part) for s in range(spins) for c in range(3) for part in range(2)]


def gathered_pairs(spins, value):
    out = {}
    for s in range(spins):
        for c in range(3):
            out[s, c] = tuple(value((s * 3 + c) * 2 + part) for part in range(2))
    return out


def chip_psi(shape, ref, part):
    return gathered_pairs(4, lambda k: ref[shape.block(k, part), :])


def chip_edge(shape, ref, row):
    return gathered_pairs(4, lambda k: ref[shape.edge(k, row), :])


def t_parity():
    return jnp.bitwise_and(lax.axis_index("ta") + lax.axis_index("gy"), 1) == 0


def chip_t_swap(value, second):
    count = lax.axis_size("ta")
    pairs = []
    for index in range(count):
        for core in range(2):
            ahead = (index % 2 == 0) != (second != (core == 1))
            partner = (index + (1 if ahead else -1)) % count
            pairs.append((index * 2 + core, partner * 2 + core))
    return lax.ppermute(value, ("ta", "gy"), pairs)


def chip_messages(shape, psi_ref, links_ref, z_second, t_second, z_first, t_first):
    t, last = shape.t, shape.t - 1
    even = t_parity()
    minus = project(chip_edge(shape, psi_ref, 0), 3, -1)
    half = project(chip_edge(shape, psi_ref, last), 3, 1)
    carried = mul_link_dag(ChipLinks(shape, links_ref, last), 3, 0, half)
    for s, c, part, k in components(2):
        rows = pl.ds(k * shape.parts, shape.parts)
        up, down = carried[s, c][part], minus[s, c][part]
        t_first[rows, :] = either(even, up, down)
        t_second[rows, :] = either(even, down, up)
    even = is_even("gy")
    links = ChipLinks(shape, links_ref)
    for y_half in range(2):
        minus = project(chip_psi(shape, psi_ref, y_half), 2, -1)
        part_last = shape.parts - 2 + y_half
        half = project(chip_psi(shape, psi_ref, part_last), 2, 1)
        carried = mul_link_dag(links, 2, part_last, half)
        for s, c, part, k in components(2):
            rows = pl.ds((k * 2 + y_half) * t, t)
            up, down = carried[s, c][part][0:t], minus[s, c][part][0:t]
            z_first[rows, :] = either(even, up, down)
            z_second[rows, :] = either(even, down, up)


def chip_bring(shape, y_half, source_ref, links_in, psi_ref, links_ref, arrived):
    t, z_extent = shape.t, 2 * shape.z
    first_plane = lax.axis_index("gy") * shape.z
    last = lax.broadcasted_iota(jnp.int32, (t, shape.lanes), 0) == t - 1
    sign = jnp.where(lax.axis_index("ta") == lax.axis_size("ta") - 1, -1.0, 1.0)
    flip = jnp.where(last, sign, 1.0)

    def bring(in_ref, out_ref, k, z, factor=None):
        value = in_ref[pl.ds(k * t * z_extent + first_plane + z, t, stride=z_extent), :]
        if factor is not None:
            value = value * factor
        at = (k * shape.parts + 2 * z + y_half) * shape.rows
        out_ref[pl.ds(pl.multiple_of(at, 8), t), :] = value

    arrived(4)
    for z in range(shape.z):
        for k in range(24):
            bring(source_ref, psi_ref, k, z)
    for direction in (3, 2, 1, 0):
        arrived(direction)
        for z in range(shape.z):
            for k in range(18 * direction, 18 * direction + 18):
                bring(links_in, links_ref, k, z, flip if direction == 3 else None)


def chip_own_kernel(
    shape, source_hbm, links_hbm, psi_ref, links_ref, rest_ref, source_ref, links_in, semaphores
):
    part = 18 * shape.t * 2 * shape.z
    copies = {4: pltpu.make_async_copy(source_hbm, source_ref, semaphores.at[4])}
    for direction in (3, 2, 1, 0):
        rows = pl.ds(direction * part, part)
        copies[direction] = pltpu.make_async_copy(
            links_hbm.at[rows], links_in.at[rows], semaphores.at[direction]
        )
    for copy in copies.values():
        copy.start()
    if shape.rows != shape.t:
        links_ref[...] = jnp.zeros_like(links_ref)
        psi_ref[...] = jnp.zeros_like(psi_ref)
    chip_bring(
        shape, lax.axis_index("gy"), source_ref, links_in, psi_ref, links_ref,
        lambda n: copies[n].wait(),
    )
    t, z_extent = shape.t, 2 * shape.z
    first_plane = (1 - lax.axis_index("gy")) * shape.z
    if shape.rows != t:
        rest_ref[...] = jnp.zeros_like(rest_ref)
    for k in range(24):
        for z in range(shape.z):
            value = source_ref[pl.ds(k * t * z_extent + first_plane + z, t, stride=z_extent), :]
            rest_ref[pl.ds((k * shape.z + z) * shape.rows, t), :] = value


def chip_prep_kernel(
    shape, source_ref, links_in, psi_in, links_held, psi_ref, links_ref, *messages
):
    chip_bring(
        shape, 1 - lax.axis_index("gy"), source_ref, links_in, psi_ref, links_ref, lambda n: None
    )
    chip_messages(shape, psi_ref, links_ref, *messages)


def chip_inner_kernel(shape, psi_ref, links_ref, total_ref):
    links = ChipLinks(shape, links_ref)
    lane, row = shape.lane(), shape.row()
    x = lane % X
    lanes, rows, t = shape.lanes, shape.rows, shape.t
    at_end, at_start = x == X - 1, x == 0
    inside_ahead = row < t - 1
    inside_behind = jnp.logical_and(row > 0, row < t)

    def x_ahead(value):
        return jnp.where(
            at_end, pltpu.roll(value, X - 1, 1), pltpu.roll(value, lanes - 1, 1)
        )

    def x_behind(value):
        return jnp.where(at_start, pltpu.roll(value, lanes - X + 1, 1), pltpu.roll(value, 1, 1))

    def t_ahead(value):
        return jnp.where(inside_ahead, pltpu.roll(value, rows - 1, 0), 0.0)

    def t_behind(value):
        return jnp.where(inside_behind, pltpu.roll(value, 1, 0), 0.0)

    for z in range(shape.z):
        for part in (2 * z, 2 * z + 1):
            psi = chip_psi(shape, psi_ref, part)
            zero = jnp.zeros((rows, lanes), jnp.float32)
            total = {key: (zero, zero) for key in psi}
            half = mapped(x_ahead, project(psi, 0, -1))
            add_rebuilt(total, mul_link(links, 0, part, half), 0, -1)
            half = mapped(x_behind, mul_link_dag(links, 0, part, project(psi, 0, 1)))
            add_rebuilt(total, half, 0, 1)
            half = mapped(t_ahead, project(psi, 3, -1))
            add_rebuilt(total, mul_link(links, 3, part, half), 3, -1)
            half = mapped(t_behind, mul_link_dag(links, 3, part, project(psi, 3, 1)))
            add_rebuilt(total, half, 3, 1)
            if z + 1 < shape.z:
                half = project(chip_psi(shape, psi_ref, part + 2), 2, -1)
                add_rebuilt(total, mul_link(links, 2, part, half), 2, -1)
            if z > 0:
                half = project(chip_psi(shape, psi_ref, part - 2), 2, 1)
                add_rebuilt(total, mul_link_dag(links, 2, part - 2, half), 2, 1)
            for s, c, n, k in components(4):
                total_ref[shape.block(k, part), :] = total[s, c][n]
        pair = (2 * z, 2 * z + 1)
        minus, carried = [], []
        for part in pair:
            psi = chip_psi(shape, psi_ref, part)
            minus.append(mapped(lambda v: pltpu.roll(v, lanes - X, 1), project(psi, 1, -1)))
            half = mul_link_dag(links, 1, part, project(psi, 1, 1))
            carried.append(mapped(lambda v: pltpu.roll(v, X, 1), half))
        for own, part in enumerate(pair):
            total = chip_psi(shape, total_ref, part)
            half = mapped(
                lambda a, b: jnp.where(lane >= lanes - X, b, a), minus[own], minus[1 - own]
            )
            add_rebuilt(total, mul_link(links, 1, part, half), 1, -1)
            half = mapped(lambda a, b: jnp.where(lane < X, b, a), carried[own], carried[1 - own])
            add_rebuilt(total, half, 1, 1)
            for s, c, n, k in components(4):
                total_ref[shape.block(k, part), :] = total[s, c][n]


def chip_sort_faces(z_second, z_first, scratch):
    z_down, z_up = scratch
    z_even = is_even("gy")
    second = 0.0 if z_second is None else z_second[...]
    first = 0.0 if z_first is None else z_first[...]
    z_down[...] = either(z_even, first, second)
    z_up[...] = either(z_even, second, first)


def chip_add_z(shape, links, part, total, scratch):
    z_down, z_up = scratch
    t, rows, lanes, parts = shape.t, shape.rows, shape.lanes, shape.parts

    def plane(ref, y_half):
        def value(k):
            face = ref[pl.ds((k * 2 + y_half) * t, t), :]
            if rows != t:
                pad = jnp.zeros((rows - t, lanes), jnp.float32)
                face = jnp.concatenate([face, pad], axis=0)
            return face

        return gathered_pairs(2, value)

    if part >= parts - 2:
        half = mul_link(links, 2, part, plane(z_down, part - parts + 2))
        add_rebuilt(total, half, 2, -1)
    if part < 2:
        add_rebuilt(total, plane(z_up, part), 2, 1)


def chip_finish(
    shape, psi_ref, links_ref, total_ref, received, scratch, out_ref, face_ref=None
):
    z_second, t_second, z_first, t_first = received
    t_even = t_parity()
    t, lanes, parts = shape.t, shape.lanes, shape.parts
    chip_sort_faces(z_second, z_first, scratch)
    links = ChipLinks(shape, links_ref)

    for part in range(parts):
        total = chip_psi(shape, total_ref, part)
        chip_add_z(shape, links, part, total, scratch)
        for s, c, n, k in components(4):
            value = total[s, c][n]
            if face_ref is not None:
                value = value + face_ref[shape.block(k, part), :]
            value = psi_ref[shape.block(k, part), :] - hop_kappa * value
            out_ref[shape.block(k, part), :] = value if s < 2 else -value

    def t_half(from_even, from_odd):
        def value(k):
            at = pl.ds(k * parts, parts)
            return either(t_even, from_even[at, :], from_odd[at, :])

        return gathered_pairs(2, value)

    down = mul_link(ChipLinks(shape, links_ref, t - 1), 3, 0, t_half(t_first, t_second))
    up = t_half(t_second, t_first)
    zero = jnp.zeros((parts, lanes), jnp.float32)
    for half, parity, row in ((down, -1, t - 1), (up, 1, 0)):
        total = {(s, c): (zero, zero) for s in range(4) for c in range(3)}
        add_rebuilt(total, half, 3, parity)
        for s, c, n, k in components(4):
            at = shape.edge(k, row)
            value = hop_kappa * total[s, c][n]
            out_ref[at, :] = out_ref[at, :] - (value if s < 2 else -value)


def chip_mid_kernel(shape, hands_over, psi_ref, links_ref, total_ref, *refs):
    received, out_ref, messages, refs = refs[:4], refs[4], refs[5:9], refs[9:]
    chip_finish(shape, psi_ref, links_ref, total_ref, received, refs[-2:], out_ref)
    chip_messages(shape, out_ref, links_ref, *messages)
    if hands_over:
        hand_over(shape, out_ref, refs[0])


def chip_sums_kernel(
    shape, links_ref, z_first, start_ref, one_ref, two_ref, three_ref,
    face_ref, copies_ref, *scratch,
):
    class View:
        def __init__(self, ref):
            self.ref = ref

        def __getitem__(self, index):
            return self.ref[shape.block(*index), :]

    wide = ChipShape(shape.t, shape.z, shape.lanes)
    wide.z = shape.parts
    row = sums_row(wide, View(two_ref), View(start_ref), View(three_ref), View(one_ref))
    copies_ref[...] = jnp.broadcast_to(row[None], copies_ref.shape)
    chip_sort_faces(None, z_first, scratch)
    zero = jnp.zeros((shape.rows, shape.lanes), jnp.float32)
    for part in range(shape.parts):
        total = {(s, c): (zero, zero) for s in range(4) for c in range(3)}
        chip_add_z(shape, ChipLinks(shape, links_ref), part, total, scratch)
        for s, c, n, k in components(4):
            face_ref[shape.block(k, part), :] = total[s, c][n]


def chip_scalars_kernel(entries, gathered, factors_ref, coefficients):
    alpha_one, beta_one, alpha_two, scale, first_factor = scalars(gathered[:, 0, :], entries)
    lanes = factors_ref.shape[1]
    values = [alpha_one, alpha_two, scale, first_factor]
    values = [jnp.broadcast_to(value, (1, lanes)) for value in values]
    values.append(jnp.zeros((4, lanes), jnp.float32))
    factors_ref[...] = jnp.concatenate(values, axis=0)
    coefficients[0] = alpha_one[0, 0]
    coefficients[1] = beta_one[0, 0]
    coefficients[2] = alpha_two[0, 0]


def y_part(shape, k, z, y_half):
    return pl.ds(pl.multiple_of((k * shape.parts + 2 * z + y_half) * shape.rows, 8), shape.rows)


def rest_rows(shape, k, z):
    return pl.ds((k * shape.z + z) * shape.rows, shape.rows)


def hand_over(shape, ref, rest_ref):
    y_half = 1 - lax.axis_index("gy")
    for k in range(24):
        for z in range(shape.z):
            rest_ref[rest_rows(shape, k, z), :] = ref[y_part(shape, k, z, y_half), :]


def chip_finish_kernel(
    shape, psi_ref, links_ref, total_ref, face_ref, z_second, t_second, t_first,
    out_ref, rest_ref, *scratch,
):
    received = z_second, t_second, None, t_first
    chip_finish(shape, psi_ref, links_ref, total_ref, received, scratch, out_ref, face_ref)
    y_half = 1 - lax.axis_index("gy")
    for k in range(24):
        for z in range(shape.z):
            value = out_ref[y_part(shape, k, z, y_half), :]
            rest_ref[dense_rows(shape, k, z), :] = value[0 : shape.t]


def dense_rows(shape, k, z):
    return pl.ds((k * shape.z + z) * shape.t, shape.t)


def chip_last_kernel(
    shape, start_ref, two_ref, four_ref, start_rest, two_rest, four_rest, factors_ref, out_ref
):
    t, z_extent = shape.t, 2 * shape.z
    alpha_one, alpha_two, scale, first_factor = (
        jnp.broadcast_to(factors_ref[k : k + 1], (t, shape.lanes)) for k in range(4)
    )
    core = lax.axis_index("gy")

    def put(k, z, start, two, four):
        remain = two - alpha_one * start
        result = (four - alpha_one * two - alpha_two * remain) * scale - first_factor * start
        out_ref[pl.ds(k * t * z_extent + z, t, stride=z_extent), :] = result

    for k in range(24):
        for z in range(shape.z):
            rows = y_part(shape, k, z, core)
            put(k, core * shape.z + z, *(ref[rows, :][0:t] for ref in (start_ref, two_ref, four_ref)))
            rows = rest_rows(shape, k, z)
            other = [ref[rows, :][0:t] for ref in (start_rest, two_rest)]
            put(k, (1 - core) * shape.z + z, *other, four_rest[dense_rows(shape, k, z), :])


def chip_shards(source, gauge_links):
    devices_all = lax.axis_size("ta") * lax.axis_size("gz") * 2
    entries = float(source.size * devices_all)
    z_extent = source.shape[4]
    shape = ChipShape(source.shape[3], z_extent // 2, source.shape[5])
    t, rows, lanes = shape.t, shape.rows, shape.lanes
    vmem = pl.BlockSpec(memory_space=pltpu.VMEM)
    smem = pl.BlockSpec(memory_space=pltpu.SMEM)

    def held(*dims):
        return pltpu.VMEM(dims, jnp.float32)

    field = held(24 * shape.parts * rows, lanes)
    links_field = held(72 * shape.parts * rows, lanes)
    z_face, t_face = held(shape.z_rows, lanes), held(shape.t_rows, lanes)
    messages = (z_face, t_face, z_face, t_face)
    z_faces = (z_face, z_face)

    def call(kernel, name, flops, out_shape, operands, **options):
        in_spec = options.pop("in_spec", vmem)
        out_specs = options.pop("out_specs", jax.tree.map(lambda _: vmem, out_shape))
        return pl.pallas_call(
            kernel,
            name=name,
            out_shape=out_shape,
            in_specs=[in_spec] * len(operands),
            out_specs=out_specs,
            compiler_params=pltpu.CompilerParams(vmem_limit_bytes=8 << 20),
            cost_estimate=pl.CostEstimate(flops=flops, bytes_accessed=1 << 20, transcendentals=0),
            **options,
        )(*operands)

    def exchanged(sent):
        z_second, t_second, z_first, t_first = sent
        z_ring = ("gz", "gy")
        return (
            swap(z_second, z_ring, True), chip_t_swap(t_second, True),
            swap(z_first, z_ring, False), chip_t_swap(t_first, False),
        )

    sites = t * z_extent * lanes
    rows_in = t * z_extent
    own = (source.reshape(24 * rows_in, lanes), gauge_links.reshape(72 * rows_in, lanes))
    other = tuple(swap(value, "gy", False) for value in own)
    rest = held(24 * shape.z * rows, lanes)
    psi, links, start_rest = call(
        functools.partial(chip_own_kernel, shape), "own", 200 * sites, (field, links_field, rest),
        [pltpu.with_memory_space_constraint(value, pltpu.HBM) for value in own],
        scratch_shapes=(
            held(24 * rows_in, lanes), held(72 * rows_in, lanes), pltpu.SemaphoreType.DMA((5,)),
        ),
        in_spec=pl.BlockSpec(memory_space=pltpu.HBM),
    )
    psi, links, *sent = call(
        functools.partial(chip_prep_kernel, shape), "prep", 400 * sites,
        (field, links_field, *messages), (*other, psi, links),
        input_output_aliases={2: 0, 3: 1},
    )
    powers = [psi]
    for step in range(3):
        halo = exchanged(sent)
        inner = functools.partial(chip_inner_kernel, shape)
        total = call(inner, "inner", 1000 * sites, field, (psi, links))
        hands_over = step == 1
        psi, *sent = call(
            functools.partial(chip_mid_kernel, shape, hands_over), "mid", 600 * sites,
            (field, *messages, rest) if hands_over else (field, *messages),
            (psi, links, total, *halo), scratch_shapes=z_faces,
        )
        powers.append(psi)
        if hands_over:
            two_rest = swap(sent.pop(), "gy", False)
    halo = exchanged(sent)
    face, copies = call(
        functools.partial(chip_sums_kernel, shape), "sums", 600 * sites,
        (field, held(devices_all, 1, lanes)), (links, halo[2], *powers), scratch_shapes=z_faces,
    )
    gathered = from_everyone(copies)
    total = call(inner, "inner", 1000 * sites, field, (psi, links))
    four, four_rest = call(
        functools.partial(chip_finish_kernel, shape), "finish", 400 * sites,
        (field, held(24 * shape.z * t, lanes)),
        (psi, links, total, face, halo[0], halo[1], halo[3]), scratch_shapes=z_faces,
    )
    four_rest = swap(four_rest, "gy", False)
    factors, coefficients = call(
        functools.partial(chip_scalars_kernel, entries), "scalars", 10**11,
        (held(8, lanes), jax.ShapeDtypeStruct((3,), jnp.float32)), (gathered,),
        out_specs=(vmem, smem),
    )
    residual = call(
        functools.partial(chip_last_kernel, shape), "last", 100 * sites,
        jax.ShapeDtypeStruct((24 * rows_in, lanes), jnp.float32),
        (powers[0], powers[2], four, start_rest, two_rest, four_rest, factors),
    )
    return (residual.reshape(source.shape), coefficients)


def solution(mesh):
    placed = (P(None, None, None, "ta", "gz", "gy"), P(None, None, None, None, "ta", "gz", "gy"))
    return jax.shard_map(
        chip_shards if mesh.shape["gy"] == 2 else shards,
        mesh=mesh,
        in_specs=placed,
        out_specs=(P(None, None, None, "ta", "gz", "gy"), P()),
        check_vma=False,
    )
```

```python
import functools
import math

import jax
import jax.numpy as jnp
from jax import lax
from jax.experimental import pallas as pl
from jax.experimental.pallas import tpu as pltpu
from jax.sharding import PartitionSpec as P

X = 32

hop_kappa = 0.19
epsilon = 1e-06
spin_table = (
    ((1, 0), (-1j, -1j)),
    ((1, 0), (-1, 1)),
    ((0, 1), (-1j, 1j)),
    ((0, 1), (1, 1)),
)
SPIN_COLOUR = [(spin, colour) for spin in range(2) for colour in range(3)]


def add_phased(left, phase, right):
    phase = complex(phase)
    if phase == 1:
        return (left[0] + right[0], left[1] + right[1])
    if phase == -1:
        return (left[0] - right[0], left[1] - right[1])
    if phase == 1j:
        return (left[0] - right[1], left[1] + right[0])
    return (left[0] + right[1], left[1] - right[0])


def project(psi, direction, parity):
    order, phases = spin_table[direction]
    return {
        (s, c): add_phased(psi[s, c], parity * phases[s], psi[2 + order[s], c])
        for s, c in SPIN_COLOUR
    }


def add_rebuilt(total, half, direction, parity):
    order, phases = spin_table[direction]
    for s, c in SPIN_COLOUR:
        total[s, c] = add_phased(total[s, c], 1, half[s, c])
        row = order[s]
        phase = parity * complex(phases[row]).conjugate()
        total[2 + s, c] = add_phased(total[2 + s, c], phase, half[row, c])


def mul_link(links, direction, z, half):
    out = {}
    for row in range(3):
        for s in range(2):
            real, imag = None, None
            for col in range(3):
                u_real, u_imag = links[direction, row, col, z]
                h_real, h_imag = half[s, col]
                term_real = u_real * h_real - u_imag * h_imag
                term_imag = u_real * h_imag + u_imag * h_real
                real = term_real if real is None else real + term_real
                imag = term_imag if imag is None else imag + term_imag
            out[s, row] = (real, imag)
    return out


def mul_link_dag(links, direction, z, half):
    out = {}
    for row in range(3):
        for s in range(2):
            real, imag = None, None
            for col in range(3):
                u_real, u_imag = links[direction, col, row, z]
                h_real, h_imag = half[s, col]
                term_real = u_real * h_real + u_imag * h_imag
                term_imag = u_real * h_imag - u_imag * h_real
                real = term_real if real is None else real + term_real
                imag = term_imag if imag is None else imag + term_imag
            out[s, row] = (real, imag)
    return out


def mapped(function, *halves):
    return {
        key: tuple(function(*(half[key][part] for half in halves)) for part in range(2))
        for key in SPIN_COLOUR
    }


class Links:
    def __init__(self, ref):
        self.ref = ref

    def __getitem__(self, index):
        direction, row, col, z = index
        first = ((direction * 3 + row) * 3 + col) * 2
        return (self.ref[first, z], self.ref[first + 1, z])


def load_psi(ref, z):
    return {
        (s, c): (ref[(s * 3 + c) * 2, z], ref[(s * 3 + c) * 2 + 1, z])
        for s in range(4)
        for c in range(3)
    }


def load_half(ref, z):
    return {
        (s, c): (ref[(s * 3 + c) * 2, z], ref[(s * 3 + c) * 2 + 1, z]) for s, c in SPIN_COLOUR
    }


def store_half(ref, z, half):
    for (s, c), pair in half.items():
        for part in range(2):
            ref[(s * 3 + c) * 2 + part, z] = pair[part]


class Shape:
    def __init__(self, t_extent, z_extent, lanes):
        self.t = t_extent
        self.z = z_extent
        self.rows = -(-t_extent // 8) * 8
        self.lanes = lanes

    def row(self):
        return lax.broadcasted_iota(jnp.int32, (self.rows, self.lanes), 0)

    def lane(self):
        return lax.broadcasted_iota(jnp.int32, (self.rows, self.lanes), 1)


def is_even(axis):
    return jnp.bitwise_and(lax.axis_index(axis), 1) == 0


def either(choice, first, second):
    return jnp.where(choice, first, second)


def emit_messages(shape, psi_ref, links, refs):
    z_second, t_second, z_first, t_first, y_msg, carried_y, carried_t = refs
    t_even, z_even = is_even("ta"), is_even("gz")
    lane = shape.lane()
    last_z, last_t = shape.z - 1, shape.t - 1
    for z in range(shape.z):
        psi = load_psi(psi_ref, z)
        minus = project(psi, 3, -1)
        carried = mul_link_dag(links, 3, z, project(psi, 3, 1))
        store_half(carried_t, z, carried)
        for s, c in SPIN_COLOUR:
            for part in range(2):
                at = ((s * 3 + c) * 2 + part) * shape.z + z
                down = minus[s, c][part][0:1]
                up = carried[s, c][part][last_t : last_t + 1]
                t_first[at : at + 1] = either(t_even, up, down)
                t_second[at : at + 1] = either(t_even, down, up)
        minus = project(psi, 1, -1)
        carried = mul_link_dag(links, 1, z, project(psi, 1, 1))
        store_half(carried_y, z, carried)
        store_half(
            y_msg,
            z,
            mapped(lambda low, high: jnp.where(lane < X, low, high), minus, carried),
        )
    minus = project(load_psi(psi_ref, 0), 2, -1)
    carried = mul_link_dag(links, 2, last_z, project(load_psi(psi_ref, last_z), 2, 1))
    for s, c in SPIN_COLOUR:
        for part in range(2):
            at = ((s * 3 + c) * 2 + part) * shape.t
            down, up = minus[s, c][part][0 : shape.t], carried[s, c][part][0 : shape.t]
            z_first[at : at + shape.t] = either(z_even, up, down)
            z_second[at : at + shape.t] = either(z_even, down, up)


def prep_kernel(shape, source_hbm, links_hbm, psi_ref, links_ref, *refs):
    messages, (source_ref, links_in, arrived) = refs[:-3], refs[-3:]
    t, z_extent = shape.t, shape.z
    part = 18 * t * z_extent
    copies = [pltpu.make_async_copy(source_hbm, source_ref, arrived.at[4])]
    for direction in (3, 2, 1, 0):
        rows = pl.ds(direction * part, part)
        copies.append(
            pltpu.make_async_copy(links_hbm.at[rows], links_in.at[rows], arrived.at[direction])
        )
    for copy in copies:
        copy.start()
    if shape.rows != t:
        links_ref[...] = jnp.zeros_like(links_ref)
        psi_ref[...] = jnp.zeros_like(psi_ref)
    last = lax.broadcasted_iota(jnp.int32, (t, shape.lanes), 0) == t - 1
    sign = jnp.where(lax.axis_index("ta") == lax.axis_size("ta") - 1, -1.0, 1.0)
    flip = jnp.where(last, sign, 1.0)
    copies[0].wait()
    for k in range(24):
        for z in range(z_extent):
            psi_ref[k, z, 0:t] = source_ref[pl.ds(k * t * z_extent + z, t, stride=z_extent), :]
    for direction in (3, 2, 1, 0):
        copies[4 - direction].wait()
        for k in range(18 * direction, 18 * direction + 18):
            for z in range(z_extent):
                value = links_in[pl.ds(k * t * z_extent + z, t, stride=z_extent), :]
                links_ref[k, z, 0:t] = value * flip if direction == 3 else value
    emit_messages(shape, psi_ref, Links(links_ref), messages)


def summed(shape, term):
    total = None
    for k in range(24):
        for z in range(shape.z):
            value = term(k, z)
            total = value if total is None else total + value
    return total


def over_lanes(total):
    return jnp.sum(jnp.sum(total, axis=0, keepdims=True), axis=1, keepdims=True)


def local_sums(shape, image, origin):
    square = summed(shape, lambda k, z: origin[k, z] * origin[k, z])
    mixed = over_lanes(summed(shape, lambda k, z: image[k, z] * origin[k, z]))
    whole = over_lanes(square)
    factor = jnp.where(whole > 0.0, mixed / jnp.where(whole > 0.0, whole, 1.0), 0.0)
    spread = jnp.broadcast_to(factor, (shape.rows, shape.lanes))
    rest_square, rest_mixed = None, None
    for k in range(24):
        for z in range(shape.z):
            start = origin[k, z]
            rest = image[k, z] - spread * start
            terms = rest * rest, rest * start
            if rest_square is None:
                rest_square, rest_mixed = terms
            else:
                rest_square, rest_mixed = rest_square + terms[0], rest_mixed + terms[1]
    return [factor, *(over_lanes(value) for value in (square, rest_square, rest_mixed))]


def inner_kernel(shape, psi_ref, links_ref, total_ref):
    links = Links(links_ref)
    x = shape.lane() % X
    lanes = shape.lanes
    at_end, at_start = x == X - 1, x == 0

    def ahead(value):
        return jnp.where(
            at_end, pltpu.roll(value, X - 1, 1), pltpu.roll(value, lanes - 1, 1)
        )

    def behind(value):
        return jnp.where(at_start, pltpu.roll(value, lanes - X + 1, 1), pltpu.roll(value, 1, 1))

    for z in range(shape.z):
        psi = load_psi(psi_ref, z)
        zero = jnp.zeros((shape.rows, lanes), jnp.float32)
        total = {key: (zero, zero) for key in psi}
        half = mapped(ahead, project(psi, 0, -1))
        add_rebuilt(total, mul_link(links, 0, z, half), 0, -1)
        half = mapped(behind, mul_link_dag(links, 0, z, project(psi, 0, 1)))
        add_rebuilt(total, half, 0, 1)
        if z + 1 < shape.z:
            half = project(load_psi(psi_ref, z + 1), 2, -1)
            add_rebuilt(total, mul_link(links, 2, z, half), 2, -1)
        if z > 0:
            half = project(load_psi(psi_ref, z - 1), 2, 1)
            add_rebuilt(total, mul_link_dag(links, 2, z - 1, half), 2, 1)
        for (s, c), pair in total.items():
            for part in range(2):
                total_ref[(s * 3 + c) * 2 + part, z] = pair[part]


def add_y_hops(shape, z, psi, total, links, carried_y, y_halo):
    lane, lanes = shape.lane(), shape.lanes
    received = load_half(y_halo, z)
    half = mapped(
        lambda own, other: pltpu.roll(jnp.where(lane < X, other, own), lanes - X, 1),
        project(psi, 1, -1),
        received,
    )
    add_rebuilt(total, mul_link(links, 1, z, half), 1, -1)
    half = mapped(
        lambda own, other: pltpu.roll(jnp.where(lane >= lanes - X, other, own), X, 1),
        load_half(carried_y, z),
        received,
    )
    add_rebuilt(total, half, 1, 1)


def finish_hops(
    shape, psi_ref, links, total_ref, carried_y, carried_t, halo, store
):
    z_second, t_second, z_first, t_first, y_msg = halo
    t_even, z_even = is_even("ta"), is_even("gz")
    row = shape.row()
    lanes, rows, t = shape.lanes, shape.rows, shape.t
    last_z = shape.z - 1

    for z in range(shape.z):
        psi = load_psi(psi_ref, z)
        total = load_psi(total_ref, z)

        def rim_rows(from_even, from_odd):
            half = {}
            for s, c in SPIN_COLOUR:
                ats = [((s * 3 + c) * 2 + part) * shape.z + z for part in range(2)]
                half[s, c] = tuple(
                    jnp.broadcast_to(
                        either(t_even, from_even[at : at + 1], from_odd[at : at + 1]),
                        (rows, lanes),
                    )
                    for at in ats
                )
            return half

        def rim_plane(from_even, from_odd):
            half = {}
            for s, c in SPIN_COLOUR:
                pair = []
                for part in range(2):
                    at = ((s * 3 + c) * 2 + part) * t
                    plane = either(z_even, from_even[at : at + t], from_odd[at : at + t])
                    if rows != t:
                        pad = jnp.zeros((rows - t, lanes), jnp.float32)
                        plane = jnp.concatenate([plane, pad], axis=0)
                    pair.append(plane)
                half[s, c] = tuple(pair)
            return half

        if y_msg is not None:
            add_y_hops(shape, z, psi, total, links, carried_y, y_msg)
        if z == last_z:
            add_rebuilt(total, mul_link(links, 2, z, rim_plane(z_first, z_second)), 2, -1)
        if z == 0:
            add_rebuilt(total, rim_plane(z_second, z_first), 2, 1)
        half = mapped(
            lambda own, other: jnp.where(row == t - 1, other, pltpu.roll(own, rows - 1, 0)),
            project(psi, 3, -1),
            rim_rows(t_first, t_second),
        )
        add_rebuilt(total, mul_link(links, 3, z, half), 3, -1)
        half = mapped(
            lambda own, other: jnp.where(row == 0, other, pltpu.roll(own, 1, 0)),
            load_half(carried_t, z),
            rim_rows(t_second, t_first),
        )
        add_rebuilt(total, half, 3, 1)
        for (s, c), pair in total.items():
            for part in range(2):
                value = psi[s, c][part] - hop_kappa * pair[part]
                value = value if s < 2 else -value
                if rows != t:
                    value = jnp.where(row < t, value, 0.0)
                store((s * 3 + c) * 2 + part, z, value)


def mid_kernel(shape, psi_ref, links_ref, total_ref, carried_y, carried_t, *refs):
    halo, out_ref, messages = refs[:5], refs[5], refs[6:]
    links = Links(links_ref)

    def store(k, z, value):
        out_ref[k, z] = value

    finish_hops(
        shape, psi_ref, links, total_ref, carried_y, carried_t, halo, store
    )
    emit_messages(shape, out_ref, links, messages)


def sums_row(shape, two, start, three, one):
    sums = local_sums(shape, two, start) + local_sums(shape, three, one)
    lane = lax.broadcasted_iota(jnp.int32, (1, shape.lanes), 1)
    row = jnp.zeros((1, shape.lanes), jnp.float32)
    for k, value in enumerate(sums):
        row = jnp.where(lane == k, value, row)
    return row


def inner_sums_kernel(
    shape, psi_ref, links_ref, start_ref, one_ref, two_ref, total_ref, copies_ref
):
    row = sums_row(shape, two_ref, start_ref, psi_ref, one_ref)
    copies_ref[...] = jnp.broadcast_to(row[None], copies_ref.shape)
    inner_kernel(shape, psi_ref, links_ref, total_ref)


def finish_kernel(shape, psi_ref, links_ref, total_ref, carried_y, carried_t, *refs):
    halo, out_ref = refs[:5], refs[5]

    def store(k, z, value):
        out_ref[k, z] = value

    finish_hops(
        shape, psi_ref, Links(links_ref), total_ref, carried_y, carried_t, halo, store
    )


def scalars(table, entries):
    columns = [table[:, k : k + 1] for k in range(8)]
    factor_two, start_square, two_square, two_mixed = columns[:4]
    factor_three, one_square, three_square, three_mixed = columns[4:]

    def over_devices(column):
        return jnp.sum(column, axis=0, keepdims=True)

    norm_square = over_devices(start_square) / entries + epsilon
    alpha_one = over_devices(one_square) / entries / norm_square
    gap = alpha_one - factor_two
    remain_square = over_devices(two_square - gap * (2.0 * two_mixed - gap * start_square)) / entries
    overlap = over_devices(two_mixed - gap * start_square) / entries
    gap = alpha_one - factor_three
    image_square = over_devices(three_square - gap * (2.0 * three_mixed - gap * one_square)) / entries
    norm = jnp.sqrt(norm_square)
    beta_one = jnp.sqrt(remain_square / norm_square + epsilon)
    overlap = overlap / (norm_square * beta_one)
    alpha_two = image_square / (norm_square * beta_one * beta_one) - beta_one * overlap
    scale = 1.0 / (norm * beta_one)
    return alpha_one, beta_one, alpha_two, scale, beta_one / norm


def last_kernel(
    shape, entries, start_ref, two_ref, four_ref, gathered, out_ref, coefficients
):
    alpha_one, beta_one, alpha_two, scale, first_factor = scalars(gathered[:, 0, :], entries)
    t, z_extent = shape.t, shape.z
    for k in range(24):
        for z in range(z_extent):
            two, start = two_ref[k, z], start_ref[k, z]
            remain = two - alpha_one * start
            result = (four_ref[k, z] - alpha_one * two - alpha_two * remain) * scale
            result = result - first_factor * start
            out_ref[pl.ds(k * t * z_extent + z, t, stride=z_extent), :] = result[0:t]
    coefficients[0] = alpha_one[0, 0]
    coefficients[1] = beta_one[0, 0]
    coefficients[2] = alpha_two[0, 0]


def swap(value, axis, second):
    count = math.prod(lax.axis_size(name) for name in (axis if isinstance(axis, tuple) else (axis,)))
    pairs = []
    for low in range(1 if second else 0, count, 2):
        high = (low + 1) % count
        pairs += [(low, high), (high, low)]
    return lax.ppermute(value, axis, pairs)


def exchange(messages, lanes):
    z_second, t_second, z_first, t_first, y_msg = messages
    halo = (
        swap(z_second, "gz", True),
        swap(t_second, "ta", True),
        swap(z_first, "gz", False),
        swap(t_first, "ta", False),
    )
    y_halo = swap(y_msg, "gy", False)
    if lax.axis_size("gy") > 2:
        even = lax.axis_index("gy") % 2 == 0
        lane = lax.broadcasted_iota(jnp.int32, y_msg.shape, y_msg.ndim - 1)
        y_halo = jnp.where((lane < lanes // 2) == even, y_halo, swap(y_msg, "gy", True))
    return (*halo, y_halo)


def from_everyone(copies):
    return lax.all_to_all(copies, ("ta", "gz", "gy"), split_axis=0, concat_axis=0, tiled=True)


def shards(source, gauge_links):
    devices_all = lax.axis_size("ta") * lax.axis_size("gz") * lax.axis_size("gy")
    entries = float(source.size * devices_all)
    shape = Shape(source.shape[3], source.shape[4], source.shape[5])
    t, z, rows, lanes = shape.t, shape.z, shape.rows, shape.lanes
    vmem = pl.BlockSpec(memory_space=pltpu.VMEM)
    smem = pl.BlockSpec(memory_space=pltpu.SMEM)

    def held(*dims):
        return pltpu.VMEM(dims, jnp.float32)

    field = held(24, z, rows, lanes)
    half = held(12, z, rows, lanes)
    z_face, t_face = held(12 * t, lanes), held(12 * z, lanes)
    messages = (z_face, t_face, z_face, t_face, half, half, half)

    def call(kernel, name, flops, out_shape, operands, out_specs=None, in_spec=vmem, scratch=()):
        return pl.pallas_call(
            kernel,
            name=name,
            out_shape=out_shape,
            in_specs=[in_spec] * len(operands),
            out_specs=out_specs or jax.tree.map(lambda _: vmem, out_shape),
            scratch_shapes=scratch,
            compiler_params=pltpu.CompilerParams(vmem_limit_bytes=8 << 20),
            cost_estimate=pl.CostEstimate(flops=flops, bytes_accessed=1 << 20, transcendentals=0),
        )(*operands)

    sites = t * z * lanes
    psi, links, *sent = call(
        functools.partial(prep_kernel, shape), "prep", 400 * sites,
        (field, held(72, z, rows, lanes), *messages),
        (
            pltpu.with_memory_space_constraint(source.reshape(24 * t * z, lanes), pltpu.HBM),
            pltpu.with_memory_space_constraint(gauge_links.reshape(72 * t * z, lanes), pltpu.HBM),
        ),
        in_spec=pl.BlockSpec(memory_space=pltpu.HBM),
        scratch=(
            held(24 * t * z, lanes), held(72 * t * z, lanes), pltpu.SemaphoreType.DMA((5,)),
        ),
    )
    powers = [psi]
    for step in range(3):
        halo = exchange(sent[:5], lanes)
        inner = functools.partial(inner_kernel, shape)
        total = call(inner, "inner", 700 * sites, field, (psi, links))
        psi, *sent = call(
            functools.partial(mid_kernel, shape), "mid", 1000 * sites,
            (field, *messages), (psi, links, total, *sent[5:], *halo),
        )
        powers.append(psi)
    halo = exchange(sent[:5], lanes)
    total, copies = call(
        functools.partial(inner_sums_kernel, shape), "inner_sums", 1100 * sites,
        (field, held(devices_all, 8, lanes)), (psi, links, *powers[:3]),
    )
    gathered = from_everyone(copies)
    four = call(
        functools.partial(finish_kernel, shape), "finish", 700 * sites, field,
        (psi, links, total, *sent[5:], *halo),
    )
    residual, coefficients = call(
        functools.partial(last_kernel, shape, entries), "last", 100 * sites,
        (
            jax.ShapeDtypeStruct((24 * t * z, lanes), jnp.float32),
            jax.ShapeDtypeStruct((3,), jnp.float32),
        ),
        (powers[0], powers[2], four, gathered), (vmem, smem),
    )
    return (residual.reshape(source.shape), coefficients)


class ChipShape(Shape):
    def __init__(self, t_extent, z_extent, lanes):
        super().__init__(t_extent, z_extent, lanes)
        self.parts = 2 * z_extent
        self.z_rows = 24 * t_extent
        self.t_rows = 12 * self.parts

    def block(self, k, part):
        first = (k * self.parts + part) * self.rows
        return pl.ds(first, self.rows)

    def edge(self, k, row):
        return pl.ds(k * self.parts * self.rows + row, self.parts, stride=self.rows)


class ChipLinks:
    def __init__(self, shape, ref, row=None):
        self.shape, self.ref, self.row = shape, ref, row

    def __getitem__(self, index):
        direction, row, col, part = index
        first = ((direction * 3 + row) * 3 + col) * 2
        if self.row is None:
            return tuple(self.ref[self.shape.block(first + n, part), :] for n in range(2))
        return tuple(self.ref[self.shape.edge(first + n, self.row), :] for n in range(2))


def components(spins):
    return [(s, c, part, (s * 3 + c) * 2 + part) for s in range(spins) for c in range(3) for part in range(2)]


def gathered_pairs(spins, value):
    out = {}
    for s in range(spins):
        for c in range(3):
            out[s, c] = tuple(value((s * 3 + c) * 2 + part) for part in range(2))
    return out


def chip_psi(shape, ref, part):
    return gathered_pairs(4, lambda k: ref[shape.block(k, part), :])


def chip_edge(shape, ref, row):
    return gathered_pairs(4, lambda k: ref[shape.edge(k, row), :])


def chip_messages(shape, psi_ref, links_ref, z_second, t_second, z_first, t_first):
    t, last = shape.t, shape.t - 1
    even = is_even("ta")
    minus = project(chip_edge(shape, psi_ref, 0), 3, -1)
    half = project(chip_edge(shape, psi_ref, last), 3, 1)
    carried = mul_link_dag(ChipLinks(shape, links_ref, last), 3, 0, half)
    for s, c, part, k in components(2):
        rows = pl.ds(k * shape.parts, shape.parts)
        up, down = carried[s, c][part], minus[s, c][part]
        t_first[rows, :] = either(even, up, down)
        t_second[rows, :] = either(even, down, up)
    even = is_even("gy")
    links = ChipLinks(shape, links_ref)
    for y_half in range(2):
        minus = project(chip_psi(shape, psi_ref, y_half), 2, -1)
        part_last = shape.parts - 2 + y_half
        half = project(chip_psi(shape, psi_ref, part_last), 2, 1)
        carried = mul_link_dag(links, 2, part_last, half)
        for s, c, part, k in components(2):
            rows = pl.ds((k * 2 + y_half) * t, t)
            up, down = carried[s, c][part][0:t], minus[s, c][part][0:t]
            z_first[rows, :] = either(even, up, down)
            z_second[rows, :] = either(even, down, up)


def both_planes(shape, ref, k, z):
    t, z_extent = shape.t, 2 * shape.z
    first = k * t * z_extent + z
    return [ref[pl.ds(first + n * shape.z, t, stride=z_extent), :] for n in range(2)]


def chip_bring(shape, y_half, source_ref, links_in, psi_ref, links_ref, arrived):
    t = shape.t
    last = lax.broadcasted_iota(jnp.int32, (t, shape.lanes), 0) == t - 1
    sign = jnp.where(lax.axis_index("ta") == lax.axis_size("ta") - 1, -1.0, 1.0)
    flip = jnp.where(last, sign, 1.0)

    def bring(in_ref, out_ref, k, z, factor=None):
        value = either(is_even("gy"), *both_planes(shape, in_ref, k, z))
        if factor is not None:
            value = value * factor
        at = (k * shape.parts + 2 * z + y_half) * shape.rows
        out_ref[pl.ds(pl.multiple_of(at, 8), t), :] = value

    arrived(4)
    for z in range(shape.z):
        for k in range(24):
            bring(source_ref, psi_ref, k, z)
    for direction in (3, 2, 1, 0):
        arrived(direction)
        for z in range(shape.z):
            for k in range(18 * direction, 18 * direction + 18):
                bring(links_in, links_ref, k, z, flip if direction == 3 else None)


def chip_own_kernel(
    shape, source_hbm, links_hbm, psi_ref, links_ref, rest_ref, source_ref, links_in, semaphores
):
    part = 18 * shape.t * 2 * shape.z
    copies = {4: pltpu.make_async_copy(source_hbm, source_ref, semaphores.at[4])}
    for direction in (3, 2, 1, 0):
        rows = pl.ds(direction * part, part)
        copies[direction] = pltpu.make_async_copy(
            links_hbm.at[rows], links_in.at[rows], semaphores.at[direction]
        )
    for copy in copies.values():
        copy.start()
    if shape.rows != shape.t:
        links_ref[...] = jnp.zeros_like(links_ref)
        psi_ref[...] = jnp.zeros_like(psi_ref)
    chip_bring(
        shape, lax.axis_index("gy"), source_ref, links_in, psi_ref, links_ref,
        lambda n: copies[n].wait(),
    )
    if shape.rows != shape.t:
        rest_ref[...] = jnp.zeros_like(rest_ref)
    for k in range(24):
        for z in range(shape.z):
            lower, upper = both_planes(shape, source_ref, k, z)
            at = pl.ds((k * shape.z + z) * shape.rows, shape.t)
            rest_ref[at, :] = either(is_even("gy"), upper, lower)


def chip_prep_kernel(
    shape, source_ref, links_in, psi_in, links_held, psi_ref, links_ref, *messages
):
    chip_bring(
        shape, 1 - lax.axis_index("gy"), source_ref, links_in, psi_ref, links_ref, lambda n: None
    )
    chip_messages(shape, psi_ref, links_ref, *messages)


def chip_inner_kernel(shape, psi_ref, links_ref, total_ref):
    links = ChipLinks(shape, links_ref)
    lane, row = shape.lane(), shape.row()
    x = lane % X
    lanes, rows, t = shape.lanes, shape.rows, shape.t
    at_end, at_start = x == X - 1, x == 0
    inside_ahead = row < t - 1
    inside_behind = jnp.logical_and(row > 0, row < t)

    def x_ahead(value):
        return jnp.where(
            at_end, pltpu.roll(value, X - 1, 1), pltpu.roll(value, lanes - 1, 1)
        )

    def x_behind(value):
        return jnp.where(at_start, pltpu.roll(value, lanes - X + 1, 1), pltpu.roll(value, 1, 1))

    def t_ahead(value):
        return jnp.where(inside_ahead, pltpu.roll(value, rows - 1, 0), 0.0)

    def t_behind(value):
        return jnp.where(inside_behind, pltpu.roll(value, 1, 0), 0.0)

    for z in range(shape.z):
        for part in (2 * z, 2 * z + 1):
            psi = chip_psi(shape, psi_ref, part)
            zero = jnp.zeros((rows, lanes), jnp.float32)
            total = {key: (zero, zero) for key in psi}
            half = mapped(x_ahead, project(psi, 0, -1))
            add_rebuilt(total, mul_link(links, 0, part, half), 0, -1)
            half = mapped(x_behind, mul_link_dag(links, 0, part, project(psi, 0, 1)))
            add_rebuilt(total, half, 0, 1)
            half = mapped(t_ahead, project(psi, 3, -1))
            add_rebuilt(total, mul_link(links, 3, part, half), 3, -1)
            half = mapped(t_behind, mul_link_dag(links, 3, part, project(psi, 3, 1)))
            add_rebuilt(total, half, 3, 1)
            if z + 1 < shape.z:
                half = project(chip_psi(shape, psi_ref, part + 2), 2, -1)
                add_rebuilt(total, mul_link(links, 2, part, half), 2, -1)
            if z > 0:
                half = project(chip_psi(shape, psi_ref, part - 2), 2, 1)
                add_rebuilt(total, mul_link_dag(links, 2, part - 2, half), 2, 1)
            for s, c, n, k in components(4):
                total_ref[shape.block(k, part), :] = total[s, c][n]
        pair = (2 * z, 2 * z + 1)
        minus, carried = [], []
        for part in pair:
            psi = chip_psi(shape, psi_ref, part)
            minus.append(mapped(lambda v: pltpu.roll(v, lanes - X, 1), project(psi, 1, -1)))
            half = mul_link_dag(links, 1, part, project(psi, 1, 1))
            carried.append(mapped(lambda v: pltpu.roll(v, X, 1), half))
        for own, part in enumerate(pair):
            total = chip_psi(shape, total_ref, part)
            half = mapped(
                lambda a, b: jnp.where(lane >= lanes - X, b, a), minus[own], minus[1 - own]
            )
            add_rebuilt(total, mul_link(links, 1, part, half), 1, -1)
            half = mapped(lambda a, b: jnp.where(lane < X, b, a), carried[own], carried[1 - own])
            add_rebuilt(total, half, 1, 1)
            for s, c, n, k in components(4):
                total_ref[shape.block(k, part), :] = total[s, c][n]


def chip_sort_faces(z_second, z_first, scratch):
    z_down, z_up = scratch
    z_even = is_even("gy")
    second = 0.0 if z_second is None else z_second[...]
    first = 0.0 if z_first is None else z_first[...]
    z_down[...] = either(z_even, first, second)
    z_up[...] = either(z_even, second, first)


def chip_add_z(shape, links, part, total, scratch):
    z_down, z_up = scratch
    t, rows, lanes, parts = shape.t, shape.rows, shape.lanes, shape.parts

    def plane(ref, y_half):
        def value(k):
            face = ref[pl.ds((k * 2 + y_half) * t, t), :]
            if rows != t:
                pad = jnp.zeros((rows - t, lanes), jnp.float32)
                face = jnp.concatenate([face, pad], axis=0)
            return face

        return gathered_pairs(2, value)

    if part >= parts - 2:
        half = mul_link(links, 2, part, plane(z_down, part - parts + 2))
        add_rebuilt(total, half, 2, -1)
    if part < 2:
        add_rebuilt(total, plane(z_up, part), 2, 1)


def chip_finish(
    shape, psi_ref, links_ref, total_ref, received, scratch, out_ref, face_ref=None
):
    z_second, t_second, z_first, t_first = received
    t_even = is_even("ta")
    t, lanes, parts = shape.t, shape.lanes, shape.parts
    chip_sort_faces(z_second, z_first, scratch)
    links = ChipLinks(shape, links_ref)

    for part in range(parts):
        total = chip_psi(shape, total_ref, part)
        chip_add_z(shape, links, part, total, scratch)
        for s, c, n, k in components(4):
            value = total[s, c][n]
            if face_ref is not None:
                value = value + face_ref[shape.block(k, part), :]
            value = psi_ref[shape.block(k, part), :] - hop_kappa * value
            out_ref[shape.block(k, part), :] = value if s < 2 else -value

    def t_half(from_even, from_odd):
        def value(k):
            at = pl.ds(k * parts, parts)
            return either(t_even, from_even[at, :], from_odd[at, :])

        return gathered_pairs(2, value)

    down = mul_link(ChipLinks(shape, links_ref, t - 1), 3, 0, t_half(t_first, t_second))
    up = t_half(t_second, t_first)
    zero = jnp.zeros((parts, lanes), jnp.float32)
    for half, parity, row in ((down, -1, t - 1), (up, 1, 0)):
        total = {(s, c): (zero, zero) for s in range(4) for c in range(3)}
        add_rebuilt(total, half, 3, parity)
        for s, c, n, k in components(4):
            at = shape.edge(k, row)
            value = hop_kappa * total[s, c][n]
            out_ref[at, :] = out_ref[at, :] - (value if s < 2 else -value)


def chip_mid_kernel(shape, hands_over, psi_ref, links_ref, total_ref, *refs):
    received, out_ref, messages, refs = refs[:4], refs[4], refs[5:9], refs[9:]
    chip_finish(shape, psi_ref, links_ref, total_ref, received, refs[-2:], out_ref)
    chip_messages(shape, out_ref, links_ref, *messages)
    if hands_over:
        hand_over(shape, out_ref, refs[0])


def chip_sums_kernel(
    shape, links_ref, z_first, start_ref, one_ref, two_ref, three_ref,
    face_ref, copies_ref, *scratch,
):
    class View:
        def __init__(self, ref):
            self.ref = ref

        def __getitem__(self, index):
            return self.ref[shape.block(*index), :]

    wide = ChipShape(shape.t, shape.z, shape.lanes)
    wide.z = shape.parts
    row = sums_row(wide, View(two_ref), View(start_ref), View(three_ref), View(one_ref))
    copies_ref[...] = jnp.broadcast_to(row[None], copies_ref.shape)
    chip_sort_faces(None, z_first, scratch)
    zero = jnp.zeros((shape.rows, shape.lanes), jnp.float32)
    for part in range(shape.parts):
        total = {(s, c): (zero, zero) for s in range(4) for c in range(3)}
        chip_add_z(shape, ChipLinks(shape, links_ref), part, total, scratch)
        for s, c, n, k in components(4):
            face_ref[shape.block(k, part), :] = total[s, c][n]


def chip_scalars_kernel(entries, gathered, factors_ref, coefficients):
    alpha_one, beta_one, alpha_two, scale, first_factor = scalars(gathered[:, 0, :], entries)
    lanes = factors_ref.shape[1]
    values = [alpha_one, alpha_two, scale, first_factor]
    values = [jnp.broadcast_to(value, (1, lanes)) for value in values]
    values.append(jnp.zeros((4, lanes), jnp.float32))
    factors_ref[...] = jnp.concatenate(values, axis=0)
    coefficients[0] = alpha_one[0, 0]
    coefficients[1] = beta_one[0, 0]
    coefficients[2] = alpha_two[0, 0]


def y_part(shape, k, z, y_half):
    return pl.ds(pl.multiple_of((k * shape.parts + 2 * z + y_half) * shape.rows, 8), shape.rows)


def rest_rows(shape, k, z):
    return pl.ds((k * shape.z + z) * shape.rows, shape.rows)


def hand_over(shape, ref, rest_ref):
    y_half = 1 - lax.axis_index("gy")
    for k in range(24):
        for z in range(shape.z):
            rest_ref[rest_rows(shape, k, z), :] = ref[y_part(shape, k, z, y_half), :]


def chip_finish_kernel(
    shape, psi_ref, links_ref, total_ref, face_ref, z_second, t_second, t_first,
    out_ref, rest_ref, *scratch,
):
    received = z_second, t_second, None, t_first
    chip_finish(shape, psi_ref, links_ref, total_ref, received, scratch, out_ref, face_ref)
    y_half = 1 - lax.axis_index("gy")
    for k in range(24):
        for z in range(shape.z):
            value = out_ref[y_part(shape, k, z, y_half), :]
            rest_ref[dense_rows(shape, k, z), :] = value[0 : shape.t]


def dense_rows(shape, k, z):
    return pl.ds((k * shape.z + z) * shape.t, shape.t)


def chip_last_kernel(
    shape, start_ref, two_ref, four_ref, start_rest, two_rest, four_rest, factors_ref, out_ref
):
    t, z_extent = shape.t, 2 * shape.z
    alpha_one, alpha_two, scale, first_factor = (
        jnp.broadcast_to(factors_ref[k : k + 1], (t, shape.lanes)) for k in range(4)
    )
    core, first_core = lax.axis_index("gy"), is_even("gy")

    def combined(start, two, four):
        remain = two - alpha_one * start
        return (four - alpha_one * two - alpha_two * remain) * scale - first_factor * start

    for k in range(24):
        for z in range(shape.z):
            rows = y_part(shape, k, z, core)
            own = combined(*(ref[rows, :][0:t] for ref in (start_ref, two_ref, four_ref)))
            rows = rest_rows(shape, k, z)
            rest = [ref[rows, :][0:t] for ref in (start_rest, two_rest)]
            other = combined(*rest, four_rest[dense_rows(shape, k, z), :])
            first = k * t * z_extent + z
            lower, upper = either(first_core, own, other), either(first_core, other, own)
            out_ref[pl.ds(first, t, stride=z_extent), :] = lower
            out_ref[pl.ds(first + shape.z, t, stride=z_extent), :] = upper


def chip_shards(source, gauge_links):
    devices_all = lax.axis_size("ta") * lax.axis_size("gz") * 2
    entries = float(source.size * devices_all)
    z_extent = source.shape[4]
    shape = ChipShape(source.shape[3], z_extent // 2, source.shape[5])
    t, rows, lanes = shape.t, shape.rows, shape.lanes
    vmem = pl.BlockSpec(memory_space=pltpu.VMEM)
    smem = pl.BlockSpec(memory_space=pltpu.SMEM)

    def held(*dims):
        return pltpu.VMEM(dims, jnp.float32)

    field = held(24 * shape.parts * rows, lanes)
    links_field = held(72 * shape.parts * rows, lanes)
    z_face, t_face = held(shape.z_rows, lanes), held(shape.t_rows, lanes)
    messages = (z_face, t_face, z_face, t_face)
    z_faces = (z_face, z_face)

    def call(kernel, name, flops, out_shape, operands, **options):
        in_spec = options.pop("in_spec", vmem)
        out_specs = options.pop("out_specs", jax.tree.map(lambda _: vmem, out_shape))
        return pl.pallas_call(
            kernel,
            name=name,
            out_shape=out_shape,
            in_specs=[in_spec] * len(operands),
            out_specs=out_specs,
            compiler_params=pltpu.CompilerParams(vmem_limit_bytes=8 << 20),
            cost_estimate=pl.CostEstimate(flops=flops, bytes_accessed=1 << 20, transcendentals=0),
            **options,
        )(*operands)

    def exchanged(sent):
        z_second, t_second, z_first, t_first = sent
        z_ring = ("gz", "gy")
        return (
            swap(z_second, z_ring, True), swap(t_second, "ta", True),
            swap(z_first, z_ring, False), swap(t_first, "ta", False),
        )

    sites = t * z_extent * lanes
    rows_in = t * z_extent
    own = (source.reshape(24 * rows_in, lanes), gauge_links.reshape(72 * rows_in, lanes))
    other = tuple(swap(value, "gy", False) for value in own)
    rest = held(24 * shape.z * rows, lanes)
    psi, links, start_rest = call(
        functools.partial(chip_own_kernel, shape), "own", 200 * sites, (field, links_field, rest),
        [pltpu.with_memory_space_constraint(value, pltpu.HBM) for value in own],
        scratch_shapes=(
            held(24 * rows_in, lanes), held(72 * rows_in, lanes), pltpu.SemaphoreType.DMA((5,)),
        ),
        in_spec=pl.BlockSpec(memory_space=pltpu.HBM),
    )
    psi, links, *sent = call(
        functools.partial(chip_prep_kernel, shape), "prep", 400 * sites,
        (field, links_field, *messages), (*other, psi, links),
        input_output_aliases={2: 0, 3: 1},
    )
    powers = [psi]
    for step in range(3):
        halo = exchanged(sent)
        inner = functools.partial(chip_inner_kernel, shape)
        total = call(inner, "inner", 1000 * sites, field, (psi, links))
        hands_over = step == 1
        psi, *sent = call(
            functools.partial(chip_mid_kernel, shape, hands_over), "mid", 600 * sites,
            (field, *messages, rest) if hands_over else (field, *messages),
            (psi, links, total, *halo), scratch_shapes=z_faces,
        )
        powers.append(psi)
        if hands_over:
            two_rest = swap(sent.pop(), "gy", False)
    halo = exchanged(sent)
    face, copies = call(
        functools.partial(chip_sums_kernel, shape), "sums", 600 * sites,
        (field, held(devices_all, 1, lanes)), (links, halo[2], *powers), scratch_shapes=z_faces,
    )
    gathered = from_everyone(copies)
    total = call(inner, "inner", 1000 * sites, field, (psi, links))
    four, four_rest = call(
        functools.partial(chip_finish_kernel, shape), "finish", 400 * sites,
        (field, held(24 * shape.z * t, lanes)),
        (psi, links, total, face, halo[0], halo[1], halo[3]), scratch_shapes=z_faces,
    )
    four_rest = swap(four_rest, "gy", False)
    factors, coefficients = call(
        functools.partial(chip_scalars_kernel, entries), "scalars", 10**11,
        (held(8, lanes), jax.ShapeDtypeStruct((3,), jnp.float32)), (gathered,),
        out_specs=(vmem, smem),
    )
    residual = call(
        functools.partial(chip_last_kernel, shape), "last", 100 * sites,
        jax.ShapeDtypeStruct((24 * rows_in, lanes), jnp.float32),
        (powers[0], powers[2], four, start_rest, two_rest, four_rest, factors),
    )
    return (residual.reshape(source.shape), coefficients)


def solution(mesh):
    placed = (P(None, None, None, "ta", "gz", "gy"), P(None, None, None, None, "ta", "gz", "gy"))
    return jax.shard_map(
        chip_shards if mesh.shape["gy"] == 2 else shards,
        mesh=mesh,
        in_specs=placed,
        out_specs=(P(None, None, None, "ta", "gz", "gy"), P()),
        check_vma=False,
    )
```
